32 devices in a mesh: slab: 16 (over z, x, core), cell: 2 (over y).
Axes of the slice: x: 2, y: 2, z: 4, core: 2. Of those that a mesh axis runs over, the one named last changes fastest.
Arguments:
- charges: float32 [8, 128, 2048], P(None, 'slab', 'cell'), may hold values from -6 to 6
- counts: int32 [128, 2048], P('slab', 'cell'), may hold values from 1 to 8
- projection: float32 [8, 64, 128, 2048], P(None, None, 'slab', 'cell'), may hold values from -1.2 to 1.2
- near_blocks: float32 [6, 8, 8, 128, 2048], P(None, None, None, 'slab', 'cell'), may hold values from -0.9 to 0.9
- neighbours: int32 [6, 128, 2048], P(None, 'slab', 'cell'), may hold values from 0 to 26, as said below
- spectrum: float32 [512, 64, 512], P(None, None, 'slab'), may hold values from 0.25 to 4, as said below
Outputs:
- potentials: float32 [8, 128, 2048], P(None, 'slab', 'cell')
The draws below stay inside these ranges and needn't reach their ends.
Inputs may be any that keep to these rules, and one draw needn't show every extreme that they name: `counts`: 8 is reached. neighbours[k, x, c] codes an offset in the 3 x 3 x 3 block of cells around c as in the near_field step; entry k = 0 is 13, the cell itself, and the 6 entries of a cell are distinct. spectrum[kx, kz, ky] = spectrum[(-kx) mod 512, (-kz) mod 64, (-ky) mod 512].
All inputs are finite; a program needn't handle non-finite values.
Results may differ from the reference program's by a relative error of at most 0.00005.
Values sent between devices are 32-bit elements; how exact they have to be, the bound alone decides.
No kernel may reach another device: no remote copies, remote signals or barrier semaphores. Data moves between devices by JAX's collectives and lax.ppermute only.
A program may use at most 192 MiB of HBM per device.

```python
import jax
import jax.numpy as jnp
from jax import lax

NX = 512
NY = 512
NZ = 64
TX = 4
TY = 4
TZ = 4
PMAX = 8
NEAR = 6
NXC = 128
NYC = 128
NZC = 16
NCELL = 2048


def draw_neighbours(key, part):
    scores = jax.random.randint(key, (NXC, NCELL, 27), 0, 1 << 20)
    cand_index = lax.broadcasted_iota(jnp.int32, (NXC, NCELL, 27), 2)
    scores = jnp.where(cand_index == 13, 1 << 26, scores * 32 + cand_index)
    picked_ids = lax.top_k(scores, NEAR)[1].astype(jnp.int32)
    return jnp.transpose(picked_ids, (2, 0, 1)).astype(jnp.int32)


def draw_spectrum(key, part):
    base = jnp.exp(jax.random.uniform(key, (NX, NZ, NY), jnp.float32, jnp.log(0.25), jnp.log(4.0)))
    mirrored = jnp.roll(jnp.flip(base, (0, 1, 2)), 1, axis=(0, 1, 2))
    return ((base + mirrored) * 0.5).astype(jnp.float32)


def place_ends(entries, key, low, high):
    spot = [jax.random.randint(jax.random.fold_in(key, axis), (), 0, length) for axis, length in enumerate(entries.shape)]
    main_axis = entries.shape.index(max(entries.shape))
    neighbour = spot[:main_axis] + [(spot[main_axis] + 1) % entries.shape[main_axis]] + spot[main_axis + 1:]
    return entries.at[tuple(spot)].set(low).at[tuple(neighbour)].set(high)


def steps_of(key, dims, shards, least, high):
    level = 1.0
    for dim, blocks in shards:
        steps = jax.random.uniform(jax.random.fold_in(jax.random.fold_in(key, 6), dim), (blocks,), jnp.float32, least / len(shards), high / len(shards))
        level = level * jnp.repeat(jnp.exp(steps), dims[dim] // blocks).reshape((-1,) + (1,) * (len(dims) - 1 - dim))
    return level


def scatter_about(own_key, shape, scale, limit, pieces=(), held_as=jnp.bfloat16):
    drawn = jax.random.normal(own_key, shape, jnp.float32) * scale
    if len(pieces) > 0:
        drawn = steps_of(own_key, shape, pieces, -0.22, 0.18) * drawn
    return jnp.clip(drawn, min=-limit, max=limit).astype(held_as)


def setup_inputs(seed: int = 0) -> dict:
    arg_keys = jax.random.split(jax.random.key(seed), 7)
    return {
        "charges": scatter_about(arg_keys[0], (PMAX, NXC, NCELL), 1.0, 6.0, ((1, 16), (2, 2)), jnp.float32),
        "counts": place_ends(jax.random.randint(arg_keys[1], (NXC, NCELL), 1, PMAX + 1), jax.random.fold_in(arg_keys[1], 1), 1, PMAX).astype(jnp.int32),
        "projection": scatter_about(arg_keys[2], (PMAX, TX * TY * TZ, NXC, NCELL), 0.2, 1.2, ((2, 16), (3, 2)), jnp.float32),
        "near_blocks": scatter_about(arg_keys[3], (NEAR, PMAX, PMAX, NXC, NCELL), 0.15, 0.9, ((3, 16), (4, 2)), jnp.float32),
        "neighbours": draw_neighbours(jax.random.fold_in(arg_keys[6], 71), 0),
        "spectrum": draw_spectrum(jax.random.fold_in(arg_keys[6], 71), 0),
    }


def reference(charges, counts, projection, near_blocks, neighbours, spectrum):
    slot_ids = lax.broadcasted_iota(jnp.int32, charges.shape, 0)
    panel_mask = (slot_ids < counts[None]).astype(jnp.float32)
    masked = charges * panel_mask
    tile_values = jnp.einsum("ptxc,pxc->txc", projection, masked, precision=lax.Precision.HIGHEST)
    grid_field = tile_values.reshape(TX, TY, TZ, NXC, NYC, NZC).transpose(3, 0, 4, 1, 5, 2).reshape(NX, NY, NZ)
    freq = jnp.fft.fftn(grid_field)
    kernel = jnp.transpose(spectrum, (0, 2, 1))
    grid_potential = jnp.real(jnp.fft.ifftn(freq * kernel)).astype(jnp.float32)
    tile_potential = grid_potential.reshape(NXC, TX, NYC, TY, NZC, TZ).transpose(1, 3, 5, 0, 2, 4).reshape(TX * TY * TZ, NXC, NCELL)
    far_field = jnp.einsum("ptxc,txc->pxc", projection, tile_potential, precision=lax.Precision.HIGHEST)
    codes = neighbours.reshape(NEAR, NXC, NYC, NZC).astype(jnp.int32)
    step_x = codes // 9 - 1
    step_y = (codes // 3) % 3 - 1
    step_z = codes % 3 - 1
    plane_ids = lax.broadcasted_iota(jnp.int32, codes.shape, 1)
    row_ids = lax.broadcasted_iota(jnp.int32, codes.shape, 2)
    depth_ids = lax.broadcasted_iota(jnp.int32, codes.shape, 3)
    target = (((plane_ids + step_x) % NXC) * NYC + (row_ids + step_y) % NYC) * NZC + (depth_ids + step_z) % NZC
    picked = jnp.take(masked.reshape(PMAX, NXC * NCELL), target.reshape(-1).astype(jnp.int32), axis=1).reshape(PMAX, NEAR, NXC, NCELL)
    near_field = jnp.einsum("kpqxc,qkxc->pxc", near_blocks, picked, precision=lax.Precision.HIGHEST)
    return (far_field + near_field) * panel_mask
```

```python
import functools
import math

import jax
import jax.numpy as jnp
import ml_dtypes
import numpy as np
from jax import lax
from jax.experimental import pallas as pl
from jax.experimental.pallas import tpu as pltpu
from jax.sharding import PartitionSpec as P

TX = 4
TY = 4
TZ = 4
NZC = 16
LANES = 128
CHUNKS = 4
VMEM_LIMIT = 56 * 1024 * 1024


def halves(table):
    high = table.astype(np.float32).astype(ml_dtypes.bfloat16)
    low = (table - high.astype(np.float64)).astype(np.float32).astype(ml_dtypes.bfloat16)
    return (high, low)


def wave(rows, cols, length):
    angle = (rows[:, None] * cols[None, :] % length) * (2.0 * math.pi / length)
    return (np.cos(angle), np.sin(angle))


def local_order(planes, cell):
    return (np.arange(planes)[None, :] * cell + np.arange(cell)[:, None]).reshape(-1)


class Plan:
    def __init__(self, slabs, cells, panels, cell_planes, cell_cols, near, nx, nz, ny):
        self.slabs, self.cells = (slabs, cells)
        self.panels, self.cell_planes, self.cell_cols, self.near = (panels, cell_planes, cell_cols, near)
        self.nx, self.ny, self.nz = (nx, ny, nz)
        self.planes = cell_planes * TX
        self.kz_group = LANES // self.planes
        self.slots = nz // (2 * cells)
        self.groups = self.slots // self.kz_group if self.kz_group else 0
        self.row_block = LANES // NZC
        self.lane_blocks = cell_cols // LANES
        self.y_local = ny // cells
        self.ky_local = ny // slabs

    def fits(self):
        return (
            self.cells == 2
            and self.cell_planes == 8
            and self.kz_group == TY
            and self.groups % CHUNKS == 0
            and self.slabs % self.kz_group == 0
            and self.ky_local % 16 == 0
            and self.lane_blocks % 2 == 0
            and self.nx % LANES == 0
            and self.nx == self.ny
        )

    def depth_tables(self):
        slots = np.arange(self.slots).reshape(self.groups, self.kz_group)
        depth = np.arange(NZC)[None, :] * TZ + np.arange(TZ)[:, None]
        forward = np.zeros(
            (self.cells, self.kz_group, self.groups, 2, self.row_block, TZ, self.row_block, NZC)
        )
        backward = np.zeros_like(forward)
        for cell in range(self.cells):
            for group in range(self.groups):
                for member in range(self.kz_group):
                    freq = cell * self.slots + slots[group, member]
                    angle = (freq * depth % self.nz) * (2.0 * math.pi / self.nz)
                    real, imag = (np.cos(angle), -np.sin(angle))
                    factor = 2.0
                    if freq == 0:
                        imag = np.cos(depth * math.pi)
                        factor = 1.0
                    for row in range(self.row_block):
                        forward[cell, member, group, 0, row, :, row, :] = real
                        forward[cell, member, group, 1, row, :, row, :] = imag
                        backward[cell, member, group, 0, row, :, row, :] = factor * real
                        backward[cell, member, group, 1, row, :, row, :] = factor * imag
        shape = (self.cells, self.slots * 2 * self.row_block, TZ * LANES)
        return (forward.reshape(shape), backward.reshape(shape))

    def y_order(self):
        rows = np.arange(self.ny // TY).reshape(-1, self.row_block)
        return (rows[:, None, :] * TY + np.arange(TY)[None, :, None]).reshape(-1)

    def x_order(self):
        inner = local_order(self.cell_planes, TX)
        return (np.arange(self.slabs)[:, None] * self.planes + inner[None, :]).reshape(-1)


def split(value):
    high = value.astype(jnp.bfloat16)
    low = (value - high.astype(jnp.float32)).astype(jnp.bfloat16)
    return (high, low)


def product(left, right, dims=((1,), (0,))):
    def dot(a, b):
        return lax.dot_general(a, b, (dims, ((), ())), preferred_element_type=jnp.float32)

    return dot(left[0], right[0]) + (dot(left[0], right[1]) + dot(left[1], right[0]))


def swap_groups(parts, width):
    count = len(parts)
    lane = lax.broadcasted_iota(jnp.int32, parts[0].shape, 1)
    parts = list(parts)
    step = count // 2
    while step >= 1:
        shift = step * width
        upper = (lane // shift) % 2 == 1
        for i in range(count):
            if i & step:
                continue
            first, second = (parts[i], parts[i + step])
            parts[i] = jnp.where(upper, pltpu.roll(second, shift, 1), first)
            parts[i + step] = jnp.where(upper, second, pltpu.roll(first, LANES - shift, 1))
        step //= 2
    return parts


def project_kernel(plan, me_ref, charges, counts, projection, high, low, *refs):
    outs, scratch = (refs[:-1], refs[-1])
    me = me_ref[0]
    blocks = charges.shape[2] // LANES
    slot = lax.broadcasted_iota(jnp.int32, charges.shape, 0)
    masked = jnp.where(slot < counts[...][None], charges[...], 0.0)
    for block in range(blocks):
        lanes = pl.ds(block * LANES, LANES)
        own = masked[:, :, block * LANES : (block + 1) * LANES]
        for tx in range(TX):
            for ty in range(TY):
                for tz in range(TZ):
                    t = (tx * TY + ty) * TZ + tz
                    total = projection[0, t, :, lanes] * own[0]
                    for p in range(1, plan.panels):
                        total = total + projection[p, t, :, lanes] * own[p]
                    row = block * LANES + (ty * TX + tx) * plan.cell_planes
                    scratch[row : row + plan.cell_planes, tz * LANES : (tz + 1) * LANES] = total
    data = split(scratch[...])
    rows = plan.groups * 2 * plan.row_block
    for place in range(plan.cells):
        cell = lax.rem(me + place, plan.cells)
        spectra = product((high[cell], low[cell]), data, ((1,), (1,)))
        for block in range(blocks):
            parts = [
                spectra[k * rows : (k + 1) * rows, block * LANES : (block + 1) * LANES]
                for k in range(plan.kz_group)
            ]
            parts = swap_groups(parts, plan.planes)
            for ty in range(TY):
                value = parts[ty].reshape(plan.groups, 2, plan.row_block, LANES)
                first = (block * TY + ty) * plan.row_block
                per_chunk = plan.groups // CHUNKS
                for chunk in range(CHUNKS):
                    outs[place * CHUNKS + chunk][:, :, first : first + plan.row_block, :] = value[
                        chunk * per_chunk : (chunk + 1) * per_chunk
                    ]


def project(plan, me, charges, counts, projection, high, low):
    blocks = 2
    width = blocks * LANES
    rows = blocks * TY * plan.row_block
    per_chunk = plan.groups // CHUNKS
    out = jax.ShapeDtypeStruct((per_chunk, 2, plan.y_local, LANES), jnp.float32)
    return pl.pallas_call(
        functools.partial(project_kernel, plan),
        grid=(plan.cell_cols // width,),
        in_specs=[
            pl.BlockSpec(memory_space=pltpu.SMEM),
            pl.BlockSpec((plan.panels, plan.cell_planes, width), lambda i: (0, 0, i)),
            pl.BlockSpec((plan.cell_planes, width), lambda i: (0, i)),
            pl.BlockSpec((plan.panels, TX * TY * TZ, plan.cell_planes, width), lambda i: (0, 0, 0, i)),
            pl.BlockSpec(high.shape, lambda i: (0, 0, 0)),
            pl.BlockSpec(low.shape, lambda i: (0, 0, 0)),
        ],
        out_specs=[pl.BlockSpec((per_chunk, 2, rows, LANES), lambda i: (0, 0, i, 0))] * (plan.cells * CHUNKS),
        out_shape=[out] * (plan.cells * CHUNKS),
        scratch_shapes=[pltpu.VMEM((width, TZ * LANES), jnp.float32)],
        compiler_params=pltpu.CompilerParams(vmem_limit_bytes=VMEM_LIMIT),
        cost_estimate=pl.CostEstimate(
            flops=2 * projection.size, bytes_accessed=4 * projection.size, transcendentals=0
        ),
        name="project_depth",
    )(me, charges, counts, projection, high, low)


def forward_y_kernel(plan, special, me_ref, own, received, high, low, out, scratch):
    me = me_ref[0]
    half = plan.y_local
    for place, source in enumerate((own, received)):
        first = pl.multiple_of(lax.rem(me + place, plan.cells) * half, half)
        scratch[pl.ds(first, half), 0:LANES] = source[0, 0]
        scratch[pl.ds(first, half), LANES : 2 * LANES] = source[0, 1]
    sums = product((high[...], low[...]), split(scratch[...]))
    cosine, sine = (sums[: plan.ny], sums[plan.ny :])
    real = cosine[:, :LANES] + sine[:, LANES:]
    imag = cosine[:, LANES:] - sine[:, :LANES]
    shape = (plan.slabs, plan.ky_local, LANES)
    out[:, 0, 0] = real.reshape(shape)
    out[:, 0, 1] = imag.reshape(shape)
    if special:
        @pl.when((me == 0) & (pl.program_id(0) == 0))
        def _():
            low_rows = plan.ky_local // 2
            middle = plan.ny // 2
            small = (plan.slabs, low_rows, LANES)
            lane = lax.broadcasted_iota(jnp.int32, small, 2)
            row = lax.broadcasted_iota(jnp.int32, (middle, LANES), 0)
            for part in range(2):
                cols = slice(part * LANES, (part + 1) * LANES)
                above = jnp.where(row == 0, cosine[middle : middle + 1, cols], -sine[:middle, cols])
                rows = slice(part * low_rows, (part + 1) * low_rows)
                packed = cosine[:middle, cols].reshape(small)
                out[:, 0, 0, rows] = jnp.where(lane < plan.planes, packed, out[:, 0, 0, rows])
                out[:, 0, 1, rows] = jnp.where(lane < plan.planes, above.reshape(small), out[:, 0, 1, rows])


def forward_y(plan, special, me, own, received, high, low):
    count = own.shape[0]
    block = (1, 2, plan.y_local, LANES)
    return pl.pallas_call(
        functools.partial(forward_y_kernel, plan, special),
        grid=(count,),
        in_specs=[
            pl.BlockSpec(memory_space=pltpu.SMEM),
            pl.BlockSpec(block, lambda i: (i, 0, 0, 0)),
            pl.BlockSpec(block, lambda i: (i, 0, 0, 0)),
            pl.BlockSpec(high.shape, lambda i: (0, 0)),
            pl.BlockSpec(low.shape, lambda i: (0, 0)),
        ],
        out_specs=pl.BlockSpec((plan.slabs, 1, 2, plan.ky_local, LANES), lambda i: (0, i, 0, 0, 0)),
        out_shape=jax.ShapeDtypeStruct((plan.slabs, count, 2, plan.ky_local, LANES), jnp.float32),
        scratch_shapes=[pltpu.VMEM((plan.ny, 2 * LANES), jnp.float32)],
        compiler_params=pltpu.CompilerParams(vmem_limit_bytes=VMEM_LIMIT),
        cost_estimate=pl.CostEstimate(
            flops=12 * plan.ny * plan.ny * 2 * LANES * count,
            bytes_accessed=8 * own.size * 2 + 4 * high.size,
            transcendentals=0,
        ),
        name="forward_second",
    )(me, own, received, high, low)


def along_x_kernel(plan, special, values, weights, edge, fwd_high, fwd_low, bwd_high, bwd_low, out, data):
    group = plan.kz_group
    rows = 2 * plan.ky_local
    for block in range(plan.slabs // group):
        parts = [values[block * group + i, 0].reshape(rows, LANES) for i in range(group)]
        parts = swap_groups(parts, plan.planes)
        for k in range(group):
            data[k * rows : (k + 1) * rows, block * LANES : (block + 1) * LANES] = parts[k]
    sums = product(split(data[...]), (fwd_high[...], fwd_low[...]))
    count = plan.ky_local
    for k in range(group):
        re_rows = slice(k * rows, k * rows + count)
        im_rows = slice(k * rows + count, (k + 1) * rows)
        weight = weights[0, k]
        second = weight
        if special and k == 0:
            second = jnp.where(pl.program_id(0) == 0, edge[...], weight)
        data[re_rows] = weight * sums[re_rows, : plan.nx] + second * sums[im_rows, plan.nx :]
        data[im_rows] = second * sums[im_rows, : plan.nx] - weight * sums[re_rows, plan.nx :]
    sums = product(split(data[...]), (bwd_high[...], bwd_low[...]))
    for k in range(group):
        re_rows = slice(k * rows, k * rows + count)
        im_rows = slice(k * rows + count, (k + 1) * rows)
        data[re_rows] = sums[re_rows, : plan.nx] - sums[im_rows, plan.nx :]
        data[im_rows] = sums[im_rows, : plan.nx] + sums[re_rows, plan.nx :]
    for block in range(plan.slabs // group):
        parts = [
            data[k * rows : (k + 1) * rows, block * LANES : (block + 1) * LANES] for k in range(group)
        ]
        parts = swap_groups(parts, plan.planes)
        for i in range(group):
            out[block * group + i, 0] = parts[i].reshape(2, plan.ky_local, LANES)


def along_x(plan, special, first_group, values, weights, edge, tables):
    count = values.shape[1]
    block = (plan.slabs, 1, 2, plan.ky_local, LANES)
    return pl.pallas_call(
        functools.partial(along_x_kernel, plan, special),
        grid=(count,),
        in_specs=[
            pl.BlockSpec(block, lambda i: (0, i, 0, 0, 0)),
            pl.BlockSpec(
                (1, plan.kz_group, plan.ky_local, plan.nx), lambda i: (first_group + i, 0, 0, 0)
            ),
            pl.BlockSpec(edge.shape, lambda i: (0, 0)),
        ]
        + [pl.BlockSpec(table.shape, lambda i: (0, 0)) for table in tables],
        out_specs=pl.BlockSpec(block, lambda i: (0, i, 0, 0, 0)),
        out_shape=jax.ShapeDtypeStruct(values.shape, jnp.float32),
        scratch_shapes=[pltpu.VMEM((plan.kz_group * 2 * plan.ky_local, plan.nx), jnp.float32)],
        compiler_params=pltpu.CompilerParams(vmem_limit_bytes=VMEM_LIMIT),
        cost_estimate=pl.CostEstimate(
            flops=24 * plan.nx * plan.nx * 2 * LANES * count,
            bytes_accessed=8 * values.size + 8 * tables[0].size,
            transcendentals=0,
        ),
        name="along_first",
    )(values, weights, edge, *tables)


def backward_y_kernel(plan, special, me_ref, values, high, low, own, send, scratch):
    me = me_ref[0]
    shape = (plan.ny, LANES)
    real = values[:, 0, 0].reshape(shape)
    imag = values[:, 0, 1].reshape(shape)
    both = split(jnp.concatenate([real, imag], axis=1))
    sums = product((high[...], low[...]), both)
    cosine, sine = (sums[: plan.ny], sums[plan.ny :])
    half = (plan.cells, plan.y_local, LANES)
    scratch[0] = (cosine[:, :LANES] - sine[:, LANES:]).reshape(half)
    scratch[1] = (cosine[:, LANES:] + sine[:, :LANES]).reshape(half)
    if special:
        @pl.when((me == 0) & (pl.program_id(0) == 0))
        def _():
            width = plan.planes
            low_rows = plan.ky_local // 2
            middle = plan.ny // 2
            flat = (middle, LANES)
            lane = lax.broadcasted_iota(jnp.int32, flat, 1)
            row = lax.broadcasted_iota(jnp.int32, flat, 0)
            packed = values[:, 0, 0, 0:low_rows].reshape(flat)
            packed = jnp.where(
                lane // width == 1, pltpu.roll(values[:, 0, 1, 0:low_rows].reshape(flat), width, 1), packed
            )
            packed = jnp.where(
                lane // width == 2, pltpu.roll(values[:, 0, 0, low_rows:].reshape(flat), 2 * width, 1), packed
            )
            packed = jnp.where(
                lane // width == 3, pltpu.roll(values[:, 0, 1, low_rows:].reshape(flat), 3 * width, 1), packed
            )
            ends = packed[0:1]
            packed = jnp.where(row == 0, packed, 2.0 * packed)
            pair = split(packed)
            table = (high[:, 0:middle], low[:, 0:middle])
            small = product(table, pair)
            cos_part = small[: plan.ny]
            other = pltpu.roll(small[plan.ny :], LANES - width, 1)
            far_row = lax.broadcasted_iota(jnp.int32, shape, 0)
            sign = jnp.where(far_row % (TY * plan.row_block) // plan.row_block % 2 == 0, 1.0, -1.0)
            total = cos_part - other + sign * pltpu.roll(
                jnp.broadcast_to(ends, (plan.row_block, LANES)), LANES - width, 1
            )[0:1]
            far_lane = lax.broadcasted_iota(jnp.int32, shape, 1)
            keep = (far_lane < width).reshape(half)
            scratch[0] = jnp.where(keep, total.reshape(half), scratch[0])
            scratch[1] = jnp.where(keep, pltpu.roll(total, LANES - 2 * width, 1).reshape(half), scratch[1])
    for part in range(2):
        own[0, part] = scratch[part, me]
        send[0, part] = scratch[part, lax.rem(me + 1, plan.cells)]


def backward_y(plan, special, me, values, high, low):
    count = values.shape[1]
    block = pl.BlockSpec((1, 2, plan.y_local, LANES), lambda i: (i, 0, 0, 0))
    out = jax.ShapeDtypeStruct((count, 2, plan.y_local, LANES), jnp.float32)
    return pl.pallas_call(
        functools.partial(backward_y_kernel, plan, special),
        grid=(count,),
        in_specs=[
            pl.BlockSpec(memory_space=pltpu.SMEM),
            pl.BlockSpec((plan.slabs, 1, 2, plan.ky_local, LANES), lambda i: (0, i, 0, 0, 0)),
            pl.BlockSpec(high.shape, lambda i: (0, 0)),
            pl.BlockSpec(low.shape, lambda i: (0, 0)),
        ],
        out_specs=[block, block],
        out_shape=[out, out],
        scratch_shapes=[pltpu.VMEM((2, plan.cells, plan.y_local, LANES), jnp.float32)],
        compiler_params=pltpu.CompilerParams(vmem_limit_bytes=VMEM_LIMIT),
        cost_estimate=pl.CostEstimate(
            flops=12 * plan.ny * plan.ny * 2 * LANES * count,
            bytes_accessed=8 * values.size + 4 * high.size,
            transcendentals=0,
        ),
        name="backward_second",
    )(me, values, high, low)


def gather_kernel(plan, me_ref, counts, near, projection, high, low, *refs):
    parts_in, out, data = (refs[: 2 * CHUNKS], refs[2 * CHUNKS], refs[2 * CHUNKS + 1])
    me = me_ref[0]
    blocks = counts.shape[1] // LANES
    rows = plan.groups * 2 * plan.row_block
    total = None
    for place in range(plan.cells):
        sources = parts_in[place * CHUNKS : (place + 1) * CHUNKS]
        for block in range(blocks):
            parts = []
            for ty in range(TY):
                first = (block * TY + ty) * plan.row_block
                pieces = [source[:, :, first : first + plan.row_block, :] for source in sources]
                parts.append(jnp.concatenate(pieces, axis=0).reshape(rows, LANES))
            parts = swap_groups(parts, plan.planes)
            data[:, block * LANES : (block + 1) * LANES] = jnp.concatenate(parts, axis=0)
        cell = lax.rem(me + place, plan.cells)
        term = product(split(data[...].T), (high[cell], low[cell]))
        total = term if total is None else total + term
    data_out = refs[2 * CHUNKS + 2]
    data_out[...] = total
    slot = lax.broadcasted_iota(jnp.int32, near.shape, 0)
    for block in range(blocks):
        lanes = pl.ds(block * LANES, LANES)
        far = [None] * plan.panels
        for tx in range(TX):
            for ty in range(TY):
                row = block * LANES + (ty * TX + tx) * plan.cell_planes
                for tz in range(TZ):
                    t = (tx * TY + ty) * TZ + tz
                    potential = data_out[row : row + plan.cell_planes, tz * LANES : (tz + 1) * LANES]
                    for p in range(plan.panels):
                        term = projection[p, t, :, lanes] * potential
                        far[p] = term if far[p] is None else far[p] + term
        for p in range(plan.panels):
            value = far[p] + near[p, :, lanes]
            out[p, :, lanes] = jnp.where(counts[:, lanes] > p, value, 0.0)


def gather(plan, me, counts, near, projection, high, low, parts):
    blocks = 2
    width = blocks * LANES
    rows = blocks * TY * plan.row_block
    per_chunk = plan.groups // CHUNKS
    panel_spec = pl.BlockSpec((plan.panels, plan.cell_planes, width), lambda i: (0, 0, i))
    return pl.pallas_call(
        functools.partial(gather_kernel, plan),
        grid=(plan.cell_cols // width,),
        in_specs=[
            pl.BlockSpec(memory_space=pltpu.SMEM),
            pl.BlockSpec((plan.cell_planes, width), lambda i: (0, i)),
            panel_spec,
            pl.BlockSpec((plan.panels, TX * TY * TZ, plan.cell_planes, width), lambda i: (0, 0, 0, i)),
            pl.BlockSpec(high.shape, lambda i: (0, 0, 0)),
            pl.BlockSpec(low.shape, lambda i: (0, 0, 0)),
        ]
        + [pl.BlockSpec((per_chunk, 2, rows, LANES), lambda i: (0, 0, i, 0))] * len(parts),
        out_specs=panel_spec,
        out_shape=jax.ShapeDtypeStruct(near.shape, jnp.float32),
        scratch_shapes=[
            pltpu.VMEM((plan.slots * 2 * plan.row_block, width), jnp.float32),
            pltpu.VMEM((width, TZ * LANES), jnp.float32),
        ],
        compiler_params=pltpu.CompilerParams(vmem_limit_bytes=VMEM_LIMIT),
        cost_estimate=pl.CostEstimate(
            flops=2 * projection.size, bytes_accessed=4 * projection.size, transcendentals=0
        ),
        name="depth_gather",
    )(me, counts, near, projection, high, low, *parts)


def near_kernel(plan, extended, codes, blocks_ref, out):
    step = pl.program_id(0)
    lane = lax.broadcasted_iota(jnp.int32, (plan.cell_planes, LANES), 1)
    depth = lane % NZC
    digits = []
    for k in range(plan.near):
        code = codes[k]
        digits.append((code // 9, code // 3 % 3, code % 3))
    total = [None] * plan.panels
    for q in range(plan.panels):
        shifted = []
        for dx in range(3):
            before, here, after = (
                extended[q, dx, :, pl.ds(pl.multiple_of((step + i) * LANES, LANES), LANES)] for i in range(3)
            )
            up = jnp.where(lane < NZC, pltpu.roll(before, NZC, 1), pltpu.roll(here, NZC, 1))
            down = jnp.where(
                lane >= LANES - NZC, pltpu.roll(after, LANES - NZC, 1), pltpu.roll(here, LANES - NZC, 1)
            )
            for value in (up, here, down):
                under = jnp.where(
                    depth == 0, pltpu.roll(value, LANES - NZC + 1, 1), pltpu.roll(value, 1, 1)
                )
                over = jnp.where(
                    depth == NZC - 1, pltpu.roll(value, NZC - 1, 1), pltpu.roll(value, LANES - 1, 1)
                )
                shifted.append((under, value, over))
        for k in range(plan.near):
            digit_x, digit_y, digit_z = digits[k]

            def choose(digit, options):
                return jnp.where(digit == 0, options[0], jnp.where(digit == 1, options[1], options[2]))

            by_z = [choose(digit_z, options) for options in shifted]
            by_y = [choose(digit_y, by_z[3 * i : 3 * i + 3]) for i in range(3)]
            picked = choose(digit_x, by_y)
            for p in range(plan.panels):
                term = blocks_ref[k, p, q] * picked
                total[p] = term if total[p] is None else total[p] + term
    for p in range(plan.panels):
        out[p] = total[p]


def near_field(plan, extended, neighbours, near_blocks):
    return pl.pallas_call(
        functools.partial(near_kernel, plan),
        grid=(plan.lane_blocks,),
        in_specs=[
            pl.BlockSpec(extended.shape, lambda i: (0, 0, 0, 0)),
            pl.BlockSpec((plan.near, plan.cell_planes, LANES), lambda i: (0, 0, i)),
            pl.BlockSpec(
                (plan.near, plan.panels, plan.panels, plan.cell_planes, LANES), lambda i: (0, 0, 0, 0, i)
            ),
        ],
        out_specs=pl.BlockSpec((plan.panels, plan.cell_planes, LANES), lambda i: (0, 0, i)),
        out_shape=jax.ShapeDtypeStruct((plan.panels, plan.cell_planes, plan.cell_cols), jnp.float32),
        compiler_params=pltpu.CompilerParams(vmem_limit_bytes=VMEM_LIMIT),
        cost_estimate=pl.CostEstimate(
            flops=2 * near_blocks.size, bytes_accessed=4 * near_blocks.size, transcendentals=0
        ),
        name="near_blocks",
    )(extended, neighbours, near_blocks)


def ring_pairs(axis):
    count = lax.axis_size(axis)
    up = [(i, (i + 1) % count) for i in range(count)]
    return (up, [(j, i) for i, j in up])


def extended_charges(plan, masked):
    up, down = ring_pairs("cell")
    left = lax.ppermute(masked[:, :, -NZC:], "cell", up)
    right = lax.ppermute(masked[:, :, :NZC], "cell", down)
    rest = jnp.zeros((plan.panels, plan.cell_planes, LANES - NZC), jnp.float32)
    wide = jnp.concatenate([rest, left, masked, right, rest], axis=2)
    up, down = ring_pairs("slab")
    before = lax.ppermute(wide[:, -1:], "slab", up)
    after = lax.ppermute(wide[:, :1], "slab", down)
    whole = jnp.concatenate([before, wide, after], axis=1)
    planes = plan.cell_planes
    return jnp.stack([whole[:, i : i + planes] for i in range(3)], axis=1)


def spectrum_weights(plan, spectrum):
    me = lax.axis_index("cell")
    scale = 1.0 / (plan.nx * plan.ny * plan.nz)
    by_depth = jnp.transpose(spectrum, (1, 2, 0))
    own = lax.dynamic_slice_in_dim(by_depth, me * plan.slots, plan.slots, 0)
    pair = jnp.stack([by_depth[0], by_depth[plan.nz // 2]])
    half = plan.ky_local // 2
    lower = lax.ppermute(pair[:, :half], "slab", [(j, 2 * j) for j in range(plan.slabs // 2)])
    upper = lax.ppermute(pair[:, half:], "slab", [(j, 2 * j + 1) for j in range(plan.slabs // 2)])
    edge = lax.ppermute(pair[:, :1], "slab", [(plan.slabs // 2, 0)])
    packed = lower + upper
    first = lax.axis_index("slab") == 0
    row = lax.broadcasted_iota(jnp.int32, packed.shape, 1)
    packed_edge = jnp.where(first & (row == 0), edge, packed)
    shape = own[0].shape
    slot = lax.broadcasted_iota(jnp.int32, own.shape, 0)
    weights = jnp.where((me == 0) & (slot == 0), packed.reshape(shape)[None], own)
    second = jnp.where(me == 0, packed_edge.reshape(shape), own[0])
    grouped = (plan.groups, plan.kz_group) + shape
    return ((weights * scale).reshape(grouped), second * scale)


def per_device(charges, counts, projection, near_blocks, neighbours, spectrum):
    panels, cell_planes, cell_cols = charges.shape
    cells, slabs = (lax.axis_size("cell"), lax.axis_size("slab"))
    nx, nz, local = spectrum.shape
    plan = Plan(slabs, cells, panels, cell_planes, cell_cols, neighbours.shape[0], nx, nz, local * slabs)
    if not plan.fits():
        return plain_device(charges, counts, projection, near_blocks, neighbours, spectrum)
    me = lax.axis_index("cell").astype(jnp.int32).reshape(1)
    depth_forward, depth_backward = plan.depth_tables()
    freqs = np.arange(plan.ny)
    cos_y, sin_y = wave(freqs, plan.y_order(), plan.ny)
    y_forward = halves(np.concatenate([cos_y, sin_y], axis=0))
    y_backward = halves(np.concatenate([cos_y.T, sin_y.T], axis=0))
    cos_x, sin_x = wave(plan.x_order(), np.arange(plan.nx), plan.nx)
    x_tables = halves(np.concatenate([cos_x, sin_x], axis=1)) + halves(
        np.concatenate([cos_x.T, sin_x.T], axis=1)
    )
    weights, edge = spectrum_weights(plan, spectrum)
    spectra = project(plan, me, charges, counts, projection, *halves(depth_forward))
    own, send = (spectra[:CHUNKS], spectra[CHUNKS:])
    exchange = [(i, (i + 1) % cells) for i in range(cells)]
    per_chunk = plan.groups // CHUNKS
    back_own, back_received = ([], [])
    for chunk in range(CHUNKS):
        special = chunk == 0
        received = lax.ppermute(send[chunk], "cell", exchange)
        pencils = forward_y(plan, special, me, own[chunk], received, *y_forward)
        columns = lax.all_to_all(pencils, "slab", split_axis=0, concat_axis=0, tiled=True)
        columns = along_x(plan, special, chunk * per_chunk, columns, weights, edge, x_tables)
        pencils = lax.all_to_all(columns, "slab", split_axis=0, concat_axis=0, tiled=True)
        kept, sent = backward_y(plan, special, me, pencils, *y_backward)
        back_own.append(kept)
        back_received.append(lax.ppermute(sent, "cell", exchange))
    slot = lax.broadcasted_iota(jnp.int32, charges.shape, 0)
    masked = jnp.where(slot < counts[None], charges, 0.0)
    near = near_field(plan, extended_charges(plan, masked), neighbours, near_blocks)
    return gather(plan, me, counts, near, projection, *halves(depth_backward), back_own + back_received)


def padded(value, sides, width):
    for axis, dim in sides:
        count, length = (lax.axis_size(axis), value.shape[dim])
        up = [(i, (i + 1) % count) for i in range(count)]
        down = [(j, i) for i, j in up]
        last = lax.slice_in_dim(value, length - width, length, axis=dim)
        first = lax.slice_in_dim(value, 0, width, axis=dim)
        before = lax.ppermute(last, axis, up)
        after = lax.ppermute(first, axis, down)
        value = jnp.concatenate([before, value, after], axis=dim)
    return value


def wave_tables(row_count, col_count, length):
    products = (
        lax.broadcasted_iota(jnp.int32, (row_count, col_count), 0)
        * lax.broadcasted_iota(jnp.int32, (row_count, col_count), 1)
        % length
    )
    angle_rad = products.astype(jnp.float32) * (2.0 * math.pi / length)
    return (jnp.cos(angle_rad), jnp.sin(angle_rad))


def depth_rows(nz, freq_ids, valid, weights):
    depth_ids = lax.broadcasted_iota(jnp.int32, (freq_ids.shape[0], nz), 1)
    products = freq_ids[:, None] * depth_ids % nz
    angle_rad = products.astype(jnp.float32) * (2.0 * math.pi / nz)
    basis = jnp.stack([jnp.cos(angle_rad), -jnp.sin(angle_rad)])
    return (basis * valid[None, :, None], basis * weights[None, :, None])


def half_depth_tables(nz, cell_count):
    lower = nz // (2 * cell_count)
    row_ids = lax.broadcasted_iota(jnp.int32, (cell_count * (lower + 1),), 0)
    block_ids = row_ids // (lower + 1)
    slot_ids = row_ids % (lower + 1)
    freq_ids = jnp.where(slot_ids < lower, block_ids * lower + slot_ids, nz // 2)
    valid = jnp.where((slot_ids < lower) | (block_ids == 0), 1.0, 0.0).astype(jnp.float32)
    doubled = jnp.where((slot_ids < lower) & (freq_ids > 0), 2.0, 1.0).astype(jnp.float32)
    forward_table, backward_table = depth_rows(nz, freq_ids, valid, valid * doubled)
    return (forward_table, backward_table, freq_ids)


def combine_halves(first_part, second, orient):
    half_width = first_part.shape[-1] // 2
    real_part = first_part[..., :half_width] + orient * second[..., half_width:]
    imag_part = first_part[..., half_width:] - orient * second[..., :half_width]
    return jnp.concatenate([real_part, imag_part], axis=-1)


def transform_axis(pattern, cosine, sine_tab, values, orient):
    first_part = jnp.einsum(pattern, cosine, values, precision=lax.Precision.HIGHEST)
    second = jnp.einsum(pattern, sine_tab, values, precision=lax.Precision.HIGHEST)
    return combine_halves(first_part, second, orient)


def twiddle(values, twist_cos, twist_sin, orient):
    half_width = values.shape[-1] // 2
    real_part = values[..., :half_width]
    imag_part = values[..., half_width:]
    new_real = real_part * twist_cos + orient * imag_part * twist_sin
    new_imag = imag_part * twist_cos - orient * real_part * twist_sin
    return jnp.concatenate([new_real, new_imag], axis=-1)


def transform_rows(planes_block, cosine, sine_tab, orient):
    flat_rows = planes_block.reshape(-1, planes_block.shape[-1])
    first_part = jnp.dot(flat_rows, cosine, precision=lax.Precision.HIGHEST).reshape(
        planes_block.shape
    )
    second = jnp.dot(flat_rows, sine_tab, precision=lax.Precision.HIGHEST).reshape(
        planes_block.shape
    )
    real_part = first_part[:, 0] + orient * second[:, 1]
    imag_part = first_part[:, 1] - orient * second[:, 0]
    return jnp.stack([real_part, imag_part], axis=1)


def plain_device(charges, counts, projection, near_blocks, neighbours, spectrum):
    panels, cell_planes, cell_cols = charges.shape
    nx, nz, ny = (spectrum.shape[0], spectrum.shape[1], spectrum.shape[2] * lax.axis_size("slab"))
    planes = cell_planes * TX
    rows_cell = cell_cols // NZC
    slot_ids = lax.broadcasted_iota(jnp.int32, charges.shape, 0)
    panel_mask = (slot_ids < counts[None]).astype(jnp.float32)
    masked = charges * panel_mask
    tile_values = jnp.einsum("ptxc,pxc->txc", projection, masked, precision=lax.Precision.HIGHEST)
    grid_field = (
        tile_values.reshape(TX, TY, TZ, cell_planes, rows_cell, NZC)
        .transpose(3, 0, 5, 2, 4, 1)
        .reshape(planes, nz, rows_cell * TY)
    )
    cell_count = lax.axis_size("cell")
    forward_table, backward_table, freq_ids = half_depth_tables(nz, cell_count)
    depth_count = forward_table.shape[1] // cell_count
    spectra_z = jnp.einsum(
        "wkz,xzy->xwky", forward_table, grid_field, precision=lax.Precision.HIGHEST
    )
    cosine_y, sine_y = wave_tables(ny, ny, ny)
    pencils = transform_rows(
        lax.all_to_all(spectra_z, "cell", split_axis=2, concat_axis=3, tiled=True),
        cosine_y,
        sine_y,
        1.0,
    )
    columns = lax.all_to_all(pencils, "slab", split_axis=3, concat_axis=0, tiled=True)
    col_width = columns.shape[2] * columns.shape[3]
    flat_rows = columns.reshape(nx, 2 * col_width)
    first_row = lax.axis_index("cell") * depth_count
    kernel_ids = lax.dynamic_slice_in_dim(freq_ids, first_row, depth_count, 0)
    kernel = jnp.take(spectrum, kernel_ids, axis=1).reshape(nx, col_width) * (1.0 / (nx * ny * nz))
    kernel_both = jnp.concatenate([kernel, kernel], axis=1)
    slab_count = lax.axis_size("slab")
    local_rows = nx // slab_count
    cosine_s, sine_s = wave_tables(slab_count, slab_count, slab_count)
    cosine_r, sine_r = wave_tables(local_rows, local_rows, local_rows)
    twist_cos, twist_sin = wave_tables(slab_count, local_rows, nx)
    twist_cos = twist_cos[:, :, None]
    twist_sin = twist_sin[:, :, None]
    section_one = transform_axis(
        "ks,src->krc",
        cosine_s,
        sine_s,
        flat_rows.reshape(slab_count, local_rows, 2 * col_width),
        1.0,
    )
    section_one = twiddle(section_one, twist_cos, twist_sin, 1.0)
    section_two = transform_axis("jr,krc->jkc", cosine_r, sine_r, section_one, 1.0)
    weighted = section_two.reshape(nx, 2 * col_width) * kernel_both
    section_one = transform_axis(
        "rj,jkc->krc",
        cosine_r,
        sine_r,
        weighted.reshape(local_rows, slab_count, 2 * col_width),
        -1.0,
    )
    section_one = twiddle(section_one, twist_cos, twist_sin, -1.0)
    section_two = transform_axis("sk,krc->src", cosine_s, sine_s, section_one, -1.0)
    returned_x = section_two.reshape(nx, 2 * col_width)
    returned = lax.all_to_all(
        returned_x.reshape(columns.shape), "slab", split_axis=0, concat_axis=3, tiled=True
    )
    inverse_rows = transform_rows(returned, cosine_y, sine_y, -1.0)
    grid_potential = jnp.einsum(
        "wkz,xwky->xzy",
        backward_table,
        lax.all_to_all(inverse_rows, "cell", split_axis=3, concat_axis=2, tiled=True),
        precision=lax.Precision.HIGHEST,
    )
    tile_potential = (
        grid_potential.reshape(cell_planes, TX, NZC, TZ, rows_cell, TY)
        .transpose(1, 5, 3, 0, 4, 2)
        .reshape(TX * TY * TZ, cell_planes, cell_cols)
    )
    far_field = jnp.einsum(
        "ptxc,txc->pxc", projection, tile_potential, precision=lax.Precision.HIGHEST
    )
    block = masked.reshape(panels, cell_planes, rows_cell, NZC)
    extended = padded(block, (("slab", 1), ("cell", 2)), 1)
    flat_ext = extended.reshape(panels, -1)
    step_x = neighbours // 9 - 1
    step_y = neighbours // 3 % 3 - 1
    step_z = neighbours % 3 - 1
    plane_ids = lax.broadcasted_iota(jnp.int32, neighbours.shape, 1)
    col_ids = lax.broadcasted_iota(jnp.int32, neighbours.shape, 2)
    row_ids = col_ids // NZC
    depth_ids = col_ids % NZC
    near_ids = ((plane_ids + step_x + 1) * (rows_cell + 2) + row_ids + step_y + 1) * NZC + (
        depth_ids + step_z
    ) % NZC
    near_count = neighbours.shape[0]
    picked = jnp.take(flat_ext, near_ids.reshape(-1), axis=1).reshape(
        panels, near_count, cell_planes, cell_cols
    )
    near_field = jnp.einsum("kpqxc,qkxc->pxc", near_blocks, picked, precision=lax.Precision.HIGHEST)
    return (far_field + near_field) * panel_mask


def solution(mesh):
    in_specs = (
        P(None, "slab", "cell"),
        P("slab", "cell"),
        P(None, None, "slab", "cell"),
        P(None, None, None, "slab", "cell"),
        P(None, "slab", "cell"),
        P(None, None, "slab"),
    )
    out_specs = P(None, "slab", "cell")
    return jax.shard_map(
        per_device, mesh=mesh, in_specs=in_specs, out_specs=out_specs, check_vma=False
    )
```

```python
import functools
import math

import jax
import jax.numpy as jnp
import ml_dtypes
import numpy as np
from jax import lax
from jax.experimental import pallas as pl
from jax.experimental.pallas import tpu as pltpu
from jax.sharding import PartitionSpec as P

TX = 4
TY = 4
TZ = 4
NZC = 16
LANES = 128
CHUNKS = 2
VMEM_LIMIT = 56 * 1024 * 1024


def halves(table):
    high = table.astype(np.float32).astype(ml_dtypes.bfloat16)
    low = (table - high.astype(np.float64)).astype(np.float32).astype(ml_dtypes.bfloat16)
    return (high, low)


def wave(rows, cols, length):
    angle = (rows[:, None] * cols[None, :] % length) * (2.0 * math.pi / length)
    return (np.cos(angle), np.sin(angle))


class Plan:
    def __init__(self, slabs, cells, panels, cell_planes, cell_cols, near, nx, nz, ny):
        self.slabs, self.cells = (slabs, cells)
        self.panels, self.cell_planes, self.cell_cols, self.near = (panels, cell_planes, cell_cols, near)
        self.nx, self.ny, self.nz = (nx, ny, nz)
        self.slots = slabs * cells
        self.tx_chunk = TX // CHUNKS
        self.width = cell_planes * self.tx_chunk
        self.y_lanes = LANES // self.width if self.width else 1
        self.row_block = LANES // NZC
        self.step_blocks = self.y_lanes // TY
        self.steps = cell_cols // (LANES * self.step_blocks) if self.step_blocks else 0
        self.x_chunk = nx // CHUNKS
        self.ky_local = ny // slabs

    def fits(self):
        return (
            self.slots * 2 == self.nz
            and self.cell_planes == 8
            and self.step_blocks * TY * self.width == LANES
            and self.slabs % self.y_lanes == 0
            and self.ky_local % 8 == 0
            and self.steps * self.step_blocks * LANES == self.cell_cols
            and self.x_chunk % LANES == 0
            and self.ny % 1024 == self.nx % 1024 == 512
        )

    def depth_tables(self):
        depth = np.arange(NZC)[None, :] * TZ + np.arange(TZ)[:, None]
        forward = np.zeros((self.slots, 2, self.row_block, TZ, self.row_block, NZC))
        backward = np.zeros_like(forward)
        for freq in range(self.slots):
            angle = (freq * depth % self.nz) * (2.0 * math.pi / self.nz)
            real, imag = (np.cos(angle), -np.sin(angle))
            factor = 2.0
            if freq == 0:
                imag = np.cos(depth * math.pi)
                factor = 1.0
            for row in range(self.row_block):
                forward[freq, 0, row, :, row, :] = real
                forward[freq, 1, row, :, row, :] = imag
                backward[freq, 0, row, :, row, :] = factor * real
                backward[freq, 1, row, :, row, :] = factor * imag
        shape = (self.slots * 2 * self.row_block, TZ * LANES)
        return (forward.reshape(shape), backward.reshape(shape))

    def y_order(self):
        rows = np.arange(self.ny // TY).reshape(-1, self.row_block)
        return (rows[:, None, :] * TY + np.arange(TY)[None, :, None]).reshape(-1)

    def x_order(self):
        chunk, slab, tile, plane = np.meshgrid(
            np.arange(CHUNKS),
            np.arange(self.slabs),
            np.arange(self.tx_chunk),
            np.arange(self.cell_planes),
            indexing="ij",
        )
        return ((slab * self.cell_planes + plane) * TX + chunk * self.tx_chunk + tile).reshape(-1)


def split(value):
    high = value.astype(jnp.bfloat16)
    low = (value - high.astype(jnp.float32)).astype(jnp.bfloat16)
    return (high, low)


def product(left, right, dims=((1,), (0,))):
    def dot(a, b):
        return lax.dot_general(a, b, (dims, ((), ())), preferred_element_type=jnp.float32)

    return dot(left[0], right[0]) + (dot(left[0], right[1]) + dot(left[1], right[0]))


def swap_groups(parts, width):
    count = len(parts)
    lane = lax.broadcasted_iota(jnp.int32, parts[0].shape, 1)
    parts = list(parts)
    step = count // 2
    while step >= 1:
        shift = step * width
        upper = (lane // shift) % 2 == 1
        for i in range(count):
            if i & step:
                continue
            first, second = (parts[i], parts[i + step])
            parts[i] = jnp.where(upper, pltpu.roll(second, shift, 1), first)
            parts[i + step] = jnp.where(upper, second, pltpu.roll(first, LANES - shift, 1))
        step //= 2
    return parts


def project_kernel(plan, charges, counts, projection, high, low, out, scratch):
    planes = plan.cell_planes
    slot = lax.broadcasted_iota(jnp.int32, charges.shape, 0)
    masked = jnp.where(slot < counts[...][None], charges[...], 0.0)
    for block in range(plan.step_blocks):
        lanes = pl.ds(block * LANES, LANES)
        own = masked[:, :, block * LANES : (block + 1) * LANES]
        for tx in range(plan.tx_chunk):
            for ty in range(TY):
                for tz in range(TZ):
                    t = (tx * TY + ty) * TZ + tz
                    total = projection[0, t, :, lanes] * own[0]
                    for p in range(1, plan.panels):
                        total = total + projection[p, t, :, lanes] * own[p]
                    row = ((block * TY + ty) * plan.tx_chunk + tx) * planes
                    scratch[row : row + planes, tz * LANES : (tz + 1) * LANES] = total
    spectra = product((high[...], low[...]), split(scratch[...]), ((1,), (1,)))
    out[:, :, 0] = spectra.reshape(plan.slots, 2, plan.row_block, LANES)


def projection_spec(plan, chunk):
    shape = (plan.panels, TX * TY * TZ // CHUNKS, plan.cell_planes, plan.step_blocks * LANES)
    return pl.BlockSpec(shape, lambda i: (0, chunk, 0, i))


def panel_spec(plan):
    return pl.BlockSpec((plan.panels, plan.cell_planes, plan.step_blocks * LANES), lambda i: (0, 0, i))


def count_spec(plan):
    return pl.BlockSpec((plan.cell_planes, plan.step_blocks * LANES), lambda i: (0, i))


def piece_shape(plan):
    return (plan.slots, 2, plan.steps, plan.row_block, LANES)


def piece_spec(plan):
    return pl.BlockSpec((plan.slots, 2, 1, plan.row_block, LANES), lambda i: (0, 0, i, 0, 0))


def whole_spec(array):
    return pl.BlockSpec(array.shape, lambda i: (0,) * array.ndim)


def project(plan, chunk, charges, counts, projection, high, low):
    return pl.pallas_call(
        functools.partial(project_kernel, plan),
        grid=(plan.steps,),
        in_specs=[
            panel_spec(plan),
            count_spec(plan),
            projection_spec(plan, chunk),
            whole_spec(high),
            whole_spec(low),
        ],
        out_specs=piece_spec(plan),
        out_shape=jax.ShapeDtypeStruct(piece_shape(plan), jnp.float32),
        scratch_shapes=[pltpu.VMEM((LANES, TZ * LANES), jnp.float32)],
        compiler_params=pltpu.CompilerParams(vmem_limit_bytes=VMEM_LIMIT),
        cost_estimate=pl.CostEstimate(
            flops=2 * projection.size // CHUNKS,
            bytes_accessed=4 * projection.size // CHUNKS,
            transcendentals=0,
        ),
        name="project_depth",
    )(charges, counts, projection, high, low)


def forward_y_kernel(plan, me_ref, pieces, high, low, out, scratch):
    rows = 2 * plan.steps * plan.row_block
    width = plan.x_chunk
    for cell in range(plan.cells):
        for group in range(plan.slabs // plan.y_lanes):
            parts = [
                pieces[(group * plan.y_lanes + i) * plan.cells + cell].reshape(rows, LANES)
                for i in range(plan.y_lanes)
            ]
            parts = swap_groups(parts, plan.width)
            for place, value in enumerate(parts):
                for part in range(2):
                    for step in range(plan.steps):
                        source = (part * plan.steps + step) * plan.row_block
                        row = ((cell * plan.steps + step) * plan.y_lanes + place) * plan.row_block
                        col = part * width + group * LANES
                        scratch[row : row + plan.row_block, col : col + LANES] = value[
                            source : source + plan.row_block
                        ]
    sums = product((high[...], low[...]), split(scratch[...]))
    cosine, sine = (sums[: plan.ny], sums[plan.ny :])
    special = me_ref[0] == 0

    @pl.when(jnp.logical_not(special))
    def _():
        out[:, :width] = cosine[:, :width] + sine[:, width:]
        out[:, width:] = cosine[:, width:] - sine[:, :width]

    @pl.when(special)
    def _():
        middle = plan.ny // 2
        row = lax.broadcasted_iota(jnp.int32, (middle, width), 0)
        for part in range(2):
            rows = slice(part * middle, (part + 1) * middle)
            cols = slice(part * width, (part + 1) * width)
            other = (1 - part) * middle
            out[rows, :width] = cosine[rows, cols]
            out[rows, width:] = jnp.where(row == 0, cosine[other : other + 1, cols], -sine[rows, cols])


def forward_y(plan, me, pieces, high, low):
    return pl.pallas_call(
        functools.partial(forward_y_kernel, plan),
        grid=(1,),
        in_specs=[
            pl.BlockSpec(memory_space=pltpu.SMEM),
            whole_spec(pieces),
            whole_spec(high),
            whole_spec(low),
        ],
        out_specs=pl.BlockSpec((plan.ny, 2 * plan.x_chunk), lambda i: (0, 0)),
        out_shape=jax.ShapeDtypeStruct((plan.ny, 2 * plan.x_chunk), jnp.float32),
        scratch_shapes=[pltpu.VMEM((plan.ny, 2 * plan.x_chunk), jnp.float32)],
        compiler_params=pltpu.CompilerParams(vmem_limit_bytes=VMEM_LIMIT),
        cost_estimate=pl.CostEstimate(
            flops=12 * plan.ny * plan.ny * 2 * plan.x_chunk,
            bytes_accessed=8 * pieces.size + 4 * high.size,
            transcendentals=0,
        ),
        name="forward_second",
    )(me, pieces, high, low)


def forward_x_kernel(plan, weights, edge, high, low, *refs):
    rows_in, (out_high, out_low) = (refs[:CHUNKS], refs[CHUNKS:])
    width = plan.x_chunk
    rows = weights.shape[0]
    real = jnp.concatenate([value[:, :width] for value in rows_in], axis=1)
    imag = jnp.concatenate([value[:, width:] for value in rows_in], axis=1)
    sums = product(split(jnp.concatenate([real, imag], axis=0)), (high[...], low[...]))
    weight = weights[...]
    row = lax.broadcasted_iota(jnp.int32, weight.shape, 0)
    second = jnp.where(row == 0, edge[0], weight)
    new_real = weight * sums[:rows, : plan.nx] + second * sums[rows:, plan.nx :]
    new_imag = second * sums[rows:, : plan.nx] - weight * sums[:rows, plan.nx :]
    out_high[0], out_low[0] = split(new_real)
    out_high[1], out_low[1] = split(new_imag)


def forward_x(plan, weights, edge, high, low, pencils):
    rows = plan.ny // edge.shape[0]
    out = jax.ShapeDtypeStruct((2, plan.ny, plan.nx), jnp.bfloat16)
    out_spec = pl.BlockSpec((2, rows, plan.nx), lambda i: (0, i, 0))
    return pl.pallas_call(
        functools.partial(forward_x_kernel, plan),
        grid=(edge.shape[0],),
        in_specs=[
            pl.BlockSpec((rows, plan.nx), lambda i: (i, 0)),
            pl.BlockSpec((1, 1, plan.nx), lambda i: (i, 0, 0)),
            whole_spec(high),
            whole_spec(low),
        ]
        + [pl.BlockSpec((rows, 2 * plan.x_chunk), lambda i: (i, 0))] * CHUNKS,
        out_specs=[out_spec, out_spec],
        out_shape=[out, out],
        compiler_params=pltpu.CompilerParams(vmem_limit_bytes=VMEM_LIMIT),
        cost_estimate=pl.CostEstimate(
            flops=24 * plan.nx * plan.nx * plan.ny,
            bytes_accessed=20 * plan.nx * plan.ny + 4 * high.size,
            transcendentals=0,
        ),
        name="forward_first",
    )(weights, edge, high, low, *pencils)


def backward_kernel(plan, me_ref, in_high, in_low, x_high, x_low, y_high, y_low, out, scratch):
    width = plan.x_chunk
    shape = (2 * plan.ny, plan.nx)
    sums = product(
        (in_high[...].reshape(shape), in_low[...].reshape(shape)), (x_high[0], x_low[0])
    )
    real = sums[: plan.ny, :width] - sums[plan.ny :, width:]
    imag = sums[plan.ny :, :width] + sums[: plan.ny, width:]
    scratch[:, :width] = real
    scratch[:, width:] = imag
    special = me_ref[0] == 0
    middle = plan.ny // 2
    ends = (scratch[0:1, width:], scratch[middle : middle + 1, width:])

    @pl.when(special)
    def _():
        row = lax.broadcasted_iota(jnp.int32, scratch.shape, 0)
        scratch[...] = jnp.where(row % middle == 0, scratch[...], 2.0 * scratch[...])

    pair = split(scratch[...])
    halves_sum = []
    for part in range(2):
        rows = slice(part * middle, (part + 1) * middle)
        halves_sum.append(
            product((y_high[:, rows], y_low[:, rows]), (pair[0][rows], pair[1][rows]))
        )
    first, second = halves_sum

    @pl.when(jnp.logical_not(special))
    def _():
        both = first + second
        scratch[:, :width] = both[: plan.ny, :width] - both[plan.ny :, width:]
        scratch[:, width:] = both[: plan.ny, width:] + both[plan.ny :, :width]

    @pl.when(special)
    def _():
        row = lax.broadcasted_iota(jnp.int32, (plan.ny, width), 0)
        sign = jnp.where(row // plan.row_block % 2 == 0, 1.0, -1.0)
        scratch[:, :width] = first[: plan.ny, :width] - first[plan.ny :, width:] + sign * ends[0]
        scratch[:, width:] = second[: plan.ny, :width] - second[plan.ny :, width:] + ends[1]

    for cell in range(plan.cells):
        for group in range(plan.slabs // plan.y_lanes):
            parts = []
            for place in range(plan.y_lanes):
                pieces = []
                for part in range(2):
                    for step in range(plan.steps):
                        row = ((cell * plan.steps + step) * plan.y_lanes + place) * plan.row_block
                        col = part * width + group * LANES
                        pieces.append(scratch[row : row + plan.row_block, col : col + LANES])
                parts.append(jnp.concatenate(pieces, axis=0))
            parts = swap_groups(parts, plan.width)
            for i in range(plan.y_lanes):
                out[(group * plan.y_lanes + i) * plan.cells + cell] = parts[i].reshape(
                    2, plan.steps, plan.row_block, LANES
                )


def backward(plan, chunk, me, high, low, x_tables, y_tables):
    x_spec = pl.BlockSpec((1, plan.nx, 2 * plan.x_chunk), lambda i: (chunk, 0, 0))
    return pl.pallas_call(
        functools.partial(backward_kernel, plan),
        grid=(1,),
        in_specs=[
            pl.BlockSpec(memory_space=pltpu.SMEM),
            whole_spec(high),
            whole_spec(low),
            x_spec,
            x_spec,
            whole_spec(y_tables[0]),
            whole_spec(y_tables[1]),
        ],
        out_specs=pl.BlockSpec(piece_shape(plan), lambda i: (0, 0, 0, 0, 0)),
        out_shape=jax.ShapeDtypeStruct(piece_shape(plan), jnp.float32),
        scratch_shapes=[pltpu.VMEM((plan.ny, 2 * plan.x_chunk), jnp.float32)],
        compiler_params=pltpu.CompilerParams(vmem_limit_bytes=VMEM_LIMIT),
        cost_estimate=pl.CostEstimate(
            flops=24 * plan.nx * plan.ny * 2 * plan.x_chunk,
            bytes_accessed=4 * high.size + 8 * plan.nx * plan.x_chunk * 2 + 4 * y_tables[0].size,
            transcendentals=0,
        ),
        name="backward_plane",
    )(me, high, low, *x_tables, *y_tables)


def gather_kernel(plan, last, counts, before, projection, high, low, pieces, out, scratch):
    planes = plan.cell_planes
    rows = plan.slots * 2 * plan.row_block
    scratch[...] = product(split(pieces[...].reshape(rows, LANES).T), (high[...], low[...]))
    for block in range(plan.step_blocks):
        lanes = pl.ds(block * LANES, LANES)
        far = [before[p, :, lanes] for p in range(plan.panels)]
        for tx in range(plan.tx_chunk):
            for ty in range(TY):
                row = ((block * TY + ty) * plan.tx_chunk + tx) * planes
                for tz in range(TZ):
                    t = (tx * TY + ty) * TZ + tz
                    potential = scratch[row : row + planes, tz * LANES : (tz + 1) * LANES]
                    for p in range(plan.panels):
                        far[p] = far[p] + projection[p, t, :, lanes] * potential
        for p in range(plan.panels):
            out[p, :, lanes] = jnp.where(counts[:, lanes] > p, far[p], 0.0) if last else far[p]


def gather(plan, chunk, counts, before, projection, high, low, pieces):
    return pl.pallas_call(
        functools.partial(gather_kernel, plan, chunk == CHUNKS - 1),
        grid=(plan.steps,),
        in_specs=[
            count_spec(plan),
            panel_spec(plan),
            projection_spec(plan, chunk),
            whole_spec(high),
            whole_spec(low),
            piece_spec(plan),
        ],
        out_specs=panel_spec(plan),
        out_shape=jax.ShapeDtypeStruct(before.shape, jnp.float32),
        scratch_shapes=[pltpu.VMEM((LANES, TZ * LANES), jnp.float32)],
        compiler_params=pltpu.CompilerParams(vmem_limit_bytes=VMEM_LIMIT),
        cost_estimate=pl.CostEstimate(
            flops=2 * projection.size // CHUNKS,
            bytes_accessed=4 * projection.size // CHUNKS,
            transcendentals=0,
        ),
        name="depth_gather",
    )(counts, before, projection, high, low, pieces)


def near_kernel(plan, extended, codes, blocks_ref, out):
    step = pl.program_id(0)
    lane = lax.broadcasted_iota(jnp.int32, (plan.cell_planes, LANES), 1)
    depth = lane % NZC
    digits = []
    for k in range(plan.near):
        code = codes[k]
        digits.append((code // 9, code // 3 % 3, code % 3))
    total = [None] * plan.panels
    for q in range(plan.panels):
        shifted = []
        for dx in range(3):
            before, here, after = (
                extended[q, dx, :, pl.ds(pl.multiple_of((step + i) * LANES, LANES), LANES)] for i in range(3)
            )
            up = jnp.where(lane < NZC, pltpu.roll(before, NZC, 1), pltpu.roll(here, NZC, 1))
            down = jnp.where(
                lane >= LANES - NZC, pltpu.roll(after, LANES - NZC, 1), pltpu.roll(here, LANES - NZC, 1)
            )
            for value in (up, here, down):
                under = jnp.where(
                    depth == 0, pltpu.roll(value, LANES - NZC + 1, 1), pltpu.roll(value, 1, 1)
                )
                over = jnp.where(
                    depth == NZC - 1, pltpu.roll(value, NZC - 1, 1), pltpu.roll(value, LANES - 1, 1)
                )
                shifted.append((under, value, over))
        for k in range(plan.near):
            digit_x, digit_y, digit_z = digits[k]

            def choose(digit, options):
                return jnp.where(digit == 0, options[0], jnp.where(digit == 1, options[1], options[2]))

            by_z = [choose(digit_z, options) for options in shifted]
            by_y = [choose(digit_y, by_z[3 * i : 3 * i + 3]) for i in range(3)]
            picked = choose(digit_x, by_y)
            for p in range(plan.panels):
                term = blocks_ref[k, p, q] * picked
                total[p] = term if total[p] is None else total[p] + term
    for p in range(plan.panels):
        out[p] = total[p]


def near_field(plan, extended, neighbours, near_blocks):
    return pl.pallas_call(
        functools.partial(near_kernel, plan),
        grid=(plan.cell_cols // LANES,),
        in_specs=[
            pl.BlockSpec(extended.shape, lambda i: (0, 0, 0, 0)),
            pl.BlockSpec((plan.near, plan.cell_planes, LANES), lambda i: (0, 0, i)),
            pl.BlockSpec(
                (plan.near, plan.panels, plan.panels, plan.cell_planes, LANES), lambda i: (0, 0, 0, 0, i)
            ),
        ],
        out_specs=pl.BlockSpec((plan.panels, plan.cell_planes, LANES), lambda i: (0, 0, i)),
        out_shape=jax.ShapeDtypeStruct((plan.panels, plan.cell_planes, plan.cell_cols), jnp.float32),
        compiler_params=pltpu.CompilerParams(vmem_limit_bytes=VMEM_LIMIT),
        cost_estimate=pl.CostEstimate(
            flops=2 * near_blocks.size, bytes_accessed=4 * near_blocks.size, transcendentals=0
        ),
        name="near_blocks",
    )(extended, neighbours, near_blocks)


def ring_pairs(axis):
    count = lax.axis_size(axis)
    up = [(i, (i + 1) % count) for i in range(count)]
    return (up, [(j, i) for i, j in up])


def extended_charges(plan, masked):
    up, down = ring_pairs("cell")
    left = lax.ppermute(masked[:, :, -NZC:], "cell", up)
    right = lax.ppermute(masked[:, :, :NZC], "cell", down)
    rest = jnp.zeros((plan.panels, plan.cell_planes, LANES - NZC), jnp.float32)
    wide = jnp.concatenate([rest, left, masked, right, rest], axis=2)
    up, down = ring_pairs("slab")
    before = lax.ppermute(wide[:, -1:], "slab", up)
    after = lax.ppermute(wide[:, :1], "slab", down)
    whole = jnp.concatenate([before, wide, after], axis=1)
    planes = plan.cell_planes
    return jnp.stack([whole[:, i : i + planes] for i in range(3)], axis=1)


def spectrum_weights(plan, spectrum):
    slab, cell = (lax.axis_index("slab"), lax.axis_index("cell"))
    scale = 1.0 / (plan.nx * plan.ny * plan.nz)
    by_depth = jnp.transpose(spectrum, (1, 2, 0))
    shape = (plan.slabs, plan.cells) + by_depth.shape[1:]
    own = lax.dynamic_index_in_dim(by_depth[: plan.slots].reshape(shape), cell, 1, keepdims=False)
    dest = lax.broadcasted_iota(jnp.int32, own.shape, 0)
    swapped = (cell == 0) & (slab >= plan.slabs // 2) & (dest == 0)
    own = jnp.where(swapped, by_depth[plan.slots][None], own) * scale
    weights = lax.all_to_all(own, "slab", split_axis=0, concat_axis=0, tiled=True)
    weights = weights.reshape(plan.ny, plan.nx)
    far = lax.ppermute(by_depth[0, :1], "slab", [(plan.slabs // 2, 0)]) * scale
    near = by_depth[plan.slots, :1] * scale
    steps = 4
    edge = weights.reshape(steps, -1, plan.nx)[:, 0]
    step = lax.broadcasted_iota(jnp.int32, edge.shape, 0)
    first = (slab == 0) & (cell == 0)
    edge = jnp.where(first & (step == 0), far, edge)
    edge = jnp.where(first & (step == steps // 2), near, edge)
    return (weights, edge[:, None])


def per_device(charges, counts, projection, near_blocks, neighbours, spectrum):
    panels, cell_planes, cell_cols = charges.shape
    cells, slabs = (lax.axis_size("cell"), lax.axis_size("slab"))
    nx, nz, local = spectrum.shape
    plan = Plan(slabs, cells, panels, cell_planes, cell_cols, neighbours.shape[0], nx, nz, local * slabs)
    if not plan.fits():
        return plain_device(charges, counts, projection, near_blocks, neighbours, spectrum)
    me = (lax.axis_index("slab") * cells + lax.axis_index("cell")).astype(jnp.int32).reshape(1)
    depth_forward, depth_backward = plan.depth_tables()
    freqs = np.arange(plan.ny)
    cos_y, sin_y = wave(freqs, plan.y_order(), plan.ny)
    y_forward = halves(np.concatenate([cos_y, sin_y], axis=0))
    y_backward = halves(np.concatenate([cos_y.T, sin_y.T], axis=0))
    cos_x, sin_x = wave(plan.x_order(), np.arange(plan.nx), plan.nx)
    x_forward = halves(np.concatenate([cos_x, sin_x], axis=1))
    chunked = (CHUNKS, plan.x_chunk, plan.nx)
    both_x = np.concatenate([cos_x.reshape(chunked), sin_x.reshape(chunked)], axis=1)
    x_backward = halves(both_x.transpose(0, 2, 1))
    axes = ("slab", "cell")
    weights, edge = spectrum_weights(plan, spectrum)
    pencils = []
    for chunk in range(CHUNKS):
        pieces = project(plan, chunk, charges, counts, projection, *halves(depth_forward))
        pieces = lax.all_to_all(pieces, axes, split_axis=0, concat_axis=0, tiled=True)
        pencils.append(forward_y(plan, me, pieces, *y_forward))
    high, low = forward_x(plan, weights, edge, *x_forward, pencils)
    slot = lax.broadcasted_iota(jnp.int32, charges.shape, 0)
    masked = jnp.where(slot < counts[None], charges, 0.0)
    total = near_field(plan, extended_charges(plan, masked), neighbours, near_blocks)
    for chunk in range(CHUNKS):
        pieces = backward(plan, chunk, me, high, low, x_backward, y_backward)
        pieces = lax.all_to_all(pieces, axes, split_axis=0, concat_axis=0, tiled=True)
        total = gather(plan, chunk, counts, total, projection, *halves(depth_backward), pieces)
    return total


def padded(value, sides, width):
    for axis, dim in sides:
        count, length = (lax.axis_size(axis), value.shape[dim])
        up = [(i, (i + 1) % count) for i in range(count)]
        down = [(j, i) for i, j in up]
        last = lax.slice_in_dim(value, length - width, length, axis=dim)
        first = lax.slice_in_dim(value, 0, width, axis=dim)
        before = lax.ppermute(last, axis, up)
        after = lax.ppermute(first, axis, down)
        value = jnp.concatenate([before, value, after], axis=dim)
    return value


def wave_tables(row_count, col_count, length):
    products = (
        lax.broadcasted_iota(jnp.int32, (row_count, col_count), 0)
        * lax.broadcasted_iota(jnp.int32, (row_count, col_count), 1)
        % length
    )
    angle_rad = products.astype(jnp.float32) * (2.0 * math.pi / length)
    return (jnp.cos(angle_rad), jnp.sin(angle_rad))


def depth_rows(nz, freq_ids, valid, weights):
    depth_ids = lax.broadcasted_iota(jnp.int32, (freq_ids.shape[0], nz), 1)
    products = freq_ids[:, None] * depth_ids % nz
    angle_rad = products.astype(jnp.float32) * (2.0 * math.pi / nz)
    basis = jnp.stack([jnp.cos(angle_rad), -jnp.sin(angle_rad)])
    return (basis * valid[None, :, None], basis * weights[None, :, None])


def half_depth_tables(nz, cell_count):
    lower = nz // (2 * cell_count)
    row_ids = lax.broadcasted_iota(jnp.int32, (cell_count * (lower + 1),), 0)
    block_ids = row_ids // (lower + 1)
    slot_ids = row_ids % (lower + 1)
    freq_ids = jnp.where(slot_ids < lower, block_ids * lower + slot_ids, nz // 2)
    valid = jnp.where((slot_ids < lower) | (block_ids == 0), 1.0, 0.0).astype(jnp.float32)
    doubled = jnp.where((slot_ids < lower) & (freq_ids > 0), 2.0, 1.0).astype(jnp.float32)
    forward_table, backward_table = depth_rows(nz, freq_ids, valid, valid * doubled)
    return (forward_table, backward_table, freq_ids)


def combine_halves(first_part, second, orient):
    half_width = first_part.shape[-1] // 2
    real_part = first_part[..., :half_width] + orient * second[..., half_width:]
    imag_part = first_part[..., half_width:] - orient * second[..., :half_width]
    return jnp.concatenate([real_part, imag_part], axis=-1)


def transform_axis(pattern, cosine, sine_tab, values, orient):
    first_part = jnp.einsum(pattern, cosine, values, precision=lax.Precision.HIGHEST)
    second = jnp.einsum(pattern, sine_tab, values, precision=lax.Precision.HIGHEST)
    return combine_halves(first_part, second, orient)


def twiddle(values, twist_cos, twist_sin, orient):
    half_width = values.shape[-1] // 2
    real_part = values[..., :half_width]
    imag_part = values[..., half_width:]
    new_real = real_part * twist_cos + orient * imag_part * twist_sin
    new_imag = imag_part * twist_cos - orient * real_part * twist_sin
    return jnp.concatenate([new_real, new_imag], axis=-1)


def transform_rows(planes_block, cosine, sine_tab, orient):
    flat_rows = planes_block.reshape(-1, planes_block.shape[-1])
    first_part = jnp.dot(flat_rows, cosine, precision=lax.Precision.HIGHEST).reshape(
        planes_block.shape
    )
    second = jnp.dot(flat_rows, sine_tab, precision=lax.Precision.HIGHEST).reshape(
        planes_block.shape
    )
    real_part = first_part[:, 0] + orient * second[:, 1]
    imag_part = first_part[:, 1] - orient * second[:, 0]
    return jnp.stack([real_part, imag_part], axis=1)


def plain_device(charges, counts, projection, near_blocks, neighbours, spectrum):
    panels, cell_planes, cell_cols = charges.shape
    nx, nz, ny = (spectrum.shape[0], spectrum.shape[1], spectrum.shape[2] * lax.axis_size("slab"))
    planes = cell_planes * TX
    rows_cell = cell_cols // NZC
    slot_ids = lax.broadcasted_iota(jnp.int32, charges.shape, 0)
    panel_mask = (slot_ids < counts[None]).astype(jnp.float32)
    masked = charges * panel_mask
    tile_values = jnp.einsum("ptxc,pxc->txc", projection, masked, precision=lax.Precision.HIGHEST)
    grid_field = (
        tile_values.reshape(TX, TY, TZ, cell_planes, rows_cell, NZC)
        .transpose(3, 0, 5, 2, 4, 1)
        .reshape(planes, nz, rows_cell * TY)
    )
    cell_count = lax.axis_size("cell")
    forward_table, backward_table, freq_ids = half_depth_tables(nz, cell_count)
    depth_count = forward_table.shape[1] // cell_count
    spectra_z = jnp.einsum(
        "wkz,xzy->xwky", forward_table, grid_field, precision=lax.Precision.HIGHEST
    )
    cosine_y, sine_y = wave_tables(ny, ny, ny)
    pencils = transform_rows(
        lax.all_to_all(spectra_z, "cell", split_axis=2, concat_axis=3, tiled=True),
        cosine_y,
        sine_y,
        1.0,
    )
    columns = lax.all_to_all(pencils, "slab", split_axis=3, concat_axis=0, tiled=True)
    col_width = columns.shape[2] * columns.shape[3]
    flat_rows = columns.reshape(nx, 2 * col_width)
    first_row = lax.axis_index("cell") * depth_count
    kernel_ids = lax.dynamic_slice_in_dim(freq_ids, first_row, depth_count, 0)
    kernel = jnp.take(spectrum, kernel_ids, axis=1).reshape(nx, col_width) * (1.0 / (nx * ny * nz))
    kernel_both = jnp.concatenate([kernel, kernel], axis=1)
    slab_count = lax.axis_size("slab")
    local_rows = nx // slab_count
    cosine_s, sine_s = wave_tables(slab_count, slab_count, slab_count)
    cosine_r, sine_r = wave_tables(local_rows, local_rows, local_rows)
    twist_cos, twist_sin = wave_tables(slab_count, local_rows, nx)
    twist_cos = twist_cos[:, :, None]
    twist_sin = twist_sin[:, :, None]
    section_one = transform_axis(
        "ks,src->krc",
        cosine_s,
        sine_s,
        flat_rows.reshape(slab_count, local_rows, 2 * col_width),
        1.0,
    )
    section_one = twiddle(section_one, twist_cos, twist_sin, 1.0)
    section_two = transform_axis("jr,krc->jkc", cosine_r, sine_r, section_one, 1.0)
    weighted = section_two.reshape(nx, 2 * col_width) * kernel_both
    section_one = transform_axis(
        "rj,jkc->krc",
        cosine_r,
        sine_r,
        weighted.reshape(local_rows, slab_count, 2 * col_width),
        -1.0,
    )
    section_one = twiddle(section_one, twist_cos, twist_sin, -1.0)
    section_two = transform_axis("sk,krc->src", cosine_s, sine_s, section_one, -1.0)
    returned_x = section_two.reshape(nx, 2 * col_width)
    returned = lax.all_to_all(
        returned_x.reshape(columns.shape), "slab", split_axis=0, concat_axis=3, tiled=True
    )
    inverse_rows = transform_rows(returned, cosine_y, sine_y, -1.0)
    grid_potential = jnp.einsum(
        "wkz,xwky->xzy",
        backward_table,
        lax.all_to_all(inverse_rows, "cell", split_axis=3, concat_axis=2, tiled=True),
        precision=lax.Precision.HIGHEST,
    )
    tile_potential = (
        grid_potential.reshape(cell_planes, TX, NZC, TZ, rows_cell, TY)
        .transpose(1, 5, 3, 0, 4, 2)
        .reshape(TX * TY * TZ, cell_planes, cell_cols)
    )
    far_field = jnp.einsum(
        "ptxc,txc->pxc", projection, tile_potential, precision=lax.Precision.HIGHEST
    )
    block = masked.reshape(panels, cell_planes, rows_cell, NZC)
    extended = padded(block, (("slab", 1), ("cell", 2)), 1)
    flat_ext = extended.reshape(panels, -1)
    step_x = neighbours // 9 - 1
    step_y = neighbours // 3 % 3 - 1
    step_z = neighbours % 3 - 1
    plane_ids = lax.broadcasted_iota(jnp.int32, neighbours.shape, 1)
    col_ids = lax.broadcasted_iota(jnp.int32, neighbours.shape, 2)
    row_ids = col_ids // NZC
    depth_ids = col_ids % NZC
    near_ids = ((plane_ids + step_x + 1) * (rows_cell + 2) + row_ids + step_y + 1) * NZC + (
        depth_ids + step_z
    ) % NZC
    near_count = neighbours.shape[0]
    picked = jnp.take(flat_ext, near_ids.reshape(-1), axis=1).reshape(
        panels, near_count, cell_planes, cell_cols
    )
    near_field = jnp.einsum("kpqxc,qkxc->pxc", near_blocks, picked, precision=lax.Precision.HIGHEST)
    return (far_field + near_field) * panel_mask


def solution(mesh):
    in_specs = (
        P(None, "slab", "cell"),
        P("slab", "cell"),
        P(None, None, "slab", "cell"),
        P(None, None, None, "slab", "cell"),
        P(None, "slab", "cell"),
        P(None, None, "slab"),
    )
    out_specs = P(None, "slab", "cell")
    return jax.shard_map(
        per_device, mesh=mesh, in_specs=in_specs, out_specs=out_specs, check_vma=False
    )
```

```python
import functools
import math

import jax
import jax.numpy as jnp
import ml_dtypes
import numpy as np
from jax import lax
from jax.experimental import pallas as pl
from jax.experimental.pallas import tpu as pltpu
from jax.sharding import PartitionSpec as P

TX = 4
TY = 4
TZ = 4
NZC = 16
LANES = 128
CHUNKS = 2
VMEM_LIMIT = 40 * 1024 * 1024


def halves(table):
    high = table.astype(np.float32).astype(ml_dtypes.bfloat16)
    low = (table - high.astype(np.float64)).astype(np.float32).astype(ml_dtypes.bfloat16)
    return (high, low)


def wave(rows, cols, length):
    angle = (rows[:, None] * cols[None, :] % length) * (2.0 * math.pi / length)
    return (np.cos(angle), np.sin(angle))


class Plan:
    def __init__(self, slabs, cells, panels, cell_planes, cell_cols, near, nx, nz, ny):
        self.slabs, self.cells = (slabs, cells)
        self.panels, self.cell_planes, self.cell_cols, self.near = (panels, cell_planes, cell_cols, near)
        self.nx, self.ny, self.nz = (nx, ny, nz)
        self.slots = slabs * cells
        self.tx_chunk = TX // CHUNKS
        self.width = cell_planes * self.tx_chunk
        self.y_lanes = LANES // self.width if self.width else 1
        self.row_block = LANES // NZC
        self.step_blocks = self.y_lanes // TY
        self.steps = cell_cols // (LANES * self.step_blocks) if self.step_blocks else 0
        self.x_chunk = nx // CHUNKS
        self.ky_local = ny // slabs

    def fits(self):
        return (
            self.slots * 2 == self.nz
            and self.cell_planes == 8
            and self.step_blocks * TY * self.width == LANES
            and self.slabs % self.y_lanes == 0
            and self.ky_local % 8 == 0
            and self.steps * self.step_blocks * LANES == self.cell_cols
            and self.x_chunk % LANES == 0
            and self.ny % 1024 == self.nx % 1024 == 512
        )

    def depth_tables(self):
        depth = np.arange(NZC)[None, :] * TZ + np.arange(TZ)[:, None]
        scale = 1.0 / (self.nx * self.ny * self.nz)
        forward = np.zeros((self.slots, 2, self.row_block, TZ, self.row_block, NZC))
        backward = np.zeros_like(forward)
        for freq in range(self.slots):
            angle = (freq * depth % self.nz) * (2.0 * math.pi / self.nz)
            real, imag = (np.cos(angle), -np.sin(angle))
            factor = 2.0 * scale
            if freq == 0:
                imag = np.cos(depth * math.pi)
                factor = scale
            for row in range(self.row_block):
                forward[freq, 0, row, :, row, :] = real
                forward[freq, 1, row, :, row, :] = imag
                backward[freq, 0, row, :, row, :] = factor * real
                backward[freq, 1, row, :, row, :] = factor * imag
        shape = (self.slots * 2 * self.row_block, TZ * LANES)
        return (forward.reshape(shape), backward.reshape(shape))

    def y_rows(self):
        parity, cell, step, block, tile, row = np.meshgrid(
            *[np.arange(n) for n in (2, self.cells, self.steps, self.step_blocks, TY // 2, self.row_block)],
            indexing="ij",
        )
        cell_row = ((cell * self.steps + step) * self.step_blocks + block) * self.row_block + row
        return (cell_row * TY + 2 * tile + parity).reshape(2, -1)

    def x_columns(self):
        parity, slab, tile, plane = np.meshgrid(
            *[np.arange(n) for n in (2, self.slabs, TX // 2, self.cell_planes)], indexing="ij"
        )
        return ((slab * self.cell_planes + plane) * TX + 2 * tile + parity).reshape(2, -1)

    def row_of(self, cell, step, place):
        block, tile = (place // TY, place % TY)
        inner = (cell * self.steps + step) * self.step_blocks + block
        return (tile % 2) * (self.ny // 2) + (inner * (TY // 2) + tile // 2) * self.row_block


def split(value):
    high = value.astype(jnp.bfloat16)
    low = (value - high.astype(jnp.float32)).astype(jnp.bfloat16)
    return (high, low)


def product(left, right, dims=((1,), (0,))):
    first = jnp.concatenate([left[0], left[0], left[1]], axis=dims[0][0])
    second = jnp.concatenate([right[0], right[1], right[0]], axis=dims[1][0])
    return lax.dot_general(first, second, (dims, ((), ())), preferred_element_type=jnp.float32)


def swap_groups(parts, width):
    count = len(parts)
    lane = lax.broadcasted_iota(jnp.int32, parts[0].shape, 1)
    parts = list(parts)
    step = count // 2
    while step >= 1:
        shift = step * width
        upper = (lane // shift) % 2 == 1
        for i in range(count):
            if i & step:
                continue
            first, second = (parts[i], parts[i + step])
            parts[i] = jnp.where(upper, pltpu.roll(second, shift, 1), first)
            parts[i + step] = jnp.where(upper, second, pltpu.roll(first, LANES - shift, 1))
        step //= 2
    return parts


def project_kernel(plan, charges, counts, projection, high, low, out, scratch):
    planes = plan.cell_planes
    first = pl.program_id(0) * LANES
    slot = lax.broadcasted_iota(jnp.int32, charges.shape, 0)
    masked = jnp.where(slot < counts[...][None], charges[...], 0.0)
    for block in range(plan.step_blocks):
        lanes = pl.ds(block * LANES, LANES)
        own = masked[:, :, block * LANES : (block + 1) * LANES]
        for tx in range(plan.tx_chunk):
            for ty in range(TY):
                row = ((block * TY + ty) * plan.tx_chunk + tx) * planes
                rows = pl.ds(pl.multiple_of(first + row, planes), planes)
                for tz in range(TZ):
                    t = ty * TZ + tz
                    total = projection[0, tx, 0, t, :, lanes] * own[0]
                    for p in range(1, plan.panels):
                        total = total + projection[p, tx, 0, t, :, lanes] * own[p]
                    scratch[rows, tz * LANES : (tz + 1) * LANES] = total

    @pl.when(pl.program_id(0) == plan.steps - 1)
    def _():
        spectra = product((high[...], low[...]), split(scratch[...]), ((1,), (1,)))
        shape = (plan.slots, 2, plan.row_block, LANES)
        for step in range(plan.steps):
            out[:, :, step] = spectra[:, step * LANES : (step + 1) * LANES].reshape(shape)


def projection_spec(plan, chunk):
    shape = (plan.panels, TX // CHUNKS, 1, TY * TZ, plan.cell_planes, plan.step_blocks * LANES)
    return pl.BlockSpec(shape, lambda i: (0, 0, chunk, 0, 0, i))


def panel_spec(plan):
    return pl.BlockSpec((plan.panels, plan.cell_planes, plan.step_blocks * LANES), lambda i: (0, 0, i))


def count_spec(plan):
    return pl.BlockSpec((plan.cell_planes, plan.step_blocks * LANES), lambda i: (0, i))


def piece_shape(plan):
    return (plan.slots, 2, plan.steps, plan.row_block, LANES)


def whole_spec(shape):
    return pl.BlockSpec(shape, lambda i: (0,) * len(shape))


def projection_cost(projection):
    return pl.CostEstimate(
        flops=2 * projection.size // CHUNKS,
        bytes_accessed=4 * projection.size // CHUNKS,
        transcendentals=0,
    )


def project(plan, chunk, charges, counts, projection, high, low):
    return pl.pallas_call(
        functools.partial(project_kernel, plan),
        grid=(plan.steps,),
        in_specs=[
            panel_spec(plan),
            count_spec(plan),
            projection_spec(plan, chunk),
            whole_spec(high.shape),
            whole_spec(low.shape),
        ],
        out_specs=whole_spec(piece_shape(plan)),
        out_shape=jax.ShapeDtypeStruct(piece_shape(plan), jnp.float32),
        scratch_shapes=[pltpu.VMEM((plan.steps * LANES, TZ * LANES), jnp.float32)],
        compiler_params=pltpu.CompilerParams(vmem_limit_bytes=VMEM_LIMIT),
        cost_estimate=projection_cost(projection),
        name="project_depth",
    )(charges, counts, projection, high, low)


def forward_plane(plan, special, pieces, y_table, x_table, rows_ref, freq_ref):
    rows = 2 * plan.steps * plan.row_block
    width = plan.x_chunk
    middle = plan.ny // 2
    for cell in range(plan.cells):
        for group in range(plan.slabs // plan.y_lanes):
            first = cell * plan.slabs + group * plan.y_lanes
            parts = [pieces[first + i].reshape(rows, LANES) for i in range(plan.y_lanes)]
            parts = swap_groups(parts, plan.width)
            for place, value in enumerate(parts):
                for part in range(2):
                    for step in range(plan.steps):
                        source = (part * plan.steps + step) * plan.row_block
                        row = plan.row_of(cell, step, place)
                        col = part * width + group * LANES
                        rows_ref[row : row + plan.row_block, col : col + LANES] = value[
                            source : source + plan.row_block
                        ]
    high, low = y_table
    even = product((high[0], low[0]), split(rows_ref[:middle]))
    odd = product((high[1], low[1]), split(rows_ref[middle:]))
    for upper, sums in ((0, even + odd), (1, even - odd)):
        cosine, sine = (sums[:middle], sums[middle:])
        start = upper * middle
        freq_ref[start : start + middle] = cosine[:, :width] + sine[:, width:]
        start += plan.ny
        freq_ref[start : start + middle] = cosine[:, width:] - sine[:, :width]

    @pl.when(special)
    def _():
        row = lax.broadcasted_iota(jnp.int32, (middle, width), 0)
        below, above = (even + odd, even - odd)
        for upper, sums, other in ((0, below, above), (1, above, below)):
            cols = slice(upper * width, (upper + 1) * width)
            start = upper * middle
            freq_ref[start : start + middle] = sums[:middle, cols]
            start += plan.ny
            freq_ref[start : start + middle] = jnp.where(row == 0, other[0:1, cols], -sums[middle:, cols])

    high, low = x_table
    return product(split(freq_ref[...]), (high[0], low[0]))


def backward_plane(plan, special, freqs, x_table, y_table, out, rows_ref):
    width = plan.x_chunk
    middle = plan.ny // 2
    high, low = x_table
    sums = product(split(freqs), (high[0], low[0]))
    real = sums[: plan.ny, :width] - sums[plan.ny :, width:]
    imag = sums[plan.ny :, :width] + sums[: plan.ny, width:]
    high, low = y_table

    @pl.when(jnp.logical_not(special))
    def _():
        for parity in range(2):
            joined = []
            for value in (real, imag):
                below, above = (value[:middle], value[middle:])
                joined.append(below + above if parity == 0 else below - above)
            pair = split(jnp.concatenate(joined, axis=1))
            rows = product((high[parity], low[parity]), pair)
            cosine, sine = (rows[:middle], rows[middle:])
            start = parity * middle
            rows_ref[start : start + middle, :width] = cosine[:, :width] - sine[:, width:]
            rows_ref[start : start + middle, width:] = cosine[:, width:] + sine[:, :width]

    @pl.when(special)
    def _():
        row = lax.broadcasted_iota(jnp.int32, (middle, width), 0)
        columns, ends = ([], [])
        for upper in range(2):
            part = slice(upper * middle, (upper + 1) * middle)
            stacked = [jnp.where(row == 0, value[part], 2.0 * value[part]) for value in (real, imag)]
            columns.append(jnp.concatenate(stacked, axis=0))
            ends.append(imag[upper * middle : upper * middle + 1])
        pair = split(jnp.concatenate(columns, axis=1))
        for parity in range(2):
            table = tuple(
                jnp.concatenate([t[parity, :middle], -t[parity, middle:]], axis=1) for t in (high, low)
            )
            rows = product(table, pair)
            sign = 1.0 - 2.0 * parity
            start = parity * middle
            rows_ref[start : start + middle, :width] = rows[:, :width] + sign * ends[0]
            rows_ref[start : start + middle, width:] = sign * rows[:, width:] + ends[1]

    for cell in range(plan.cells):
        for group in range(plan.slabs // plan.y_lanes):
            parts = []
            for place in range(plan.y_lanes):
                tiles = []
                for part in range(2):
                    for step in range(plan.steps):
                        row = plan.row_of(cell, step, place)
                        col = part * width + group * LANES
                        tiles.append(rows_ref[row : row + plan.row_block, col : col + LANES])
                parts.append(jnp.concatenate(tiles, axis=0))
            parts = swap_groups(parts, plan.width)
            first = cell * plan.slabs + group * plan.y_lanes
            for i in range(plan.y_lanes):
                out[first + i] = parts[i].reshape(2, plan.steps, plan.row_block, LANES)


def first_plane_kernel(plan, me_ref, pieces, y_high, y_low, x_high, x_low, out, rows_ref, freq_ref):
    special = me_ref[0] == 0
    out[...] = forward_plane(plan, special, pieces, (y_high, y_low), (x_high, x_low), rows_ref, freq_ref)


def middle_plane_kernel(
    plan, me_ref, pieces, even, weights, edge, yf_high, yf_low, xf_high, xf_low, xb_high, xb_low,
    yb_high, yb_low, out, rest, rows_ref, freq_ref, sum_ref
):
    special = me_ref[0] == 0
    width = plan.x_chunk
    odd = forward_plane(plan, special, pieces, (yf_high, yf_low), (xf_high, xf_low), rows_ref, freq_ref)
    row = lax.broadcasted_iota(jnp.int32, (plan.ny, width), 0)
    results = []
    for upper in range(2):
        sums = even[...] - odd if upper else even[...] + odd
        cols = slice(upper * width, (upper + 1) * width)
        weight = weights[:, cols]
        second = jnp.where(special & (row == 0), edge[0:1, cols], weight)
        second = jnp.where(special & (row == plan.ny // 2), edge[1:2, cols], second)
        real = weight * sums[: plan.ny, :width] + second * sums[plan.ny :, width:]
        imag = second * sums[plan.ny :, :width] - weight * sums[: plan.ny, width:]
        results.append((real, imag))
    for part in range(2):
        rows = slice(part * plan.ny, (part + 1) * plan.ny)
        below, above = (results[0][part], results[1][part])
        sum_ref[rows] = below + above
        rest[rows] = below - above
    backward_plane(plan, special, sum_ref[...], (xb_high, xb_low), (yb_high, yb_low), out, rows_ref)


def last_plane_kernel(plan, me_ref, freqs, x_high, x_low, y_high, y_low, out, rows_ref):
    special = me_ref[0] == 0
    backward_plane(plan, special, freqs[...], (x_high, x_low), (y_high, y_low), out, rows_ref)


def plane_call(plan, kernel, name, chunks, me, arrays, tables, out_shapes, scratch, work):
    def table_spec(table, chunk):
        if chunk is None:
            return whole_spec(table.shape)
        return pl.BlockSpec((1,) + table.shape[1:], lambda i: (chunk, 0, 0))

    specs = [whole_spec(array.shape) for array in arrays]
    flat = []
    for pair, chunk in zip(tables, chunks):
        for table in pair:
            specs.append(table_spec(table, chunk))
            flat.append(table)
    size = sum(4 * array.size for array in arrays) + sum(2 * table.size for table in flat)
    return pl.pallas_call(
        functools.partial(kernel, plan),
        grid=(1,),
        in_specs=[pl.BlockSpec(memory_space=pltpu.SMEM)] + specs,
        out_specs=[whole_spec(shape) for shape in out_shapes],
        out_shape=[jax.ShapeDtypeStruct(shape, jnp.float32) for shape in out_shapes],
        scratch_shapes=[pltpu.VMEM(shape, jnp.float32) for shape in scratch],
        compiler_params=pltpu.CompilerParams(vmem_limit_bytes=VMEM_LIMIT),
        cost_estimate=pl.CostEstimate(
            flops=work * 12 * plan.nx * plan.ny * plan.x_chunk, bytes_accessed=size, transcendentals=0
        ),
        name=name,
    )(me, *arrays, *flat)


def gather_kernel(plan, last, counts, before, projection, high, low, pieces, out, scratch):
    planes = plan.cell_planes
    rows = plan.slots * 2 * plan.row_block
    first = pl.program_id(0) * LANES

    @pl.when(pl.program_id(0) == 0)
    def _():
        columns = [pieces[:, :, step].reshape(rows, LANES) for step in range(plan.steps)]
        scratch[...] = product(split(jnp.concatenate(columns, axis=1).T), (high[...], low[...]))

    for block in range(plan.step_blocks):
        lanes = pl.ds(block * LANES, LANES)
        far = [before[p, :, lanes] for p in range(plan.panels)]
        for tx in range(plan.tx_chunk):
            for ty in range(TY):
                row = ((block * TY + ty) * plan.tx_chunk + tx) * planes
                rows_at = pl.ds(pl.multiple_of(first + row, planes), planes)
                for tz in range(TZ):
                    t = ty * TZ + tz
                    potential = scratch[rows_at, tz * LANES : (tz + 1) * LANES]
                    for p in range(plan.panels):
                        far[p] = far[p] + projection[p, tx, 0, t, :, lanes] * potential
        for p in range(plan.panels):
            out[p, :, lanes] = jnp.where(counts[:, lanes] > p, far[p], 0.0) if last else far[p]


def gather(plan, chunk, counts, before, projection, high, low, pieces):
    return pl.pallas_call(
        functools.partial(gather_kernel, plan, chunk == CHUNKS - 1),
        grid=(plan.steps,),
        in_specs=[
            count_spec(plan),
            panel_spec(plan),
            projection_spec(plan, chunk),
            whole_spec(high.shape),
            whole_spec(low.shape),
            whole_spec(pieces.shape),
        ],
        out_specs=panel_spec(plan),
        out_shape=jax.ShapeDtypeStruct(before.shape, jnp.float32),
        scratch_shapes=[pltpu.VMEM((plan.steps * LANES, TZ * LANES), jnp.float32)],
        compiler_params=pltpu.CompilerParams(vmem_limit_bytes=VMEM_LIMIT),
        cost_estimate=projection_cost(projection),
        name="depth_gather",
    )(counts, before, projection, high, low, pieces)


def near_kernel(plan, extended, codes, blocks_ref, out):
    step = pl.program_id(0)
    lane = lax.broadcasted_iota(jnp.int32, (plan.cell_planes, LANES), 1)
    depth = lane % NZC
    digits = []
    for k in range(plan.near):
        code = codes[k]
        digits.append((code // 9, code // 3 % 3, code % 3))
    total = [None] * plan.panels
    for q in range(plan.panels):
        shifted = []
        for dx in range(3):
            before, here, after = (
                extended[q, dx, :, pl.ds(pl.multiple_of((step + i) * LANES, LANES), LANES)] for i in range(3)
            )
            up = jnp.where(lane < NZC, pltpu.roll(before, NZC, 1), pltpu.roll(here, NZC, 1))
            down = jnp.where(
                lane >= LANES - NZC, pltpu.roll(after, LANES - NZC, 1), pltpu.roll(here, LANES - NZC, 1)
            )
            for value in (up, here, down):
                under = jnp.where(
                    depth == 0, pltpu.roll(value, LANES - NZC + 1, 1), pltpu.roll(value, 1, 1)
                )
                over = jnp.where(
                    depth == NZC - 1, pltpu.roll(value, NZC - 1, 1), pltpu.roll(value, LANES - 1, 1)
                )
                shifted.append((under, value, over))
        for k in range(plan.near):
            digit_x, digit_y, digit_z = digits[k]

            def choose(digit, options):
                return jnp.where(digit == 0, options[0], jnp.where(digit == 1, options[1], options[2]))

            by_z = [choose(digit_z, options) for options in shifted]
            by_y = [choose(digit_y, by_z[3 * i : 3 * i + 3]) for i in range(3)]
            picked = choose(digit_x, by_y)
            for p in range(plan.panels):
                term = blocks_ref[k, p, q] * picked
                total[p] = term if total[p] is None else total[p] + term
    for p in range(plan.panels):
        out[p] = total[p]


def near_field(plan, extended, neighbours, near_blocks):
    return pl.pallas_call(
        functools.partial(near_kernel, plan),
        grid=(plan.cell_cols // LANES,),
        in_specs=[
            whole_spec(extended.shape),
            pl.BlockSpec((plan.near, plan.cell_planes, LANES), lambda i: (0, 0, i)),
            pl.BlockSpec(
                (plan.near, plan.panels, plan.panels, plan.cell_planes, LANES), lambda i: (0, 0, 0, 0, i)
            ),
        ],
        out_specs=pl.BlockSpec((plan.panels, plan.cell_planes, LANES), lambda i: (0, 0, i)),
        out_shape=jax.ShapeDtypeStruct((plan.panels, plan.cell_planes, plan.cell_cols), jnp.float32),
        compiler_params=pltpu.CompilerParams(vmem_limit_bytes=VMEM_LIMIT),
        cost_estimate=pl.CostEstimate(
            flops=2 * near_blocks.size, bytes_accessed=4 * near_blocks.size, transcendentals=0
        ),
        name="near_blocks",
    )(extended, neighbours, near_blocks)


def ring_pairs(axis):
    count = lax.axis_size(axis)
    up = [(i, (i + 1) % count) for i in range(count)]
    return (up, [(j, i) for i, j in up])


def extend_rows(plan, masked):
    up, down = ring_pairs("cell")
    left = lax.ppermute(masked[:, :, -NZC:], "cell", up)
    right = lax.ppermute(masked[:, :, :NZC], "cell", down)
    return (left, right)


def extend_planes(plan, masked, left, right):
    rest = jnp.zeros((plan.panels, plan.cell_planes, LANES - NZC), jnp.float32)
    wide = jnp.concatenate([rest, left, masked, right, rest], axis=2)
    up, down = ring_pairs("slab")
    before = lax.ppermute(wide[:, -1:], "slab", up)
    after = lax.ppermute(wide[:, :1], "slab", down)
    whole = jnp.concatenate([before, wide, after], axis=1)
    planes = plan.cell_planes
    return jnp.stack([whole[:, i : i + planes] for i in range(3)], axis=1)


def spectrum_weights(plan, spectrum):
    slab, cell = (lax.axis_index("slab"), lax.axis_index("cell"))
    by_depth = jnp.transpose(spectrum, (1, 2, 0))
    own = lax.dynamic_slice_in_dim(by_depth, cell * plan.slabs, plan.slabs, 0)
    dest = lax.broadcasted_iota(jnp.int32, own.shape, 0)
    swapped = (cell == 0) & (slab >= plan.slabs // 2) & (dest == 0)
    own = jnp.where(swapped, by_depth[plan.slots][None], own)
    weights = lax.all_to_all(own, "slab", split_axis=0, concat_axis=0, tiled=True)
    far = lax.ppermute(by_depth[0, :1], "slab", [(plan.slabs // 2, 0)])
    return (weights.reshape(plan.ny, plan.nx), far, by_depth[plan.slots, :1])


def per_device(charges, counts, projection, near_blocks, neighbours, spectrum):
    panels, cell_planes, cell_cols = charges.shape
    cells, slabs = (lax.axis_size("cell"), lax.axis_size("slab"))
    nx, nz, local = spectrum.shape
    plan = Plan(slabs, cells, panels, cell_planes, cell_cols, neighbours.shape[0], nx, nz, local * slabs)
    if not plan.fits():
        return plain_device(charges, counts, projection, near_blocks, neighbours, spectrum)
    me = (lax.axis_index("cell") * slabs + lax.axis_index("slab")).astype(jnp.int32).reshape(1)
    depth_forward, depth_backward = [halves(table) for table in plan.depth_tables()]
    y_rows, x_cols, low_ids = (plan.y_rows(), plan.x_columns(), np.arange(plan.ny // 2))
    y_waves = [wave(low_ids, rows, plan.ny) for rows in y_rows]
    x_waves = [wave(cols, low_ids, plan.nx) for cols in x_cols]
    y_forward = halves(np.stack([np.concatenate(pair, axis=0) for pair in y_waves]))
    y_backward = halves(np.stack([np.concatenate([t.T for t in pair], axis=0) for pair in y_waves]))
    x_forward = halves(np.stack([np.concatenate(pair, axis=1) for pair in x_waves]))
    x_backward = halves(np.stack([np.concatenate([t.T for t in pair], axis=1) for pair in x_waves]))
    split_projection = projection.reshape(
        (panels, TX // CHUNKS, CHUNKS, TY * TZ, cell_planes, cell_cols)
    )
    axes = ("cell", "slab")

    def exchange(pieces):
        return lax.all_to_all(pieces, axes, split_axis=0, concat_axis=0, tiled=True)

    rows_shape = (plan.ny, 2 * plan.x_chunk)
    freq_shape = (2 * plan.ny, plan.x_chunk)
    both_shape = (2 * plan.ny, plan.nx)
    weights, far, near = spectrum_weights(plan, spectrum)
    slot = lax.broadcasted_iota(jnp.int32, charges.shape, 0)
    masked = jnp.where(slot < counts[None], charges, 0.0)
    left, right = extend_rows(plan, masked)
    pieces = [project(plan, i, charges, counts, split_projection, *depth_forward) for i in range(CHUNKS)]
    pieces[0], far, left, right = lax.optimization_barrier((pieces[0], far, left, right))
    edge = jnp.concatenate([far, near], axis=0)
    extended = extend_planes(plan, masked, left, right)
    even_pieces = exchange(pieces[0])
    pieces[1], extended = lax.optimization_barrier((pieces[1], extended))
    odd_pieces = exchange(pieces[1])
    (even,) = plane_call(
        plan, first_plane_kernel, "even_planes", (None, 0), me, [even_pieces], [y_forward, x_forward],
        [both_shape], [rows_shape, freq_shape], 2,
    )
    total = near_field(plan, extended, neighbours, near_blocks)
    even, total = lax.optimization_barrier((even, total))
    back, rest = plane_call(
        plan, middle_plane_kernel, "middle_planes", (None, 1, 0, None), me,
        [odd_pieces, even, weights, edge], [y_forward, x_forward, x_backward, y_backward],
        [piece_shape(plan), freq_shape], [rows_shape, freq_shape, freq_shape], 4,
    )
    even_back = exchange(back)
    (back,) = plane_call(
        plan, last_plane_kernel, "odd_planes", (1, None), me, [rest], [x_backward, y_backward],
        [piece_shape(plan)], [rows_shape], 2,
    )
    odd_back = exchange(back)
    total = gather(plan, 0, counts, total, split_projection, *depth_backward, even_back)
    return gather(plan, 1, counts, total, split_projection, *depth_backward, odd_back)


def padded(value, sides, width):
    for axis, dim in sides:
        count, length = (lax.axis_size(axis), value.shape[dim])
        up = [(i, (i + 1) % count) for i in range(count)]
        down = [(j, i) for i, j in up]
        last = lax.slice_in_dim(value, length - width, length, axis=dim)
        first = lax.slice_in_dim(value, 0, width, axis=dim)
        before = lax.ppermute(last, axis, up)
        after = lax.ppermute(first, axis, down)
        value = jnp.concatenate([before, value, after], axis=dim)
    return value


def wave_tables(row_count, col_count, length):
    products = (
        lax.broadcasted_iota(jnp.int32, (row_count, col_count), 0)
        * lax.broadcasted_iota(jnp.int32, (row_count, col_count), 1)
        % length
    )
    angle_rad = products.astype(jnp.float32) * (2.0 * math.pi / length)
    return (jnp.cos(angle_rad), jnp.sin(angle_rad))


def depth_rows(nz, freq_ids, valid, weights):
    depth_ids = lax.broadcasted_iota(jnp.int32, (freq_ids.shape[0], nz), 1)
    products = freq_ids[:, None] * depth_ids % nz
    angle_rad = products.astype(jnp.float32) * (2.0 * math.pi / nz)
    basis = jnp.stack([jnp.cos(angle_rad), -jnp.sin(angle_rad)])
    return (basis * valid[None, :, None], basis * weights[None, :, None])


def half_depth_tables(nz, cell_count):
    lower = nz // (2 * cell_count)
    row_ids = lax.broadcasted_iota(jnp.int32, (cell_count * (lower + 1),), 0)
    block_ids = row_ids // (lower + 1)
    slot_ids = row_ids % (lower + 1)
    freq_ids = jnp.where(slot_ids < lower, block_ids * lower + slot_ids, nz // 2)
    valid = jnp.where((slot_ids < lower) | (block_ids == 0), 1.0, 0.0).astype(jnp.float32)
    doubled = jnp.where((slot_ids < lower) & (freq_ids > 0), 2.0, 1.0).astype(jnp.float32)
    forward_table, backward_table = depth_rows(nz, freq_ids, valid, valid * doubled)
    return (forward_table, backward_table, freq_ids)


def combine_halves(first_part, second, orient):
    half_width = first_part.shape[-1] // 2
    real_part = first_part[..., :half_width] + orient * second[..., half_width:]
    imag_part = first_part[..., half_width:] - orient * second[..., :half_width]
    return jnp.concatenate([real_part, imag_part], axis=-1)


def transform_axis(pattern, cosine, sine_tab, values, orient):
    first_part = jnp.einsum(pattern, cosine, values, precision=lax.Precision.HIGHEST)
    second = jnp.einsum(pattern, sine_tab, values, precision=lax.Precision.HIGHEST)
    return combine_halves(first_part, second, orient)


def twiddle(values, twist_cos, twist_sin, orient):
    half_width = values.shape[-1] // 2
    real_part = values[..., :half_width]
    imag_part = values[..., half_width:]
    new_real = real_part * twist_cos + orient * imag_part * twist_sin
    new_imag = imag_part * twist_cos - orient * real_part * twist_sin
    return jnp.concatenate([new_real, new_imag], axis=-1)


def transform_rows(planes_block, cosine, sine_tab, orient):
    flat_rows = planes_block.reshape(-1, planes_block.shape[-1])
    first_part = jnp.dot(flat_rows, cosine, precision=lax.Precision.HIGHEST).reshape(
        planes_block.shape
    )
    second = jnp.dot(flat_rows, sine_tab, precision=lax.Precision.HIGHEST).reshape(
        planes_block.shape
    )
    real_part = first_part[:, 0] + orient * second[:, 1]
    imag_part = first_part[:, 1] - orient * second[:, 0]
    return jnp.stack([real_part, imag_part], axis=1)


def plain_device(charges, counts, projection, near_blocks, neighbours, spectrum):
    panels, cell_planes, cell_cols = charges.shape
    nx, nz, ny = (spectrum.shape[0], spectrum.shape[1], spectrum.shape[2] * lax.axis_size("slab"))
    planes = cell_planes * TX
    rows_cell = cell_cols // NZC
    slot_ids = lax.broadcasted_iota(jnp.int32, charges.shape, 0)
    panel_mask = (slot_ids < counts[None]).astype(jnp.float32)
    masked = charges * panel_mask
    tile_values = jnp.einsum("ptxc,pxc->txc", projection, masked, precision=lax.Precision.HIGHEST)
    grid_field = (
        tile_values.reshape(TX, TY, TZ, cell_planes, rows_cell, NZC)
        .transpose(3, 0, 5, 2, 4, 1)
        .reshape(planes, nz, rows_cell * TY)
    )
    cell_count = lax.axis_size("cell")
    forward_table, backward_table, freq_ids = half_depth_tables(nz, cell_count)
    depth_count = forward_table.shape[1] // cell_count
    spectra_z = jnp.einsum(
        "wkz,xzy->xwky", forward_table, grid_field, precision=lax.Precision.HIGHEST
    )
    cosine_y, sine_y = wave_tables(ny, ny, ny)
    pencils = transform_rows(
        lax.all_to_all(spectra_z, "cell", split_axis=2, concat_axis=3, tiled=True),
        cosine_y,
        sine_y,
        1.0,
    )
    columns = lax.all_to_all(pencils, "slab", split_axis=3, concat_axis=0, tiled=True)
    col_width = columns.shape[2] * columns.shape[3]
    flat_rows = columns.reshape(nx, 2 * col_width)
    first_row = lax.axis_index("cell") * depth_count
    kernel_ids = lax.dynamic_slice_in_dim(freq_ids, first_row, depth_count, 0)
    kernel = jnp.take(spectrum, kernel_ids, axis=1).reshape(nx, col_width) * (1.0 / (nx * ny * nz))
    kernel_both = jnp.concatenate([kernel, kernel], axis=1)
    slab_count = lax.axis_size("slab")
    local_rows = nx // slab_count
    cosine_s, sine_s = wave_tables(slab_count, slab_count, slab_count)
    cosine_r, sine_r = wave_tables(local_rows, local_rows, local_rows)
    twist_cos, twist_sin = wave_tables(slab_count, local_rows, nx)
    twist_cos = twist_cos[:, :, None]
    twist_sin = twist_sin[:, :, None]
    section_one = transform_axis(
        "ks,src->krc",
        cosine_s,
        sine_s,
        flat_rows.reshape(slab_count, local_rows, 2 * col_width),
        1.0,
    )
    section_one = twiddle(section_one, twist_cos, twist_sin, 1.0)
    section_two = transform_axis("jr,krc->jkc", cosine_r, sine_r, section_one, 1.0)
    weighted = section_two.reshape(nx, 2 * col_width) * kernel_both
    section_one = transform_axis(
        "rj,jkc->krc",
        cosine_r,
        sine_r,
        weighted.reshape(local_rows, slab_count, 2 * col_width),
        -1.0,
    )
    section_one = twiddle(section_one, twist_cos, twist_sin, -1.0)
    section_two = transform_axis("sk,krc->src", cosine_s, sine_s, section_one, -1.0)
    returned_x = section_two.reshape(nx, 2 * col_width)
    returned = lax.all_to_all(
        returned_x.reshape(columns.shape), "slab", split_axis=0, concat_axis=3, tiled=True
    )
    inverse_rows = transform_rows(returned, cosine_y, sine_y, -1.0)
    grid_potential = jnp.einsum(
        "wkz,xwky->xzy",
        backward_table,
        lax.all_to_all(inverse_rows, "cell", split_axis=3, concat_axis=2, tiled=True),
        precision=lax.Precision.HIGHEST,
    )
    tile_potential = (
        grid_potential.reshape(cell_planes, TX, NZC, TZ, rows_cell, TY)
        .transpose(1, 5, 3, 0, 4, 2)
        .reshape(TX * TY * TZ, cell_planes, cell_cols)
    )
    far_field = jnp.einsum(
        "ptxc,txc->pxc", projection, tile_potential, precision=lax.Precision.HIGHEST
    )
    block = masked.reshape(panels, cell_planes, rows_cell, NZC)
    extended = padded(block, (("slab", 1), ("cell", 2)), 1)
    flat_ext = extended.reshape(panels, -1)
    step_x = neighbours // 9 - 1
    step_y = neighbours // 3 % 3 - 1
    step_z = neighbours % 3 - 1
    plane_ids = lax.broadcasted_iota(jnp.int32, neighbours.shape, 1)
    col_ids = lax.broadcasted_iota(jnp.int32, neighbours.shape, 2)
    row_ids = col_ids // NZC
    depth_ids = col_ids % NZC
    near_ids = ((plane_ids + step_x + 1) * (rows_cell + 2) + row_ids + step_y + 1) * NZC + (
        depth_ids + step_z
    ) % NZC
    near_count = neighbours.shape[0]
    picked = jnp.take(flat_ext, near_ids.reshape(-1), axis=1).reshape(
        panels, near_count, cell_planes, cell_cols
    )
    near_field = jnp.einsum("kpqxc,qkxc->pxc", near_blocks, picked, precision=lax.Precision.HIGHEST)
    return (far_field + near_field) * panel_mask


def solution(mesh):
    in_specs = (
        P(None, "slab", "cell"),
        P("slab", "cell"),
        P(None, None, "slab", "cell"),
        P(None, None, None, "slab", "cell"),
        P(None, "slab", "cell"),
        P(None, None, "slab"),
    )
    out_specs = P(None, "slab", "cell")
    return jax.shard_map(
        per_device, mesh=mesh, in_specs=in_specs, out_specs=out_specs, check_vma=False
    )
```

```python
import functools
import math

import jax
import jax.numpy as jnp
import ml_dtypes
import numpy as np
from jax import lax
from jax.experimental import pallas as pl
from jax.experimental.pallas import tpu as pltpu
from jax.sharding import PartitionSpec as P

TX = 4
TY = 4
TZ = 4
NZC = 16
LANES = 128
CHUNKS = 2
VMEM_LIMIT = 60 * 1024 * 1024


def halves(table):
    high = table.astype(np.float32).astype(ml_dtypes.bfloat16)
    low = (table - high.astype(np.float64)).astype(np.float32).astype(ml_dtypes.bfloat16)
    return (high, low)


def wave(rows, cols, length):
    angle = (rows[:, None] * cols[None, :] % length) * (2.0 * math.pi / length)
    return (np.cos(angle), np.sin(angle))


class Plan:
    def __init__(self, slabs, cells, panels, cell_planes, cell_cols, near, nx, nz, ny):
        self.slabs, self.cells = (slabs, cells)
        self.panels, self.cell_planes, self.cell_cols, self.near = (panels, cell_planes, cell_cols, near)
        self.nx, self.ny, self.nz = (nx, ny, nz)
        self.slots = slabs * cells
        self.tx_chunk = TX // CHUNKS
        self.width = cell_planes * self.tx_chunk
        self.y_lanes = LANES // self.width if self.width else 1
        self.row_block = LANES // NZC
        self.step_blocks = self.y_lanes // TY
        self.steps = cell_cols // (LANES * self.step_blocks) if self.step_blocks else 0
        self.x_chunk = nx // CHUNKS
        self.ky_local = ny // slabs
        self.outer = math.gcd(slabs, 4)
        self.inner = slabs // self.outer

    def fits(self):
        return (
            self.slots * 2 == self.nz
            and self.cell_planes == 8
            and self.step_blocks * TY * self.width == LANES
            and self.slabs % self.y_lanes == 0
            and self.ky_local % 8 == 0
            and self.steps * self.step_blocks * LANES == self.cell_cols
            and self.x_chunk % LANES == 0
            and self.ny % 1024 == self.nx % 1024 == 512
        )

    def depth_tables(self):
        depth = np.arange(NZC)[None, :] * TZ + np.arange(TZ)[:, None]
        scale = 1.0 / (self.nx * self.ny * self.nz)
        forward = np.zeros((self.slots, 2, self.row_block, TZ, self.row_block, NZC))
        backward = np.zeros_like(forward)
        for freq in range(self.slots):
            angle = (freq * depth % self.nz) * (2.0 * math.pi / self.nz)
            real, imag = (np.cos(angle), -np.sin(angle))
            factor = 2.0 * scale
            if freq == 0:
                imag = np.cos(depth * math.pi)
                factor = scale
            for row in range(self.row_block):
                forward[freq, 0, row, :, row, :] = real
                forward[freq, 1, row, :, row, :] = imag
                backward[freq, 0, row, :, row, :] = factor * real
                backward[freq, 1, row, :, row, :] = factor * imag
        shape = (self.slots * 2 * self.row_block, TZ * LANES)
        return (forward.reshape(shape), backward.reshape(shape))

    def y_rows(self):
        parity, cell, step, block, tile, row = np.meshgrid(
            *[np.arange(n) for n in (2, self.cells, self.steps, self.step_blocks, TY // 2, self.row_block)],
            indexing="ij",
        )
        cell_row = ((cell * self.steps + step) * self.step_blocks + block) * self.row_block + row
        return (cell_row * TY + 2 * tile + parity).reshape(2, -1)

    def x_columns(self):
        parity, slab, tile, plane = np.meshgrid(
            *[np.arange(n) for n in (2, self.slabs, TX // 2, self.cell_planes)], indexing="ij"
        )
        return ((slab * self.cell_planes + plane) * TX + 2 * tile + parity).reshape(2, -1)

    def row_of(self, cell, step, place):
        block, tile = (place // TY, place % TY)
        inner = (cell * self.steps + step) * self.step_blocks + block
        return (tile % 2) * (self.ny // 2) + (inner * (TY // 2) + tile // 2) * self.row_block


def split(value):
    high = value.astype(jnp.bfloat16)
    low = (value - high.astype(jnp.float32)).astype(jnp.bfloat16)
    return (high, low)


def product(left, right, dims=((1,), (0,))):
    first = jnp.concatenate([left[0], left[0], left[1]], axis=dims[0][0])
    second = jnp.concatenate([right[0], right[1], right[0]], axis=dims[1][0])
    return lax.dot_general(first, second, (dims, ((), ())), preferred_element_type=jnp.float32)


def swap_groups(parts, width):
    count = len(parts)
    lane = lax.broadcasted_iota(jnp.int32, parts[0].shape, 1)
    parts = list(parts)
    step = count // 2
    while step >= 1:
        shift = step * width
        upper = (lane // shift) % 2 == 1
        for i in range(count):
            if i & step:
                continue
            first, second = (parts[i], parts[i + step])
            parts[i] = jnp.where(upper, pltpu.roll(second, shift, 1), first)
            parts[i + step] = jnp.where(upper, second, pltpu.roll(first, LANES - shift, 1))
        step //= 2
    return parts


def lane_copies(plan, chunk, projection, held, sems):
    width = plan.step_blocks * LANES
    return [
        pltpu.make_async_copy(
            projection.at[:, :, chunk, :, :, pl.ds(step * width, width)], held.at[step], sems.at[step]
        )
        for step in range(plan.steps)
    ]


def wait_lanes(held, sems, step):
    pltpu.make_async_copy(held.at[step], held.at[step], sems.at[step]).wait()


def project_kernel(plan, chunk, charges, counts, high, low, projection, out, scratch, held, sems):
    planes = plan.cell_planes
    for copy in lane_copies(plan, chunk, projection, held, sems):
        copy.start()

    def body(step, carry):
        wait_lanes(held, sems, step)
        for block in range(plan.step_blocks):
            start = pl.multiple_of((step * plan.step_blocks + block) * LANES, LANES)
            count = counts[:, pl.ds(start, LANES)]
            own = [jnp.where(count > p, charges[p, :, pl.ds(start, LANES)], 0.0) for p in range(plan.panels)]
            lanes = slice(block * LANES, (block + 1) * LANES)
            for tx in range(plan.tx_chunk):
                for ty in range(TY):
                    row = step * LANES + ((block * TY + ty) * plan.tx_chunk + tx) * planes
                    rows = pl.ds(pl.multiple_of(row, planes), planes)
                    for tz in range(TZ):
                        t = ty * TZ + tz
                        total = held[step, 0, tx, t, :, lanes] * own[0]
                        for p in range(1, plan.panels):
                            total = total + held[step, p, tx, t, :, lanes] * own[p]
                        scratch[rows, tz * LANES : (tz + 1) * LANES] = total
        return carry

    lax.fori_loop(0, plan.steps, body, 0)
    spectra = product((high[...], low[...]), split(scratch[...]), ((1,), (1,)))
    shape = (plan.slots, 2, plan.row_block, LANES)
    for step in range(plan.steps):
        out[:, :, step] = spectra[:, step * LANES : (step + 1) * LANES].reshape(shape)


def held_shape(plan):
    return (plan.steps, plan.panels, plan.tx_chunk, TY * TZ, plan.cell_planes, plan.step_blocks * LANES)


def piece_shape(plan):
    return (plan.slots, 2, plan.steps, plan.row_block, LANES)


def whole_spec(shape):
    return pl.BlockSpec(shape, lambda i: (0,) * len(shape))


def projection_call(plan, kernel, name, arrays, projection, out_shape):
    return pl.pallas_call(
        kernel,
        grid=(1,),
        in_specs=[whole_spec(array.shape) for array in arrays] + [pl.BlockSpec(memory_space=pl.ANY)],
        out_specs=whole_spec(out_shape),
        out_shape=jax.ShapeDtypeStruct(out_shape, jnp.float32),
        scratch_shapes=[
            pltpu.VMEM((plan.steps * LANES, TZ * LANES), jnp.float32),
            pltpu.VMEM(held_shape(plan), jnp.float32),
            pltpu.SemaphoreType.DMA((plan.steps,)),
        ],
        compiler_params=pltpu.CompilerParams(vmem_limit_bytes=VMEM_LIMIT),
        cost_estimate=pl.CostEstimate(
            flops=2 * projection.size // CHUNKS,
            bytes_accessed=4 * projection.size // CHUNKS,
            transcendentals=0,
        ),
        name=name,
    )(*arrays, projection)


def project(plan, chunk, charges, counts, projection, high, low):
    kernel = functools.partial(project_kernel, plan, chunk)
    arrays = [charges, counts, high, low]
    return projection_call(plan, kernel, "project_depth", arrays, projection, piece_shape(plan))


def forward_plane(plan, special, pieces, y_table, x_table, rows_ref, freq_ref):
    rows = 2 * plan.steps * plan.row_block
    width = plan.x_chunk
    middle = plan.ny // 2
    for cell in range(plan.cells):
        for group in range(plan.slabs // plan.y_lanes):
            first = cell * plan.slabs + group * plan.y_lanes
            parts = [pieces[first + i].reshape(rows, LANES) for i in range(plan.y_lanes)]
            parts = swap_groups(parts, plan.width)
            for place, value in enumerate(parts):
                for part in range(2):
                    for step in range(plan.steps):
                        source = (part * plan.steps + step) * plan.row_block
                        row = plan.row_of(cell, step, place)
                        col = part * width + group * LANES
                        rows_ref[row : row + plan.row_block, col : col + LANES] = value[
                            source : source + plan.row_block
                        ]
    high, low = y_table
    even = product((high[0], low[0]), split(rows_ref[:middle]))
    odd = product((high[1], low[1]), split(rows_ref[middle:]))
    for upper, sums in ((0, even + odd), (1, even - odd)):
        cosine, sine = (sums[:middle], sums[middle:])
        start = upper * middle
        freq_ref[start : start + middle] = cosine[:, :width] + sine[:, width:]
        start += plan.ny
        freq_ref[start : start + middle] = cosine[:, width:] - sine[:, :width]

    @pl.when(special)
    def _():
        row = lax.broadcasted_iota(jnp.int32, (middle, width), 0)
        below, above = (even + odd, even - odd)
        for upper, sums, other in ((0, below, above), (1, above, below)):
            cols = slice(upper * width, (upper + 1) * width)
            start = upper * middle
            freq_ref[start : start + middle] = sums[:middle, cols]
            start += plan.ny
            freq_ref[start : start + middle] = jnp.where(row == 0, other[0:1, cols], -sums[middle:, cols])

    high, low = x_table
    return product(split(freq_ref[...]), (high[0], low[0]))


def backward_plane(plan, special, freqs, x_table, y_table, out, rows_ref):
    width = plan.x_chunk
    middle = plan.ny // 2
    high, low = x_table
    sums = product(split(freqs), (high[0], low[0]))
    real = sums[: plan.ny, :width] - sums[plan.ny :, width:]
    imag = sums[plan.ny :, :width] + sums[: plan.ny, width:]
    high, low = y_table

    @pl.when(jnp.logical_not(special))
    def _():
        for parity in range(2):
            joined = []
            for value in (real, imag):
                below, above = (value[:middle], value[middle:])
                joined.append(below + above if parity == 0 else below - above)
            pair = split(jnp.concatenate(joined, axis=1))
            rows = product((high[parity], low[parity]), pair)
            cosine, sine = (rows[:middle], rows[middle:])
            start = parity * middle
            rows_ref[start : start + middle, :width] = cosine[:, :width] - sine[:, width:]
            rows_ref[start : start + middle, width:] = cosine[:, width:] + sine[:, :width]

    @pl.when(special)
    def _():
        row = lax.broadcasted_iota(jnp.int32, (middle, width), 0)
        columns, ends = ([], [])
        for upper in range(2):
            part = slice(upper * middle, (upper + 1) * middle)
            stacked = [jnp.where(row == 0, value[part], 2.0 * value[part]) for value in (real, imag)]
            columns.append(jnp.concatenate(stacked, axis=0))
            ends.append(imag[upper * middle : upper * middle + 1])
        pair = split(jnp.concatenate(columns, axis=1))
        for parity in range(2):
            table = tuple(
                jnp.concatenate([t[parity, :middle], -t[parity, middle:]], axis=1) for t in (high, low)
            )
            rows = product(table, pair)
            sign = 1.0 - 2.0 * parity
            start = parity * middle
            rows_ref[start : start + middle, :width] = rows[:, :width] + sign * ends[0]
            rows_ref[start : start + middle, width:] = sign * rows[:, width:] + ends[1]

    for cell in range(plan.cells):
        for group in range(plan.slabs // plan.y_lanes):
            parts = []
            for place in range(plan.y_lanes):
                tiles = []
                for part in range(2):
                    for step in range(plan.steps):
                        row = plan.row_of(cell, step, place)
                        col = part * width + group * LANES
                        tiles.append(rows_ref[row : row + plan.row_block, col : col + LANES])
                parts.append(jnp.concatenate(tiles, axis=0))
            parts = swap_groups(parts, plan.width)
            first = cell * plan.slabs + group * plan.y_lanes
            for i in range(plan.y_lanes):
                out[first + i] = parts[i].reshape(2, plan.steps, plan.row_block, LANES)


def first_plane_kernel(plan, me_ref, pieces, y_high, y_low, x_high, x_low, out, rows_ref, freq_ref):
    special = me_ref[0] == 0
    out[...] = forward_plane(plan, special, pieces, (y_high, y_low), (x_high, x_low), rows_ref, freq_ref)


def middle_plane_kernel(plan, me_ref, edge, pieces, yf_high, yf_low, xf_high, xf_low, *refs):
    late, refs = (refs[:5], refs[5:])
    strips, refs = (refs[: plan.inner], refs[plan.inner :])
    out, rest, rows_ref, freq_ref, sum_ref, weights = refs[:6]
    even, xb_high, xb_low, yb_high, yb_low, sems = refs[6:]
    slab = lax.rem(me_ref[0], plan.slabs)
    outer_id, inner_id = (slab // plan.inner, lax.rem(slab, plan.inner))
    held = (even, xb_high, xb_low, yb_high, yb_low)
    copies = [pltpu.make_async_copy(late[0], even, sems.at[0])]
    for i in range(plan.inner):
        for j in range(plan.outer):
            owner = lax.rem(outer_id - j + plan.outer, plan.outer) * plan.inner
            owner = owner + lax.rem(inner_id - i + plan.inner, plan.inner)
            rows = pl.ds(pl.multiple_of(owner * plan.ky_local, plan.ky_local), plan.ky_local)
            copies.append(
                pltpu.make_async_copy(
                    strips[i].at[j], weights.at[rows], sems.at[len(held) + i * plan.outer + j]
                )
            )
    early = len(copies)
    for n in range(1, len(held)):
        copies.append(pltpu.make_async_copy(late[n], held[n], sems.at[n]))
    for copy in copies:
        copy.start()
    special = me_ref[0] == 0
    width = plan.x_chunk
    odd = forward_plane(plan, special, pieces, (yf_high, yf_low), (xf_high, xf_low), rows_ref, freq_ref)
    for copy in copies[:early]:
        copy.wait()
    row = lax.broadcasted_iota(jnp.int32, (plan.ny, width), 0)
    results = []
    for upper in range(2):
        sums = even[...] - odd if upper else even[...] + odd
        cols = slice(upper * width, (upper + 1) * width)
        weight = weights[:, cols]
        second = jnp.where(special & (row == 0), edge[0:1, cols], weight)
        second = jnp.where(special & (row == plan.ny // 2), edge[1:2, cols], second)
        real = weight * sums[: plan.ny, :width] + second * sums[plan.ny :, width:]
        imag = second * sums[plan.ny :, :width] - weight * sums[: plan.ny, width:]
        results.append((real, imag))
    for part in range(2):
        rows = slice(part * plan.ny, (part + 1) * plan.ny)
        below, above = (results[0][part], results[1][part])
        sum_ref[rows] = below + above
        rest[rows] = below - above
    for copy in copies[early:]:
        copy.wait()
    x_table = (xb_high.at[pl.ds(0, 1)], xb_low.at[pl.ds(0, 1)])
    backward_plane(plan, special, sum_ref[...], x_table, (yb_high, yb_low), out, rows_ref)


def last_plane_kernel(plan, me_ref, freqs, x_high, x_low, y_high, y_low, out, rows_ref):
    special = me_ref[0] == 0
    backward_plane(plan, special, freqs[...], (x_high, x_low), (y_high, y_low), out, rows_ref)


def plane_call(plan, kernel, name, me, arrays, tables, late, out_shapes, scratch, work):
    specs = [whole_spec(array.shape) for array in arrays]
    flat = []
    for pair, chunk in tables:
        for table in pair:
            shape = table.shape if chunk is None else (1,) + table.shape[1:]
            first = 0 if chunk is None else chunk
            specs.append(pl.BlockSpec(shape, lambda i, first=first: (first, 0, 0)))
            flat.append(table)
    specs += [pl.BlockSpec(memory_space=pl.ANY)] * len(late)
    size = sum(4 * array.size for array in list(arrays) + list(late)) + sum(2 * t.size for t in flat)
    return pl.pallas_call(
        functools.partial(kernel, plan),
        grid=(1,),
        in_specs=[pl.BlockSpec(memory_space=pltpu.SMEM)] + specs,
        out_specs=[whole_spec(shape) for shape in out_shapes],
        out_shape=[jax.ShapeDtypeStruct(shape, jnp.float32) for shape in out_shapes],
        scratch_shapes=scratch,
        compiler_params=pltpu.CompilerParams(vmem_limit_bytes=VMEM_LIMIT),
        cost_estimate=pl.CostEstimate(
            flops=work * 12 * plan.nx * plan.ny * plan.x_chunk, bytes_accessed=size, transcendentals=0
        ),
        name=name,
    )(me, *arrays, *flat, *late)


def gather_kernel(plan, chunk, counts, before, pieces, high, low, projection, out, scratch, held, sems):
    planes = plan.cell_planes
    rows = plan.slots * 2 * plan.row_block
    for copy in lane_copies(plan, chunk, projection, held, sems):
        copy.start()
    columns = [pieces[:, :, step].reshape(rows, LANES) for step in range(plan.steps)]
    scratch[...] = product(split(jnp.concatenate(columns, axis=1).T), (high[...], low[...]))

    def body(step, carry):
        wait_lanes(held, sems, step)
        for block in range(plan.step_blocks):
            cells = pl.ds(pl.multiple_of((step * plan.step_blocks + block) * LANES, LANES), LANES)
            lanes = slice(block * LANES, (block + 1) * LANES)
            far = [before[p, :, cells] for p in range(plan.panels)]
            for tx in range(plan.tx_chunk):
                for ty in range(TY):
                    row = step * LANES + ((block * TY + ty) * plan.tx_chunk + tx) * planes
                    rows_at = pl.ds(pl.multiple_of(row, planes), planes)
                    for tz in range(TZ):
                        t = ty * TZ + tz
                        potential = scratch[rows_at, tz * LANES : (tz + 1) * LANES]
                        for p in range(plan.panels):
                            far[p] = far[p] + held[step, p, tx, t, :, lanes] * potential
            for p in range(plan.panels):
                value = jnp.where(counts[:, cells] > p, far[p], 0.0) if chunk == CHUNKS - 1 else far[p]
                out[p, :, cells] = value
        return carry

    lax.fori_loop(0, plan.steps, body, 0)


def gather(plan, chunk, counts, before, projection, high, low, pieces):
    kernel = functools.partial(gather_kernel, plan, chunk)
    arrays = [counts, before, pieces, high, low]
    return projection_call(plan, kernel, "depth_gather", arrays, projection, before.shape)


def near_kernel(plan, extended, codes, blocks_ref, out):
    step = pl.program_id(0)
    lane = lax.broadcasted_iota(jnp.int32, (plan.cell_planes, LANES), 1)
    depth = lane % NZC
    digits = []
    for k in range(plan.near):
        code = codes[k]
        digits.append((code // 9, code // 3 % 3, code % 3))
    total = [None] * plan.panels
    for q in range(plan.panels):
        shifted = []
        for dx in range(3):
            before, here, after = (
                extended[q, dx, :, pl.ds(pl.multiple_of((step + i) * LANES, LANES), LANES)] for i in range(3)
            )
            up = jnp.where(lane < NZC, pltpu.roll(before, NZC, 1), pltpu.roll(here, NZC, 1))
            down = jnp.where(
                lane >= LANES - NZC, pltpu.roll(after, LANES - NZC, 1), pltpu.roll(here, LANES - NZC, 1)
            )
            for value in (up, here, down):
                under = jnp.where(
                    depth == 0, pltpu.roll(value, LANES - NZC + 1, 1), pltpu.roll(value, 1, 1)
                )
                over = jnp.where(
                    depth == NZC - 1, pltpu.roll(value, NZC - 1, 1), pltpu.roll(value, LANES - 1, 1)
                )
                shifted.append((under, value, over))
        for k in range(plan.near):
            digit_x, digit_y, digit_z = digits[k]

            def choose(digit, options):
                return jnp.where(digit == 0, options[0], jnp.where(digit == 1, options[1], options[2]))

            by_z = [choose(digit_z, options) for options in shifted]
            by_y = [choose(digit_y, by_z[3 * i : 3 * i + 3]) for i in range(3)]
            picked = choose(digit_x, by_y)
            for p in range(plan.panels):
                term = blocks_ref[k, p, q] * picked
                total[p] = term if total[p] is None else total[p] + term
    for p in range(plan.panels):
        out[p] = total[p]


def near_field(plan, extended, neighbours, near_blocks):
    return pl.pallas_call(
        functools.partial(near_kernel, plan),
        grid=(plan.cell_cols // LANES,),
        in_specs=[
            whole_spec(extended.shape),
            pl.BlockSpec((plan.near, plan.cell_planes, LANES), lambda i: (0, 0, i)),
            pl.BlockSpec(
                (plan.near, plan.panels, plan.panels, plan.cell_planes, LANES), lambda i: (0, 0, 0, 0, i)
            ),
        ],
        out_specs=pl.BlockSpec((plan.panels, plan.cell_planes, LANES), lambda i: (0, 0, i)),
        out_shape=jax.ShapeDtypeStruct((plan.panels, plan.cell_planes, plan.cell_cols), jnp.float32),
        compiler_params=pltpu.CompilerParams(vmem_limit_bytes=VMEM_LIMIT),
        cost_estimate=pl.CostEstimate(
            flops=2 * near_blocks.size, bytes_accessed=4 * near_blocks.size, transcendentals=0
        ),
        name="near_blocks",
    )(extended, neighbours, near_blocks)


def ring_pairs(axis):
    count = lax.axis_size(axis)
    up = [(i, (i + 1) % count) for i in range(count)]
    return (up, [(j, i) for i, j in up])


def extend_rows(plan, masked):
    up, down = ring_pairs("cell")
    left = lax.ppermute(masked[:, :, -NZC:], "cell", up)
    right = lax.ppermute(masked[:, :, :NZC], "cell", down)
    return (left, right)


def extend_planes(plan, masked, left, right):
    rest = jnp.zeros((plan.panels, plan.cell_planes, LANES - NZC), jnp.float32)
    wide = jnp.concatenate([rest, left, masked, right, rest], axis=2)
    up, down = ring_pairs("slab")
    before = lax.ppermute(wide[:, -1:], "slab", up)
    after = lax.ppermute(wide[:, :1], "slab", down)
    whole = jnp.concatenate([before, wide, after], axis=1)
    planes = plan.cell_planes
    return jnp.stack([whole[:, i : i + planes] for i in range(3)], axis=1)


def first_weights(plan, spectrum):
    slab, cell = (lax.axis_index("slab"), lax.axis_index("cell"))
    by_depth = jnp.transpose(spectrum, (1, 2, 0))
    far = lax.ppermute(by_depth[0, :1], "slab", [(plan.slabs // 2, 0)])
    blocks = []
    for j in range(plan.outer):
        group = lax.rem(slab // plan.inner + j, plan.outer)
        own = lax.dynamic_slice_in_dim(by_depth, cell * plan.slabs + group * plan.inner, plan.inner, 0)
        dest = lax.broadcasted_iota(jnp.int32, own.shape, 0)
        swapped = (cell == 0) & (slab >= plan.slabs // 2) & (group == 0) & (dest == 0)
        own = jnp.where(swapped, by_depth[plan.slots][None], own)
        if j > 0:
            shift = j * plan.inner
            own = lax.ppermute(own, "slab", [(i, (i + shift) % plan.slabs) for i in range(plan.slabs)])
        blocks.append(own)
    return (blocks, far, by_depth[plan.slots, :1])


def second_weights(plan, blocks):
    slab = lax.axis_index("slab")
    strips = []
    for i in range(plan.inner):
        place = lax.rem(slab + i, plan.inner)
        strip = jnp.concatenate([lax.dynamic_slice_in_dim(b, place, 1, 0) for b in blocks], axis=0)
        if i > 0:
            pairs = []
            for source in range(plan.slabs):
                group = source // plan.inner * plan.inner
                pairs.append((source, group + (source + i) % plan.inner))
            strip = lax.ppermute(strip, "slab", pairs)
        strips.append(strip)
    return strips


def per_device(charges, counts, projection, near_blocks, neighbours, spectrum):
    panels, cell_planes, cell_cols = charges.shape
    cells, slabs = (lax.axis_size("cell"), lax.axis_size("slab"))
    nx, nz, local = spectrum.shape
    plan = Plan(slabs, cells, panels, cell_planes, cell_cols, neighbours.shape[0], nx, nz, local * slabs)
    if not plan.fits():
        return plain_device(charges, counts, projection, near_blocks, neighbours, spectrum)
    me = (lax.axis_index("cell") * slabs + lax.axis_index("slab")).astype(jnp.int32).reshape(1)
    depth_forward, depth_backward = [halves(table) for table in plan.depth_tables()]
    y_rows, x_cols, low_ids = (plan.y_rows(), plan.x_columns(), np.arange(plan.ny // 2))
    y_waves = [wave(low_ids, rows, plan.ny) for rows in y_rows]
    x_waves = [wave(cols, low_ids, plan.nx) for cols in x_cols]
    y_forward = halves(np.stack([np.concatenate(pair, axis=0) for pair in y_waves]))
    y_backward = halves(np.stack([np.concatenate([t.T for t in pair], axis=0) for pair in y_waves]))
    x_forward = halves(np.stack([np.concatenate(pair, axis=1) for pair in x_waves]))
    x_backward = halves(np.stack([np.concatenate([t.T for t in pair], axis=1) for pair in x_waves]))
    split_projection = projection.reshape(
        (panels, TX // CHUNKS, CHUNKS, TY * TZ, cell_planes, cell_cols)
    )
    axes = ("cell", "slab")

    def exchange(pieces):
        return lax.all_to_all(pieces, axes, split_axis=0, concat_axis=0, tiled=True)

    def values(*shapes):
        return [pltpu.VMEM(shape, jnp.float32) for shape in shapes]

    rows_shape = (plan.ny, 2 * plan.x_chunk)
    freq_shape = (2 * plan.ny, plan.x_chunk)
    both_shape = (2 * plan.ny, plan.nx)
    blocks, far, near = first_weights(plan, spectrum)
    slot = lax.broadcasted_iota(jnp.int32, charges.shape, 0)
    masked = jnp.where(slot < counts[None], charges, 0.0)
    left, right = extend_rows(plan, masked)
    pieces = [project(plan, i, charges, counts, split_projection, *depth_forward) for i in range(CHUNKS)]
    pieces[0], blocks[1], far = lax.optimization_barrier((pieces[0], blocks[1], far))
    even_pieces = exchange(pieces[0])
    pieces[1], left, right, *blocks[2:] = lax.optimization_barrier(
        (pieces[1], left, right, *blocks[2:])
    )
    odd_pieces = exchange(pieces[1])
    strips = second_weights(plan, blocks)
    (even,) = plane_call(
        plan, first_plane_kernel, "even_planes", me, [even_pieces], [(y_forward, None), (x_forward, 0)], [],
        [both_shape], values(rows_shape, freq_shape), 2,
    )
    edge = jnp.concatenate([far, near], axis=0)
    late = [even, x_backward[0][:1], x_backward[1][:1], *y_backward]
    copies = [pltpu.VMEM(array.shape, array.dtype) for array in late]
    copies.append(pltpu.SemaphoreType.DMA((len(late) + plan.slabs,)))
    back, rest = plane_call(
        plan, middle_plane_kernel, "middle_planes", me, [edge, odd_pieces],
        [(y_forward, None), (x_forward, 1)], late + strips, [piece_shape(plan), freq_shape],
        values(rows_shape, freq_shape, freq_shape, (plan.ny, plan.nx)) + copies, 4,
    )
    even_back = exchange(back)
    (back,) = plane_call(
        plan, last_plane_kernel, "odd_planes", me, [rest], [(x_backward, 1), (y_backward, None)], [],
        [piece_shape(plan)], values(rows_shape), 2,
    )
    total = near_field(plan, extend_planes(plan, masked, left, right), neighbours, near_blocks)
    back, total = lax.optimization_barrier((back, total))
    odd_back = exchange(back)
    total = gather(plan, 0, counts, total, split_projection, *depth_backward, even_back)
    return gather(plan, 1, counts, total, split_projection, *depth_backward, odd_back)


def padded(value, sides, width):
    for axis, dim in sides:
        count, length = (lax.axis_size(axis), value.shape[dim])
        up = [(i, (i + 1) % count) for i in range(count)]
        down = [(j, i) for i, j in up]
        last = lax.slice_in_dim(value, length - width, length, axis=dim)
        first = lax.slice_in_dim(value, 0, width, axis=dim)
        before = lax.ppermute(last, axis, up)
        after = lax.ppermute(first, axis, down)
        value = jnp.concatenate([before, value, after], axis=dim)
    return value


def wave_tables(row_count, col_count, length):
    products = (
        lax.broadcasted_iota(jnp.int32, (row_count, col_count), 0)
        * lax.broadcasted_iota(jnp.int32, (row_count, col_count), 1)
        % length
    )
    angle_rad = products.astype(jnp.float32) * (2.0 * math.pi / length)
    return (jnp.cos(angle_rad), jnp.sin(angle_rad))


def depth_rows(nz, freq_ids, valid, weights):
    depth_ids = lax.broadcasted_iota(jnp.int32, (freq_ids.shape[0], nz), 1)
    products = freq_ids[:, None] * depth_ids % nz
    angle_rad = products.astype(jnp.float32) * (2.0 * math.pi / nz)
    basis = jnp.stack([jnp.cos(angle_rad), -jnp.sin(angle_rad)])
    return (basis * valid[None, :, None], basis * weights[None, :, None])


def half_depth_tables(nz, cell_count):
    lower = nz // (2 * cell_count)
    row_ids = lax.broadcasted_iota(jnp.int32, (cell_count * (lower + 1),), 0)
    block_ids = row_ids // (lower + 1)
    slot_ids = row_ids % (lower + 1)
    freq_ids = jnp.where(slot_ids < lower, block_ids * lower + slot_ids, nz // 2)
    valid = jnp.where((slot_ids < lower) | (block_ids == 0), 1.0, 0.0).astype(jnp.float32)
    doubled = jnp.where((slot_ids < lower) & (freq_ids > 0), 2.0, 1.0).astype(jnp.float32)
    forward_table, backward_table = depth_rows(nz, freq_ids, valid, valid * doubled)
    return (forward_table, backward_table, freq_ids)


def combine_halves(first_part, second, orient):
    half_width = first_part.shape[-1] // 2
    real_part = first_part[..., :half_width] + orient * second[..., half_width:]
    imag_part = first_part[..., half_width:] - orient * second[..., :half_width]
    return jnp.concatenate([real_part, imag_part], axis=-1)


def transform_axis(pattern, cosine, sine_tab, values, orient):
    first_part = jnp.einsum(pattern, cosine, values, precision=lax.Precision.HIGHEST)
    second = jnp.einsum(pattern, sine_tab, values, precision=lax.Precision.HIGHEST)
    return combine_halves(first_part, second, orient)


def twiddle(values, twist_cos, twist_sin, orient):
    half_width = values.shape[-1] // 2
    real_part = values[..., :half_width]
    imag_part = values[..., half_width:]
    new_real = real_part * twist_cos + orient * imag_part * twist_sin
    new_imag = imag_part * twist_cos - orient * real_part * twist_sin
    return jnp.concatenate([new_real, new_imag], axis=-1)


def transform_rows(planes_block, cosine, sine_tab, orient):
    flat_rows = planes_block.reshape(-1, planes_block.shape[-1])
    first_part = jnp.dot(flat_rows, cosine, precision=lax.Precision.HIGHEST).reshape(
        planes_block.shape
    )
    second = jnp.dot(flat_rows, sine_tab, precision=lax.Precision.HIGHEST).reshape(
        planes_block.shape
    )
    real_part = first_part[:, 0] + orient * second[:, 1]
    imag_part = first_part[:, 1] - orient * second[:, 0]
    return jnp.stack([real_part, imag_part], axis=1)


def plain_device(charges, counts, projection, near_blocks, neighbours, spectrum):
    panels, cell_planes, cell_cols = charges.shape
    nx, nz, ny = (spectrum.shape[0], spectrum.shape[1], spectrum.shape[2] * lax.axis_size("slab"))
    planes = cell_planes * TX
    rows_cell = cell_cols // NZC
    slot_ids = lax.broadcasted_iota(jnp.int32, charges.shape, 0)
    panel_mask = (slot_ids < counts[None]).astype(jnp.float32)
    masked = charges * panel_mask
    tile_values = jnp.einsum("ptxc,pxc->txc", projection, masked, precision=lax.Precision.HIGHEST)
    grid_field = (
        tile_values.reshape(TX, TY, TZ, cell_planes, rows_cell, NZC)
        .transpose(3, 0, 5, 2, 4, 1)
        .reshape(planes, nz, rows_cell * TY)
    )
    cell_count = lax.axis_size("cell")
    forward_table, backward_table, freq_ids = half_depth_tables(nz, cell_count)
    depth_count = forward_table.shape[1] // cell_count
    spectra_z = jnp.einsum(
        "wkz,xzy->xwky", forward_table, grid_field, precision=lax.Precision.HIGHEST
    )
    cosine_y, sine_y = wave_tables(ny, ny, ny)
    pencils = transform_rows(
        lax.all_to_all(spectra_z, "cell", split_axis=2, concat_axis=3, tiled=True),
        cosine_y,
        sine_y,
        1.0,
    )
    columns = lax.all_to_all(pencils, "slab", split_axis=3, concat_axis=0, tiled=True)
    col_width = columns.shape[2] * columns.shape[3]
    flat_rows = columns.reshape(nx, 2 * col_width)
    first_row = lax.axis_index("cell") * depth_count
    kernel_ids = lax.dynamic_slice_in_dim(freq_ids, first_row, depth_count, 0)
    kernel = jnp.take(spectrum, kernel_ids, axis=1).reshape(nx, col_width) * (1.0 / (nx * ny * nz))
    kernel_both = jnp.concatenate([kernel, kernel], axis=1)
    slab_count = lax.axis_size("slab")
    local_rows = nx // slab_count
    cosine_s, sine_s = wave_tables(slab_count, slab_count, slab_count)
    cosine_r, sine_r = wave_tables(local_rows, local_rows, local_rows)
    twist_cos, twist_sin = wave_tables(slab_count, local_rows, nx)
    twist_cos = twist_cos[:, :, None]
    twist_sin = twist_sin[:, :, None]
    section_one = transform_axis(
        "ks,src->krc",
        cosine_s,
        sine_s,
        flat_rows.reshape(slab_count, local_rows, 2 * col_width),
        1.0,
    )
    section_one = twiddle(section_one, twist_cos, twist_sin, 1.0)
    section_two = transform_axis("jr,krc->jkc", cosine_r, sine_r, section_one, 1.0)
    weighted = section_two.reshape(nx, 2 * col_width) * kernel_both
    section_one = transform_axis(
        "rj,jkc->krc",
        cosine_r,
        sine_r,
        weighted.reshape(local_rows, slab_count, 2 * col_width),
        -1.0,
    )
    section_one = twiddle(section_one, twist_cos, twist_sin, -1.0)
    section_two = transform_axis("sk,krc->src", cosine_s, sine_s, section_one, -1.0)
    returned_x = section_two.reshape(nx, 2 * col_width)
    returned = lax.all_to_all(
        returned_x.reshape(columns.shape), "slab", split_axis=0, concat_axis=3, tiled=True
    )
    inverse_rows = transform_rows(returned, cosine_y, sine_y, -1.0)
    grid_potential = jnp.einsum(
        "wkz,xwky->xzy",
        backward_table,
        lax.all_to_all(inverse_rows, "cell", split_axis=3, concat_axis=2, tiled=True),
        precision=lax.Precision.HIGHEST,
    )
    tile_potential = (
        grid_potential.reshape(cell_planes, TX, NZC, TZ, rows_cell, TY)
        .transpose(1, 5, 3, 0, 4, 2)
        .reshape(TX * TY * TZ, cell_planes, cell_cols)
    )
    far_field = jnp.einsum(
        "ptxc,txc->pxc", projection, tile_potential, precision=lax.Precision.HIGHEST
    )
    block = masked.reshape(panels, cell_planes, rows_cell, NZC)
    extended = padded(block, (("slab", 1), ("cell", 2)), 1)
    flat_ext = extended.reshape(panels, -1)
    step_x = neighbours // 9 - 1
    step_y = neighbours // 3 % 3 - 1
    step_z = neighbours % 3 - 1
    plane_ids = lax.broadcasted_iota(jnp.int32, neighbours.shape, 1)
    col_ids = lax.broadcasted_iota(jnp.int32, neighbours.shape, 2)
    row_ids = col_ids // NZC
    depth_ids = col_ids % NZC
    near_ids = ((plane_ids + step_x + 1) * (rows_cell + 2) + row_ids + step_y + 1) * NZC + (
        depth_ids + step_z
    ) % NZC
    near_count = neighbours.shape[0]
    picked = jnp.take(flat_ext, near_ids.reshape(-1), axis=1).reshape(
        panels, near_count, cell_planes, cell_cols
    )
    near_field = jnp.einsum("kpqxc,qkxc->pxc", near_blocks, picked, precision=lax.Precision.HIGHEST)
    return (far_field + near_field) * panel_mask


def solution(mesh):
    in_specs = (
        P(None, "slab", "cell"),
        P("slab", "cell"),
        P(None, None, "slab", "cell"),
        P(None, None, None, "slab", "cell"),
        P(None, "slab", "cell"),
        P(None, None, "slab"),
    )
    out_specs = P(None, "slab", "cell")
    return jax.shard_map(
        per_device, mesh=mesh, in_specs=in_specs, out_specs=out_specs, check_vma=False
    )
```

```python
import functools
import math

import jax
import jax.numpy as jnp
import ml_dtypes
import numpy as np
from jax import lax
from jax.experimental import pallas as pl
from jax.experimental.pallas import tpu as pltpu
from jax.sharding import PartitionSpec as P

TX = 4
TY = 4
TZ = 4
NZC = 16
LANES = 128
CHUNKS = 2
VMEM_LIMIT = 60 * 1024 * 1024


def halves(table):
    high = table.astype(np.float32).astype(ml_dtypes.bfloat16)
    low = (table - high.astype(np.float64)).astype(np.float32).astype(ml_dtypes.bfloat16)
    return (high, low)


def wave(rows, cols, length):
    angle = (rows[:, None] * cols[None, :] % length) * (2.0 * math.pi / length)
    return (np.cos(angle), np.sin(angle))


class Plan:
    def __init__(self, slabs, cells, panels, cell_planes, cell_cols, near, nx, nz, ny):
        self.slabs, self.cells = (slabs, cells)
        self.panels, self.cell_planes, self.cell_cols, self.near = (panels, cell_planes, cell_cols, near)
        self.nx, self.ny, self.nz = (nx, ny, nz)
        self.slots = slabs * cells
        self.tx_chunk = TX // CHUNKS
        self.width = cell_planes * self.tx_chunk
        self.y_lanes = LANES // self.width if self.width else 1
        self.row_block = LANES // NZC
        self.step_blocks = self.y_lanes // TY
        self.steps = cell_cols // (LANES * self.step_blocks) if self.step_blocks else 0
        self.x_chunk = nx // CHUNKS
        self.ky_local = ny // slabs
        self.half = slabs // 2
        self.outer = math.gcd(self.half, 2)
        self.inner = self.half // self.outer

    def fits(self):
        return (
            self.slots * 2 == self.nz
            and self.cell_planes == 8
            and self.step_blocks * TY * self.width == LANES
            and self.slabs % self.y_lanes == 0
            and self.ky_local % 8 == 0
            and self.steps * self.step_blocks * LANES == self.cell_cols
            and self.x_chunk % LANES == 0
            and self.ny % 1024 == self.nx % 1024 == 512
        )

    def depth_tables(self):
        depth = np.arange(NZC)[None, :] * TZ + np.arange(TZ)[:, None]
        scale = 1.0 / (self.nx * self.ny * self.nz)
        forward = np.zeros((self.slots, 2, self.row_block, TZ, self.row_block, NZC))
        backward = np.zeros_like(forward)
        for freq in range(self.slots):
            angle = (freq * depth % self.nz) * (2.0 * math.pi / self.nz)
            real, imag = (np.cos(angle), -np.sin(angle))
            factor = 2.0 * scale
            if freq == 0:
                imag = np.cos(depth * math.pi)
                factor = scale
            for row in range(self.row_block):
                forward[freq, 0, row, :, row, :] = real
                forward[freq, 1, row, :, row, :] = imag
                backward[freq, 0, row, :, row, :] = factor * real
                backward[freq, 1, row, :, row, :] = factor * imag
        shape = (self.slots * 2 * self.row_block, TZ * LANES)
        return (forward.reshape(shape), backward.reshape(shape))

    def y_rows(self):
        parity, cell, step, block, tile, row = np.meshgrid(
            *[np.arange(n) for n in (2, self.cells, self.steps, self.step_blocks, TY // 2, self.row_block)],
            indexing="ij",
        )
        cell_row = ((cell * self.steps + step) * self.step_blocks + block) * self.row_block + row
        return (cell_row * TY + 2 * tile + parity).reshape(2, -1)

    def x_columns(self):
        parity, slab, tile, plane = np.meshgrid(
            *[np.arange(n) for n in (2, self.slabs, TX // 2, self.cell_planes)], indexing="ij"
        )
        return ((slab * self.cell_planes + plane) * TX + 2 * tile + parity).reshape(2, -1)

    def row_of(self, cell, step, place):
        block, tile = (place // TY, place % TY)
        inner = (cell * self.steps + step) * self.step_blocks + block
        return (tile % 2) * (self.ny // 2) + (inner * (TY // 2) + tile // 2) * self.row_block


def split(value):
    high = value.astype(jnp.bfloat16)
    low = (value - high.astype(jnp.float32)).astype(jnp.bfloat16)
    return (high, low)


def product(left, right, dims=((1,), (0,))):
    first = jnp.concatenate([left[0], left[0], left[1]], axis=dims[0][0])
    second = jnp.concatenate([right[0], right[1], right[0]], axis=dims[1][0])
    return lax.dot_general(first, second, (dims, ((), ())), preferred_element_type=jnp.float32)


def swap_groups(parts, width):
    count = len(parts)
    lane = lax.broadcasted_iota(jnp.int32, parts[0].shape, 1)
    parts = list(parts)
    step = count // 2
    while step >= 1:
        shift = step * width
        upper = (lane // shift) % 2 == 1
        for i in range(count):
            if i & step:
                continue
            first, second = (parts[i], parts[i + step])
            parts[i] = jnp.where(upper, pltpu.roll(second, shift, 1), first)
            parts[i + step] = jnp.where(upper, second, pltpu.roll(first, LANES - shift, 1))
        step //= 2
    return parts


def tile_copies(plan, chunk, projection, held, sems):
    return [
        pltpu.make_async_copy(projection.at[:, tx, chunk], held.at[tx], sems.at[tx])
        for tx in range(plan.tx_chunk)
    ]


def project_kernel(plan, chunk, charges, counts, high, low, projection, out, scratch, held, sems):
    planes = plan.cell_planes
    copies = tile_copies(plan, chunk, projection, held, sems)
    for copy in copies:
        copy.start()
    for tx, copy in enumerate(copies):
        copy.wait()

        def body(place, carry, tx=tx):
            lanes = pl.ds(pl.multiple_of(place * LANES, LANES), LANES)
            count = counts[:, lanes]
            own = [jnp.where(count > p, charges[p, :, lanes], 0.0) for p in range(plan.panels)]
            for ty in range(TY):
                row = ((place * TY + ty) * plan.tx_chunk + tx) * planes
                rows = pl.ds(pl.multiple_of(row, planes), planes)
                for tz in range(TZ):
                    t = ty * TZ + tz
                    total = held[tx, 0, t, :, lanes] * own[0]
                    for p in range(1, plan.panels):
                        total = total + held[tx, p, t, :, lanes] * own[p]
                    scratch[rows, tz * LANES : (tz + 1) * LANES] = total
            return carry

        lax.fori_loop(0, plan.steps * plan.step_blocks, body, 0)
    spectra = product((high[...], low[...]), split(scratch[...]), ((1,), (1,)))
    shape = (plan.slots, 2, plan.row_block, LANES)
    for step in range(plan.steps):
        out[:, :, step] = spectra[:, step * LANES : (step + 1) * LANES].reshape(shape)


def held_shape(plan):
    cols = plan.steps * plan.step_blocks * LANES
    return (plan.tx_chunk, plan.panels, TY * TZ, plan.cell_planes, cols)


def piece_shape(plan):
    return (plan.slots, 2, plan.steps, plan.row_block, LANES)


def whole_spec(shape):
    return pl.BlockSpec(shape, lambda i: (0,) * len(shape))


def projection_call(plan, kernel, name, arrays, projection, out_shape):
    return pl.pallas_call(
        kernel,
        grid=(1,),
        in_specs=[whole_spec(array.shape) for array in arrays] + [pl.BlockSpec(memory_space=pl.ANY)],
        out_specs=whole_spec(out_shape),
        out_shape=jax.ShapeDtypeStruct(out_shape, jnp.float32),
        scratch_shapes=[
            pltpu.VMEM((plan.steps * LANES, TZ * LANES), jnp.float32),
            pltpu.VMEM(held_shape(plan), jnp.float32),
            pltpu.SemaphoreType.DMA((plan.tx_chunk,)),
        ],
        compiler_params=pltpu.CompilerParams(vmem_limit_bytes=VMEM_LIMIT),
        cost_estimate=pl.CostEstimate(
            flops=2 * projection.size // CHUNKS,
            bytes_accessed=4 * projection.size // CHUNKS,
            transcendentals=0,
        ),
        name=name,
    )(*arrays, projection)


def project(plan, chunk, charges, counts, projection, high, low):
    kernel = functools.partial(project_kernel, plan, chunk)
    arrays = [charges, counts, high, low]
    return projection_call(plan, kernel, "project_depth", arrays, projection, piece_shape(plan))


def far_sign(plan, me_ref):
    slab = lax.rem(me_ref[0], plan.slabs)
    return jnp.where(slab >= plan.half, -1.0, 1.0)


def forward_plane(plan, me_ref, pieces, y_table, x_table, rows_ref, freq_ref):
    special = me_ref[0] == 0
    sign = far_sign(plan, me_ref)
    rows = 2 * plan.steps * plan.row_block
    width = plan.x_chunk
    middle = plan.ny // 2
    for cell in range(plan.cells):
        for group in range(plan.slabs // plan.y_lanes):
            first = cell * plan.slabs + group * plan.y_lanes
            parts = [pieces[first + i].reshape(rows, LANES) for i in range(plan.y_lanes)]
            parts = swap_groups(parts, plan.width)
            for place, value in enumerate(parts):
                if place % 2 == 1:
                    value = value * sign
                for part in range(2):
                    for step in range(plan.steps):
                        source = (part * plan.steps + step) * plan.row_block
                        row = plan.row_of(cell, step, place)
                        col = part * width + group * LANES
                        rows_ref[row : row + plan.row_block, col : col + LANES] = value[
                            source : source + plan.row_block
                        ]
    sums = product((y_table[0][...], y_table[1][...]), split(rows_ref[...]))
    cos_re, cos_im = (sums[:middle, :width], sums[:middle, width:])
    sin_re, sin_im = (sums[middle:, :width], sums[middle:, width:])
    first = lax.broadcasted_iota(jnp.int32, (middle, width), 0) == 0

    @pl.when(jnp.logical_not(special))
    def _():
        freq_ref[:middle] = jnp.where(first, cos_re, cos_re + sin_im)
        freq_ref[middle : 2 * middle] = jnp.where(first, cos_im, cos_im - sin_re)
        freq_ref[2 * middle : 3 * middle] = jnp.where(first, sin_re, cos_re - sin_im)
        freq_ref[3 * middle :] = jnp.where(first, sin_im, cos_im + sin_re)

    @pl.when(special)
    def _():
        freq_ref[:middle] = cos_re
        freq_ref[middle : 2 * middle] = jnp.where(first, sin_re, -sin_re)
        freq_ref[2 * middle : 3 * middle] = cos_im
        freq_ref[3 * middle :] = sin_im

    return product(split(freq_ref[...]), (x_table[0][0], x_table[1][0]))


def backward_plane(plan, me_ref, freqs, x_table, y_table, out, rows_ref):
    special = me_ref[0] == 0
    sign = far_sign(plan, me_ref)
    width = plan.x_chunk
    middle = plan.ny // 2
    sums = product(split(freqs), (x_table[0][0], x_table[1][0]))
    parts = []
    for mirrored, turn in ((0, 1.0), (1, -1.0)):
        re = slice(2 * mirrored * middle, (2 * mirrored + 1) * middle)
        im = slice((2 * mirrored + 1) * middle, (2 * mirrored + 2) * middle)
        parts.append(sums[re, :width] - turn * sums[im, width:])
        parts.append(sums[im, :width] + turn * sums[re, width:])
    re_n, im_n, re_m, im_m = parts
    first = lax.broadcasted_iota(jnp.int32, (middle, width), 0) == 0

    @pl.when(jnp.logical_not(special))
    def _():
        rows_ref[:middle, :width] = jnp.where(first, re_n, re_n + re_m)
        rows_ref[:middle, width:] = jnp.where(first, im_n, im_n + im_m)
        rows_ref[middle:, :width] = jnp.where(first, -re_m, im_n - im_m)
        rows_ref[middle:, width:] = jnp.where(first, -im_m, re_m - re_n)

    @pl.when(special)
    def _():
        rows_ref[:middle, :width] = jnp.where(first, re_n, 2.0 * re_n)
        rows_ref[:middle, width:] = jnp.where(first, re_m, 2.0 * re_m)
        rows_ref[middle:, :width] = jnp.where(first, -im_n, 2.0 * im_n)
        rows_ref[middle:, width:] = jnp.where(first, -im_m, -2.0 * im_m)

    rows_ref[...] = product((y_table[0][...], y_table[1][...]), split(rows_ref[...]))
    for cell in range(plan.cells):
        for group in range(plan.slabs // plan.y_lanes):
            parts = []
            for place in range(plan.y_lanes):
                tiles = []
                for part in range(2):
                    for step in range(plan.steps):
                        row = plan.row_of(cell, step, place)
                        col = part * width + group * LANES
                        tiles.append(rows_ref[row : row + plan.row_block, col : col + LANES])
                value = jnp.concatenate(tiles, axis=0)
                parts.append(value * sign if place % 2 == 1 else value)
            parts = swap_groups(parts, plan.width)
            first = cell * plan.slabs + group * plan.y_lanes
            for i in range(plan.y_lanes):
                out[first + i] = parts[i].reshape(2, plan.steps, plan.row_block, LANES)


def first_plane_kernel(plan, me_ref, pieces, y_high, y_low, x_high, x_low, out, rows_ref, freq_ref):
    out[...] = forward_plane(plan, me_ref, pieces, (y_high, y_low), (x_high, x_low), rows_ref, freq_ref)


def middle_plane_kernel(plan, me_ref, edge, pieces, yf_high, yf_low, xf_high, xf_low, *refs):
    late, refs = (refs[:5], refs[5:])
    strips, refs = (refs[: plan.inner], refs[plan.inner :])
    out, rest, rows_ref, freq_ref, sum_ref, rest_ref, weights = refs[:7]
    even, xb_high, xb_low, yb_high, yb_low, sems = refs[7:]
    slab = lax.rem(me_ref[0], plan.slabs)
    place = lax.rem(slab, plan.half)
    outer_id, inner_id = (place // plan.inner, lax.rem(place, plan.inner))
    held = (even, xb_high, xb_low, yb_high, yb_low)
    copies = [pltpu.make_async_copy(late[0], even, sems.at[0])]
    for i in range(plan.inner):
        for j in range(plan.outer):
            owner = lax.rem(outer_id - j + plan.outer, plan.outer) * plan.inner
            owner = owner + lax.rem(inner_id - i + plan.inner, plan.inner)
            rows = pl.ds(pl.multiple_of(owner * plan.ky_local, plan.ky_local), plan.ky_local)
            copies.append(
                pltpu.make_async_copy(
                    strips[i].at[j], weights.at[:, rows], sems.at[len(held) + i * plan.outer + j]
                )
            )
    early = len(copies)
    for n in range(1, len(held)):
        copies.append(pltpu.make_async_copy(late[n], held[n], sems.at[n]))
    for copy in copies:
        copy.start()
    special = me_ref[0] == 0
    width = plan.x_chunk
    middle = plan.ny // 2
    odd = forward_plane(plan, me_ref, pieces, (yf_high, yf_low), (xf_high, xf_low), rows_ref, freq_ref)
    for copy in copies[:early]:
        copy.wait()
    row = lax.broadcasted_iota(jnp.int32, (middle, width), 0)
    at_first = row == 0
    own_edge = edge[pl.ds(slab, 1)]
    for mirrored, turn in ((0, 1.0), (1, -1.0)):
        re = slice(2 * mirrored * middle, (2 * mirrored + 1) * middle)
        im = slice((2 * mirrored + 1) * middle, (2 * mirrored + 2) * middle)
        results = []
        for upper in range(2):
            cols = slice(upper * width, (upper + 1) * width)
            plane = weights[mirrored, :, cols]
            if mirrored:
                weight = jnp.where(at_first & jnp.logical_not(special), own_edge[:, cols], plane)
                second = jnp.where(at_first, own_edge[:, cols], plane)
            else:
                weight = plane
                second = jnp.where(at_first & special, edge[plan.slabs : plan.slabs + 1, cols], plane)
            re_sums = even[re] - odd[re] if upper else even[re] + odd[re]
            im_sums = even[im] - odd[im] if upper else even[im] + odd[im]
            real = weight * re_sums[:, :width] + (turn * second) * im_sums[:, width:]
            imag = second * im_sums[:, :width] - (turn * weight) * re_sums[:, width:]
            results.append((real, imag))
        for part, rows in enumerate((re, im)):
            below, above = (results[0][part], results[1][part])
            sum_ref[rows] = below + above
            rest_ref[rows] = below - above
    last = pltpu.make_async_copy(rest_ref, rest, sems.at[len(held) + plan.half])
    last.start()
    for copy in copies[early:]:
        copy.wait()
    backward_plane(plan, me_ref, sum_ref[...], (xb_high, xb_low), (yb_high, yb_low), out, rows_ref)
    last.wait()


def last_plane_kernel(plan, me_ref, freqs, x_high, x_low, y_high, y_low, out, rows_ref):
    backward_plane(plan, me_ref, freqs[...], (x_high, x_low), (y_high, y_low), out, rows_ref)


def plane_call(plan, kernel, name, me, arrays, tables, late, out_shapes, scratch, work):
    specs = [whole_spec(array.shape) for array in arrays]
    flat = []
    for pair, chunk in tables:
        for table in pair:
            if chunk is None:
                specs.append(whole_spec(table.shape))
            else:
                specs.append(pl.BlockSpec((1,) + table.shape[1:], lambda i, chunk=chunk: (chunk, 0, 0)))
            flat.append(table)
    specs += [pl.BlockSpec(memory_space=pl.ANY)] * len(late)
    size = sum(4 * array.size for array in list(arrays) + list(late)) + sum(2 * t.size for t in flat)
    return pl.pallas_call(
        functools.partial(kernel, plan),
        grid=(1,),
        in_specs=[pl.BlockSpec(memory_space=pltpu.SMEM)] + specs,
        out_specs=[whole_spec(out_shapes[0])] + [pl.BlockSpec(memory_space=pl.ANY)] * (len(out_shapes) - 1),
        out_shape=[jax.ShapeDtypeStruct(shape, jnp.float32) for shape in out_shapes],
        scratch_shapes=scratch,
        compiler_params=pltpu.CompilerParams(vmem_limit_bytes=VMEM_LIMIT),
        cost_estimate=pl.CostEstimate(
            flops=work * 12 * plan.nx * plan.ny * plan.x_chunk, bytes_accessed=size, transcendentals=0
        ),
        name=name,
    )(me, *arrays, *flat, *late)


def gather_kernel(plan, chunk, counts, before, pieces, high, low, projection, out, scratch, held, sems):
    planes = plan.cell_planes
    rows = plan.slots * 2 * plan.row_block
    copies = tile_copies(plan, chunk, projection, held, sems)
    for copy in copies:
        copy.start()
    columns = [pieces[:, :, step].reshape(rows, LANES) for step in range(plan.steps)]
    scratch[...] = product(split(jnp.concatenate(columns, axis=1).T), (high[...], low[...]))
    for tx, copy in enumerate(copies):
        copy.wait()
        last = chunk == CHUNKS - 1 and tx == plan.tx_chunk - 1

        def body(place, carry, tx=tx, last=last):
            lanes = pl.ds(pl.multiple_of(place * LANES, LANES), LANES)
            far = [(before if tx == 0 else out)[p, :, lanes] for p in range(plan.panels)]
            for ty in range(TY):
                row = ((place * TY + ty) * plan.tx_chunk + tx) * planes
                rows_at = pl.ds(pl.multiple_of(row, planes), planes)
                for tz in range(TZ):
                    t = ty * TZ + tz
                    potential = scratch[rows_at, tz * LANES : (tz + 1) * LANES]
                    for p in range(plan.panels):
                        far[p] = far[p] + held[tx, p, t, :, lanes] * potential
            for p in range(plan.panels):
                out[p, :, lanes] = jnp.where(counts[:, lanes] > p, far[p], 0.0) if last else far[p]
            return carry

        lax.fori_loop(0, plan.steps * plan.step_blocks, body, 0)


def gather(plan, chunk, counts, before, projection, high, low, pieces):
    kernel = functools.partial(gather_kernel, plan, chunk)
    arrays = [counts, before, pieces, high, low]
    return projection_call(plan, kernel, "depth_gather", arrays, projection, before.shape)


def near_kernel(plan, extended, codes, blocks_ref, out):
    step = pl.program_id(0)
    lane = lax.broadcasted_iota(jnp.int32, (plan.cell_planes, LANES), 1)
    depth = lane % NZC
    digits = []
    for k in range(plan.near):
        code = codes[k]
        digits.append((code // 9, code // 3 % 3, code % 3))
    total = [None] * plan.panels
    for q in range(plan.panels):
        shifted = []
        for dx in range(3):
            before, here, after = (
                extended[q, dx, :, pl.ds(pl.multiple_of((step + i) * LANES, LANES), LANES)] for i in range(3)
            )
            up = jnp.where(lane < NZC, pltpu.roll(before, NZC, 1), pltpu.roll(here, NZC, 1))
            down = jnp.where(
                lane >= LANES - NZC, pltpu.roll(after, LANES - NZC, 1), pltpu.roll(here, LANES - NZC, 1)
            )
            for value in (up, here, down):
                under = jnp.where(
                    depth == 0, pltpu.roll(value, LANES - NZC + 1, 1), pltpu.roll(value, 1, 1)
                )
                over = jnp.where(
                    depth == NZC - 1, pltpu.roll(value, NZC - 1, 1), pltpu.roll(value, LANES - 1, 1)
                )
                shifted.append((under, value, over))
        for k in range(plan.near):
            digit_x, digit_y, digit_z = digits[k]

            def choose(digit, options):
                return jnp.where(digit == 0, options[0], jnp.where(digit == 1, options[1], options[2]))

            by_z = [choose(digit_z, options) for options in shifted]
            by_y = [choose(digit_y, by_z[3 * i : 3 * i + 3]) for i in range(3)]
            picked = choose(digit_x, by_y)
            for p in range(plan.panels):
                term = blocks_ref[k, p, q] * picked
                total[p] = term if total[p] is None else total[p] + term
    for p in range(plan.panels):
        out[p] = total[p]


def near_field(plan, extended, neighbours, near_blocks):
    return pl.pallas_call(
        functools.partial(near_kernel, plan),
        grid=(plan.cell_cols // LANES,),
        in_specs=[
            whole_spec(extended.shape),
            pl.BlockSpec((plan.near, plan.cell_planes, LANES), lambda i: (0, 0, i)),
            pl.BlockSpec(
                (plan.near, plan.panels, plan.panels, plan.cell_planes, LANES), lambda i: (0, 0, 0, 0, i)
            ),
        ],
        out_specs=pl.BlockSpec((plan.panels, plan.cell_planes, LANES), lambda i: (0, 0, i)),
        out_shape=jax.ShapeDtypeStruct((plan.panels, plan.cell_planes, plan.cell_cols), jnp.float32),
        compiler_params=pltpu.CompilerParams(vmem_limit_bytes=VMEM_LIMIT),
        cost_estimate=pl.CostEstimate(
            flops=2 * near_blocks.size, bytes_accessed=4 * near_blocks.size, transcendentals=0
        ),
        name="near_blocks",
    )(extended, neighbours, near_blocks)


def ring_pairs(axis):
    count = lax.axis_size(axis)
    up = [(i, (i + 1) % count) for i in range(count)]
    return (up, [(j, i) for i, j in up])


def extend_rows(plan, masked):
    up, down = ring_pairs("cell")
    left = lax.ppermute(masked[:, :, -NZC:], "cell", up)
    right = lax.ppermute(masked[:, :, :NZC], "cell", down)
    return (left, right)


def extend_planes(plan, masked, left, right):
    rest = jnp.zeros((plan.panels, plan.cell_planes, LANES - NZC), jnp.float32)
    wide = jnp.concatenate([rest, left, masked, right, rest], axis=2)
    up, down = ring_pairs("slab")
    before = lax.ppermute(wide[:, -1:], "slab", up)
    after = lax.ppermute(wide[:, :1], "slab", down)
    whole = jnp.concatenate([before, wide, after], axis=1)
    planes = plan.cell_planes
    return jnp.stack([whole[:, i : i + planes] for i in range(3)], axis=1)


def first_weights(plan, spectrum):
    slab, cell = (lax.axis_index("slab"), lax.axis_index("cell"))
    by_depth = jnp.transpose(spectrum, (1, 2, 0))
    half_id, place = (slab // plan.half, lax.rem(slab, plan.half))
    blocks = []
    for j in range(plan.outer):
        group = lax.rem(place // plan.inner + j, plan.outer)
        base = cell * plan.slabs + half_id * plan.half + group * plan.inner
        planes = []
        for q in range(plan.inner):
            freq = base + q
            mirror = jnp.where(freq == 0, plan.nz // 2, plan.nz - freq)
            for index in (freq, mirror):
                planes.append(lax.dynamic_slice_in_dim(by_depth, index, 1, 0))
        block = jnp.concatenate(planes, axis=0).reshape((plan.inner, 2) + by_depth.shape[1:])
        if j > 0:
            pairs = []
            for source in range(plan.slabs):
                base_id = source // plan.half * plan.half
                pairs.append((source, base_id + (source - base_id + j * plan.inner) % plan.half))
            block = lax.ppermute(block, "slab", pairs)
        blocks.append(block)
    return blocks


def edge_weights(plan, spectrum):
    slab, cell = (lax.axis_index("slab"), lax.axis_index("cell"))
    rows = jnp.transpose(spectrum[:, :, 0], (1, 0))
    turned = jnp.concatenate([rows[plan.nz // 2 : plan.nz // 2 + 1], jnp.flip(rows, 0)], axis=0)
    own = lax.dynamic_slice_in_dim(turned, cell * plan.slabs, plan.slabs, 0)
    own = jnp.concatenate([own, rows[:1]], axis=0)
    dest = lax.broadcasted_iota(jnp.int32, own.shape, 0)
    from_middle = (dest < plan.half) | (dest == plan.slabs)
    keep = jnp.where(from_middle, slab == plan.half, slab == 0)
    return lax.psum(jnp.where(keep, own, 0.0), "slab")


def second_weights(plan, blocks):
    slab = lax.axis_index("slab")
    strips = []
    for i in range(plan.inner):
        place = lax.rem(slab + i, plan.inner)
        strip = jnp.concatenate([lax.dynamic_slice_in_dim(b, place, 1, 0) for b in blocks], axis=0)
        if i > 0:
            pairs = []
            for source in range(plan.slabs):
                group = source // plan.inner * plan.inner
                pairs.append((source, group + (source + i) % plan.inner))
            strip = lax.ppermute(strip, "slab", pairs)
        strips.append(strip)
    return strips


def per_device(charges, counts, projection, near_blocks, neighbours, spectrum):
    panels, cell_planes, cell_cols = charges.shape
    cells, slabs = (lax.axis_size("cell"), lax.axis_size("slab"))
    nx, nz, local = spectrum.shape
    plan = Plan(slabs, cells, panels, cell_planes, cell_cols, neighbours.shape[0], nx, nz, local * slabs)
    if not plan.fits():
        return plain_device(charges, counts, projection, near_blocks, neighbours, spectrum)
    me = (lax.axis_index("cell") * slabs + lax.axis_index("slab")).astype(jnp.int32).reshape(1)
    depth_forward, depth_backward = [halves(table) for table in plan.depth_tables()]
    y_rows, x_cols, low_ids = (plan.y_rows().reshape(-1), plan.x_columns(), np.arange(plan.ny // 2))
    cos_y, sin_y = wave(low_ids, y_rows, plan.ny)
    sin_y[0] = 1.0 - 2.0 * (y_rows % 2)
    y_forward = halves(np.concatenate([cos_y, sin_y], axis=0))
    y_backward = halves(np.concatenate([cos_y.T, -sin_y.T], axis=1))
    x_waves = [wave(cols, low_ids, plan.nx) for cols in x_cols]
    x_forward = halves(np.stack([np.concatenate(pair, axis=1) for pair in x_waves]))
    x_backward = halves(np.stack([np.concatenate([t.T for t in pair], axis=1) for pair in x_waves]))
    split_projection = projection.reshape(
        (panels, TX // CHUNKS, CHUNKS, TY * TZ, cell_planes, cell_cols)
    )
    axes = ("cell", "slab")

    def exchange(pieces):
        return lax.all_to_all(pieces, axes, split_axis=0, concat_axis=0, tiled=True)

    def values(*shapes):
        return [pltpu.VMEM(shape, jnp.float32) for shape in shapes]

    rows_shape = (plan.ny, 2 * plan.x_chunk)
    freq_shape = (2 * plan.ny, plan.x_chunk)
    both_shape = (2 * plan.ny, plan.nx)
    blocks = first_weights(plan, spectrum)
    edge = edge_weights(plan, spectrum)
    slot = lax.broadcasted_iota(jnp.int32, charges.shape, 0)
    masked = jnp.where(slot < counts[None], charges, 0.0)
    left, right = extend_rows(plan, masked)
    pieces = [project(plan, i, charges, counts, split_projection, *depth_forward) for i in range(CHUNKS)]
    pieces[0], left, right = lax.optimization_barrier((pieces[0], left, right))
    even_pieces = exchange(pieces[0])
    extended = extend_planes(plan, masked, left, right)
    pieces[1], extended, *blocks = lax.optimization_barrier((pieces[1], extended, *blocks))
    odd_pieces = exchange(pieces[1])
    strips = second_weights(plan, blocks)
    (even,) = plane_call(
        plan, first_plane_kernel, "even_planes", me, [even_pieces], [(y_forward, None), (x_forward, 0)], [],
        [both_shape], values(rows_shape, freq_shape), 2,
    )
    late = [even, x_backward[0][:1], x_backward[1][:1], *y_backward]
    copies = [pltpu.VMEM(array.shape, array.dtype) for array in late]
    copies.append(pltpu.SemaphoreType.DMA((len(late) + plan.half + 1,)))
    back, rest = plane_call(
        plan, middle_plane_kernel, "middle_planes", me, [edge, odd_pieces],
        [(y_forward, None), (x_forward, 1)], late + strips, [piece_shape(plan), freq_shape],
        values(rows_shape, freq_shape, freq_shape, freq_shape, (2, plan.ny // 2, plan.nx)) + copies, 4,
    )
    even_back = exchange(back)
    (back,) = plane_call(
        plan, last_plane_kernel, "odd_planes", me, [rest], [(x_backward, 1), (y_backward, None)], [],
        [piece_shape(plan)], values(rows_shape), 2,
    )
    total = near_field(plan, extended, neighbours, near_blocks)
    back, total = lax.optimization_barrier((back, total))
    odd_back = exchange(back)
    total = gather(plan, 0, counts, total, split_projection, *depth_backward, even_back)
    return gather(plan, 1, counts, total, split_projection, *depth_backward, odd_back)


def padded(value, sides, width):
    for axis, dim in sides:
        count, length = (lax.axis_size(axis), value.shape[dim])
        up = [(i, (i + 1) % count) for i in range(count)]
        down = [(j, i) for i, j in up]
        last = lax.slice_in_dim(value, length - width, length, axis=dim)
        first = lax.slice_in_dim(value, 0, width, axis=dim)
        before = lax.ppermute(last, axis, up)
        after = lax.ppermute(first, axis, down)
        value = jnp.concatenate([before, value, after], axis=dim)
    return value


def wave_tables(row_count, col_count, length):
    products = (
        lax.broadcasted_iota(jnp.int32, (row_count, col_count), 0)
        * lax.broadcasted_iota(jnp.int32, (row_count, col_count), 1)
        % length
    )
    angle_rad = products.astype(jnp.float32) * (2.0 * math.pi / length)
    return (jnp.cos(angle_rad), jnp.sin(angle_rad))


def depth_rows(nz, freq_ids, valid, weights):
    depth_ids = lax.broadcasted_iota(jnp.int32, (freq_ids.shape[0], nz), 1)
    products = freq_ids[:, None] * depth_ids % nz
    angle_rad = products.astype(jnp.float32) * (2.0 * math.pi / nz)
    basis = jnp.stack([jnp.cos(angle_rad), -jnp.sin(angle_rad)])
    return (basis * valid[None, :, None], basis * weights[None, :, None])


def half_depth_tables(nz, cell_count):
    lower = nz // (2 * cell_count)
    row_ids = lax.broadcasted_iota(jnp.int32, (cell_count * (lower + 1),), 0)
    block_ids = row_ids // (lower + 1)
    slot_ids = row_ids % (lower + 1)
    freq_ids = jnp.where(slot_ids < lower, block_ids * lower + slot_ids, nz // 2)
    valid = jnp.where((slot_ids < lower) | (block_ids == 0), 1.0, 0.0).astype(jnp.float32)
    doubled = jnp.where((slot_ids < lower) & (freq_ids > 0), 2.0, 1.0).astype(jnp.float32)
    forward_table, backward_table = depth_rows(nz, freq_ids, valid, valid * doubled)
    return (forward_table, backward_table, freq_ids)


def combine_halves(first_part, second, orient):
    half_width = first_part.shape[-1] // 2
    real_part = first_part[..., :half_width] + orient * second[..., half_width:]
    imag_part = first_part[..., half_width:] - orient * second[..., :half_width]
    return jnp.concatenate([real_part, imag_part], axis=-1)


def transform_axis(pattern, cosine, sine_tab, values, orient):
    first_part = jnp.einsum(pattern, cosine, values, precision=lax.Precision.HIGHEST)
    second = jnp.einsum(pattern, sine_tab, values, precision=lax.Precision.HIGHEST)
    return combine_halves(first_part, second, orient)


def twiddle(values, twist_cos, twist_sin, orient):
    half_width = values.shape[-1] // 2
    real_part = values[..., :half_width]
    imag_part = values[..., half_width:]
    new_real = real_part * twist_cos + orient * imag_part * twist_sin
    new_imag = imag_part * twist_cos - orient * real_part * twist_sin
    return jnp.concatenate([new_real, new_imag], axis=-1)


def transform_rows(planes_block, cosine, sine_tab, orient):
    flat_rows = planes_block.reshape(-1, planes_block.shape[-1])
    first_part = jnp.dot(flat_rows, cosine, precision=lax.Precision.HIGHEST).reshape(
        planes_block.shape
    )
    second = jnp.dot(flat_rows, sine_tab, precision=lax.Precision.HIGHEST).reshape(
        planes_block.shape
    )
    real_part = first_part[:, 0] + orient * second[:, 1]
    imag_part = first_part[:, 1] - orient * second[:, 0]
    return jnp.stack([real_part, imag_part], axis=1)


def plain_device(charges, counts, projection, near_blocks, neighbours, spectrum):
    panels, cell_planes, cell_cols = charges.shape
    nx, nz, ny = (spectrum.shape[0], spectrum.shape[1], spectrum.shape[2] * lax.axis_size("slab"))
    planes = cell_planes * TX
    rows_cell = cell_cols // NZC
    slot_ids = lax.broadcasted_iota(jnp.int32, charges.shape, 0)
    panel_mask = (slot_ids < counts[None]).astype(jnp.float32)
    masked = charges * panel_mask
    tile_values = jnp.einsum("ptxc,pxc->txc", projection, masked, precision=lax.Precision.HIGHEST)
    grid_field = (
        tile_values.reshape(TX, TY, TZ, cell_planes, rows_cell, NZC)
        .transpose(3, 0, 5, 2, 4, 1)
        .reshape(planes, nz, rows_cell * TY)
    )
    cell_count = lax.axis_size("cell")
    forward_table, backward_table, freq_ids = half_depth_tables(nz, cell_count)
    depth_count = forward_table.shape[1] // cell_count
    spectra_z = jnp.einsum(
        "wkz,xzy->xwky", forward_table, grid_field, precision=lax.Precision.HIGHEST
    )
    cosine_y, sine_y = wave_tables(ny, ny, ny)
    pencils = transform_rows(
        lax.all_to_all(spectra_z, "cell", split_axis=2, concat_axis=3, tiled=True),
        cosine_y,
        sine_y,
        1.0,
    )
    columns = lax.all_to_all(pencils, "slab", split_axis=3, concat_axis=0, tiled=True)
    col_width = columns.shape[2] * columns.shape[3]
    flat_rows = columns.reshape(nx, 2 * col_width)
    first_row = lax.axis_index("cell") * depth_count
    kernel_ids = lax.dynamic_slice_in_dim(freq_ids, first_row, depth_count, 0)
    kernel = jnp.take(spectrum, kernel_ids, axis=1).reshape(nx, col_width) * (1.0 / (nx * ny * nz))
    kernel_both = jnp.concatenate([kernel, kernel], axis=1)
    slab_count = lax.axis_size("slab")
    local_rows = nx // slab_count
    cosine_s, sine_s = wave_tables(slab_count, slab_count, slab_count)
    cosine_r, sine_r = wave_tables(local_rows, local_rows, local_rows)
    twist_cos, twist_sin = wave_tables(slab_count, local_rows, nx)
    twist_cos = twist_cos[:, :, None]
    twist_sin = twist_sin[:, :, None]
    section_one = transform_axis(
        "ks,src->krc",
        cosine_s,
        sine_s,
        flat_rows.reshape(slab_count, local_rows, 2 * col_width),
        1.0,
    )
    section_one = twiddle(section_one, twist_cos, twist_sin, 1.0)
    section_two = transform_axis("jr,krc->jkc", cosine_r, sine_r, section_one, 1.0)
    weighted = section_two.reshape(nx, 2 * col_width) * kernel_both
    section_one = transform_axis(
        "rj,jkc->krc",
        cosine_r,
        sine_r,
        weighted.reshape(local_rows, slab_count, 2 * col_width),
        -1.0,
    )
    section_one = twiddle(section_one, twist_cos, twist_sin, -1.0)
    section_two = transform_axis("sk,krc->src", cosine_s, sine_s, section_one, -1.0)
    returned_x = section_two.reshape(nx, 2 * col_width)
    returned = lax.all_to_all(
        returned_x.reshape(columns.shape), "slab", split_axis=0, concat_axis=3, tiled=True
    )
    inverse_rows = transform_rows(returned, cosine_y, sine_y, -1.0)
    grid_potential = jnp.einsum(
        "wkz,xwky->xzy",
        backward_table,
        lax.all_to_all(inverse_rows, "cell", split_axis=3, concat_axis=2, tiled=True),
        precision=lax.Precision.HIGHEST,
    )
    tile_potential = (
        grid_potential.reshape(cell_planes, TX, NZC, TZ, rows_cell, TY)
        .transpose(1, 5, 3, 0, 4, 2)
        .reshape(TX * TY * TZ, cell_planes, cell_cols)
    )
    far_field = jnp.einsum(
        "ptxc,txc->pxc", projection, tile_potential, precision=lax.Precision.HIGHEST
    )
    block = masked.reshape(panels, cell_planes, rows_cell, NZC)
    extended = padded(block, (("slab", 1), ("cell", 2)), 1)
    flat_ext = extended.reshape(panels, -1)
    step_x = neighbours // 9 - 1
    step_y = neighbours // 3 % 3 - 1
    step_z = neighbours % 3 - 1
    plane_ids = lax.broadcasted_iota(jnp.int32, neighbours.shape, 1)
    col_ids = lax.broadcasted_iota(jnp.int32, neighbours.shape, 2)
    row_ids = col_ids // NZC
    depth_ids = col_ids % NZC
    near_ids = ((plane_ids + step_x + 1) * (rows_cell + 2) + row_ids + step_y + 1) * NZC + (
        depth_ids + step_z
    ) % NZC
    near_count = neighbours.shape[0]
    picked = jnp.take(flat_ext, near_ids.reshape(-1), axis=1).reshape(
        panels, near_count, cell_planes, cell_cols
    )
    near_field = jnp.einsum("kpqxc,qkxc->pxc", near_blocks, picked, precision=lax.Precision.HIGHEST)
    return (far_field + near_field) * panel_mask


def solution(mesh):
    in_specs = (
        P(None, "slab", "cell"),
        P("slab", "cell"),
        P(None, None, "slab", "cell"),
        P(None, None, None, "slab", "cell"),
        P(None, "slab", "cell"),
        P(None, None, "slab"),
    )
    out_specs = P(None, "slab", "cell")
    return jax.shard_map(
        per_device, mesh=mesh, in_specs=in_specs, out_specs=out_specs, check_vma=False
    )
```

```python
import functools
import math

import jax
import jax.numpy as jnp
import ml_dtypes
import numpy as np
from jax import lax
from jax.experimental import pallas as pl
from jax.experimental.pallas import tpu as pltpu
from jax.sharding import PartitionSpec as P

TX = 4
TY = 4
TZ = 4
NZC = 16
LANES = 128
CHUNKS = 2
VMEM_LIMIT = 62 * 1024 * 1024


def halves(table):
    high = table.astype(np.float32).astype(ml_dtypes.bfloat16)
    low = (table - high.astype(np.float64)).astype(np.float32).astype(ml_dtypes.bfloat16)
    return (high, low)


def wave(rows, cols, length):
    angle = (rows[:, None] * cols[None, :] % length) * (2.0 * math.pi / length)
    return (np.cos(angle), np.sin(angle))


class Plan:
    def __init__(self, slabs, cells, panels, cell_planes, cell_cols, near, nx, nz, ny):
        self.slabs, self.cells = (slabs, cells)
        self.panels, self.cell_planes, self.cell_cols, self.near = (panels, cell_planes, cell_cols, near)
        self.nx, self.ny, self.nz = (nx, ny, nz)
        self.slots = slabs * cells
        self.tx_chunk = TX // CHUNKS
        self.width = cell_planes * self.tx_chunk
        self.y_lanes = LANES // self.width if self.width else 1
        self.row_block = LANES // NZC
        self.step_blocks = self.y_lanes // TY
        self.steps = cell_cols // (LANES * self.step_blocks) if self.step_blocks else 0
        self.x_chunk = nx // CHUNKS
        self.ky_local = ny // slabs
        self.half = slabs // 2
        self.outer = math.gcd(self.half, 2)
        self.inner = self.half // self.outer

    def fits(self):
        return (
            self.slots * 2 == self.nz
            and self.cell_planes == 8
            and self.step_blocks * TY * self.width == LANES
            and self.slabs % self.y_lanes == 0
            and self.ky_local % 8 == 0
            and self.steps * self.step_blocks * LANES == self.cell_cols
            and self.x_chunk % LANES == 0
            and self.ny % 1024 == self.nx % 1024 == 512
        )

    def depth_tables(self):
        depth = np.arange(NZC)[None, :] * TZ + np.arange(TZ)[:, None]
        scale = 1.0 / (self.nx * self.ny * self.nz)
        forward = np.zeros((self.slots, 2, self.row_block, TZ, self.row_block, NZC))
        backward = np.zeros_like(forward)
        for freq in range(self.slots):
            angle = (freq * depth % self.nz) * (2.0 * math.pi / self.nz)
            real, imag = (np.cos(angle), -np.sin(angle))
            factor = 2.0 * scale
            if freq == 0:
                imag = np.cos(depth * math.pi)
                factor = scale
            for row in range(self.row_block):
                forward[freq, 0, row, :, row, :] = real
                forward[freq, 1, row, :, row, :] = imag
                backward[freq, 0, row, :, row, :] = factor * real
                backward[freq, 1, row, :, row, :] = factor * imag
        shape = (self.slots * 2 * self.row_block, TZ * LANES)
        return (forward.reshape(shape), backward.reshape(shape))

    def y_rows(self):
        parity, cell, step, block, tile, row = np.meshgrid(
            *[np.arange(n) for n in (2, self.cells, self.steps, self.step_blocks, TY // 2, self.row_block)],
            indexing="ij",
        )
        cell_row = ((cell * self.steps + step) * self.step_blocks + block) * self.row_block + row
        return (cell_row * TY + 2 * tile + parity).reshape(2, -1)

    def x_columns(self):
        parity, slab, tile, plane = np.meshgrid(
            *[np.arange(n) for n in (2, self.slabs, TX // 2, self.cell_planes)], indexing="ij"
        )
        return ((slab * self.cell_planes + plane) * TX + 2 * tile + parity).reshape(2, -1)

    def row_of(self, cell, step, place):
        block, tile = (place // TY, place % TY)
        inner = (cell * self.steps + step) * self.step_blocks + block
        return (tile % 2) * (self.ny // 2) + (inner * (TY // 2) + tile // 2) * self.row_block


def split(value):
    high = value.astype(jnp.bfloat16)
    low = (value - high.astype(jnp.float32)).astype(jnp.bfloat16)
    return (high, low)


def product(left, right, dims=((1,), (0,))):
    first = jnp.concatenate([left[0], left[0], left[1]], axis=dims[0][0])
    second = jnp.concatenate([right[0], right[1], right[0]], axis=dims[1][0])
    return lax.dot_general(first, second, (dims, ((), ())), preferred_element_type=jnp.float32)


def swap_groups(parts, width):
    count = len(parts)
    lane = lax.broadcasted_iota(jnp.int32, parts[0].shape, 1)
    parts = list(parts)
    step = count // 2
    while step >= 1:
        shift = step * width
        upper = (lane // shift) % 2 == 1
        for i in range(count):
            if i & step:
                continue
            first, second = (parts[i], parts[i + step])
            parts[i] = jnp.where(upper, pltpu.roll(second, shift, 1), first)
            parts[i + step] = jnp.where(upper, second, pltpu.roll(first, LANES - shift, 1))
        step //= 2
    return parts


def tile_copies(plan, chunk, projection, held, sems):
    return [
        pltpu.make_async_copy(projection.at[:, tx, chunk], held.at[tx], sems.at[tx])
        for tx in range(plan.tx_chunk)
    ]


def project_kernel(plan, chunk, charges, counts, high, low, projection, out, scratch, held, sems):
    planes = plan.cell_planes
    copies = tile_copies(plan, chunk, projection, held, sems)
    for copy in copies:
        copy.start()
    for tx, copy in enumerate(copies):
        copy.wait()

        def body(place, carry, tx=tx):
            lanes = pl.ds(pl.multiple_of(place * LANES, LANES), LANES)
            count = counts[:, lanes]
            own = [jnp.where(count > p, charges[p, :, lanes], 0.0) for p in range(plan.panels)]
            for ty in range(TY):
                row = ((place * TY + ty) * plan.tx_chunk + tx) * planes
                rows = pl.ds(pl.multiple_of(row, planes), planes)
                for tz in range(TZ):
                    t = ty * TZ + tz
                    total = held[tx, 0, t, :, lanes] * own[0]
                    for p in range(1, plan.panels):
                        total = total + held[tx, p, t, :, lanes] * own[p]
                    scratch[rows, tz * LANES : (tz + 1) * LANES] = total
            return carry

        lax.fori_loop(0, plan.steps * plan.step_blocks, body, 0)
    spectra = product((high[...], low[...]), split(scratch[...]), ((1,), (1,)))
    shape = (plan.slots, 2, plan.row_block, LANES)
    for step in range(plan.steps):
        out[:, :, step] = spectra[:, step * LANES : (step + 1) * LANES].reshape(shape)


def held_shape(plan):
    cols = plan.steps * plan.step_blocks * LANES
    return (plan.tx_chunk, plan.panels, TY * TZ, plan.cell_planes, cols)


def piece_shape(plan):
    return (plan.slots, 2, plan.steps, plan.row_block, LANES)


def whole_spec(shape):
    return pl.BlockSpec(shape, lambda i: (0,) * len(shape))


def projection_call(plan, kernel, name, arrays, late, out_shape, scratch):
    return pl.pallas_call(
        kernel,
        grid=(1,),
        in_specs=[whole_spec(array.shape) for array in arrays]
        + [pl.BlockSpec(memory_space=pl.ANY)] * len(late),
        out_specs=whole_spec(out_shape),
        out_shape=jax.ShapeDtypeStruct(out_shape, jnp.float32),
        scratch_shapes=[
            pltpu.VMEM((plan.steps * LANES, TZ * LANES), jnp.float32),
            pltpu.VMEM(held_shape(plan), jnp.float32),
            pltpu.SemaphoreType.DMA((plan.tx_chunk + 1,)),
        ]
        + scratch,
        compiler_params=pltpu.CompilerParams(vmem_limit_bytes=VMEM_LIMIT),
        cost_estimate=pl.CostEstimate(
            flops=2 * late[0].size // CHUNKS,
            bytes_accessed=4 * late[0].size // CHUNKS,
            transcendentals=0,
        ),
        name=name,
    )(*arrays, *late)


def project(plan, chunk, charges, counts, projection, high, low):
    kernel = functools.partial(project_kernel, plan, chunk)
    arrays = [charges, counts, high, low]
    return projection_call(plan, kernel, "project_depth", arrays, [projection], piece_shape(plan), [])


def far_sign(plan, me_ref):
    slab = lax.rem(me_ref[0], plan.slabs)
    return jnp.where(slab >= plan.half, -1.0, 1.0)


def forward_plane(plan, me_ref, pieces, y_table, x_table, rows_ref, freq_ref):
    special = me_ref[0] == 0
    sign = far_sign(plan, me_ref)
    rows = 2 * plan.steps * plan.row_block
    width = plan.x_chunk
    middle = plan.ny // 2
    for cell in range(plan.cells):
        for group in range(plan.slabs // plan.y_lanes):
            first = cell * plan.slabs + group * plan.y_lanes
            parts = [pieces[first + i].reshape(rows, LANES) for i in range(plan.y_lanes)]
            parts = swap_groups(parts, plan.width)
            for place, value in enumerate(parts):
                if place % 2 == 1:
                    value = value * sign
                for part in range(2):
                    for step in range(plan.steps):
                        source = (part * plan.steps + step) * plan.row_block
                        row = plan.row_of(cell, step, place)
                        col = part * width + group * LANES
                        rows_ref[row : row + plan.row_block, col : col + LANES] = value[
                            source : source + plan.row_block
                        ]
    sums = product((y_table[0][...], y_table[1][...]), split(rows_ref[...]))
    cos_re, cos_im = (sums[:middle, :width], sums[:middle, width:])
    sin_re, sin_im = (sums[middle:, :width], sums[middle:, width:])
    first = lax.broadcasted_iota(jnp.int32, (middle, width), 0) == 0

    @pl.when(jnp.logical_not(special))
    def _():
        freq_ref[:middle] = jnp.where(first, cos_re, cos_re + sin_im)
        freq_ref[middle : 2 * middle] = jnp.where(first, cos_im, cos_im - sin_re)
        freq_ref[2 * middle : 3 * middle] = jnp.where(first, sin_re, cos_re - sin_im)
        freq_ref[3 * middle :] = jnp.where(first, sin_im, cos_im + sin_re)

    @pl.when(special)
    def _():
        freq_ref[:middle] = cos_re
        freq_ref[middle : 2 * middle] = jnp.where(first, sin_re, -sin_re)
        freq_ref[2 * middle : 3 * middle] = cos_im
        freq_ref[3 * middle :] = sin_im

    return product(split(freq_ref[...]), (x_table[0][0], x_table[1][0]))


def backward_plane(plan, me_ref, freqs, x_table, y_table, out, rows_ref):
    special = me_ref[0] == 0
    sign = far_sign(plan, me_ref)
    width = plan.x_chunk
    middle = plan.ny // 2
    sums = product(split(freqs), (x_table[0][0], x_table[1][0]))
    parts = []
    for mirrored, turn in ((0, 1.0), (1, -1.0)):
        re = slice(2 * mirrored * middle, (2 * mirrored + 1) * middle)
        im = slice((2 * mirrored + 1) * middle, (2 * mirrored + 2) * middle)
        parts.append(sums[re, :width] - turn * sums[im, width:])
        parts.append(sums[im, :width] + turn * sums[re, width:])
    re_n, im_n, re_m, im_m = parts
    first = lax.broadcasted_iota(jnp.int32, (middle, width), 0) == 0

    @pl.when(jnp.logical_not(special))
    def _():
        rows_ref[:middle, :width] = jnp.where(first, re_n, re_n + re_m)
        rows_ref[:middle, width:] = jnp.where(first, im_n, im_n + im_m)
        rows_ref[middle:, :width] = jnp.where(first, -re_m, im_n - im_m)
        rows_ref[middle:, width:] = jnp.where(first, -im_m, re_m - re_n)

    @pl.when(special)
    def _():
        rows_ref[:middle, :width] = jnp.where(first, re_n, 2.0 * re_n)
        rows_ref[:middle, width:] = jnp.where(first, re_m, 2.0 * re_m)
        rows_ref[middle:, :width] = jnp.where(first, -im_n, 2.0 * im_n)
        rows_ref[middle:, width:] = jnp.where(first, -im_m, -2.0 * im_m)

    rows_ref[...] = product((y_table[0][...], y_table[1][...]), split(rows_ref[...]))
    for cell in range(plan.cells):
        for group in range(plan.slabs // plan.y_lanes):
            parts = []
            for place in range(plan.y_lanes):
                tiles = []
                for part in range(2):
                    for step in range(plan.steps):
                        row = plan.row_of(cell, step, place)
                        col = part * width + group * LANES
                        tiles.append(rows_ref[row : row + plan.row_block, col : col + LANES])
                value = jnp.concatenate(tiles, axis=0)
                parts.append(value * sign if place % 2 == 1 else value)
            parts = swap_groups(parts, plan.width)
            first = cell * plan.slabs + group * plan.y_lanes
            for i in range(plan.y_lanes):
                out[first + i] = parts[i].reshape(2, plan.steps, plan.row_block, LANES)


def first_plane_kernel(plan, me_ref, pieces, y_high, y_low, x_high, x_low, out, rows_ref, freq_ref):
    out[...] = forward_plane(plan, me_ref, pieces, (y_high, y_low), (x_high, x_low), rows_ref, freq_ref)


def middle_plane_kernel(plan, me_ref, edge, yf_high, yf_low, xf_high, xf_low, *refs):
    late, refs = (refs[:6], refs[6:])
    strips, refs = (refs[: plan.inner], refs[plan.inner :])
    out, rest, rows_ref, freq_ref, sum_ref, rest_ref, weights = refs[:7]
    pieces, even, xb_high, xb_low, yb_high, yb_low, sems = refs[7:]
    slab = lax.rem(me_ref[0], plan.slabs)
    place = lax.rem(slab, plan.half)
    outer_id, inner_id = (place // plan.inner, lax.rem(place, plan.inner))
    held = (pieces, even, xb_high, xb_low, yb_high, yb_low)
    copies = [pltpu.make_async_copy(late[n], held[n], sems.at[n]) for n in range(2)]
    for i in range(plan.inner):
        for j in range(plan.outer):
            owner = lax.rem(outer_id - j + plan.outer, plan.outer) * plan.inner
            owner = owner + lax.rem(inner_id - i + plan.inner, plan.inner)
            rows = pl.ds(pl.multiple_of(owner * plan.ky_local, plan.ky_local), plan.ky_local)
            copies.append(
                pltpu.make_async_copy(
                    strips[i].at[j], weights.at[:, rows], sems.at[len(held) + i * plan.outer + j]
                )
            )
    early = len(copies)
    for n in range(2, len(held)):
        copies.append(pltpu.make_async_copy(late[n], held[n], sems.at[n]))
    for copy in copies:
        copy.start()
    copies[0].wait()
    special = me_ref[0] == 0
    width = plan.x_chunk
    middle = plan.ny // 2
    odd = forward_plane(plan, me_ref, pieces, (yf_high, yf_low), (xf_high, xf_low), rows_ref, freq_ref)
    for copy in copies[1:early]:
        copy.wait()
    row = lax.broadcasted_iota(jnp.int32, (middle, width), 0)
    at_first = row == 0
    for mirrored, turn in ((0, 1.0), (1, -1.0)):
        re = slice(2 * mirrored * middle, (2 * mirrored + 1) * middle)
        im = slice((2 * mirrored + 1) * middle, (2 * mirrored + 2) * middle)
        results = []
        for upper in range(2):
            cols = slice(upper * width, (upper + 1) * width)
            plane = weights[mirrored, :, cols]
            change = at_first & special
            if mirrored:
                weight = jnp.where(change, edge[1:2, cols], plane)
                second = plane
            else:
                weight = plane
                second = jnp.where(change, edge[0:1, cols], plane)
            re_sums = even[re] - odd[re] if upper else even[re] + odd[re]
            im_sums = even[im] - odd[im] if upper else even[im] + odd[im]
            real = weight * re_sums[:, :width] + (turn * second) * im_sums[:, width:]
            imag = second * im_sums[:, :width] - (turn * weight) * re_sums[:, width:]
            results.append((real, imag))
        for part, rows in enumerate((re, im)):
            below, above = (results[0][part], results[1][part])
            sum_ref[rows] = below + above
            rest_ref[rows] = below - above
    last = pltpu.make_async_copy(rest_ref, rest, sems.at[len(held) + plan.half])
    last.start()
    for copy in copies[early:]:
        copy.wait()
    backward_plane(plan, me_ref, sum_ref[...], (xb_high, xb_low), (yb_high, yb_low), out, rows_ref)
    last.wait()


def last_plane_kernel(plan, me_ref, freqs, x_high, x_low, y_high, y_low, out, rows_ref):
    backward_plane(plan, me_ref, freqs[...], (x_high, x_low), (y_high, y_low), out, rows_ref)


def plane_call(plan, kernel, name, me, arrays, tables, late, out_shapes, scratch, work):
    specs = [whole_spec(array.shape) for array in arrays]
    flat = []
    for pair, chunk in tables:
        for table in pair:
            if chunk is None:
                specs.append(whole_spec(table.shape))
            else:
                specs.append(pl.BlockSpec((1,) + table.shape[1:], lambda i, chunk=chunk: (chunk, 0, 0)))
            flat.append(table)
    specs += [pl.BlockSpec(memory_space=pl.ANY)] * len(late)
    size = sum(4 * array.size for array in list(arrays) + list(late)) + sum(2 * t.size for t in flat)
    return pl.pallas_call(
        functools.partial(kernel, plan),
        grid=(1,),
        in_specs=[pl.BlockSpec(memory_space=pltpu.SMEM)] + specs,
        out_specs=[whole_spec(out_shapes[0])] + [pl.BlockSpec(memory_space=pl.ANY)] * (len(out_shapes) - 1),
        out_shape=[jax.ShapeDtypeStruct(shape, jnp.float32) for shape in out_shapes],
        scratch_shapes=scratch,
        compiler_params=pltpu.CompilerParams(vmem_limit_bytes=VMEM_LIMIT),
        cost_estimate=pl.CostEstimate(
            flops=work * 12 * plan.nx * plan.ny * plan.x_chunk, bytes_accessed=size, transcendentals=0
        ),
        name=name,
    )(me, *arrays, *flat, *late)


def gather_kernel(
    plan, chunk, counts, before, high, low, projection, sent, out, scratch, held, sems, pieces
):
    planes = plan.cell_planes
    rows = plan.slots * 2 * plan.row_block
    fetch = pltpu.make_async_copy(sent, pieces, sems.at[plan.tx_chunk])
    fetch.start()
    copies = tile_copies(plan, chunk, projection, held, sems)
    for copy in copies:
        copy.start()
    fetch.wait()
    columns = [pieces[:, :, step].reshape(rows, LANES) for step in range(plan.steps)]
    scratch[...] = product(split(jnp.concatenate(columns, axis=1).T), (high[...], low[...]))
    for tx, copy in enumerate(copies):
        copy.wait()
        last = chunk == CHUNKS - 1 and tx == plan.tx_chunk - 1

        def body(place, carry, tx=tx, last=last):
            lanes = pl.ds(pl.multiple_of(place * LANES, LANES), LANES)
            far = [(before if tx == 0 else out)[p, :, lanes] for p in range(plan.panels)]
            for ty in range(TY):
                row = ((place * TY + ty) * plan.tx_chunk + tx) * planes
                rows_at = pl.ds(pl.multiple_of(row, planes), planes)
                for tz in range(TZ):
                    t = ty * TZ + tz
                    potential = scratch[rows_at, tz * LANES : (tz + 1) * LANES]
                    for p in range(plan.panels):
                        far[p] = far[p] + held[tx, p, t, :, lanes] * potential
            for p in range(plan.panels):
                out[p, :, lanes] = jnp.where(counts[:, lanes] > p, far[p], 0.0) if last else far[p]
            return carry

        lax.fori_loop(0, plan.steps * plan.step_blocks, body, 0)


def gather(plan, chunk, counts, before, projection, high, low, pieces):
    kernel = functools.partial(gather_kernel, plan, chunk)
    arrays = [counts, before, high, low]
    scratch = [pltpu.VMEM(pieces.shape, jnp.float32)]
    return projection_call(
        plan, kernel, "depth_gather", arrays, [projection, pieces], before.shape, scratch
    )


def near_kernel(plan, extended, codes, blocks_ref, out):
    step = pl.program_id(0)
    lane = lax.broadcasted_iota(jnp.int32, (plan.cell_planes, LANES), 1)
    depth = lane % NZC
    digits = []
    for k in range(plan.near):
        code = codes[k]
        digits.append((code // 9, code // 3 % 3, code % 3))
    total = [None] * plan.panels
    for q in range(plan.panels):
        shifted = []
        for dx in range(3):
            before, here, after = (
                extended[q, dx, :, pl.ds(pl.multiple_of((step + i) * LANES, LANES), LANES)] for i in range(3)
            )
            up = jnp.where(lane < NZC, pltpu.roll(before, NZC, 1), pltpu.roll(here, NZC, 1))
            down = jnp.where(
                lane >= LANES - NZC, pltpu.roll(after, LANES - NZC, 1), pltpu.roll(here, LANES - NZC, 1)
            )
            for value in (up, here, down):
                under = jnp.where(
                    depth == 0, pltpu.roll(value, LANES - NZC + 1, 1), pltpu.roll(value, 1, 1)
                )
                over = jnp.where(
                    depth == NZC - 1, pltpu.roll(value, NZC - 1, 1), pltpu.roll(value, LANES - 1, 1)
                )
                shifted.append((under, value, over))
        for k in range(plan.near):
            digit_x, digit_y, digit_z = digits[k]

            def choose(digit, options):
                return jnp.where(digit == 0, options[0], jnp.where(digit == 1, options[1], options[2]))

            by_z = [choose(digit_z, options) for options in shifted]
            by_y = [choose(digit_y, by_z[3 * i : 3 * i + 3]) for i in range(3)]
            picked = choose(digit_x, by_y)
            for p in range(plan.panels):
                term = blocks_ref[k, p, q] * picked
                total[p] = term if total[p] is None else total[p] + term
    for p in range(plan.panels):
        out[p] = total[p]


def near_field(plan, extended, neighbours, near_blocks):
    return pl.pallas_call(
        functools.partial(near_kernel, plan),
        grid=(plan.cell_cols // LANES,),
        in_specs=[
            whole_spec(extended.shape),
            pl.BlockSpec((plan.near, plan.cell_planes, LANES), lambda i: (0, 0, i)),
            pl.BlockSpec(
                (plan.near, plan.panels, plan.panels, plan.cell_planes, LANES), lambda i: (0, 0, 0, 0, i)
            ),
        ],
        out_specs=pl.BlockSpec((plan.panels, plan.cell_planes, LANES), lambda i: (0, 0, i)),
        out_shape=jax.ShapeDtypeStruct((plan.panels, plan.cell_planes, plan.cell_cols), jnp.float32),
        compiler_params=pltpu.CompilerParams(vmem_limit_bytes=VMEM_LIMIT),
        cost_estimate=pl.CostEstimate(
            flops=2 * near_blocks.size, bytes_accessed=4 * near_blocks.size, transcendentals=0
        ),
        name="near_blocks",
    )(extended, neighbours, near_blocks)


def ring_pairs(axis):
    count = lax.axis_size(axis)
    up = [(i, (i + 1) % count) for i in range(count)]
    return (up, [(j, i) for i, j in up])


def extend_rows(plan, masked):
    up, down = ring_pairs("cell")
    left = lax.ppermute(masked[:, :, -NZC:], "cell", up)
    right = lax.ppermute(masked[:, :, :NZC], "cell", down)
    return (left, right)


def extend_planes(plan, masked, left, right):
    rest = jnp.zeros((plan.panels, plan.cell_planes, LANES - NZC), jnp.float32)
    wide = jnp.concatenate([rest, left, masked, right, rest], axis=2)
    up, down = ring_pairs("slab")
    before = lax.ppermute(wide[:, -1:], "slab", up)
    after = lax.ppermute(wide[:, :1], "slab", down)
    whole = jnp.concatenate([before, wide, after], axis=1)
    planes = plan.cell_planes
    return jnp.stack([whole[:, i : i + planes] for i in range(3)], axis=1)


def pick_kernel(plan, ids_ref, turned, by_depth, out, sems):
    cell, slab = (ids_ref[0], ids_ref[1])
    half_id, place = (slab // plan.half, lax.rem(slab, plan.half))
    copies = []
    for j in range(plan.outer):
        group = lax.rem(place // plan.inner + j, plan.outer)
        base = cell * plan.slabs + half_id * plan.half + group * plan.inner
        for q in range(plan.inner):
            freq = base + q
            mirror = jnp.where(freq == 0, plan.nz // 2, plan.nz - freq)
            for m, index in enumerate((freq, mirror)):
                n = (j * plan.inner + q) * 2 + m
                copies.append(pltpu.make_async_copy(by_depth.at[index], out.at[j, q, m], sems.at[n]))
    for copy in copies:
        copy.start()
    for copy in copies:
        copy.wait()

    @pl.when(place == 0)
    def _():
        row = lax.broadcasted_iota(jnp.int32, (8, plan.nx), 0)
        for j in range(plan.outer):
            group = lax.rem(place // plan.inner + j, plan.outer)
            for q in range(plan.inner):
                value = turned[pl.ds(group * plan.inner + q, 1)]
                out[j, q, 1, 0:8] = jnp.where(row == 0, value, out[j, q, 1, 0:8])


def edge_weights(plan, spectrum):
    slab, cell = (lax.axis_index("slab"), lax.axis_index("cell"))
    rows = jnp.transpose(spectrum[:, :, 0], (1, 0))
    middle = plan.nz // 2
    turned = jnp.concatenate([rows[middle : middle + 1], jnp.flip(rows, 0)], axis=0)
    other = cell * plan.slabs + (1 - slab // plan.half) * plan.half
    sent = jnp.concatenate([lax.dynamic_slice_in_dim(turned, other, plan.half, 0), rows[:1]], axis=0)
    return (lax.ppermute(sent, "slab", [(0, plan.half), (plan.half, 0)]), rows[middle : middle + 1])


def first_weights(plan, spectrum, turned):
    slab, cell = (lax.axis_index("slab"), lax.axis_index("cell"))
    by_depth = jnp.transpose(spectrum, (1, 2, 0))
    shape = (plan.outer, plan.inner, 2) + by_depth.shape[1:]
    picked = pl.pallas_call(
        functools.partial(pick_kernel, plan),
        in_specs=[
            pl.BlockSpec(memory_space=pltpu.SMEM),
            pl.BlockSpec(memory_space=pltpu.VMEM),
            pl.BlockSpec(memory_space=pl.ANY),
        ],
        out_specs=pl.BlockSpec(memory_space=pltpu.VMEM),
        out_shape=jax.ShapeDtypeStruct(shape, jnp.float32),
        scratch_shapes=[pltpu.SemaphoreType.DMA((2 * plan.half,))],
        cost_estimate=pl.CostEstimate(flops=0, bytes_accessed=8 * math.prod(shape), transcendentals=0),
        name="pick_planes",
    )(jnp.stack([cell, slab]).astype(jnp.int32), turned, by_depth)
    blocks = [picked[0]]
    for j in range(1, plan.outer):
        pairs = []
        for source in range(plan.slabs):
            base_id = source // plan.half * plan.half
            pairs.append((source, base_id + (source - base_id + j * plan.inner) % plan.half))
        blocks.append(lax.ppermute(picked[j], "slab", pairs))
    return blocks


def second_weights(plan, blocks):
    slab = lax.axis_index("slab")
    strips = []
    for i in range(plan.inner):
        place = lax.rem(slab + i, plan.inner)
        strip = jnp.concatenate([lax.dynamic_slice_in_dim(b, place, 1, 0) for b in blocks], axis=0)
        if i > 0:
            pairs = []
            for source in range(plan.slabs):
                group = source // plan.inner * plan.inner
                pairs.append((source, group + (source + i) % plan.inner))
            strip = lax.ppermute(strip, "slab", pairs)
        strips.append(strip)
    return strips


def per_device(charges, counts, projection, near_blocks, neighbours, spectrum):
    panels, cell_planes, cell_cols = charges.shape
    cells, slabs = (lax.axis_size("cell"), lax.axis_size("slab"))
    nx, nz, local = spectrum.shape
    plan = Plan(slabs, cells, panels, cell_planes, cell_cols, neighbours.shape[0], nx, nz, local * slabs)
    if not plan.fits():
        return plain_device(charges, counts, projection, near_blocks, neighbours, spectrum)
    me = (lax.axis_index("cell") * slabs + lax.axis_index("slab")).astype(jnp.int32).reshape(1)
    depth_forward, depth_backward = [halves(table) for table in plan.depth_tables()]
    y_rows, x_cols, low_ids = (plan.y_rows().reshape(-1), plan.x_columns(), np.arange(plan.ny // 2))
    cos_y, sin_y = wave(low_ids, y_rows, plan.ny)
    sin_y[0] = 1.0 - 2.0 * (y_rows % 2)
    y_forward = halves(np.concatenate([cos_y, sin_y], axis=0))
    y_backward = halves(np.concatenate([cos_y.T, -sin_y.T], axis=1))
    x_waves = [wave(cols, low_ids, plan.nx) for cols in x_cols]
    x_forward = halves(np.stack([np.concatenate(pair, axis=1) for pair in x_waves]))
    x_backward = halves(np.stack([np.concatenate([t.T for t in pair], axis=1) for pair in x_waves]))
    split_projection = projection.reshape(
        (panels, TX // CHUNKS, CHUNKS, TY * TZ, cell_planes, cell_cols)
    )
    axes = ("cell", "slab")

    def exchange(pieces):
        return lax.all_to_all(pieces, axes, split_axis=0, concat_axis=0, tiled=True)

    def values(*shapes):
        return [pltpu.VMEM(shape, jnp.float32) for shape in shapes]

    rows_shape = (plan.ny, 2 * plan.x_chunk)
    freq_shape = (2 * plan.ny, plan.x_chunk)
    both_shape = (2 * plan.ny, plan.nx)
    turned, own_row = edge_weights(plan, spectrum)
    slot = lax.broadcasted_iota(jnp.int32, charges.shape, 0)
    masked = jnp.where(slot < counts[None], charges, 0.0)
    left, right = extend_rows(plan, masked)
    pieces = [project(plan, i, charges, counts, split_projection, *depth_forward) for i in range(CHUNKS)]
    pieces[0], left, right, turned = lax.optimization_barrier((pieces[0], left, right, turned))
    even_pieces = exchange(pieces[0])
    blocks = first_weights(plan, spectrum, turned)
    edge = jnp.concatenate([turned[plan.half :], own_row], axis=0)
    extended = extend_planes(plan, masked, left, right)
    pieces[1], extended, *blocks = lax.optimization_barrier((pieces[1], extended, *blocks))
    odd_pieces = exchange(pieces[1])
    strips = second_weights(plan, blocks)
    (even,) = plane_call(
        plan, first_plane_kernel, "even_planes", me, [even_pieces], [(y_forward, None), (x_forward, 0)], [],
        [both_shape], values(rows_shape, freq_shape), 2,
    )
    late = [odd_pieces, even, x_backward[0][:1], x_backward[1][:1], *y_backward]
    copies = [pltpu.VMEM(array.shape, array.dtype) for array in late]
    copies.append(pltpu.SemaphoreType.DMA((len(late) + plan.half + 1,)))
    back, rest = plane_call(
        plan, middle_plane_kernel, "middle_planes", me, [edge],
        [(y_forward, None), (x_forward, 1)], late + strips, [piece_shape(plan), freq_shape],
        values(rows_shape, freq_shape, freq_shape, freq_shape, (2, plan.ny // 2, plan.nx)) + copies, 4,
    )
    even_back = exchange(back)
    (back,) = plane_call(
        plan, last_plane_kernel, "odd_planes", me, [rest], [(x_backward, 1), (y_backward, None)], [],
        [piece_shape(plan)], values(rows_shape), 2,
    )
    total = near_field(plan, extended, neighbours, near_blocks)
    back, total = lax.optimization_barrier((back, total))
    odd_back = exchange(back)
    total = gather(plan, 0, counts, total, split_projection, *depth_backward, even_back)
    return gather(plan, 1, counts, total, split_projection, *depth_backward, odd_back)


def padded(value, sides, width):
    for axis, dim in sides:
        count, length = (lax.axis_size(axis), value.shape[dim])
        up = [(i, (i + 1) % count) for i in range(count)]
        down = [(j, i) for i, j in up]
        last = lax.slice_in_dim(value, length - width, length, axis=dim)
        first = lax.slice_in_dim(value, 0, width, axis=dim)
        before = lax.ppermute(last, axis, up)
        after = lax.ppermute(first, axis, down)
        value = jnp.concatenate([before, value, after], axis=dim)
    return value


def wave_tables(row_count, col_count, length):
    products = (
        lax.broadcasted_iota(jnp.int32, (row_count, col_count), 0)
        * lax.broadcasted_iota(jnp.int32, (row_count, col_count), 1)
        % length
    )
    angle_rad = products.astype(jnp.float32) * (2.0 * math.pi / length)
    return (jnp.cos(angle_rad), jnp.sin(angle_rad))


def depth_rows(nz, freq_ids, valid, weights):
    depth_ids = lax.broadcasted_iota(jnp.int32, (freq_ids.shape[0], nz), 1)
    products = freq_ids[:, None] * depth_ids % nz
    angle_rad = products.astype(jnp.float32) * (2.0 * math.pi / nz)
    basis = jnp.stack([jnp.cos(angle_rad), -jnp.sin(angle_rad)])
    return (basis * valid[None, :, None], basis * weights[None, :, None])


def half_depth_tables(nz, cell_count):
    lower = nz // (2 * cell_count)
    row_ids = lax.broadcasted_iota(jnp.int32, (cell_count * (lower + 1),), 0)
    block_ids = row_ids // (lower + 1)
    slot_ids = row_ids % (lower + 1)
    freq_ids = jnp.where(slot_ids < lower, block_ids * lower + slot_ids, nz // 2)
    valid = jnp.where((slot_ids < lower) | (block_ids == 0), 1.0, 0.0).astype(jnp.float32)
    doubled = jnp.where((slot_ids < lower) & (freq_ids > 0), 2.0, 1.0).astype(jnp.float32)
    forward_table, backward_table = depth_rows(nz, freq_ids, valid, valid * doubled)
    return (forward_table, backward_table, freq_ids)


def combine_halves(first_part, second, orient):
    half_width = first_part.shape[-1] // 2
    real_part = first_part[..., :half_width] + orient * second[..., half_width:]
    imag_part = first_part[..., half_width:] - orient * second[..., :half_width]
    return jnp.concatenate([real_part, imag_part], axis=-1)


def transform_axis(pattern, cosine, sine_tab, values, orient):
    first_part = jnp.einsum(pattern, cosine, values, precision=lax.Precision.HIGHEST)
    second = jnp.einsum(pattern, sine_tab, values, precision=lax.Precision.HIGHEST)
    return combine_halves(first_part, second, orient)


def twiddle(values, twist_cos, twist_sin, orient):
    half_width = values.shape[-1] // 2
    real_part = values[..., :half_width]
    imag_part = values[..., half_width:]
    new_real = real_part * twist_cos + orient * imag_part * twist_sin
    new_imag = imag_part * twist_cos - orient * real_part * twist_sin
    return jnp.concatenate([new_real, new_imag], axis=-1)


def transform_rows(planes_block, cosine, sine_tab, orient):
    flat_rows = planes_block.reshape(-1, planes_block.shape[-1])
    first_part = jnp.dot(flat_rows, cosine, precision=lax.Precision.HIGHEST).reshape(
        planes_block.shape
    )
    second = jnp.dot(flat_rows, sine_tab, precision=lax.Precision.HIGHEST).reshape(
        planes_block.shape
    )
    real_part = first_part[:, 0] + orient * second[:, 1]
    imag_part = first_part[:, 1] - orient * second[:, 0]
    return jnp.stack([real_part, imag_part], axis=1)


def plain_device(charges, counts, projection, near_blocks, neighbours, spectrum):
    panels, cell_planes, cell_cols = charges.shape
    nx, nz, ny = (spectrum.shape[0], spectrum.shape[1], spectrum.shape[2] * lax.axis_size("slab"))
    planes = cell_planes * TX
    rows_cell = cell_cols // NZC
    slot_ids = lax.broadcasted_iota(jnp.int32, charges.shape, 0)
    panel_mask = (slot_ids < counts[None]).astype(jnp.float32)
    masked = charges * panel_mask
    tile_values = jnp.einsum("ptxc,pxc->txc", projection, masked, precision=lax.Precision.HIGHEST)
    grid_field = (
        tile_values.reshape(TX, TY, TZ, cell_planes, rows_cell, NZC)
        .transpose(3, 0, 5, 2, 4, 1)
        .reshape(planes, nz, rows_cell * TY)
    )
    cell_count = lax.axis_size("cell")
    forward_table, backward_table, freq_ids = half_depth_tables(nz, cell_count)
    depth_count = forward_table.shape[1] // cell_count
    spectra_z = jnp.einsum(
        "wkz,xzy->xwky", forward_table, grid_field, precision=lax.Precision.HIGHEST
    )
    cosine_y, sine_y = wave_tables(ny, ny, ny)
    pencils = transform_rows(
        lax.all_to_all(spectra_z, "cell", split_axis=2, concat_axis=3, tiled=True),
        cosine_y,
        sine_y,
        1.0,
    )
    columns = lax.all_to_all(pencils, "slab", split_axis=3, concat_axis=0, tiled=True)
    col_width = columns.shape[2] * columns.shape[3]
    flat_rows = columns.reshape(nx, 2 * col_width)
    first_row = lax.axis_index("cell") * depth_count
    kernel_ids = lax.dynamic_slice_in_dim(freq_ids, first_row, depth_count, 0)
    kernel = jnp.take(spectrum, kernel_ids, axis=1).reshape(nx, col_width) * (1.0 / (nx * ny * nz))
    kernel_both = jnp.concatenate([kernel, kernel], axis=1)
    slab_count = lax.axis_size("slab")
    local_rows = nx // slab_count
    cosine_s, sine_s = wave_tables(slab_count, slab_count, slab_count)
    cosine_r, sine_r = wave_tables(local_rows, local_rows, local_rows)
    twist_cos, twist_sin = wave_tables(slab_count, local_rows, nx)
    twist_cos = twist_cos[:, :, None]
    twist_sin = twist_sin[:, :, None]
    section_one = transform_axis(
        "ks,src->krc",
        cosine_s,
        sine_s,
        flat_rows.reshape(slab_count, local_rows, 2 * col_width),
        1.0,
    )
    section_one = twiddle(section_one, twist_cos, twist_sin, 1.0)
    section_two = transform_axis("jr,krc->jkc", cosine_r, sine_r, section_one, 1.0)
    weighted = section_two.reshape(nx, 2 * col_width) * kernel_both
    section_one = transform_axis(
        "rj,jkc->krc",
        cosine_r,
        sine_r,
        weighted.reshape(local_rows, slab_count, 2 * col_width),
        -1.0,
    )
    section_one = twiddle(section_one, twist_cos, twist_sin, -1.0)
    section_two = transform_axis("sk,krc->src", cosine_s, sine_s, section_one, -1.0)
    returned_x = section_two.reshape(nx, 2 * col_width)
    returned = lax.all_to_all(
        returned_x.reshape(columns.shape), "slab", split_axis=0, concat_axis=3, tiled=True
    )
    inverse_rows = transform_rows(returned, cosine_y, sine_y, -1.0)
    grid_potential = jnp.einsum(
        "wkz,xwky->xzy",
        backward_table,
        lax.all_to_all(inverse_rows, "cell", split_axis=3, concat_axis=2, tiled=True),
        precision=lax.Precision.HIGHEST,
    )
    tile_potential = (
        grid_potential.reshape(cell_planes, TX, NZC, TZ, rows_cell, TY)
        .transpose(1, 5, 3, 0, 4, 2)
        .reshape(TX * TY * TZ, cell_planes, cell_cols)
    )
    far_field = jnp.einsum(
        "ptxc,txc->pxc", projection, tile_potential, precision=lax.Precision.HIGHEST
    )
    block = masked.reshape(panels, cell_planes, rows_cell, NZC)
    extended = padded(block, (("slab", 1), ("cell", 2)), 1)
    flat_ext = extended.reshape(panels, -1)
    step_x = neighbours // 9 - 1
    step_y = neighbours // 3 % 3 - 1
    step_z = neighbours % 3 - 1
    plane_ids = lax.broadcasted_iota(jnp.int32, neighbours.shape, 1)
    col_ids = lax.broadcasted_iota(jnp.int32, neighbours.shape, 2)
    row_ids = col_ids // NZC
    depth_ids = col_ids % NZC
    near_ids = ((plane_ids + step_x + 1) * (rows_cell + 2) + row_ids + step_y + 1) * NZC + (
        depth_ids + step_z
    ) % NZC
    near_count = neighbours.shape[0]
    picked = jnp.take(flat_ext, near_ids.reshape(-1), axis=1).reshape(
        panels, near_count, cell_planes, cell_cols
    )
    near_field = jnp.einsum("kpqxc,qkxc->pxc", near_blocks, picked, precision=lax.Precision.HIGHEST)
    return (far_field + near_field) * panel_mask


def solution(mesh):
    in_specs = (
        P(None, "slab", "cell"),
        P("slab", "cell"),
        P(None, None, "slab", "cell"),
        P(None, None, None, "slab", "cell"),
        P(None, "slab", "cell"),
        P(None, None, "slab"),
    )
    out_specs = P(None, "slab", "cell")
    return jax.shard_map(
        per_device, mesh=mesh, in_specs=in_specs, out_specs=out_specs, check_vma=False
    )
```

```python
import functools
import math

import jax
import jax.numpy as jnp
import ml_dtypes
import numpy as np
from jax import lax
from jax.experimental import pallas as pl
from jax.experimental.pallas import tpu as pltpu
from jax.sharding import PartitionSpec as P

TX = 4
TY = 4
TZ = 4
NZC = 16
LANES = 128
CHUNKS = 2
VMEM_LIMIT = 62 * 1024 * 1024


def halves(table):
    high = table.astype(np.float32).astype(ml_dtypes.bfloat16)
    low = (table - high.astype(np.float64)).astype(np.float32).astype(ml_dtypes.bfloat16)
    return (high, low)


def wave(rows, cols, length):
    angle = (rows[:, None] * cols[None, :] % length) * (2.0 * math.pi / length)
    return (np.cos(angle), np.sin(angle))


class Plan:
    def __init__(self, slabs, cells, panels, cell_planes, cell_cols, near, nx, nz, ny):
        self.slabs, self.cells = (slabs, cells)
        self.panels, self.cell_planes, self.cell_cols, self.near = (panels, cell_planes, cell_cols, near)
        self.nx, self.ny, self.nz = (nx, ny, nz)
        self.slots = slabs * cells
        self.tx_chunk = TX // CHUNKS
        self.width = cell_planes * self.tx_chunk
        self.y_lanes = LANES // self.width if self.width else 1
        self.row_block = LANES // NZC
        self.step_blocks = self.y_lanes // TY
        self.steps = cell_cols // (LANES * self.step_blocks) if self.step_blocks else 0
        self.x_chunk = nx // CHUNKS
        self.ky_local = ny // slabs
        self.half = slabs // 2
        self.outer = math.gcd(self.half, 2)
        self.inner = self.half // self.outer

    def fits(self):
        return (
            self.slots * 2 == self.nz
            and self.cell_planes == 8
            and self.step_blocks * TY * self.width == LANES
            and self.slabs % self.y_lanes == 0
            and self.ky_local % 8 == 0
            and self.steps * self.step_blocks * LANES == self.cell_cols
            and self.x_chunk % LANES == 0
            and self.ny % 1024 == self.nx % 1024 == 512
        )

    def depth_tables(self):
        depth = np.arange(NZC)[None, :] * TZ + np.arange(TZ)[:, None]
        scale = 1.0 / (self.nx * self.ny * self.nz)
        forward = np.zeros((self.slots, 2, self.row_block, TZ, self.row_block, NZC))
        backward = np.zeros_like(forward)
        for freq in range(self.slots):
            angle = (freq * depth % self.nz) * (2.0 * math.pi / self.nz)
            real, imag = (np.cos(angle), -np.sin(angle))
            factor = 2.0 * scale
            if freq == 0:
                imag = np.cos(depth * math.pi)
                factor = scale
            for row in range(self.row_block):
                forward[freq, 0, row, :, row, :] = real
                forward[freq, 1, row, :, row, :] = imag
                backward[freq, 0, row, :, row, :] = factor * real
                backward[freq, 1, row, :, row, :] = factor * imag
        shape = (self.slots * 2 * self.row_block, TZ * LANES)
        return (forward.reshape(shape), backward.reshape(shape))

    def y_rows(self):
        parity, cell, step, block, tile, row = np.meshgrid(
            *[np.arange(n) for n in (2, self.cells, self.steps, self.step_blocks, TY // 2, self.row_block)],
            indexing="ij",
        )
        cell_row = ((cell * self.steps + step) * self.step_blocks + block) * self.row_block + row
        return (cell_row * TY + 2 * tile + parity).reshape(2, -1)

    def x_columns(self):
        parity, slab, tile, plane = np.meshgrid(
            *[np.arange(n) for n in (2, self.slabs, TX // 2, self.cell_planes)], indexing="ij"
        )
        return ((slab * self.cell_planes + plane) * TX + 2 * tile + parity).reshape(2, -1)

    def row_of(self, cell, step, place):
        block, tile = (place // TY, place % TY)
        inner = (cell * self.steps + step) * self.step_blocks + block
        return (tile % 2) * (self.ny // 2) + (inner * (TY // 2) + tile // 2) * self.row_block


def split(value):
    high = value.astype(jnp.bfloat16)
    low = (value - high.astype(jnp.float32)).astype(jnp.bfloat16)
    return (high, low)


def product(left, right, dims=((1,), (0,))):
    first = jnp.concatenate([left[0], left[0], left[1]], axis=dims[0][0])
    second = jnp.concatenate([right[0], right[1], right[0]], axis=dims[1][0])
    return lax.dot_general(first, second, (dims, ((), ())), preferred_element_type=jnp.float32)


def swap_groups(parts, width):
    count = len(parts)
    lane = lax.broadcasted_iota(jnp.int32, parts[0].shape, 1)
    parts = list(parts)
    step = count // 2
    while step >= 1:
        shift = step * width
        upper = (lane // shift) % 2 == 1
        for i in range(count):
            if i & step:
                continue
            first, second = (parts[i], parts[i + step])
            parts[i] = jnp.where(upper, pltpu.roll(second, shift, 1), first)
            parts[i + step] = jnp.where(upper, second, pltpu.roll(first, LANES - shift, 1))
        step //= 2
    return parts


def tile_copies(plan, chunk, projection, held, sems):
    return [
        pltpu.make_async_copy(projection.at[:, tx, chunk], held.at[tx], sems.at[tx])
        for tx in range(plan.tx_chunk)
    ]


def project_kernel(plan, chunk, charges, counts, high, low, projection, out, scratch, held, sems):
    planes = plan.cell_planes
    copies = tile_copies(plan, chunk, projection, held, sems)
    for copy in copies:
        copy.start()
    for tx, copy in enumerate(copies):
        copy.wait()

        def body(place, carry, tx=tx):
            lanes = pl.ds(pl.multiple_of(place * LANES, LANES), LANES)
            count = counts[:, lanes]
            own = [jnp.where(count > p, charges[p, :, lanes], 0.0) for p in range(plan.panels)]
            for ty in range(TY):
                row = ((place * TY + ty) * plan.tx_chunk + tx) * planes
                rows = pl.ds(pl.multiple_of(row, planes), planes)
                for tz in range(TZ):
                    t = ty * TZ + tz
                    total = held[tx, 0, t, :, lanes] * own[0]
                    for p in range(1, plan.panels):
                        total = total + held[tx, p, t, :, lanes] * own[p]
                    scratch[rows, tz * LANES : (tz + 1) * LANES] = total
            return carry

        lax.fori_loop(0, plan.steps * plan.step_blocks, body, 0)
    spectra = product(split(scratch[...]), (high[...], low[...])).T
    shape = (plan.slots, 2, plan.row_block, LANES)
    for step in range(plan.steps):
        out[:, :, step] = spectra[:, step * LANES : (step + 1) * LANES].reshape(shape)


def held_shape(plan):
    cols = plan.steps * plan.step_blocks * LANES
    return (plan.tx_chunk, plan.panels, TY * TZ, plan.cell_planes, cols)


def piece_shape(plan):
    return (plan.slots, 2, plan.steps, plan.row_block, LANES)


def whole_spec(shape):
    return pl.BlockSpec(shape, lambda i: (0,) * len(shape))


def projection_call(plan, kernel, name, arrays, late, out_shape, scratch):
    return pl.pallas_call(
        kernel,
        grid=(1,),
        in_specs=[whole_spec(array.shape) for array in arrays]
        + [pl.BlockSpec(memory_space=pl.ANY)] * len(late),
        out_specs=whole_spec(out_shape),
        out_shape=jax.ShapeDtypeStruct(out_shape, jnp.float32),
        scratch_shapes=[
            pltpu.VMEM((plan.steps * LANES, TZ * LANES), jnp.float32),
            pltpu.VMEM(held_shape(plan), jnp.float32),
            pltpu.SemaphoreType.DMA((plan.tx_chunk + 1,)),
        ]
        + scratch,
        compiler_params=pltpu.CompilerParams(vmem_limit_bytes=VMEM_LIMIT),
        cost_estimate=pl.CostEstimate(
            flops=2 * late[0].size // CHUNKS,
            bytes_accessed=4 * late[0].size // CHUNKS,
            transcendentals=0,
        ),
        name=name,
    )(*arrays, *late)


def project(plan, chunk, charges, counts, projection, high, low):
    kernel = functools.partial(project_kernel, plan, chunk)
    arrays = [charges, counts, high, low]
    return projection_call(plan, kernel, "project_depth", arrays, [projection], piece_shape(plan), [])


def far_sign(plan, me_ref):
    slab = lax.rem(me_ref[0], plan.slabs)
    return jnp.where(slab >= plan.half, -1.0, 1.0)


def forward_plane(plan, me_ref, pieces, y_table, x_table, rows_ref, freq_ref):
    special = me_ref[0] == 0
    sign = far_sign(plan, me_ref)
    rows = 2 * plan.steps * plan.row_block
    width = plan.x_chunk
    middle = plan.ny // 2
    for cell in range(plan.cells):
        for group in range(plan.slabs // plan.y_lanes):
            first = cell * plan.slabs + group * plan.y_lanes
            parts = [pieces[first + i].reshape(rows, LANES) for i in range(plan.y_lanes)]
            parts = swap_groups(parts, plan.width)
            for place, value in enumerate(parts):
                if place % 2 == 1:
                    value = value * sign
                for part in range(2):
                    for step in range(plan.steps):
                        source = (part * plan.steps + step) * plan.row_block
                        row = plan.row_of(cell, step, place)
                        col = part * width + group * LANES
                        rows_ref[row : row + plan.row_block, col : col + LANES] = value[
                            source : source + plan.row_block
                        ]
    sums = product((y_table[0][...], y_table[1][...]), split(rows_ref[...]))
    cos_re, cos_im = (sums[:middle, :width], sums[:middle, width:])
    sin_re, sin_im = (sums[middle:, :width], sums[middle:, width:])
    first = lax.broadcasted_iota(jnp.int32, (middle, width), 0) == 0

    @pl.when(jnp.logical_not(special))
    def _():
        freq_ref[:middle] = jnp.where(first, cos_re, cos_re + sin_im)
        freq_ref[middle : 2 * middle] = jnp.where(first, cos_im, cos_im - sin_re)
        freq_ref[2 * middle : 3 * middle] = jnp.where(first, sin_re, cos_re - sin_im)
        freq_ref[3 * middle :] = jnp.where(first, sin_im, cos_im + sin_re)

    @pl.when(special)
    def _():
        freq_ref[:middle] = cos_re
        freq_ref[middle : 2 * middle] = jnp.where(first, sin_re, -sin_re)
        freq_ref[2 * middle : 3 * middle] = cos_im
        freq_ref[3 * middle :] = sin_im

    return product(split(freq_ref[...]), (x_table[0][0], x_table[1][0]))


def backward_plane(plan, me_ref, freqs, x_table, y_table, out, rows_ref):
    special = me_ref[0] == 0
    sign = far_sign(plan, me_ref)
    width = plan.x_chunk
    middle = plan.ny // 2
    sums = product(split(freqs), (x_table[0][0], x_table[1][0]))
    parts = []
    for mirrored, turn in ((0, 1.0), (1, -1.0)):
        re = slice(2 * mirrored * middle, (2 * mirrored + 1) * middle)
        im = slice((2 * mirrored + 1) * middle, (2 * mirrored + 2) * middle)
        parts.append(sums[re, :width] - turn * sums[im, width:])
        parts.append(sums[im, :width] + turn * sums[re, width:])
    re_n, im_n, re_m, im_m = parts
    first = lax.broadcasted_iota(jnp.int32, (middle, width), 0) == 0

    @pl.when(jnp.logical_not(special))
    def _():
        rows_ref[:middle, :width] = jnp.where(first, re_n, re_n + re_m)
        rows_ref[:middle, width:] = jnp.where(first, im_n, im_n + im_m)
        rows_ref[middle:, :width] = jnp.where(first, -re_m, im_n - im_m)
        rows_ref[middle:, width:] = jnp.where(first, -im_m, re_m - re_n)

    @pl.when(special)
    def _():
        rows_ref[:middle, :width] = jnp.where(first, re_n, 2.0 * re_n)
        rows_ref[:middle, width:] = jnp.where(first, re_m, 2.0 * re_m)
        rows_ref[middle:, :width] = jnp.where(first, -im_n, 2.0 * im_n)
        rows_ref[middle:, width:] = jnp.where(first, -im_m, -2.0 * im_m)

    rows_ref[...] = product((y_table[0][...], y_table[1][...]), split(rows_ref[...]))
    for cell in range(plan.cells):
        for group in range(plan.slabs // plan.y_lanes):
            parts = []
            for place in range(plan.y_lanes):
                tiles = []
                for part in range(2):
                    for step in range(plan.steps):
                        row = plan.row_of(cell, step, place)
                        col = part * width + group * LANES
                        tiles.append(rows_ref[row : row + plan.row_block, col : col + LANES])
                value = jnp.concatenate(tiles, axis=0)
                parts.append(value * sign if place % 2 == 1 else value)
            parts = swap_groups(parts, plan.width)
            first = cell * plan.slabs + group * plan.y_lanes
            for i in range(plan.y_lanes):
                out[first + i] = parts[i].reshape(2, plan.steps, plan.row_block, LANES)


def first_plane_kernel(plan, me_ref, pieces, y_high, y_low, x_high, x_low, out, rows_ref, freq_ref):
    out[...] = forward_plane(plan, me_ref, pieces, (y_high, y_low), (x_high, x_low), rows_ref, freq_ref)


def middle_plane_kernel(plan, me_ref, edge, yf_high, yf_low, xf_high, xf_low, *refs):
    late, refs = (refs[:6], refs[6:])
    strips, refs = (refs[: plan.inner], refs[plan.inner :])
    out, rest, rows_ref, freq_ref, sum_ref, rest_ref, weights = refs[:7]
    pieces, even, xb_high, xb_low, yb_high, yb_low, sems = refs[7:]
    slab = lax.rem(me_ref[0], plan.slabs)
    place = lax.rem(slab, plan.half)
    outer_id, inner_id = (place // plan.inner, lax.rem(place, plan.inner))
    held = (pieces, even, xb_high, xb_low, yb_high, yb_low)
    copies = [pltpu.make_async_copy(late[n], held[n], sems.at[n]) for n in range(2)]
    for i in range(plan.inner):
        for j in range(plan.outer):
            owner = lax.rem(outer_id - j + plan.outer, plan.outer) * plan.inner
            owner = owner + lax.rem(inner_id - i + plan.inner, plan.inner)
            rows = pl.ds(pl.multiple_of(owner * plan.ky_local, plan.ky_local), plan.ky_local)
            copies.append(
                pltpu.make_async_copy(
                    strips[i].at[j], weights.at[:, rows], sems.at[len(held) + i * plan.outer + j]
                )
            )
    early = len(copies)
    for n in range(2, len(held)):
        copies.append(pltpu.make_async_copy(late[n], held[n], sems.at[n]))
    for copy in copies:
        copy.start()
    copies[0].wait()
    special = me_ref[0] == 0
    width = plan.x_chunk
    middle = plan.ny // 2
    odd = forward_plane(plan, me_ref, pieces, (yf_high, yf_low), (xf_high, xf_low), rows_ref, freq_ref)
    for copy in copies[1:early]:
        copy.wait()
    row = lax.broadcasted_iota(jnp.int32, (middle, width), 0)
    at_first = row == 0
    for mirrored, turn in ((0, 1.0), (1, -1.0)):
        re = slice(2 * mirrored * middle, (2 * mirrored + 1) * middle)
        im = slice((2 * mirrored + 1) * middle, (2 * mirrored + 2) * middle)
        results = []
        for upper in range(2):
            cols = slice(upper * width, (upper + 1) * width)
            plane = weights[mirrored, :, cols]
            change = at_first & special
            if mirrored:
                weight = jnp.where(change, edge[1:2, cols], plane)
                second = plane
            else:
                weight = plane
                second = jnp.where(change, edge[0:1, cols], plane)
            re_sums = even[re] - odd[re] if upper else even[re] + odd[re]
            im_sums = even[im] - odd[im] if upper else even[im] + odd[im]
            real = weight * re_sums[:, :width] + (turn * second) * im_sums[:, width:]
            imag = second * im_sums[:, :width] - (turn * weight) * re_sums[:, width:]
            results.append((real, imag))
        for part, rows in enumerate((re, im)):
            below, above = (results[0][part], results[1][part])
            sum_ref[rows] = below + above
            rest_ref[rows] = below - above
    last = pltpu.make_async_copy(rest_ref, rest, sems.at[len(held) + plan.half])
    last.start()
    for copy in copies[early:]:
        copy.wait()
    backward_plane(plan, me_ref, sum_ref[...], (xb_high, xb_low), (yb_high, yb_low), out, rows_ref)
    last.wait()


def last_plane_kernel(plan, me_ref, freqs, x_high, x_low, y_high, y_low, out, rows_ref):
    backward_plane(plan, me_ref, freqs[...], (x_high, x_low), (y_high, y_low), out, rows_ref)


def plane_call(plan, kernel, name, me, arrays, tables, late, out_shapes, scratch, work):
    specs = [whole_spec(array.shape) for array in arrays]
    flat = []
    for pair, chunk in tables:
        for table in pair:
            if chunk is None:
                specs.append(whole_spec(table.shape))
            else:
                specs.append(pl.BlockSpec((1,) + table.shape[1:], lambda i, chunk=chunk: (chunk, 0, 0)))
            flat.append(table)
    specs += [pl.BlockSpec(memory_space=pl.ANY)] * len(late)
    size = sum(4 * array.size for array in list(arrays) + list(late)) + sum(2 * t.size for t in flat)
    return pl.pallas_call(
        functools.partial(kernel, plan),
        grid=(1,),
        in_specs=[pl.BlockSpec(memory_space=pltpu.SMEM)] + specs,
        out_specs=[whole_spec(out_shapes[0])] + [pl.BlockSpec(memory_space=pl.ANY)] * (len(out_shapes) - 1),
        out_shape=[jax.ShapeDtypeStruct(shape, jnp.float32) for shape in out_shapes],
        scratch_shapes=scratch,
        compiler_params=pltpu.CompilerParams(vmem_limit_bytes=VMEM_LIMIT),
        cost_estimate=pl.CostEstimate(
            flops=work * 12 * plan.nx * plan.ny * plan.x_chunk, bytes_accessed=size, transcendentals=0
        ),
        name=name,
    )(me, *arrays, *flat, *late)


def gather_kernel(
    plan, chunk, counts, before, high, low, projection, sent, out, scratch, held, sems, pieces
):
    planes = plan.cell_planes
    rows = plan.slots * 2 * plan.row_block
    fetch = pltpu.make_async_copy(sent, pieces, sems.at[plan.tx_chunk])
    fetch.start()
    copies = tile_copies(plan, chunk, projection, held, sems)
    for copy in copies:
        copy.start()
    fetch.wait()
    columns = [pieces[:, :, step].reshape(rows, LANES) for step in range(plan.steps)]
    scratch[...] = product(split(jnp.concatenate(columns, axis=1).T), (high[...], low[...]))
    for tx, copy in enumerate(copies):
        copy.wait()
        last = chunk == CHUNKS - 1 and tx == plan.tx_chunk - 1

        def body(place, carry, tx=tx, last=last):
            lanes = pl.ds(pl.multiple_of(place * LANES, LANES), LANES)
            far = [(before if tx == 0 else out)[p, :, lanes] for p in range(plan.panels)]
            for ty in range(TY):
                row = ((place * TY + ty) * plan.tx_chunk + tx) * planes
                rows_at = pl.ds(pl.multiple_of(row, planes), planes)
                for tz in range(TZ):
                    t = ty * TZ + tz
                    potential = scratch[rows_at, tz * LANES : (tz + 1) * LANES]
                    for p in range(plan.panels):
                        far[p] = far[p] + held[tx, p, t, :, lanes] * potential
            for p in range(plan.panels):
                out[p, :, lanes] = jnp.where(counts[:, lanes] > p, far[p], 0.0) if last else far[p]
            return carry

        lax.fori_loop(0, plan.steps * plan.step_blocks, body, 0)


def gather(plan, chunk, counts, before, projection, high, low, pieces):
    kernel = functools.partial(gather_kernel, plan, chunk)
    arrays = [counts, before, high, low]
    scratch = [pltpu.VMEM(pieces.shape, jnp.float32)]
    return projection_call(
        plan, kernel, "depth_gather", arrays, [projection, pieces], before.shape, scratch
    )


def near_kernel(plan, extended, codes, blocks_ref, out):
    step = pl.program_id(0)
    lane = lax.broadcasted_iota(jnp.int32, (plan.cell_planes, LANES), 1)
    depth = lane % NZC
    digits = []
    for k in range(plan.near):
        code = codes[k]
        digits.append((code // 9, code // 3 % 3, code % 3))
    total = [None] * plan.panels
    for q in range(plan.panels):
        shifted = []
        for dx in range(3):
            before, here, after = (
                extended[q, dx, :, pl.ds(pl.multiple_of((step + i) * LANES, LANES), LANES)] for i in range(3)
            )
            up = jnp.where(lane < NZC, pltpu.roll(before, NZC, 1), pltpu.roll(here, NZC, 1))
            down = jnp.where(
                lane >= LANES - NZC, pltpu.roll(after, LANES - NZC, 1), pltpu.roll(here, LANES - NZC, 1)
            )
            for value in (up, here, down):
                under = jnp.where(
                    depth == 0, pltpu.roll(value, LANES - NZC + 1, 1), pltpu.roll(value, 1, 1)
                )
                over = jnp.where(
                    depth == NZC - 1, pltpu.roll(value, NZC - 1, 1), pltpu.roll(value, LANES - 1, 1)
                )
                shifted.append((under, value, over))
        for k in range(plan.near):
            digit_x, digit_y, digit_z = digits[k]

            def choose(digit, options):
                return jnp.where(digit == 0, options[0], jnp.where(digit == 1, options[1], options[2]))

            by_z = [choose(digit_z, options) for options in shifted]
            by_y = [choose(digit_y, by_z[3 * i : 3 * i + 3]) for i in range(3)]
            picked = choose(digit_x, by_y)
            for p in range(plan.panels):
                term = blocks_ref[k, p, q] * picked
                total[p] = term if total[p] is None else total[p] + term
    for p in range(plan.panels):
        out[p] = total[p]


def near_field(plan, extended, neighbours, near_blocks):
    return pl.pallas_call(
        functools.partial(near_kernel, plan),
        grid=(plan.cell_cols // LANES,),
        in_specs=[
            whole_spec(extended.shape),
            pl.BlockSpec((plan.near, plan.cell_planes, LANES), lambda i: (0, 0, i)),
            pl.BlockSpec(
                (plan.near, plan.panels, plan.panels, plan.cell_planes, LANES), lambda i: (0, 0, 0, 0, i)
            ),
        ],
        out_specs=pl.BlockSpec((plan.panels, plan.cell_planes, LANES), lambda i: (0, 0, i)),
        out_shape=jax.ShapeDtypeStruct((plan.panels, plan.cell_planes, plan.cell_cols), jnp.float32),
        compiler_params=pltpu.CompilerParams(vmem_limit_bytes=VMEM_LIMIT),
        cost_estimate=pl.CostEstimate(
            flops=2 * near_blocks.size, bytes_accessed=4 * near_blocks.size, transcendentals=0
        ),
        name="near_blocks",
    )(extended, neighbours, near_blocks)


def ring_pairs(axis):
    count = lax.axis_size(axis)
    up = [(i, (i + 1) % count) for i in range(count)]
    return (up, [(j, i) for i, j in up])


def extend_rows(plan, masked):
    up, down = ring_pairs("cell")
    left = lax.ppermute(masked[:, :, -NZC:], "cell", up)
    right = lax.ppermute(masked[:, :, :NZC], "cell", down)
    return (left, right)


def extend_planes(plan, masked, left, right):
    rest = jnp.zeros((plan.panels, plan.cell_planes, LANES - NZC), jnp.float32)
    wide = jnp.concatenate([rest, left, masked, right, rest], axis=2)
    up, down = ring_pairs("slab")
    before = lax.ppermute(wide[:, -1:], "slab", up)
    after = lax.ppermute(wide[:, :1], "slab", down)
    whole = jnp.concatenate([before, wide, after], axis=1)
    planes = plan.cell_planes
    return jnp.stack([whole[:, i : i + planes] for i in range(3)], axis=1)


def pick_kernel(plan, ids_ref, by_depth, *refs):
    outs, sems = (refs[:-1], refs[-1])
    cell, slab = (ids_ref[0], ids_ref[1])
    half_id, place = (slab // plan.half, lax.rem(slab, plan.half))
    copies = []
    for j in range(plan.outer):
        group = lax.rem(place // plan.inner + j, plan.outer)
        base = cell * plan.slabs + half_id * plan.half + group * plan.inner
        for q in range(plan.inner):
            freq = base + q
            mirror = jnp.where(freq == 0, plan.nz // 2, plan.nz - freq)
            for m, index in enumerate((freq, mirror)):
                n = (j * plan.inner + q) * 2 + m
                out = outs[2 * j + m]
                copies.append(pltpu.make_async_copy(by_depth.at[index], out.at[q], sems.at[n]))
    for copy in copies:
        copy.start()
    for copy in copies:
        copy.wait()


def pick_planes(plan, spectrum):
    by_depth = jnp.transpose(spectrum, (1, 2, 0))
    shape = (plan.inner,) + by_depth.shape[1:]
    count = 2 * plan.outer
    ids = jnp.stack([lax.axis_index("cell"), lax.axis_index("slab")]).astype(jnp.int32)
    return pl.pallas_call(
        functools.partial(pick_kernel, plan),
        in_specs=[pl.BlockSpec(memory_space=pltpu.SMEM), pl.BlockSpec(memory_space=pl.ANY)],
        out_specs=[pl.BlockSpec(memory_space=pl.ANY)] * count,
        out_shape=[jax.ShapeDtypeStruct(shape, jnp.float32)] * count,
        scratch_shapes=[pltpu.SemaphoreType.DMA((2 * plan.half,))],
        cost_estimate=pl.CostEstimate(
            flops=0, bytes_accessed=8 * count * math.prod(shape), transcendentals=0
        ),
        name="pick_planes",
    )(ids, by_depth)


def outer_shift(plan, value, j):
    if j == 0:
        return value
    pairs = []
    for source in range(plan.slabs):
        base = source // plan.half * plan.half
        pairs.append((source, base + (source - base + j * plan.inner) % plan.half))
    return lax.ppermute(value, "slab", pairs)


def edge_weights(plan, spectrum):
    slab, cell = (lax.axis_index("slab"), lax.axis_index("cell"))
    rows = jnp.transpose(spectrum[:, :, 0], (1, 0))
    middle = plan.nz // 2
    turned = jnp.concatenate([rows[middle : middle + 1], jnp.flip(rows, 0)], axis=0)
    other = cell * plan.slabs + (1 - slab // plan.half) * plan.half
    total = 0.0
    for j in range(plan.outer):
        sent = lax.dynamic_slice_in_dim(turned, other + j * plan.inner, plan.inner, 0)
        sent = jnp.concatenate([sent, rows[:1]], axis=0)
        pairs = [(plan.half, j * plan.inner), (0, plan.half + j * plan.inner)]
        total = total + lax.ppermute(sent, "slab", pairs)
    return (total, rows[middle : middle + 1])


def second_weights(plan, blocks, turned):
    slab = lax.axis_index("slab")
    part = lax.rem(slab, plan.half) // plan.inner
    strips = []
    for i in range(plan.inner):
        place = lax.rem(slab + i, plan.inner)
        rows = [lax.dynamic_slice_in_dim(block, place, 1, 0) for pair in blocks for block in pair]
        strip = jnp.stack(rows).reshape((plan.outer, 2) + blocks[0][0].shape[1:])
        ids = [lax.broadcasted_iota(jnp.int32, strip.shape, n) for n in range(3)]
        change = (ids[0] == part) & (ids[1] == 1) & (ids[2] == 0) & (slab % plan.inner == 0)
        strip = jnp.where(change, lax.dynamic_slice_in_dim(turned, place, 1, 0), strip)
        if i > 0:
            pairs = []
            for source in range(plan.slabs):
                group = source // plan.inner * plan.inner
                pairs.append((source, group + (source + i) % plan.inner))
            strip = lax.ppermute(strip, "slab", pairs)
        strips.append(strip)
    return strips


def per_device(charges, counts, projection, near_blocks, neighbours, spectrum):
    panels, cell_planes, cell_cols = charges.shape
    cells, slabs = (lax.axis_size("cell"), lax.axis_size("slab"))
    nx, nz, local = spectrum.shape
    plan = Plan(slabs, cells, panels, cell_planes, cell_cols, neighbours.shape[0], nx, nz, local * slabs)
    if not plan.fits():
        return plain_device(charges, counts, projection, near_blocks, neighbours, spectrum)
    me = (lax.axis_index("cell") * slabs + lax.axis_index("slab")).astype(jnp.int32).reshape(1)
    forward_table, backward_table = plan.depth_tables()
    depth_forward, depth_backward = (halves(forward_table.T), halves(backward_table))
    y_rows, x_cols, low_ids = (plan.y_rows().reshape(-1), plan.x_columns(), np.arange(plan.ny // 2))
    cos_y, sin_y = wave(low_ids, y_rows, plan.ny)
    sin_y[0] = 1.0 - 2.0 * (y_rows % 2)
    y_forward = halves(np.concatenate([cos_y, sin_y], axis=0))
    y_backward = halves(np.concatenate([cos_y.T, -sin_y.T], axis=1))
    x_waves = [wave(cols, low_ids, plan.nx) for cols in x_cols]
    x_forward = halves(np.stack([np.concatenate(pair, axis=1) for pair in x_waves]))
    x_backward = halves(np.stack([np.concatenate([t.T for t in pair], axis=1) for pair in x_waves]))
    split_projection = projection.reshape(
        (panels, TX // CHUNKS, CHUNKS, TY * TZ, cell_planes, cell_cols)
    )
    axes = ("cell", "slab")

    def exchange(pieces):
        return lax.all_to_all(pieces, axes, split_axis=0, concat_axis=0, tiled=True)

    def values(*shapes):
        return [pltpu.VMEM(shape, jnp.float32) for shape in shapes]

    rows_shape = (plan.ny, 2 * plan.x_chunk)
    freq_shape = (2 * plan.ny, plan.x_chunk)
    both_shape = (2 * plan.ny, plan.nx)
    picked = pick_planes(plan, spectrum)
    start, *picked = lax.optimization_barrier((charges, *picked))
    plain = [outer_shift(plan, picked[2 * j], j) for j in range(plan.outer)]
    mirror = [outer_shift(plan, picked[2 * j + 1], j) for j in range(plan.outer)]
    slot = lax.broadcasted_iota(jnp.int32, charges.shape, 0)
    masked = jnp.where(slot < counts[None], charges, 0.0)
    left, right = extend_rows(plan, masked)
    turned, own_row = edge_weights(plan, spectrum)
    pieces = [
        project(plan, i, part, counts, split_projection, *depth_forward)
        for i, part in enumerate((start, charges))
    ]
    pieces[0], *plain = lax.optimization_barrier((pieces[0], *plain))
    even_pieces = exchange(pieces[0])
    pieces[1], left, right, turned, *mirror = lax.optimization_barrier(
        (pieces[1], left, right, turned, *mirror)
    )
    odd_pieces = exchange(pieces[1])
    strips = second_weights(plan, list(zip(plain, mirror)), turned)
    edge = jnp.concatenate([turned[plan.inner :], own_row], axis=0)
    extended = extend_planes(plan, masked, left, right)
    (even,) = plane_call(
        plan, first_plane_kernel, "even_planes", me, [even_pieces], [(y_forward, None), (x_forward, 0)], [],
        [both_shape], values(rows_shape, freq_shape), 2,
    )
    even, extended = lax.optimization_barrier((even, extended))
    late = [odd_pieces, even, x_backward[0][:1], x_backward[1][:1], *y_backward]
    copies = [pltpu.VMEM(array.shape, array.dtype) for array in late]
    copies.append(pltpu.SemaphoreType.DMA((len(late) + plan.half + 1,)))
    back, rest = plane_call(
        plan, middle_plane_kernel, "middle_planes", me, [edge],
        [(y_forward, None), (x_forward, 1)], late + strips, [piece_shape(plan), freq_shape],
        values(rows_shape, freq_shape, freq_shape, freq_shape, (2, plan.ny // 2, plan.nx)) + copies, 4,
    )
    even_back = exchange(back)
    (back,) = plane_call(
        plan, last_plane_kernel, "odd_planes", me, [rest], [(x_backward, 1), (y_backward, None)], [],
        [piece_shape(plan)], values(rows_shape), 2,
    )
    total = near_field(plan, extended, neighbours, near_blocks)
    back, total = lax.optimization_barrier((back, total))
    odd_back = exchange(back)
    total = gather(plan, 0, counts, total, split_projection, *depth_backward, even_back)
    return gather(plan, 1, counts, total, split_projection, *depth_backward, odd_back)


def padded(value, sides, width):
    for axis, dim in sides:
        count, length = (lax.axis_size(axis), value.shape[dim])
        up = [(i, (i + 1) % count) for i in range(count)]
        down = [(j, i) for i, j in up]
        last = lax.slice_in_dim(value, length - width, length, axis=dim)
        first = lax.slice_in_dim(value, 0, width, axis=dim)
        before = lax.ppermute(last, axis, up)
        after = lax.ppermute(first, axis, down)
        value = jnp.concatenate([before, value, after], axis=dim)
    return value


def wave_tables(row_count, col_count, length):
    products = (
        lax.broadcasted_iota(jnp.int32, (row_count, col_count), 0)
        * lax.broadcasted_iota(jnp.int32, (row_count, col_count), 1)
        % length
    )
    angle_rad = products.astype(jnp.float32) * (2.0 * math.pi / length)
    return (jnp.cos(angle_rad), jnp.sin(angle_rad))


def depth_rows(nz, freq_ids, valid, weights):
    depth_ids = lax.broadcasted_iota(jnp.int32, (freq_ids.shape[0], nz), 1)
    products = freq_ids[:, None] * depth_ids % nz
    angle_rad = products.astype(jnp.float32) * (2.0 * math.pi / nz)
    basis = jnp.stack([jnp.cos(angle_rad), -jnp.sin(angle_rad)])
    return (basis * valid[None, :, None], basis * weights[None, :, None])


def half_depth_tables(nz, cell_count):
    lower = nz // (2 * cell_count)
    row_ids = lax.broadcasted_iota(jnp.int32, (cell_count * (lower + 1),), 0)
    block_ids = row_ids // (lower + 1)
    slot_ids = row_ids % (lower + 1)
    freq_ids = jnp.where(slot_ids < lower, block_ids * lower + slot_ids, nz // 2)
    valid = jnp.where((slot_ids < lower) | (block_ids == 0), 1.0, 0.0).astype(jnp.float32)
    doubled = jnp.where((slot_ids < lower) & (freq_ids > 0), 2.0, 1.0).astype(jnp.float32)
    forward_table, backward_table = depth_rows(nz, freq_ids, valid, valid * doubled)
    return (forward_table, backward_table, freq_ids)


def combine_halves(first_part, second, orient):
    half_width = first_part.shape[-1] // 2
    real_part = first_part[..., :half_width] + orient * second[..., half_width:]
    imag_part = first_part[..., half_width:] - orient * second[..., :half_width]
    return jnp.concatenate([real_part, imag_part], axis=-1)


def transform_axis(pattern, cosine, sine_tab, values, orient):
    first_part = jnp.einsum(pattern, cosine, values, precision=lax.Precision.HIGHEST)
    second = jnp.einsum(pattern, sine_tab, values, precision=lax.Precision.HIGHEST)
    return combine_halves(first_part, second, orient)


def twiddle(values, twist_cos, twist_sin, orient):
    half_width = values.shape[-1] // 2
    real_part = values[..., :half_width]
    imag_part = values[..., half_width:]
    new_real = real_part * twist_cos + orient * imag_part * twist_sin
    new_imag = imag_part * twist_cos - orient * real_part * twist_sin
    return jnp.concatenate([new_real, new_imag], axis=-1)


def transform_rows(planes_block, cosine, sine_tab, orient):
    flat_rows = planes_block.reshape(-1, planes_block.shape[-1])
    first_part = jnp.dot(flat_rows, cosine, precision=lax.Precision.HIGHEST).reshape(
        planes_block.shape
    )
    second = jnp.dot(flat_rows, sine_tab, precision=lax.Precision.HIGHEST).reshape(
        planes_block.shape
    )
    real_part = first_part[:, 0] + orient * second[:, 1]
    imag_part = first_part[:, 1] - orient * second[:, 0]
    return jnp.stack([real_part, imag_part], axis=1)


def plain_device(charges, counts, projection, near_blocks, neighbours, spectrum):
    panels, cell_planes, cell_cols = charges.shape
    nx, nz, ny = (spectrum.shape[0], spectrum.shape[1], spectrum.shape[2] * lax.axis_size("slab"))
    planes = cell_planes * TX
    rows_cell = cell_cols // NZC
    slot_ids = lax.broadcasted_iota(jnp.int32, charges.shape, 0)
    panel_mask = (slot_ids < counts[None]).astype(jnp.float32)
    masked = charges * panel_mask
    tile_values = jnp.einsum("ptxc,pxc->txc", projection, masked, precision=lax.Precision.HIGHEST)
    grid_field = (
        tile_values.reshape(TX, TY, TZ, cell_planes, rows_cell, NZC)
        .transpose(3, 0, 5, 2, 4, 1)
        .reshape(planes, nz, rows_cell * TY)
    )
    cell_count = lax.axis_size("cell")
    forward_table, backward_table, freq_ids = half_depth_tables(nz, cell_count)
    depth_count = forward_table.shape[1] // cell_count
    spectra_z = jnp.einsum(
        "wkz,xzy->xwky", forward_table, grid_field, precision=lax.Precision.HIGHEST
    )
    cosine_y, sine_y = wave_tables(ny, ny, ny)
    pencils = transform_rows(
        lax.all_to_all(spectra_z, "cell", split_axis=2, concat_axis=3, tiled=True),
        cosine_y,
        sine_y,
        1.0,
    )
    columns = lax.all_to_all(pencils, "slab", split_axis=3, concat_axis=0, tiled=True)
    col_width = columns.shape[2] * columns.shape[3]
    flat_rows = columns.reshape(nx, 2 * col_width)
    first_row = lax.axis_index("cell") * depth_count
    kernel_ids = lax.dynamic_slice_in_dim(freq_ids, first_row, depth_count, 0)
    kernel = jnp.take(spectrum, kernel_ids, axis=1).reshape(nx, col_width) * (1.0 / (nx * ny * nz))
    kernel_both = jnp.concatenate([kernel, kernel], axis=1)
    slab_count = lax.axis_size("slab")
    local_rows = nx // slab_count
    cosine_s, sine_s = wave_tables(slab_count, slab_count, slab_count)
    cosine_r, sine_r = wave_tables(local_rows, local_rows, local_rows)
    twist_cos, twist_sin = wave_tables(slab_count, local_rows, nx)
    twist_cos = twist_cos[:, :, None]
    twist_sin = twist_sin[:, :, None]
    section_one = transform_axis(
        "ks,src->krc",
        cosine_s,
        sine_s,
        flat_rows.reshape(slab_count, local_rows, 2 * col_width),
        1.0,
    )
    section_one = twiddle(section_one, twist_cos, twist_sin, 1.0)
    section_two = transform_axis("jr,krc->jkc", cosine_r, sine_r, section_one, 1.0)
    weighted = section_two.reshape(nx, 2 * col_width) * kernel_both
    section_one = transform_axis(
        "rj,jkc->krc",
        cosine_r,
        sine_r,
        weighted.reshape(local_rows, slab_count, 2 * col_width),
        -1.0,
    )
    section_one = twiddle(section_one, twist_cos, twist_sin, -1.0)
    section_two = transform_axis("sk,krc->src", cosine_s, sine_s, section_one, -1.0)
    returned_x = section_two.reshape(nx, 2 * col_width)
    returned = lax.all_to_all(
        returned_x.reshape(columns.shape), "slab", split_axis=0, concat_axis=3, tiled=True
    )
    inverse_rows = transform_rows(returned, cosine_y, sine_y, -1.0)
    grid_potential = jnp.einsum(
        "wkz,xwky->xzy",
        backward_table,
        lax.all_to_all(inverse_rows, "cell", split_axis=3, concat_axis=2, tiled=True),
        precision=lax.Precision.HIGHEST,
    )
    tile_potential = (
        grid_potential.reshape(cell_planes, TX, NZC, TZ, rows_cell, TY)
        .transpose(1, 5, 3, 0, 4, 2)
        .reshape(TX * TY * TZ, cell_planes, cell_cols)
    )
    far_field = jnp.einsum(
        "ptxc,txc->pxc", projection, tile_potential, precision=lax.Precision.HIGHEST
    )
    block = masked.reshape(panels, cell_planes, rows_cell, NZC)
    extended = padded(block, (("slab", 1), ("cell", 2)), 1)
    flat_ext = extended.reshape(panels, -1)
    step_x = neighbours // 9 - 1
    step_y = neighbours // 3 % 3 - 1
    step_z = neighbours % 3 - 1
    plane_ids = lax.broadcasted_iota(jnp.int32, neighbours.shape, 1)
    col_ids = lax.broadcasted_iota(jnp.int32, neighbours.shape, 2)
    row_ids = col_ids // NZC
    depth_ids = col_ids % NZC
    near_ids = ((plane_ids + step_x + 1) * (rows_cell + 2) + row_ids + step_y + 1) * NZC + (
        depth_ids + step_z
    ) % NZC
    near_count = neighbours.shape[0]
    picked = jnp.take(flat_ext, near_ids.reshape(-1), axis=1).reshape(
        panels, near_count, cell_planes, cell_cols
    )
    near_field = jnp.einsum("kpqxc,qkxc->pxc", near_blocks, picked, precision=lax.Precision.HIGHEST)
    return (far_field + near_field) * panel_mask


def solution(mesh):
    in_specs = (
        P(None, "slab", "cell"),
        P("slab", "cell"),
        P(None, None, "slab", "cell"),
        P(None, None, None, "slab", "cell"),
        P(None, "slab", "cell"),
        P(None, None, "slab"),
    )
    out_specs = P(None, "slab", "cell")
    return jax.shard_map(
        per_device, mesh=mesh, in_specs=in_specs, out_specs=out_specs, check_vma=False
    )
```

```python
import functools
import math

import jax
import jax.numpy as jnp
import ml_dtypes
import numpy as np
from jax import lax
from jax.experimental import pallas as pl
from jax.experimental.pallas import tpu as pltpu
from jax.sharding import PartitionSpec as P

TX = 4
TY = 4
TZ = 4
NZC = 16
LANES = 128
CHUNKS = 2
VMEM_LIMIT = 62 * 1024 * 1024


def halves(table):
    high = table.astype(np.float32).astype(ml_dtypes.bfloat16)
    low = (table - high.astype(np.float64)).astype(np.float32).astype(ml_dtypes.bfloat16)
    return (high, low)


def wave(rows, cols, length):
    angle = (rows[:, None] * cols[None, :] % length) * (2.0 * math.pi / length)
    return (np.cos(angle), np.sin(angle))


class Plan:
    def __init__(self, slabs, cells, panels, cell_planes, cell_cols, near, nx, nz, ny):
        self.slabs, self.cells = (slabs, cells)
        self.panels, self.cell_planes, self.cell_cols, self.near = (panels, cell_planes, cell_cols, near)
        self.nx, self.ny, self.nz = (nx, ny, nz)
        self.slots = slabs * cells
        self.tx_chunk = TX // CHUNKS
        self.width = cell_planes * self.tx_chunk
        self.y_lanes = LANES // self.width if self.width else 1
        self.row_block = LANES // NZC
        self.step_blocks = self.y_lanes // TY
        self.steps = cell_cols // (LANES * self.step_blocks) if self.step_blocks else 0
        self.x_chunk = nx // CHUNKS
        self.ky_local = ny // slabs
        self.half = slabs // 2
        self.outer = math.gcd(self.half, 2)
        self.inner = self.half // self.outer

    def fits(self):
        return (
            self.slots * 2 == self.nz
            and self.cell_planes == 8
            and self.step_blocks * TY * self.width == LANES
            and self.slabs % self.y_lanes == 0
            and self.ky_local % 8 == 0
            and self.steps * self.step_blocks * LANES == self.cell_cols
            and self.x_chunk % LANES == 0
            and self.ny % 1024 == self.nx % 1024 == 512
        )

    def depth_tables(self):
        depth = np.arange(NZC)[None, :] * TZ + np.arange(TZ)[:, None]
        scale = 1.0 / (self.nx * self.ny * self.nz)
        forward = np.zeros((self.slots, 2, self.row_block, TZ, self.row_block, NZC))
        backward = np.zeros_like(forward)
        for freq in range(self.slots):
            angle = (freq * depth % self.nz) * (2.0 * math.pi / self.nz)
            real, imag = (np.cos(angle), -np.sin(angle))
            factor = 2.0 * scale
            if freq == 0:
                imag = np.cos(depth * math.pi)
                factor = scale
            for row in range(self.row_block):
                forward[freq, 0, row, :, row, :] = real
                forward[freq, 1, row, :, row, :] = imag
                backward[freq, 0, row, :, row, :] = factor * real
                backward[freq, 1, row, :, row, :] = factor * imag
        shape = (self.slots * 2 * self.row_block, TZ * LANES)
        return (forward.reshape(shape), backward.reshape(shape))

    def y_rows(self):
        parity, cell, step, block, tile, row = np.meshgrid(
            *[np.arange(n) for n in (2, self.cells, self.steps, self.step_blocks, TY // 2, self.row_block)],
            indexing="ij",
        )
        cell_row = ((cell * self.steps + step) * self.step_blocks + block) * self.row_block + row
        return (cell_row * TY + 2 * tile + parity).reshape(2, -1)

    def x_columns(self):
        parity, slab, tile, plane = np.meshgrid(
            *[np.arange(n) for n in (2, self.slabs, TX // 2, self.cell_planes)], indexing="ij"
        )
        return ((slab * self.cell_planes + plane) * TX + 2 * tile + parity).reshape(2, -1)

    def row_of(self, cell, step, place):
        block, tile = (place // TY, place % TY)
        inner = (cell * self.steps + step) * self.step_blocks + block
        return (tile % 2) * (self.ny // 2) + (inner * (TY // 2) + tile // 2) * self.row_block


def split(value):
    high = value.astype(jnp.bfloat16)
    low = (value - high.astype(jnp.float32)).astype(jnp.bfloat16)
    return (high, low)


def product(left, right, dims=((1,), (0,))):
    first = jnp.concatenate([left[0], left[0], left[1]], axis=dims[0][0])
    second = jnp.concatenate([right[0], right[1], right[0]], axis=dims[1][0])
    return lax.dot_general(first, second, (dims, ((), ())), preferred_element_type=jnp.float32)


def swap_groups(parts, width):
    count = len(parts)
    lane = lax.broadcasted_iota(jnp.int32, parts[0].shape, 1)
    parts = list(parts)
    step = count // 2
    while step >= 1:
        shift = step * width
        upper = (lane // shift) % 2 == 1
        for i in range(count):
            if i & step:
                continue
            first, second = (parts[i], parts[i + step])
            parts[i] = jnp.where(upper, pltpu.roll(second, shift, 1), first)
            parts[i + step] = jnp.where(upper, second, pltpu.roll(first, LANES - shift, 1))
        step //= 2
    return parts


def tile_copies(plan, chunk, projection, held, sems):
    return [
        pltpu.make_async_copy(projection.at[:, tx, chunk], held.at[tx], sems.at[tx])
        for tx in range(plan.tx_chunk)
    ]


def project_kernel(plan, chunk, charges_in, counts_in, high_in, low_in, projection, out, scratch, held, sems,
                   charges, counts, high, low):
    planes = plan.cell_planes
    first = plan.tx_chunk
    pairs = ((charges_in, charges), (counts_in, counts), (high_in, high), (low_in, low))
    loads = [pltpu.make_async_copy(*pair, sems.at[first + n]) for n, pair in enumerate(pairs)]
    copies = tile_copies(plan, chunk, projection, held, sems)
    for copy in loads[:2] + copies + loads[2:]:
        copy.start()
    for copy in loads[:2]:
        copy.wait()
    for tx, copy in enumerate(copies):
        copy.wait()

        def body(place, carry, tx=tx):
            lanes = pl.ds(pl.multiple_of(place * LANES, LANES), LANES)
            count = counts[:, lanes]
            own = [jnp.where(count > p, charges[p, :, lanes], 0.0) for p in range(plan.panels)]
            for ty in range(TY):
                row = ((place * TY + ty) * plan.tx_chunk + tx) * planes
                rows = pl.ds(pl.multiple_of(row, planes), planes)
                for tz in range(TZ):
                    t = ty * TZ + tz
                    total = held[tx, 0, t, :, lanes] * own[0]
                    for p in range(1, plan.panels):
                        total = total + held[tx, p, t, :, lanes] * own[p]
                    scratch[rows, tz * LANES : (tz + 1) * LANES] = total
            return carry

        lax.fori_loop(0, plan.steps * plan.step_blocks, body, 0)
    for copy in loads[2:]:
        copy.wait()
    spectra = product(split(scratch[...]), (high[...], low[...])).T
    shape = (plan.slots, 2, plan.row_block, LANES)
    for step in range(plan.steps):
        out[:, :, step] = spectra[:, step * LANES : (step + 1) * LANES].reshape(shape)


def held_shape(plan):
    cols = plan.steps * plan.step_blocks * LANES
    return (plan.tx_chunk, plan.panels, TY * TZ, plan.cell_planes, cols)


def piece_shape(plan):
    return (plan.slots, 2, plan.steps, plan.row_block, LANES)


def whole_spec(shape):
    return pl.BlockSpec(shape, lambda i: (0,) * len(shape))


def projection_call(plan, kernel, name, arrays, projection, out_shape, fits_held):
    scratch = [pltpu.VMEM((plan.steps * LANES, TZ * LANES), jnp.float32)]
    space = pltpu.VMEM
    limit = VMEM_LIMIT - 20 * 1024 * 1024
    if fits_held:
        scratch.append(pltpu.VMEM(held_shape(plan), jnp.float32))
        space = pl.ANY
        limit = VMEM_LIMIT
    scratch.append(pltpu.SemaphoreType.DMA((plan.tx_chunk + len(arrays),)))
    scratch += [pltpu.VMEM(array.shape, array.dtype) for array in arrays]
    return pl.pallas_call(
        kernel,
        in_specs=[pl.BlockSpec(memory_space=pl.ANY)] * len(arrays) + [pl.BlockSpec(memory_space=space)],
        out_specs=pl.BlockSpec(memory_space=pltpu.VMEM),
        out_shape=jax.ShapeDtypeStruct(out_shape, jnp.float32),
        scratch_shapes=scratch,
        compiler_params=pltpu.CompilerParams(vmem_limit_bytes=limit),
        cost_estimate=pl.CostEstimate(
            flops=2 * math.prod(held_shape(plan)),
            bytes_accessed=4 * math.prod(held_shape(plan)),
            transcendentals=0,
        ),
        name=name,
    )(*arrays, projection)


def project(plan, chunk, charges, counts, projection, high, low):
    kernel = functools.partial(project_kernel, plan, chunk)
    arrays = [charges, counts, high, low]
    return projection_call(plan, kernel, "project_depth", arrays, projection, piece_shape(plan), True)


def hold_kernel(plan, chunk, projection, after, out, sems):
    copies = tile_copies(plan, chunk, projection, out, sems)
    for copy in copies:
        copy.start()
    for copy in copies:
        copy.wait()


def hold_projection(plan, chunk, projection, after):
    return pl.pallas_call(
        functools.partial(hold_kernel, plan, chunk),
        in_specs=[pl.BlockSpec(memory_space=pl.ANY)] * 2,
        out_specs=pl.BlockSpec(memory_space=pltpu.VMEM),
        out_shape=jax.ShapeDtypeStruct(held_shape(plan), jnp.float32),
        scratch_shapes=[pltpu.SemaphoreType.DMA((plan.tx_chunk,))],
        cost_estimate=pl.CostEstimate(
            flops=0, bytes_accessed=8 * math.prod(held_shape(plan)), transcendentals=0
        ),
        name="hold_projection",
    )(projection, after)


def far_sign(plan, me_ref):
    slab = lax.rem(me_ref[0], plan.slabs)
    return jnp.where(slab >= plan.half, -1.0, 1.0)


def forward_plane(plan, me_ref, pieces, y_table, x_table, rows_ref, freq_ref, waits=()):
    special = me_ref[0] == 0
    sign = far_sign(plan, me_ref)
    rows = 2 * plan.steps * plan.row_block
    width = plan.x_chunk
    middle = plan.ny // 2
    for cell in range(plan.cells):
        for group in range(plan.slabs // plan.y_lanes):
            first = cell * plan.slabs + group * plan.y_lanes
            parts = [pieces[first + i].reshape(rows, LANES) for i in range(plan.y_lanes)]
            parts = swap_groups(parts, plan.width)
            for place, value in enumerate(parts):
                if place % 2 == 1:
                    value = value * sign
                for part in range(2):
                    for step in range(plan.steps):
                        source = (part * plan.steps + step) * plan.row_block
                        row = plan.row_of(cell, step, place)
                        col = part * width + group * LANES
                        rows_ref[row : row + plan.row_block, col : col + LANES] = value[
                            source : source + plan.row_block
                        ]
    for copy in waits:
        copy.wait()
    sums = product((y_table[0][...], y_table[1][...]), split(rows_ref[...]))
    cos_re, cos_im = (sums[:middle, :width], sums[:middle, width:])
    sin_re, sin_im = (sums[middle:, :width], sums[middle:, width:])
    first = lax.broadcasted_iota(jnp.int32, (middle, width), 0) == 0

    @pl.when(jnp.logical_not(special))
    def _():
        freq_ref[:middle] = jnp.where(first, cos_re, cos_re + sin_im)
        freq_ref[middle : 2 * middle] = jnp.where(first, cos_im, cos_im - sin_re)
        freq_ref[2 * middle : 3 * middle] = jnp.where(first, sin_re, cos_re - sin_im)
        freq_ref[3 * middle :] = jnp.where(first, sin_im, cos_im + sin_re)

    @pl.when(special)
    def _():
        freq_ref[:middle] = cos_re
        freq_ref[middle : 2 * middle] = jnp.where(first, sin_re, -sin_re)
        freq_ref[2 * middle : 3 * middle] = cos_im
        freq_ref[3 * middle :] = sin_im

    return product(split(freq_ref[...]), (x_table[0][0], x_table[1][0]))


def backward_plane(plan, me_ref, freqs, x_table, y_table, out, rows_ref):
    special = me_ref[0] == 0
    sign = far_sign(plan, me_ref)
    width = plan.x_chunk
    middle = plan.ny // 2
    sums = product(split(freqs), (x_table[0][0], x_table[1][0]))
    parts = []
    for mirrored, turn in ((0, 1.0), (1, -1.0)):
        re = slice(2 * mirrored * middle, (2 * mirrored + 1) * middle)
        im = slice((2 * mirrored + 1) * middle, (2 * mirrored + 2) * middle)
        parts.append(sums[re, :width] - turn * sums[im, width:])
        parts.append(sums[im, :width] + turn * sums[re, width:])
    re_n, im_n, re_m, im_m = parts
    first = lax.broadcasted_iota(jnp.int32, (middle, width), 0) == 0

    @pl.when(jnp.logical_not(special))
    def _():
        rows_ref[:middle, :width] = jnp.where(first, re_n, re_n + re_m)
        rows_ref[:middle, width:] = jnp.where(first, im_n, im_n + im_m)
        rows_ref[middle:, :width] = jnp.where(first, -re_m, im_n - im_m)
        rows_ref[middle:, width:] = jnp.where(first, -im_m, re_m - re_n)

    @pl.when(special)
    def _():
        rows_ref[:middle, :width] = jnp.where(first, re_n, 2.0 * re_n)
        rows_ref[:middle, width:] = jnp.where(first, re_m, 2.0 * re_m)
        rows_ref[middle:, :width] = jnp.where(first, -im_n, 2.0 * im_n)
        rows_ref[middle:, width:] = jnp.where(first, -im_m, -2.0 * im_m)

    rows_ref[...] = product((y_table[0][...], y_table[1][...]), split(rows_ref[...]))
    for cell in range(plan.cells):
        for group in range(plan.slabs // plan.y_lanes):
            parts = []
            for place in range(plan.y_lanes):
                tiles = []
                for part in range(2):
                    for step in range(plan.steps):
                        row = plan.row_of(cell, step, place)
                        col = part * width + group * LANES
                        tiles.append(rows_ref[row : row + plan.row_block, col : col + LANES])
                value = jnp.concatenate(tiles, axis=0)
                parts.append(value * sign if place % 2 == 1 else value)
            parts = swap_groups(parts, plan.width)
            first = cell * plan.slabs + group * plan.y_lanes
            for i in range(plan.y_lanes):
                out[first + i] = parts[i].reshape(2, plan.steps, plan.row_block, LANES)


def first_plane_kernel(plan, me_ref, pieces, y_high, y_low, x_high, x_low, out, rows_ref, freq_ref):
    out[...] = forward_plane(plan, me_ref, pieces, (y_high, y_low), (x_high, x_low), rows_ref, freq_ref)


def middle_plane_kernel(plan, me_ref, edge, *refs):
    late, refs = (refs[:10], refs[10:])
    strips, refs = (refs[: plan.inner], refs[plan.inner :])
    out, rest, rows_ref, freq_ref, sum_ref, rest_ref, weights = refs[:7]
    pieces, yf_high, yf_low, xf_high, xf_low, even, xb_high, xb_low, yb_high, yb_low, sems = refs[7:]
    slab = lax.rem(me_ref[0], plan.slabs)
    place = lax.rem(slab, plan.half)
    outer_id, inner_id = (place // plan.inner, lax.rem(place, plan.inner))
    held = (pieces, yf_high, yf_low, xf_high, xf_low, even, xb_high, xb_low, yb_high, yb_low)
    copies = [pltpu.make_async_copy(late[n], held[n], sems.at[n]) for n in range(6)]
    for i in range(plan.inner):
        for j in range(plan.outer):
            owner = lax.rem(outer_id - j + plan.outer, plan.outer) * plan.inner
            owner = owner + lax.rem(inner_id - i + plan.inner, plan.inner)
            rows = pl.ds(pl.multiple_of(owner * plan.ky_local, plan.ky_local), plan.ky_local)
            copies.append(
                pltpu.make_async_copy(
                    strips[i].at[j], weights.at[:, rows], sems.at[len(held) + i * plan.outer + j]
                )
            )
    early = len(copies)
    for n in range(6, len(held)):
        copies.append(pltpu.make_async_copy(late[n], held[n], sems.at[n]))
    for copy in copies:
        copy.start()
    copies[0].wait()
    special = me_ref[0] == 0
    width = plan.x_chunk
    middle = plan.ny // 2
    x_table = (xf_high.at[pl.ds(0, 1)], xf_low.at[pl.ds(0, 1)])
    odd = forward_plane(
        plan, me_ref, pieces, (yf_high, yf_low), x_table, rows_ref, freq_ref, copies[1:5]
    )
    for copy in copies[5:early]:
        copy.wait()
    row = lax.broadcasted_iota(jnp.int32, (middle, width), 0)
    at_first = row == 0
    for mirrored, turn in ((0, 1.0), (1, -1.0)):
        re = slice(2 * mirrored * middle, (2 * mirrored + 1) * middle)
        im = slice((2 * mirrored + 1) * middle, (2 * mirrored + 2) * middle)
        results = []
        for upper in range(2):
            cols = slice(upper * width, (upper + 1) * width)
            plane = weights[mirrored, :, cols]
            change = at_first & special
            if mirrored:
                weight = jnp.where(change, edge[1:2, cols], plane)
                second = plane
            else:
                weight = plane
                second = jnp.where(change, edge[0:1, cols], plane)
            re_sums = even[re] - odd[re] if upper else even[re] + odd[re]
            im_sums = even[im] - odd[im] if upper else even[im] + odd[im]
            real = weight * re_sums[:, :width] + (turn * second) * im_sums[:, width:]
            imag = second * im_sums[:, :width] - (turn * weight) * re_sums[:, width:]
            results.append((real, imag))
        for part, rows in enumerate((re, im)):
            below, above = (results[0][part], results[1][part])
            sum_ref[rows] = below + above
            rest_ref[rows] = below - above
    last = pltpu.make_async_copy(rest_ref, rest, sems.at[len(held) + plan.half])
    last.start()
    for copy in copies[early:]:
        copy.wait()
    backward_plane(plan, me_ref, sum_ref[...], (xb_high, xb_low), (yb_high, yb_low), out, rows_ref)
    last.wait()


def last_plane_kernel(plan, me_ref, freqs, x_high, x_low, y_high, y_low, out, rows_ref):
    backward_plane(plan, me_ref, freqs[...], (x_high, x_low), (y_high, y_low), out, rows_ref)


def plane_call(plan, kernel, name, me, arrays, tables, late, out_shapes, scratch, work):
    specs = [whole_spec(array.shape) for array in arrays]
    flat = []
    for pair, chunk in tables:
        for table in pair:
            if chunk is None:
                specs.append(whole_spec(table.shape))
            else:
                specs.append(pl.BlockSpec((1,) + table.shape[1:], lambda i, chunk=chunk: (chunk, 0, 0)))
            flat.append(table)
    specs += [pl.BlockSpec(memory_space=pl.ANY)] * len(late)
    size = sum(4 * array.size for array in list(arrays) + list(late)) + sum(2 * t.size for t in flat)
    return pl.pallas_call(
        functools.partial(kernel, plan),
        grid=(1,),
        in_specs=[pl.BlockSpec(memory_space=pltpu.SMEM)] + specs,
        out_specs=[whole_spec(out_shapes[0])] + [pl.BlockSpec(memory_space=pl.ANY)] * (len(out_shapes) - 1),
        out_shape=[jax.ShapeDtypeStruct(shape, jnp.float32) for shape in out_shapes],
        scratch_shapes=scratch,
        compiler_params=pltpu.CompilerParams(vmem_limit_bytes=VMEM_LIMIT),
        cost_estimate=pl.CostEstimate(
            flops=work * 12 * plan.nx * plan.ny * plan.x_chunk, bytes_accessed=size, transcendentals=0
        ),
        name=name,
    )(me, *arrays, *flat, *late)


def gather_kernel(plan, chunk, sent, high_in, low_in, before_in, counts_in, *refs):
    planes = plan.cell_planes
    rows = plan.slots * 2 * plan.row_block
    first = plan.tx_chunk
    if chunk == CHUNKS - 1:
        held, out, scratch, sems, pieces, high, low, before, counts = refs
        copies = []
    else:
        projection, out, scratch, held, sems, pieces, high, low, before, counts = refs
        copies = tile_copies(plan, chunk, projection, held, sems)
    pairs = ((sent, pieces), (high_in, high), (low_in, low), (before_in, before), (counts_in, counts))
    loads = [pltpu.make_async_copy(*pair, sems.at[first + n]) for n, pair in enumerate(pairs)]
    for copy in loads + copies:
        copy.start()
    for copy in loads:
        copy.wait()
    columns = [pieces[:, :, step].reshape(rows, LANES) for step in range(plan.steps)]
    scratch[...] = product(split(jnp.concatenate(columns, axis=1).T), (high[...], low[...]))
    for tx in range(plan.tx_chunk):
        if copies:
            copies[tx].wait()
        last = chunk == CHUNKS - 1 and tx == plan.tx_chunk - 1

        def body(place, carry, tx=tx, last=last):
            lanes = pl.ds(pl.multiple_of(place * LANES, LANES), LANES)
            far = [(before if tx == 0 else out)[p, :, lanes] for p in range(plan.panels)]
            for ty in range(TY):
                row = ((place * TY + ty) * plan.tx_chunk + tx) * planes
                rows_at = pl.ds(pl.multiple_of(row, planes), planes)
                for tz in range(TZ):
                    t = ty * TZ + tz
                    potential = scratch[rows_at, tz * LANES : (tz + 1) * LANES]
                    for p in range(plan.panels):
                        far[p] = far[p] + held[tx, p, t, :, lanes] * potential
            for p in range(plan.panels):
                out[p, :, lanes] = jnp.where(counts[:, lanes] > p, far[p], 0.0) if last else far[p]
            return carry

        lax.fori_loop(0, plan.steps * plan.step_blocks, body, 0)


def gather(plan, chunk, counts, before, projection, high, low, pieces):
    kernel = functools.partial(gather_kernel, plan, chunk)
    arrays = [pieces, high, low, before, counts]
    held_here = chunk < CHUNKS - 1
    return projection_call(plan, kernel, "depth_gather", arrays, projection, before.shape, held_here)


def near_kernel(plan, extended, codes, blocks_ref, out):
    step = pl.program_id(0)
    lane = lax.broadcasted_iota(jnp.int32, (plan.cell_planes, LANES), 1)
    depth = lane % NZC
    digits = []
    for k in range(plan.near):
        code = codes[k]
        digits.append((code // 9, code // 3 % 3, code % 3))
    total = [None] * plan.panels
    for q in range(plan.panels):
        shifted = []
        for dx in range(3):
            before, here, after = (
                extended[q, dx, :, pl.ds(pl.multiple_of((step + i) * LANES, LANES), LANES)] for i in range(3)
            )
            up = jnp.where(lane < NZC, pltpu.roll(before, NZC, 1), pltpu.roll(here, NZC, 1))
            down = jnp.where(
                lane >= LANES - NZC, pltpu.roll(after, LANES - NZC, 1), pltpu.roll(here, LANES - NZC, 1)
            )
            for value in (up, here, down):
                under = jnp.where(
                    depth == 0, pltpu.roll(value, LANES - NZC + 1, 1), pltpu.roll(value, 1, 1)
                )
                over = jnp.where(
                    depth == NZC - 1, pltpu.roll(value, NZC - 1, 1), pltpu.roll(value, LANES - 1, 1)
                )
                shifted.append((under, value, over))
        for k in range(plan.near):
            digit_x, digit_y, digit_z = digits[k]

            def choose(digit, options):
                return jnp.where(digit == 0, options[0], jnp.where(digit == 1, options[1], options[2]))

            by_z = [choose(digit_z, options) for options in shifted]
            by_y = [choose(digit_y, by_z[3 * i : 3 * i + 3]) for i in range(3)]
            picked = choose(digit_x, by_y)
            for p in range(plan.panels):
                term = blocks_ref[k, p, q] * picked
                total[p] = term if total[p] is None else total[p] + term
    for p in range(plan.panels):
        out[p] = total[p]


def near_field(plan, extended, neighbours, near_blocks):
    return pl.pallas_call(
        functools.partial(near_kernel, plan),
        grid=(plan.cell_cols // LANES,),
        in_specs=[
            whole_spec(extended.shape),
            pl.BlockSpec((plan.near, plan.cell_planes, LANES), lambda i: (0, 0, i)),
            pl.BlockSpec(
                (plan.near, plan.panels, plan.panels, plan.cell_planes, LANES), lambda i: (0, 0, 0, 0, i)
            ),
        ],
        out_specs=pl.BlockSpec((plan.panels, plan.cell_planes, LANES), lambda i: (0, 0, i)),
        out_shape=jax.ShapeDtypeStruct((plan.panels, plan.cell_planes, plan.cell_cols), jnp.float32),
        compiler_params=pltpu.CompilerParams(vmem_limit_bytes=VMEM_LIMIT),
        cost_estimate=pl.CostEstimate(
            flops=2 * near_blocks.size, bytes_accessed=4 * near_blocks.size, transcendentals=0
        ),
        name="near_blocks",
    )(extended, neighbours, near_blocks)


def ring_pairs(axis):
    count = lax.axis_size(axis)
    up = [(i, (i + 1) % count) for i in range(count)]
    return (up, [(j, i) for i, j in up])


def extend_rows(plan, masked):
    up, down = ring_pairs("cell")
    left = lax.ppermute(masked[:, :, -NZC:], "cell", up)
    right = lax.ppermute(masked[:, :, :NZC], "cell", down)
    return (left, right)


def extend_planes(plan, masked, left, right):
    rest = jnp.zeros((plan.panels, plan.cell_planes, LANES - NZC), jnp.float32)
    wide = jnp.concatenate([rest, left, masked, right, rest], axis=2)
    up, down = ring_pairs("slab")
    before = lax.ppermute(wide[:, -1:], "slab", up)
    after = lax.ppermute(wide[:, :1], "slab", down)
    whole = jnp.concatenate([before, wide, after], axis=1)
    planes = plan.cell_planes
    return jnp.stack([whole[:, i : i + planes] for i in range(3)], axis=1)


def pick_kernel(plan, ids_ref, by_depth, *refs):
    outs, sems = (refs[:-1], refs[-1])
    cell, slab = (ids_ref[0], ids_ref[1])
    half_id, place = (slab // plan.half, lax.rem(slab, plan.half))
    copies = []
    for j in range(plan.outer):
        group = lax.rem(place // plan.inner + j, plan.outer)
        base = cell * plan.slabs + half_id * plan.half + group * plan.inner
        for q in range(plan.inner):
            freq = base + q
            mirror = jnp.where(freq == 0, plan.nz // 2, plan.nz - freq)
            for m, index in enumerate((freq, mirror)):
                n = (j * plan.inner + q) * 2 + m
                out = outs[2 * j + m]
                copies.append(pltpu.make_async_copy(by_depth.at[index], out.at[q], sems.at[n]))
    for copy in copies:
        copy.start()
    for copy in copies:
        copy.wait()


def pick_planes(plan, ids, spectrum):
    by_depth = jnp.transpose(spectrum, (1, 2, 0))
    shape = (plan.inner,) + by_depth.shape[1:]
    count = 2 * plan.outer
    return pl.pallas_call(
        functools.partial(pick_kernel, plan),
        in_specs=[pl.BlockSpec(memory_space=pltpu.SMEM), pl.BlockSpec(memory_space=pl.ANY)],
        out_specs=[pl.BlockSpec(memory_space=pltpu.VMEM)] * count,
        out_shape=[jax.ShapeDtypeStruct(shape, jnp.float32)] * count,
        scratch_shapes=[pltpu.SemaphoreType.DMA((2 * plan.half,))],
        cost_estimate=pl.CostEstimate(
            flops=0, bytes_accessed=8 * count * math.prod(shape), transcendentals=0
        ),
        name="pick_planes",
    )(ids, by_depth)


def outer_shift(plan, value, j):
    if j == 0:
        return value
    pairs = []
    for source in range(plan.slabs):
        base = source // plan.half * plan.half
        pairs.append((source, base + (source - base + j * plan.inner) % plan.half))
    return lax.ppermute(value, "slab", pairs)


def edge_weights(plan, rows):
    slab, cell = (lax.axis_index("slab"), lax.axis_index("cell"))
    middle = plan.nz // 2
    turned = jnp.concatenate([rows[middle : middle + 1], jnp.flip(rows, 0)], axis=0)
    other = cell * plan.slabs + (1 - slab // plan.half) * plan.half
    total = 0.0
    for j in range(plan.outer):
        sent = lax.dynamic_slice_in_dim(turned, other + j * plan.inner, plan.inner, 0)
        sent = jnp.concatenate([sent, rows[:1]], axis=0)
        pairs = [(plan.half, j * plan.inner), (0, plan.half + j * plan.inner)]
        total = total + lax.ppermute(sent, "slab", pairs)
    return (total, rows[middle : middle + 1])


def second_weights(plan, blocks, turned):
    slab = lax.axis_index("slab")
    part = lax.rem(slab, plan.half) // plan.inner
    strips = []
    for i in range(plan.inner):
        place = lax.rem(slab + i, plan.inner)
        rows = [lax.dynamic_slice_in_dim(block, place, 1, 0) for pair in blocks for block in pair]
        strip = jnp.stack(rows).reshape((plan.outer, 2) + blocks[0][0].shape[1:])
        ids = [lax.broadcasted_iota(jnp.int32, strip.shape, n) for n in range(3)]
        change = (ids[0] == part) & (ids[1] == 1) & (ids[2] == 0) & (slab % plan.inner == 0)
        strip = jnp.where(change, lax.dynamic_slice_in_dim(turned, place, 1, 0), strip)
        if i > 0:
            pairs = []
            for source in range(plan.slabs):
                group = source // plan.inner * plan.inner
                pairs.append((source, group + (source + i) % plan.inner))
            strip = lax.ppermute(strip, "slab", pairs)
        strips.append(strip)
    return strips


def per_device(charges, counts, projection, near_blocks, neighbours, spectrum):
    panels, cell_planes, cell_cols = charges.shape
    cells, slabs = (lax.axis_size("cell"), lax.axis_size("slab"))
    nx, nz, local = spectrum.shape
    plan = Plan(slabs, cells, panels, cell_planes, cell_cols, neighbours.shape[0], nx, nz, local * slabs)
    if not plan.fits():
        return plain_device(charges, counts, projection, near_blocks, neighbours, spectrum)
    me = (lax.axis_index("cell") * slabs + lax.axis_index("slab")).astype(jnp.int32).reshape(1)
    forward_table, backward_table = plan.depth_tables()
    depth_forward, depth_backward = (halves(forward_table.T), halves(backward_table))
    y_rows, x_cols, low_ids = (plan.y_rows().reshape(-1), plan.x_columns(), np.arange(plan.ny // 2))
    cos_y, sin_y = wave(low_ids, y_rows, plan.ny)
    sin_y[0] = 1.0 - 2.0 * (y_rows % 2)
    y_forward = halves(np.concatenate([cos_y, sin_y], axis=0))
    y_backward = halves(np.concatenate([cos_y.T, -sin_y.T], axis=1))
    x_waves = [wave(cols, low_ids, plan.nx) for cols in x_cols]
    x_forward = halves(np.stack([np.concatenate(pair, axis=1) for pair in x_waves]))
    x_backward = halves(np.stack([np.concatenate([t.T for t in pair], axis=1) for pair in x_waves]))
    split_projection = projection.reshape(
        (panels, TX // CHUNKS, CHUNKS, TY * TZ, cell_planes, cell_cols)
    )
    axes = ("cell", "slab")

    def exchange(pieces):
        return lax.all_to_all(pieces, axes, split_axis=0, concat_axis=0, tiled=True)

    def values(*shapes):
        return [pltpu.VMEM(shape, jnp.float32) for shape in shapes]

    rows_shape = (plan.ny, 2 * plan.x_chunk)
    freq_shape = (2 * plan.ny, plan.x_chunk)
    both_shape = (2 * plan.ny, plan.nx)
    ids = jnp.stack([lax.axis_index("cell"), lax.axis_index("slab")]).astype(jnp.int32)
    slot = lax.broadcasted_iota(jnp.int32, charges.shape, 0)
    masked = jnp.where(slot < counts[None], charges, 0.0)
    rows = jnp.transpose(spectrum[:, :, 0], (1, 0))
    pieces = [project(plan, i, charges, counts, split_projection, *depth_forward) for i in range(CHUNKS)]
    pieces[0], ids = lax.optimization_barrier((pieces[0], ids))
    even_pieces = exchange(pieces[0])
    picked = pick_planes(plan, ids, spectrum)
    masked, rows, *picked = lax.optimization_barrier((masked, rows, *picked))
    plain = [outer_shift(plan, picked[2 * j], j) for j in range(plan.outer)]
    mirror = [outer_shift(plan, picked[2 * j + 1], j) for j in range(plan.outer)]
    turned, own_row = edge_weights(plan, rows)
    left, right = extend_rows(plan, masked)
    pieces[1], left, right, turned, *moved = lax.optimization_barrier(
        (pieces[1], left, right, turned, *plain, *mirror)
    )
    plain, mirror = (moved[: plan.outer], moved[plan.outer :])
    odd_pieces = exchange(pieces[1])
    strips = second_weights(plan, list(zip(plain, mirror)), turned)
    edge = jnp.concatenate([turned[plan.inner :], own_row], axis=0)
    (even,) = plane_call(
        plan, first_plane_kernel, "even_planes", me, [even_pieces], [(y_forward, None), (x_forward, 0)], [],
        [both_shape], values(rows_shape, freq_shape), 2,
    )
    late = [odd_pieces, *y_forward, x_forward[0][1:], x_forward[1][1:], even]
    late += [x_backward[0][:1], x_backward[1][:1], *y_backward]
    copies = [pltpu.VMEM(array.shape, array.dtype) for array in late]
    copies.append(pltpu.SemaphoreType.DMA((len(late) + plan.half + 1,)))
    back, rest = plane_call(
        plan, middle_plane_kernel, "middle_planes", me, [edge],
        [], late + strips, [piece_shape(plan), freq_shape],
        values(rows_shape, freq_shape, freq_shape, freq_shape, (2, plan.ny // 2, plan.nx)) + copies, 4,
    )
    even_back = exchange(back)
    (back,) = plane_call(
        plan, last_plane_kernel, "odd_planes", me, [rest], [(x_backward, 1), (y_backward, None)], [],
        [piece_shape(plan)], values(rows_shape), 2,
    )
    extended = extend_planes(plan, masked, left, right)
    back, extended = lax.optimization_barrier((back, extended))
    odd_back = exchange(back)
    total = near_field(plan, extended, neighbours, near_blocks)
    total = gather(plan, 0, counts, total, split_projection, *depth_backward, even_back)
    held = hold_projection(plan, 1, split_projection, total)
    return gather(plan, 1, counts, total, held, *depth_backward, odd_back)


def padded(value, sides, width):
    for axis, dim in sides:
        count, length = (lax.axis_size(axis), value.shape[dim])
        up = [(i, (i + 1) % count) for i in range(count)]
        down = [(j, i) for i, j in up]
        last = lax.slice_in_dim(value, length - width, length, axis=dim)
        first = lax.slice_in_dim(value, 0, width, axis=dim)
        before = lax.ppermute(last, axis, up)
        after = lax.ppermute(first, axis, down)
        value = jnp.concatenate([before, value, after], axis=dim)
    return value


def wave_tables(row_count, col_count, length):
    products = (
        lax.broadcasted_iota(jnp.int32, (row_count, col_count), 0)
        * lax.broadcasted_iota(jnp.int32, (row_count, col_count), 1)
        % length
    )
    angle_rad = products.astype(jnp.float32) * (2.0 * math.pi / length)
    return (jnp.cos(angle_rad), jnp.sin(angle_rad))


def depth_rows(nz, freq_ids, valid, weights):
    depth_ids = lax.broadcasted_iota(jnp.int32, (freq_ids.shape[0], nz), 1)
    products = freq_ids[:, None] * depth_ids % nz
    angle_rad = products.astype(jnp.float32) * (2.0 * math.pi / nz)
    basis = jnp.stack([jnp.cos(angle_rad), -jnp.sin(angle_rad)])
    return (basis * valid[None, :, None], basis * weights[None, :, None])


def half_depth_tables(nz, cell_count):
    lower = nz // (2 * cell_count)
    row_ids = lax.broadcasted_iota(jnp.int32, (cell_count * (lower + 1),), 0)
    block_ids = row_ids // (lower + 1)
    slot_ids = row_ids % (lower + 1)
    freq_ids = jnp.where(slot_ids < lower, block_ids * lower + slot_ids, nz // 2)
    valid = jnp.where((slot_ids < lower) | (block_ids == 0), 1.0, 0.0).astype(jnp.float32)
    doubled = jnp.where((slot_ids < lower) & (freq_ids > 0), 2.0, 1.0).astype(jnp.float32)
    forward_table, backward_table = depth_rows(nz, freq_ids, valid, valid * doubled)
    return (forward_table, backward_table, freq_ids)


def combine_halves(first_part, second, orient):
    half_width = first_part.shape[-1] // 2
    real_part = first_part[..., :half_width] + orient * second[..., half_width:]
    imag_part = first_part[..., half_width:] - orient * second[..., :half_width]
    return jnp.concatenate([real_part, imag_part], axis=-1)


def transform_axis(pattern, cosine, sine_tab, values, orient):
    first_part = jnp.einsum(pattern, cosine, values, precision=lax.Precision.HIGHEST)
    second = jnp.einsum(pattern, sine_tab, values, precision=lax.Precision.HIGHEST)
    return combine_halves(first_part, second, orient)


def twiddle(values, twist_cos, twist_sin, orient):
    half_width = values.shape[-1] // 2
    real_part = values[..., :half_width]
    imag_part = values[..., half_width:]
    new_real = real_part * twist_cos + orient * imag_part * twist_sin
    new_imag = imag_part * twist_cos - orient * real_part * twist_sin
    return jnp.concatenate([new_real, new_imag], axis=-1)


def transform_rows(planes_block, cosine, sine_tab, orient):
    flat_rows = planes_block.reshape(-1, planes_block.shape[-1])
    first_part = jnp.dot(flat_rows, cosine, precision=lax.Precision.HIGHEST).reshape(
        planes_block.shape
    )
    second = jnp.dot(flat_rows, sine_tab, precision=lax.Precision.HIGHEST).reshape(
        planes_block.shape
    )
    real_part = first_part[:, 0] + orient * second[:, 1]
    imag_part = first_part[:, 1] - orient * second[:, 0]
    return jnp.stack([real_part, imag_part], axis=1)


def plain_device(charges, counts, projection, near_blocks, neighbours, spectrum):
    panels, cell_planes, cell_cols = charges.shape
    nx, nz, ny = (spectrum.shape[0], spectrum.shape[1], spectrum.shape[2] * lax.axis_size("slab"))
    planes = cell_planes * TX
    rows_cell = cell_cols // NZC
    slot_ids = lax.broadcasted_iota(jnp.int32, charges.shape, 0)
    panel_mask = (slot_ids < counts[None]).astype(jnp.float32)
    masked = charges * panel_mask
    tile_values = jnp.einsum("ptxc,pxc->txc", projection, masked, precision=lax.Precision.HIGHEST)
    grid_field = (
        tile_values.reshape(TX, TY, TZ, cell_planes, rows_cell, NZC)
        .transpose(3, 0, 5, 2, 4, 1)
        .reshape(planes, nz, rows_cell * TY)
    )
    cell_count = lax.axis_size("cell")
    forward_table, backward_table, freq_ids = half_depth_tables(nz, cell_count)
    depth_count = forward_table.shape[1] // cell_count
    spectra_z = jnp.einsum(
        "wkz,xzy->xwky", forward_table, grid_field, precision=lax.Precision.HIGHEST
    )
    cosine_y, sine_y = wave_tables(ny, ny, ny)
    pencils = transform_rows(
        lax.all_to_all(spectra_z, "cell", split_axis=2, concat_axis=3, tiled=True),
        cosine_y,
        sine_y,
        1.0,
    )
    columns = lax.all_to_all(pencils, "slab", split_axis=3, concat_axis=0, tiled=True)
    col_width = columns.shape[2] * columns.shape[3]
    flat_rows = columns.reshape(nx, 2 * col_width)
    first_row = lax.axis_index("cell") * depth_count
    kernel_ids = lax.dynamic_slice_in_dim(freq_ids, first_row, depth_count, 0)
    kernel = jnp.take(spectrum, kernel_ids, axis=1).reshape(nx, col_width) * (1.0 / (nx * ny * nz))
    kernel_both = jnp.concatenate([kernel, kernel], axis=1)
    slab_count = lax.axis_size("slab")
    local_rows = nx // slab_count
    cosine_s, sine_s = wave_tables(slab_count, slab_count, slab_count)
    cosine_r, sine_r = wave_tables(local_rows, local_rows, local_rows)
    twist_cos, twist_sin = wave_tables(slab_count, local_rows, nx)
    twist_cos = twist_cos[:, :, None]
    twist_sin = twist_sin[:, :, None]
    section_one = transform_axis(
        "ks,src->krc",
        cosine_s,
        sine_s,
        flat_rows.reshape(slab_count, local_rows, 2 * col_width),
        1.0,
    )
    section_one = twiddle(section_one, twist_cos, twist_sin, 1.0)
    section_two = transform_axis("jr,krc->jkc", cosine_r, sine_r, section_one, 1.0)
    weighted = section_two.reshape(nx, 2 * col_width) * kernel_both
    section_one = transform_axis(
        "rj,jkc->krc",
        cosine_r,
        sine_r,
        weighted.reshape(local_rows, slab_count, 2 * col_width),
        -1.0,
    )
    section_one = twiddle(section_one, twist_cos, twist_sin, -1.0)
    section_two = transform_axis("sk,krc->src", cosine_s, sine_s, section_one, -1.0)
    returned_x = section_two.reshape(nx, 2 * col_width)
    returned = lax.all_to_all(
        returned_x.reshape(columns.shape), "slab", split_axis=0, concat_axis=3, tiled=True
    )
    inverse_rows = transform_rows(returned, cosine_y, sine_y, -1.0)
    grid_potential = jnp.einsum(
        "wkz,xwky->xzy",
        backward_table,
        lax.all_to_all(inverse_rows, "cell", split_axis=3, concat_axis=2, tiled=True),
        precision=lax.Precision.HIGHEST,
    )
    tile_potential = (
        grid_potential.reshape(cell_planes, TX, NZC, TZ, rows_cell, TY)
        .transpose(1, 5, 3, 0, 4, 2)
        .reshape(TX * TY * TZ, cell_planes, cell_cols)
    )
    far_field = jnp.einsum(
        "ptxc,txc->pxc", projection, tile_potential, precision=lax.Precision.HIGHEST
    )
    block = masked.reshape(panels, cell_planes, rows_cell, NZC)
    extended = padded(block, (("slab", 1), ("cell", 2)), 1)
    flat_ext = extended.reshape(panels, -1)
    step_x = neighbours // 9 - 1
    step_y = neighbours // 3 % 3 - 1
    step_z = neighbours % 3 - 1
    plane_ids = lax.broadcasted_iota(jnp.int32, neighbours.shape, 1)
    col_ids = lax.broadcasted_iota(jnp.int32, neighbours.shape, 2)
    row_ids = col_ids // NZC
    depth_ids = col_ids % NZC
    near_ids = ((plane_ids + step_x + 1) * (rows_cell + 2) + row_ids + step_y + 1) * NZC + (
        depth_ids + step_z
    ) % NZC
    near_count = neighbours.shape[0]
    picked = jnp.take(flat_ext, near_ids.reshape(-1), axis=1).reshape(
        panels, near_count, cell_planes, cell_cols
    )
    near_field = jnp.einsum("kpqxc,qkxc->pxc", near_blocks, picked, precision=lax.Precision.HIGHEST)
    return (far_field + near_field) * panel_mask


def solution(mesh):
    in_specs = (
        P(None, "slab", "cell"),
        P("slab", "cell"),
        P(None, None, "slab", "cell"),
        P(None, None, None, "slab", "cell"),
        P(None, "slab", "cell"),
        P(None, None, "slab"),
    )
    out_specs = P(None, "slab", "cell")
    return jax.shard_map(
        per_device, mesh=mesh, in_specs=in_specs, out_specs=out_specs, check_vma=False
    )
```

```python
import functools
import math

import jax
import jax.numpy as jnp
import ml_dtypes
import numpy as np
from jax import lax
from jax.experimental import pallas as pl
from jax.experimental.pallas import tpu as pltpu
from jax.sharding import PartitionSpec as P

TX = 4
TY = 4
TZ = 4
NZC = 16
LANES = 128
CHUNKS = 2
VMEM_LIMIT = 60 * 1024 * 1024


def halves(table):
    high = table.astype(np.float32).astype(ml_dtypes.bfloat16)
    low = (table - high.astype(np.float64)).astype(np.float32).astype(ml_dtypes.bfloat16)
    return (high, low)


def wave(rows, cols, length):
    angle = (rows[:, None] * cols[None, :] % length) * (2.0 * math.pi / length)
    return (np.cos(angle), np.sin(angle))


class Plan:
    def __init__(self, slabs, cells, panels, cell_planes, cell_cols, near, nx, nz, ny):
        self.slabs, self.cells = (slabs, cells)
        self.panels, self.cell_planes, self.cell_cols, self.near = (panels, cell_planes, cell_cols, near)
        self.nx, self.ny, self.nz = (nx, ny, nz)
        self.slots = slabs * cells
        self.tx_chunk = TX // CHUNKS
        self.width = cell_planes * self.tx_chunk
        self.y_lanes = LANES // self.width if self.width else 1
        self.row_block = LANES // NZC
        self.step_blocks = self.y_lanes // TY
        self.steps = cell_cols // (LANES * self.step_blocks) if self.step_blocks else 0
        self.x_chunk = nx // CHUNKS
        self.ky_local = ny // slabs
        self.half = slabs // 2
        self.outer = math.gcd(self.half, 2)
        self.inner = self.half // self.outer

    def fits(self):
        return (
            self.slots * 2 == self.nz
            and self.cell_planes == 8
            and self.step_blocks * TY * self.width == LANES
            and self.slabs % self.y_lanes == 0
            and self.ky_local % 8 == 0
            and self.steps * self.step_blocks * LANES == self.cell_cols
            and self.x_chunk % LANES == 0
            and self.ny % 1024 == self.nx % 1024 == 512
        )

    def depth_tables(self):
        depth = np.arange(NZC)[None, :] * TZ + np.arange(TZ)[:, None]
        scale = 1.0 / (self.nx * self.ny * self.nz)
        forward = np.zeros((self.slots, 2, self.row_block, TZ, self.row_block, NZC))
        backward = np.zeros_like(forward)
        for freq in range(self.slots):
            angle = (freq * depth % self.nz) * (2.0 * math.pi / self.nz)
            real, imag = (np.cos(angle), -np.sin(angle))
            factor = 2.0 * scale
            if freq == 0:
                imag = np.cos(depth * math.pi)
                factor = scale
            for row in range(self.row_block):
                forward[freq, 0, row, :, row, :] = real
                forward[freq, 1, row, :, row, :] = imag
                backward[freq, 0, row, :, row, :] = factor * real
                backward[freq, 1, row, :, row, :] = factor * imag
        shape = (self.slots * 2 * self.row_block, TZ * LANES)
        return (forward.reshape(shape), backward.reshape(shape))

    def y_rows(self):
        parity, cell, step, block, tile, row = np.meshgrid(
            *[np.arange(n) for n in (2, self.cells, self.steps, self.step_blocks, TY // 2, self.row_block)],
            indexing="ij",
        )
        cell_row = ((cell * self.steps + step) * self.step_blocks + block) * self.row_block + row
        return (cell_row * TY + 2 * tile + parity).reshape(2, -1)

    def x_columns(self):
        parity, slab, tile, plane = np.meshgrid(
            *[np.arange(n) for n in (2, self.slabs, TX // 2, self.cell_planes)], indexing="ij"
        )
        return ((slab * self.cell_planes + plane) * TX + 2 * tile + parity).reshape(2, -1)

    def row_of(self, cell, step, place):
        block, tile = (place // TY, place % TY)
        inner = (cell * self.steps + step) * self.step_blocks + block
        return (tile % 2) * (self.ny // 2) + (inner * (TY // 2) + tile // 2) * self.row_block


def split(value):
    high = value.astype(jnp.bfloat16)
    low = (value - high.astype(jnp.float32)).astype(jnp.bfloat16)
    return (high, low)


def product(left, right, dims=((1,), (0,))):
    first = jnp.concatenate([left[0], left[0], left[1]], axis=dims[0][0])
    second = jnp.concatenate([right[0], right[1], right[0]], axis=dims[1][0])
    return lax.dot_general(first, second, (dims, ((), ())), preferred_element_type=jnp.float32)


def swap_groups(parts, width):
    count = len(parts)
    lane = lax.broadcasted_iota(jnp.int32, parts[0].shape, 1)
    parts = list(parts)
    step = count // 2
    while step >= 1:
        shift = step * width
        upper = (lane // shift) % 2 == 1
        for i in range(count):
            if i & step:
                continue
            first, second = (parts[i], parts[i + step])
            parts[i] = jnp.where(upper, pltpu.roll(second, shift, 1), first)
            parts[i + step] = jnp.where(upper, second, pltpu.roll(first, LANES - shift, 1))
        step //= 2
    return parts


def tile_copies(plan, chunk, projection, held, sems):
    return [
        pltpu.make_async_copy(projection.at[:, tx, chunk], held.at[tx], sems.at[tx])
        for tx in range(plan.tx_chunk)
    ]


def project_kernel(plan, chunk, charges_in, counts_in, high_in, low_in, projection, out, scratch, held, sems,
                   charges, counts, high, low):
    planes = plan.cell_planes
    first = plan.tx_chunk
    pairs = ((charges_in, charges), (counts_in, counts), (high_in, high), (low_in, low))
    loads = [pltpu.make_async_copy(*pair, sems.at[first + n]) for n, pair in enumerate(pairs)]
    copies = tile_copies(plan, chunk, projection, held, sems)
    for copy in loads[:2] + copies + loads[2:]:
        copy.start()
    for copy in loads[:2]:
        copy.wait()
    for tx, copy in enumerate(copies):
        copy.wait()

        def body(place, carry, tx=tx):
            lanes = pl.ds(pl.multiple_of(place * LANES, LANES), LANES)
            count = counts[:, lanes]
            own = [jnp.where(count > p, charges[p, :, lanes], 0.0) for p in range(plan.panels)]
            for ty in range(TY):
                row = ((place * TY + ty) * plan.tx_chunk + tx) * planes
                rows = pl.ds(pl.multiple_of(row, planes), planes)
                for tz in range(TZ):
                    t = ty * TZ + tz
                    total = held[tx, 0, t, :, lanes] * own[0]
                    for p in range(1, plan.panels):
                        total = total + held[tx, p, t, :, lanes] * own[p]
                    scratch[rows, tz * LANES : (tz + 1) * LANES] = total
            return carry

        lax.fori_loop(0, plan.steps * plan.step_blocks, body, 0)
    for copy in loads[2:]:
        copy.wait()
    spectra = product(split(scratch[...]), (high[...], low[...])).T
    shape = (plan.slots, 2, plan.row_block, LANES)
    for step in range(plan.steps):
        out[:, :, step] = spectra[:, step * LANES : (step + 1) * LANES].reshape(shape)


def held_shape(plan):
    cols = plan.steps * plan.step_blocks * LANES
    return (plan.tx_chunk, plan.panels, TY * TZ, plan.cell_planes, cols)


def piece_shape(plan):
    return (plan.slots, 2, plan.steps, plan.row_block, LANES)


def whole_spec(shape):
    return pl.BlockSpec(shape, lambda i: (0,) * len(shape))


def projection_call(plan, kernel, name, ready, arrays, projection, out_shape):
    return pl.pallas_call(
        kernel,
        in_specs=[pl.BlockSpec(memory_space=pltpu.VMEM)] * len(ready)
        + [pl.BlockSpec(memory_space=pl.ANY)] * (len(arrays) + 1),
        out_specs=pl.BlockSpec(memory_space=pltpu.VMEM),
        out_shape=jax.ShapeDtypeStruct(out_shape, jnp.float32),
        scratch_shapes=[
            pltpu.VMEM((plan.steps * LANES, TZ * LANES), jnp.float32),
            pltpu.VMEM(held_shape(plan), jnp.float32),
            pltpu.SemaphoreType.DMA((plan.tx_chunk + len(arrays),)),
        ]
        + [pltpu.VMEM(array.shape, array.dtype) for array in arrays],
        compiler_params=pltpu.CompilerParams(vmem_limit_bytes=VMEM_LIMIT),
        cost_estimate=pl.CostEstimate(
            flops=2 * math.prod(held_shape(plan)),
            bytes_accessed=4 * math.prod(held_shape(plan)),
            transcendentals=0,
        ),
        name=name,
    )(*ready, *arrays, projection)


def project(plan, chunk, charges, counts, projection, high, low):
    kernel = functools.partial(project_kernel, plan, chunk)
    arrays = [charges, counts, high, low]
    return projection_call(plan, kernel, "project_depth", [], arrays, projection, piece_shape(plan))


def far_sign(plan, me_ref):
    slab = lax.rem(me_ref[0], plan.slabs)
    return jnp.where(slab >= plan.half, -1.0, 1.0)


def forward_plane(plan, me_ref, pieces, y_table, x_table, rows_ref, freq_ref, waits=()):
    special = me_ref[0] == 0
    sign = far_sign(plan, me_ref)
    rows = 2 * plan.steps * plan.row_block
    width = plan.x_chunk
    middle = plan.ny // 2
    for cell in range(plan.cells):
        for group in range(plan.slabs // plan.y_lanes):
            first = cell * plan.slabs + group * plan.y_lanes
            parts = [pieces[first + i].reshape(rows, LANES) for i in range(plan.y_lanes)]
            parts = swap_groups(parts, plan.width)
            for place, value in enumerate(parts):
                if place % 2 == 1:
                    value = value * sign
                for part in range(2):
                    for step in range(plan.steps):
                        source = (part * plan.steps + step) * plan.row_block
                        row = plan.row_of(cell, step, place)
                        col = part * width + group * LANES
                        rows_ref[row : row + plan.row_block, col : col + LANES] = value[
                            source : source + plan.row_block
                        ]
    for copy in waits:
        copy.wait()
    sums = product((y_table[0][...], y_table[1][...]), split(rows_ref[...]))
    cos_re, cos_im = (sums[:middle, :width], sums[:middle, width:])
    sin_re, sin_im = (sums[middle:, :width], sums[middle:, width:])
    first = lax.broadcasted_iota(jnp.int32, (middle, width), 0) == 0

    @pl.when(jnp.logical_not(special))
    def _():
        freq_ref[:middle] = jnp.where(first, cos_re, cos_re + sin_im)
        freq_ref[middle : 2 * middle] = jnp.where(first, cos_im, cos_im - sin_re)
        freq_ref[2 * middle : 3 * middle] = jnp.where(first, sin_re, cos_re - sin_im)
        freq_ref[3 * middle :] = jnp.where(first, sin_im, cos_im + sin_re)

    @pl.when(special)
    def _():
        freq_ref[:middle] = cos_re
        freq_ref[middle : 2 * middle] = jnp.where(first, sin_re, -sin_re)
        freq_ref[2 * middle : 3 * middle] = cos_im
        freq_ref[3 * middle :] = sin_im

    return product(split(freq_ref[...]), (x_table[0][0], x_table[1][0]))


def backward_plane(plan, me_ref, freqs, x_table, y_table, out, rows_ref):
    special = me_ref[0] == 0
    sign = far_sign(plan, me_ref)
    width = plan.x_chunk
    middle = plan.ny // 2
    sums = product(split(freqs), (x_table[0][0], x_table[1][0]))
    parts = []
    for mirrored, turn in ((0, 1.0), (1, -1.0)):
        re = slice(2 * mirrored * middle, (2 * mirrored + 1) * middle)
        im = slice((2 * mirrored + 1) * middle, (2 * mirrored + 2) * middle)
        parts.append(sums[re, :width] - turn * sums[im, width:])
        parts.append(sums[im, :width] + turn * sums[re, width:])
    re_n, im_n, re_m, im_m = parts
    first = lax.broadcasted_iota(jnp.int32, (middle, width), 0) == 0

    @pl.when(jnp.logical_not(special))
    def _():
        rows_ref[:middle, :width] = jnp.where(first, re_n, re_n + re_m)
        rows_ref[:middle, width:] = jnp.where(first, im_n, im_n + im_m)
        rows_ref[middle:, :width] = jnp.where(first, -re_m, im_n - im_m)
        rows_ref[middle:, width:] = jnp.where(first, -im_m, re_m - re_n)

    @pl.when(special)
    def _():
        rows_ref[:middle, :width] = jnp.where(first, re_n, 2.0 * re_n)
        rows_ref[:middle, width:] = jnp.where(first, re_m, 2.0 * re_m)
        rows_ref[middle:, :width] = jnp.where(first, -im_n, 2.0 * im_n)
        rows_ref[middle:, width:] = jnp.where(first, -im_m, -2.0 * im_m)

    rows_ref[...] = product((y_table[0][...], y_table[1][...]), split(rows_ref[...]))
    for cell in range(plan.cells):
        for group in range(plan.slabs // plan.y_lanes):
            parts = []
            for place in range(plan.y_lanes):
                tiles = []
                for part in range(2):
                    for step in range(plan.steps):
                        row = plan.row_of(cell, step, place)
                        col = part * width + group * LANES
                        tiles.append(rows_ref[row : row + plan.row_block, col : col + LANES])
                value = jnp.concatenate(tiles, axis=0)
                parts.append(value * sign if place % 2 == 1 else value)
            parts = swap_groups(parts, plan.width)
            first = cell * plan.slabs + group * plan.y_lanes
            for i in range(plan.y_lanes):
                out[first + i] = parts[i].reshape(2, plan.steps, plan.row_block, LANES)


def first_plane_kernel(plan, me_ref, pieces, y_high, y_low, x_high, x_low, out, rows_ref, freq_ref):
    out[...] = forward_plane(plan, me_ref, pieces, (y_high, y_low), (x_high, x_low), rows_ref, freq_ref)


def middle_plane_kernel(plan, me_ref, pieces, edge, *refs):
    late, refs = (refs[:9], refs[9:])
    strips, refs = (refs[: plan.inner], refs[plan.inner :])
    out, rest, rows_ref, freq_ref, sum_ref, rest_ref, weights = refs[:7]
    yf_high, yf_low, xf_high, xf_low, even, xb_high, xb_low, yb_high, yb_low, sems = refs[7:]
    slab = lax.rem(me_ref[0], plan.slabs)
    place = lax.rem(slab, plan.half)
    outer_id, inner_id = (place // plan.inner, lax.rem(place, plan.inner))
    held = (yf_high, yf_low, xf_high, xf_low, even, xb_high, xb_low, yb_high, yb_low)
    copies = [pltpu.make_async_copy(late[n], held[n], sems.at[n]) for n in range(5)]
    for i in range(plan.inner):
        for j in range(plan.outer):
            owner = lax.rem(outer_id - j + plan.outer, plan.outer) * plan.inner
            owner = owner + lax.rem(inner_id - i + plan.inner, plan.inner)
            rows = pl.ds(pl.multiple_of(owner * plan.ky_local, plan.ky_local), plan.ky_local)
            copies.append(
                pltpu.make_async_copy(
                    strips[i].at[j], weights.at[:, rows], sems.at[len(held) + i * plan.outer + j]
                )
            )
    early = len(copies)
    for n in range(5, len(held)):
        copies.append(pltpu.make_async_copy(late[n], held[n], sems.at[n]))
    for copy in copies:
        copy.start()
    special = me_ref[0] == 0
    width = plan.x_chunk
    middle = plan.ny // 2
    x_table = (xf_high.at[pl.ds(0, 1)], xf_low.at[pl.ds(0, 1)])
    odd = forward_plane(
        plan, me_ref, pieces, (yf_high, yf_low), x_table, rows_ref, freq_ref, copies[:4]
    )
    for copy in copies[4:early]:
        copy.wait()
    row = lax.broadcasted_iota(jnp.int32, (middle, width), 0)
    at_first = row == 0
    for mirrored, turn in ((0, 1.0), (1, -1.0)):
        re = slice(2 * mirrored * middle, (2 * mirrored + 1) * middle)
        im = slice((2 * mirrored + 1) * middle, (2 * mirrored + 2) * middle)
        results = []
        for upper in range(2):
            cols = slice(upper * width, (upper + 1) * width)
            plane = weights[mirrored, :, cols]
            change = at_first & special
            if mirrored:
                weight = jnp.where(change, edge[1:2, cols], plane)
                second = plane
            else:
                weight = plane
                second = jnp.where(change, edge[0:1, cols], plane)
            re_sums = even[re] - odd[re] if upper else even[re] + odd[re]
            im_sums = even[im] - odd[im] if upper else even[im] + odd[im]
            real = weight * re_sums[:, :width] + (turn * second) * im_sums[:, width:]
            imag = second * im_sums[:, :width] - (turn * weight) * re_sums[:, width:]
            results.append((real, imag))
        for part, rows in enumerate((re, im)):
            below, above = (results[0][part], results[1][part])
            sum_ref[rows] = below + above
            rest_ref[rows] = below - above
    last = pltpu.make_async_copy(rest_ref, rest, sems.at[len(held) + plan.half])
    last.start()
    for copy in copies[early:]:
        copy.wait()
    backward_plane(plan, me_ref, sum_ref[...], (xb_high, xb_low), (yb_high, yb_low), out, rows_ref)
    last.wait()


def last_plane_kernel(plan, me_ref, freqs, x_high, x_low, y_high, y_low, out, rows_ref):
    backward_plane(plan, me_ref, freqs[...], (x_high, x_low), (y_high, y_low), out, rows_ref)


def plane_call(plan, kernel, name, me, ready, arrays, tables, late, out_shapes, scratch, work):
    specs = [pl.BlockSpec(memory_space=pltpu.VMEM)] * len(ready)
    specs += [whole_spec(array.shape) for array in arrays]
    flat = []
    for pair, chunk in tables:
        for table in pair:
            if chunk is None:
                specs.append(whole_spec(table.shape))
            else:
                specs.append(pl.BlockSpec((1,) + table.shape[1:], lambda i, chunk=chunk: (chunk, 0, 0)))
            flat.append(table)
    specs += [pl.BlockSpec(memory_space=pl.ANY)] * len(late)
    size = sum(4 * array.size for array in list(ready) + list(arrays) + list(late)) + sum(2 * t.size for t in flat)
    return pl.pallas_call(
        functools.partial(kernel, plan),
        grid=(1,),
        in_specs=[pl.BlockSpec(memory_space=pltpu.SMEM)] + specs,
        out_specs=[whole_spec(out_shapes[0])] + [pl.BlockSpec(memory_space=pl.ANY)] * (len(out_shapes) - 1),
        out_shape=[jax.ShapeDtypeStruct(shape, jnp.float32) for shape in out_shapes],
        scratch_shapes=scratch,
        compiler_params=pltpu.CompilerParams(vmem_limit_bytes=VMEM_LIMIT),
        cost_estimate=pl.CostEstimate(
            flops=work * 12 * plan.nx * plan.ny * plan.x_chunk, bytes_accessed=size, transcendentals=0
        ),
        name=name,
    )(me, *ready, *arrays, *flat, *late)


def gather_kernel(
    plan, chunk, pieces, high_in, low_in, before_in, counts_in, projection, out, scratch, held, sems,
    high, low, before, counts
):
    planes = plan.cell_planes
    rows = plan.slots * 2 * plan.row_block
    first = plan.tx_chunk
    copies = tile_copies(plan, chunk, projection, held, sems)
    pairs = ((high_in, high), (low_in, low), (before_in, before), (counts_in, counts))
    loads = [pltpu.make_async_copy(*pair, sems.at[first + n]) for n, pair in enumerate(pairs)]
    for copy in loads[:2] + copies + loads[2:]:
        copy.start()
    for copy in loads[:2]:
        copy.wait()
    columns = [pieces[:, :, step].reshape(rows, LANES) for step in range(plan.steps)]
    scratch[...] = product(split(jnp.concatenate(columns, axis=1).T), (high[...], low[...]))
    for copy in loads[2:]:
        copy.wait()
    for tx in range(plan.tx_chunk):
        copies[tx].wait()
        last = chunk == CHUNKS - 1 and tx == plan.tx_chunk - 1

        def body(place, carry, tx=tx, last=last):
            lanes = pl.ds(pl.multiple_of(place * LANES, LANES), LANES)
            far = [(before if tx == 0 else out)[p, :, lanes] for p in range(plan.panels)]
            for ty in range(TY):
                row = ((place * TY + ty) * plan.tx_chunk + tx) * planes
                rows_at = pl.ds(pl.multiple_of(row, planes), planes)
                for tz in range(TZ):
                    t = ty * TZ + tz
                    potential = scratch[rows_at, tz * LANES : (tz + 1) * LANES]
                    for p in range(plan.panels):
                        far[p] = far[p] + held[tx, p, t, :, lanes] * potential
            for p in range(plan.panels):
                out[p, :, lanes] = jnp.where(counts[:, lanes] > p, far[p], 0.0) if last else far[p]
            return carry

        lax.fori_loop(0, plan.steps * plan.step_blocks, body, 0)


def gather(plan, chunk, counts, before, projection, high, low, pieces):
    kernel = functools.partial(gather_kernel, plan, chunk)
    arrays = [high, low, before, counts]
    return projection_call(plan, kernel, "depth_gather", [pieces], arrays, projection, before.shape)


def near_kernel(plan, extended, codes, blocks_ref, out):
    step = pl.program_id(0)
    lane = lax.broadcasted_iota(jnp.int32, (plan.cell_planes, LANES), 1)
    depth = lane % NZC
    digits = []
    for k in range(plan.near):
        code = codes[k]
        digits.append((code // 9, code // 3 % 3, code % 3))
    total = [None] * plan.panels
    for q in range(plan.panels):
        shifted = []
        for dx in range(3):
            before, here, after = (
                extended[q, dx, :, pl.ds(pl.multiple_of((step + i) * LANES, LANES), LANES)] for i in range(3)
            )
            up = jnp.where(lane < NZC, pltpu.roll(before, NZC, 1), pltpu.roll(here, NZC, 1))
            down = jnp.where(
                lane >= LANES - NZC, pltpu.roll(after, LANES - NZC, 1), pltpu.roll(here, LANES - NZC, 1)
            )
            for value in (up, here, down):
                under = jnp.where(
                    depth == 0, pltpu.roll(value, LANES - NZC + 1, 1), pltpu.roll(value, 1, 1)
                )
                over = jnp.where(
                    depth == NZC - 1, pltpu.roll(value, NZC - 1, 1), pltpu.roll(value, LANES - 1, 1)
                )
                shifted.append((under, value, over))
        for k in range(plan.near):
            digit_x, digit_y, digit_z = digits[k]

            def choose(digit, options):
                return jnp.where(digit == 0, options[0], jnp.where(digit == 1, options[1], options[2]))

            by_z = [choose(digit_z, options) for options in shifted]
            by_y = [choose(digit_y, by_z[3 * i : 3 * i + 3]) for i in range(3)]
            picked = choose(digit_x, by_y)
            for p in range(plan.panels):
                term = blocks_ref[k, p, q] * picked
                total[p] = term if total[p] is None else total[p] + term
    for p in range(plan.panels):
        out[p] = total[p]


def near_field(plan, extended, neighbours, near_blocks):
    return pl.pallas_call(
        functools.partial(near_kernel, plan),
        grid=(plan.cell_cols // LANES,),
        in_specs=[
            whole_spec(extended.shape),
            pl.BlockSpec((plan.near, plan.cell_planes, LANES), lambda i: (0, 0, i)),
            pl.BlockSpec(
                (plan.near, plan.panels, plan.panels, plan.cell_planes, LANES), lambda i: (0, 0, 0, 0, i)
            ),
        ],
        out_specs=pl.BlockSpec((plan.panels, plan.cell_planes, LANES), lambda i: (0, 0, i)),
        out_shape=jax.ShapeDtypeStruct((plan.panels, plan.cell_planes, plan.cell_cols), jnp.float32),
        compiler_params=pltpu.CompilerParams(vmem_limit_bytes=VMEM_LIMIT),
        cost_estimate=pl.CostEstimate(
            flops=2 * near_blocks.size, bytes_accessed=4 * near_blocks.size, transcendentals=0
        ),
        name="near_blocks",
    )(extended, neighbours, near_blocks)


def ring_pairs(axis):
    count = lax.axis_size(axis)
    up = [(i, (i + 1) % count) for i in range(count)]
    return (up, [(j, i) for i, j in up])


def extend_rows(plan, masked):
    up, down = ring_pairs("cell")
    left = lax.ppermute(masked[:, :, -NZC:], "cell", up)
    right = lax.ppermute(masked[:, :, :NZC], "cell", down)
    return (left, right)


def extend_planes(plan, masked, left, right):
    rest = jnp.zeros((plan.panels, plan.cell_planes, LANES - NZC), jnp.float32)
    wide = jnp.concatenate([rest, left, masked, right, rest], axis=2)
    up, down = ring_pairs("slab")
    before = lax.ppermute(wide[:, -1:], "slab", up)
    after = lax.ppermute(wide[:, :1], "slab", down)
    whole = jnp.concatenate([before, wide, after], axis=1)
    planes = plan.cell_planes
    return jnp.stack([whole[:, i : i + planes] for i in range(3)], axis=1)


def pick_kernel(plan, ids_ref, by_depth, *refs):
    outs, sems = (refs[:-1], refs[-1])
    cell, slab = (ids_ref[0], ids_ref[1])
    half_id, place = (slab // plan.half, lax.rem(slab, plan.half))
    copies = []
    for j in range(plan.outer):
        group = lax.rem(place // plan.inner + j, plan.outer)
        base = cell * plan.slabs + half_id * plan.half + group * plan.inner
        for q in range(plan.inner):
            freq = base + q
            mirror = jnp.where(freq == 0, plan.nz // 2, plan.nz - freq)
            for m, index in enumerate((freq, mirror)):
                n = (j * plan.inner + q) * 2 + m
                out = outs[2 * j + m]
                copies.append(pltpu.make_async_copy(by_depth.at[index], out.at[q], sems.at[n]))
    for copy in copies:
        copy.start()
    for copy in copies:
        copy.wait()


def pick_planes(plan, ids, spectrum):
    by_depth = jnp.transpose(spectrum, (1, 2, 0))
    shape = (plan.inner,) + by_depth.shape[1:]
    count = 2 * plan.outer
    return pl.pallas_call(
        functools.partial(pick_kernel, plan),
        in_specs=[pl.BlockSpec(memory_space=pltpu.SMEM), pl.BlockSpec(memory_space=pl.ANY)],
        out_specs=[pl.BlockSpec(memory_space=pltpu.VMEM)] * count,
        out_shape=[jax.ShapeDtypeStruct(shape, jnp.float32)] * count,
        scratch_shapes=[pltpu.SemaphoreType.DMA((2 * plan.half,))],
        cost_estimate=pl.CostEstimate(
            flops=0, bytes_accessed=8 * count * math.prod(shape), transcendentals=0
        ),
        name="pick_planes",
    )(ids, by_depth)


def outer_shift(plan, value, j):
    if j == 0:
        return value
    pairs = []
    for source in range(plan.slabs):
        base = source // plan.half * plan.half
        pairs.append((source, base + (source - base + j * plan.inner) % plan.half))
    return lax.ppermute(value, "slab", pairs)


def edge_weights(plan, rows):
    slab, cell = (lax.axis_index("slab"), lax.axis_index("cell"))
    middle = plan.nz // 2
    turned = jnp.concatenate([rows[middle : middle + 1], jnp.flip(rows, 0)], axis=0)
    other = cell * plan.slabs + (1 - slab // plan.half) * plan.half
    total = 0.0
    for j in range(plan.outer):
        sent = lax.dynamic_slice_in_dim(turned, other + j * plan.inner, plan.inner, 0)
        sent = jnp.concatenate([sent, rows[:1]], axis=0)
        pairs = [(plan.half, j * plan.inner), (0, plan.half + j * plan.inner)]
        total = total + lax.ppermute(sent, "slab", pairs)
    return (total, rows[middle : middle + 1])


def second_weights(plan, blocks, turned):
    slab = lax.axis_index("slab")
    part = lax.rem(slab, plan.half) // plan.inner
    strips = []
    for i in range(plan.inner):
        place = lax.rem(slab + i, plan.inner)
        rows = [lax.dynamic_slice_in_dim(block, place, 1, 0) for pair in blocks for block in pair]
        strip = jnp.stack(rows).reshape((plan.outer, 2) + blocks[0][0].shape[1:])
        ids = [lax.broadcasted_iota(jnp.int32, strip.shape, n) for n in range(3)]
        change = (ids[0] == part) & (ids[1] == 1) & (ids[2] == 0) & (slab % plan.inner == 0)
        strip = jnp.where(change, lax.dynamic_slice_in_dim(turned, place, 1, 0), strip)
        if i > 0:
            pairs = []
            for source in range(plan.slabs):
                group = source // plan.inner * plan.inner
                pairs.append((source, group + (source + i) % plan.inner))
            strip = lax.ppermute(strip, "slab", pairs)
        strips.append(strip)
    return strips


def per_device(charges, counts, projection, near_blocks, neighbours, spectrum):
    panels, cell_planes, cell_cols = charges.shape
    cells, slabs = (lax.axis_size("cell"), lax.axis_size("slab"))
    nx, nz, local = spectrum.shape
    plan = Plan(slabs, cells, panels, cell_planes, cell_cols, neighbours.shape[0], nx, nz, local * slabs)
    if not plan.fits():
        return plain_device(charges, counts, projection, near_blocks, neighbours, spectrum)
    me = (lax.axis_index("cell") * slabs + lax.axis_index("slab")).astype(jnp.int32).reshape(1)
    forward_table, backward_table = plan.depth_tables()
    depth_forward, depth_backward = (halves(forward_table.T), halves(backward_table))
    y_rows, x_cols, low_ids = (plan.y_rows().reshape(-1), plan.x_columns(), np.arange(plan.ny // 2))
    cos_y, sin_y = wave(low_ids, y_rows, plan.ny)
    sin_y[0] = 1.0 - 2.0 * (y_rows % 2)
    y_forward = halves(np.concatenate([cos_y, sin_y], axis=0))
    y_backward = halves(np.concatenate([cos_y.T, -sin_y.T], axis=1))
    x_waves = [wave(cols, low_ids, plan.nx) for cols in x_cols]
    x_forward = halves(np.stack([np.concatenate(pair, axis=1) for pair in x_waves]))
    x_backward = halves(np.stack([np.concatenate([t.T for t in pair], axis=1) for pair in x_waves]))
    split_projection = projection.reshape(
        (panels, TX // CHUNKS, CHUNKS, TY * TZ, cell_planes, cell_cols)
    )
    axes = ("cell", "slab")

    def exchange(pieces):
        return lax.all_to_all(pieces, axes, split_axis=0, concat_axis=0, tiled=True)

    def values(*shapes):
        return [pltpu.VMEM(shape, jnp.float32) for shape in shapes]

    rows_shape = (plan.ny, 2 * plan.x_chunk)
    freq_shape = (2 * plan.ny, plan.x_chunk)
    both_shape = (2 * plan.ny, plan.nx)
    ids = jnp.stack([lax.axis_index("cell"), lax.axis_index("slab")]).astype(jnp.int32)
    slot = lax.broadcasted_iota(jnp.int32, charges.shape, 0)
    masked = jnp.where(slot < counts[None], charges, 0.0)
    rows = jnp.transpose(spectrum[:, :, 0], (1, 0))
    pieces = [project(plan, i, charges, counts, split_projection, *depth_forward) for i in range(CHUNKS)]
    pieces[0], ids = lax.optimization_barrier((pieces[0], ids))
    even_pieces = exchange(pieces[0])
    picked = pick_planes(plan, ids, spectrum)
    plain = [outer_shift(plan, picked[2 * j], j) for j in range(plan.outer)]
    mirror = [outer_shift(plan, picked[2 * j + 1], j) for j in range(plan.outer)]
    pieces[1], masked, rows = lax.optimization_barrier((pieces[1], masked, rows))
    turned, own_row = edge_weights(plan, rows)
    left, right = extend_rows(plan, masked)
    pieces[1], left, right, turned, *moved = lax.optimization_barrier(
        (pieces[1], left, right, turned, *plain, *mirror)
    )
    plain, mirror = (moved[: plan.outer], moved[plan.outer :])
    odd_pieces = exchange(pieces[1])
    strips = second_weights(plan, list(zip(plain, mirror)), turned)
    edge = jnp.concatenate([turned[plan.inner :], own_row], axis=0)
    (even,) = plane_call(
        plan, first_plane_kernel, "even_planes", me, [even_pieces], [], [(y_forward, None), (x_forward, 0)], [],
        [both_shape], values(rows_shape, freq_shape), 2,
    )
    even, masked = lax.optimization_barrier((even, masked))
    extended = extend_planes(plan, masked, left, right)
    odd_pieces, extended = lax.optimization_barrier((odd_pieces, extended))
    late = [*y_forward, x_forward[0][1:], x_forward[1][1:], even]
    late += [x_backward[0][:1], x_backward[1][:1], *y_backward]
    copies = [pltpu.VMEM(array.shape, array.dtype) for array in late]
    copies.append(pltpu.SemaphoreType.DMA((len(late) + plan.half + 1,)))
    back, rest = plane_call(
        plan, middle_plane_kernel, "middle_planes", me, [odd_pieces], [edge],
        [], late + strips, [piece_shape(plan), freq_shape],
        values(rows_shape, freq_shape, freq_shape, freq_shape, (2, plan.ny // 2, plan.nx)) + copies, 4,
    )
    even_back = exchange(back)
    (back,) = plane_call(
        plan, last_plane_kernel, "odd_planes", me, [], [rest], [(x_backward, 1), (y_backward, None)], [],
        [piece_shape(plan)], values(rows_shape), 2,
    )
    total = near_field(plan, extended, neighbours, near_blocks)
    back, total = lax.optimization_barrier((back, total))
    odd_back = exchange(back)
    total = gather(plan, 0, counts, total, split_projection, *depth_backward, even_back)
    return gather(plan, 1, counts, total, split_projection, *depth_backward, odd_back)


def padded(value, sides, width):
    for axis, dim in sides:
        count, length = (lax.axis_size(axis), value.shape[dim])
        up = [(i, (i + 1) % count) for i in range(count)]
        down = [(j, i) for i, j in up]
        last = lax.slice_in_dim(value, length - width, length, axis=dim)
        first = lax.slice_in_dim(value, 0, width, axis=dim)
        before = lax.ppermute(last, axis, up)
        after = lax.ppermute(first, axis, down)
        value = jnp.concatenate([before, value, after], axis=dim)
    return value


def wave_tables(row_count, col_count, length):
    products = (
        lax.broadcasted_iota(jnp.int32, (row_count, col_count), 0)
        * lax.broadcasted_iota(jnp.int32, (row_count, col_count), 1)
        % length
    )
    angle_rad = products.astype(jnp.float32) * (2.0 * math.pi / length)
    return (jnp.cos(angle_rad), jnp.sin(angle_rad))


def depth_rows(nz, freq_ids, valid, weights):
    depth_ids = lax.broadcasted_iota(jnp.int32, (freq_ids.shape[0], nz), 1)
    products = freq_ids[:, None] * depth_ids % nz
    angle_rad = products.astype(jnp.float32) * (2.0 * math.pi / nz)
    basis = jnp.stack([jnp.cos(angle_rad), -jnp.sin(angle_rad)])
    return (basis * valid[None, :, None], basis * weights[None, :, None])


def half_depth_tables(nz, cell_count):
    lower = nz // (2 * cell_count)
    row_ids = lax.broadcasted_iota(jnp.int32, (cell_count * (lower + 1),), 0)
    block_ids = row_ids // (lower + 1)
    slot_ids = row_ids % (lower + 1)
    freq_ids = jnp.where(slot_ids < lower, block_ids * lower + slot_ids, nz // 2)
    valid = jnp.where((slot_ids < lower) | (block_ids == 0), 1.0, 0.0).astype(jnp.float32)
    doubled = jnp.where((slot_ids < lower) & (freq_ids > 0), 2.0, 1.0).astype(jnp.float32)
    forward_table, backward_table = depth_rows(nz, freq_ids, valid, valid * doubled)
    return (forward_table, backward_table, freq_ids)


def combine_halves(first_part, second, orient):
    half_width = first_part.shape[-1] // 2
    real_part = first_part[..., :half_width] + orient * second[..., half_width:]
    imag_part = first_part[..., half_width:] - orient * second[..., :half_width]
    return jnp.concatenate([real_part, imag_part], axis=-1)


def transform_axis(pattern, cosine, sine_tab, values, orient):
    first_part = jnp.einsum(pattern, cosine, values, precision=lax.Precision.HIGHEST)
    second = jnp.einsum(pattern, sine_tab, values, precision=lax.Precision.HIGHEST)
    return combine_halves(first_part, second, orient)


def twiddle(values, twist_cos, twist_sin, orient):
    half_width = values.shape[-1] // 2
    real_part = values[..., :half_width]
    imag_part = values[..., half_width:]
    new_real = real_part * twist_cos + orient * imag_part * twist_sin
    new_imag = imag_part * twist_cos - orient * real_part * twist_sin
    return jnp.concatenate([new_real, new_imag], axis=-1)


def transform_rows(planes_block, cosine, sine_tab, orient):
    flat_rows = planes_block.reshape(-1, planes_block.shape[-1])
    first_part = jnp.dot(flat_rows, cosine, precision=lax.Precision.HIGHEST).reshape(
        planes_block.shape
    )
    second = jnp.dot(flat_rows, sine_tab, precision=lax.Precision.HIGHEST).reshape(
        planes_block.shape
    )
    real_part = first_part[:, 0] + orient * second[:, 1]
    imag_part = first_part[:, 1] - orient * second[:, 0]
    return jnp.stack([real_part, imag_part], axis=1)


def plain_device(charges, counts, projection, near_blocks, neighbours, spectrum):
    panels, cell_planes, cell_cols = charges.shape
    nx, nz, ny = (spectrum.shape[0], spectrum.shape[1], spectrum.shape[2] * lax.axis_size("slab"))
    planes = cell_planes * TX
    rows_cell = cell_cols // NZC
    slot_ids = lax.broadcasted_iota(jnp.int32, charges.shape, 0)
    panel_mask = (slot_ids < counts[None]).astype(jnp.float32)
    masked = charges * panel_mask
    tile_values = jnp.einsum("ptxc,pxc->txc", projection, masked, precision=lax.Precision.HIGHEST)
    grid_field = (
        tile_values.reshape(TX, TY, TZ, cell_planes, rows_cell, NZC)
        .transpose(3, 0, 5, 2, 4, 1)
        .reshape(planes, nz, rows_cell * TY)
    )
    cell_count = lax.axis_size("cell")
    forward_table, backward_table, freq_ids = half_depth_tables(nz, cell_count)
    depth_count = forward_table.shape[1] // cell_count
    spectra_z = jnp.einsum(
        "wkz,xzy->xwky", forward_table, grid_field, precision=lax.Precision.HIGHEST
    )
    cosine_y, sine_y = wave_tables(ny, ny, ny)
    pencils = transform_rows(
        lax.all_to_all(spectra_z, "cell", split_axis=2, concat_axis=3, tiled=True),
        cosine_y,
        sine_y,
        1.0,
    )
    columns = lax.all_to_all(pencils, "slab", split_axis=3, concat_axis=0, tiled=True)
    col_width = columns.shape[2] * columns.shape[3]
    flat_rows = columns.reshape(nx, 2 * col_width)
    first_row = lax.axis_index("cell") * depth_count
    kernel_ids = lax.dynamic_slice_in_dim(freq_ids, first_row, depth_count, 0)
    kernel = jnp.take(spectrum, kernel_ids, axis=1).reshape(nx, col_width) * (1.0 / (nx * ny * nz))
    kernel_both = jnp.concatenate([kernel, kernel], axis=1)
    slab_count = lax.axis_size("slab")
    local_rows = nx // slab_count
    cosine_s, sine_s = wave_tables(slab_count, slab_count, slab_count)
    cosine_r, sine_r = wave_tables(local_rows, local_rows, local_rows)
    twist_cos, twist_sin = wave_tables(slab_count, local_rows, nx)
    twist_cos = twist_cos[:, :, None]
    twist_sin = twist_sin[:, :, None]
    section_one = transform_axis(
        "ks,src->krc",
        cosine_s,
        sine_s,
        flat_rows.reshape(slab_count, local_rows, 2 * col_width),
        1.0,
    )
    section_one = twiddle(section_one, twist_cos, twist_sin, 1.0)
    section_two = transform_axis("jr,krc->jkc", cosine_r, sine_r, section_one, 1.0)
    weighted = section_two.reshape(nx, 2 * col_width) * kernel_both
    section_one = transform_axis(
        "rj,jkc->krc",
        cosine_r,
        sine_r,
        weighted.reshape(local_rows, slab_count, 2 * col_width),
        -1.0,
    )
    section_one = twiddle(section_one, twist_cos, twist_sin, -1.0)
    section_two = transform_axis("sk,krc->src", cosine_s, sine_s, section_one, -1.0)
    returned_x = section_two.reshape(nx, 2 * col_width)
    returned = lax.all_to_all(
        returned_x.reshape(columns.shape), "slab", split_axis=0, concat_axis=3, tiled=True
    )
    inverse_rows = transform_rows(returned, cosine_y, sine_y, -1.0)
    grid_potential = jnp.einsum(
        "wkz,xwky->xzy",
        backward_table,
        lax.all_to_all(inverse_rows, "cell", split_axis=3, concat_axis=2, tiled=True),
        precision=lax.Precision.HIGHEST,
    )
    tile_potential = (
        grid_potential.reshape(cell_planes, TX, NZC, TZ, rows_cell, TY)
        .transpose(1, 5, 3, 0, 4, 2)
        .reshape(TX * TY * TZ, cell_planes, cell_cols)
    )
    far_field = jnp.einsum(
        "ptxc,txc->pxc", projection, tile_potential, precision=lax.Precision.HIGHEST
    )
    block = masked.reshape(panels, cell_planes, rows_cell, NZC)
    extended = padded(block, (("slab", 1), ("cell", 2)), 1)
    flat_ext = extended.reshape(panels, -1)
    step_x = neighbours // 9 - 1
    step_y = neighbours // 3 % 3 - 1
    step_z = neighbours % 3 - 1
    plane_ids = lax.broadcasted_iota(jnp.int32, neighbours.shape, 1)
    col_ids = lax.broadcasted_iota(jnp.int32, neighbours.shape, 2)
    row_ids = col_ids // NZC
    depth_ids = col_ids % NZC
    near_ids = ((plane_ids + step_x + 1) * (rows_cell + 2) + row_ids + step_y + 1) * NZC + (
        depth_ids + step_z
    ) % NZC
    near_count = neighbours.shape[0]
    picked = jnp.take(flat_ext, near_ids.reshape(-1), axis=1).reshape(
        panels, near_count, cell_planes, cell_cols
    )
    near_field = jnp.einsum("kpqxc,qkxc->pxc", near_blocks, picked, precision=lax.Precision.HIGHEST)
    return (far_field + near_field) * panel_mask


def solution(mesh):
    in_specs = (
        P(None, "slab", "cell"),
        P("slab", "cell"),
        P(None, None, "slab", "cell"),
        P(None, None, None, "slab", "cell"),
        P(None, "slab", "cell"),
        P(None, None, "slab"),
    )
    out_specs = P(None, "slab", "cell")
    return jax.shard_map(
        per_device, mesh=mesh, in_specs=in_specs, out_specs=out_specs, check_vma=False
    )
```

```python
import functools
import math

import jax
import jax.numpy as jnp
import ml_dtypes
import numpy as np
from jax import lax
from jax.experimental import pallas as pl
from jax.experimental.pallas import tpu as pltpu
from jax.sharding import PartitionSpec as P

TX = 4
TY = 4
TZ = 4
NZC = 16
LANES = 128
CHUNKS = 2
VMEM_LIMIT = 60 * 1024 * 1024
PLANE_LIMIT = 50 * 1024 * 1024


def halves(table):
    high = table.astype(np.float32).astype(ml_dtypes.bfloat16)
    low = (table - high.astype(np.float64)).astype(np.float32).astype(ml_dtypes.bfloat16)
    return (high, low)


def wave(rows, cols, length):
    angle = (rows[:, None] * cols[None, :] % length) * (2.0 * math.pi / length)
    return (np.cos(angle), np.sin(angle))


class Plan:
    def __init__(self, slabs, cells, panels, cell_planes, cell_cols, near, nx, nz, ny):
        self.slabs, self.cells = (slabs, cells)
        self.panels, self.cell_planes, self.cell_cols, self.near = (panels, cell_planes, cell_cols, near)
        self.nx, self.ny, self.nz = (nx, ny, nz)
        self.slots = slabs * cells
        self.tx_chunk = TX // CHUNKS
        self.width = cell_planes * self.tx_chunk
        self.y_lanes = LANES // self.width if self.width else 1
        self.row_block = LANES // NZC
        self.step_blocks = self.y_lanes // TY
        self.steps = cell_cols // (LANES * self.step_blocks) if self.step_blocks else 0
        self.x_chunk = nx // CHUNKS
        self.ky_local = ny // slabs
        self.half = slabs // 2
        self.outer = math.gcd(self.half, 2)
        self.inner = self.half // self.outer

    def fits(self):
        return (
            self.slots * 2 == self.nz
            and self.cell_planes == 8
            and self.step_blocks * TY * self.width == LANES
            and self.slabs % self.y_lanes == 0
            and self.ky_local % 8 == 0
            and self.steps * self.step_blocks * LANES == self.cell_cols
            and self.x_chunk % LANES == 0
            and self.ny % 1024 == self.nx % 1024 == 512
        )

    def depth_tables(self):
        depth = np.arange(NZC)[None, :] * TZ + np.arange(TZ)[:, None]
        scale = 1.0 / (self.nx * self.ny * self.nz)
        forward = np.zeros((self.slots, 2, self.row_block, TZ, self.row_block, NZC))
        backward = np.zeros_like(forward)
        for freq in range(self.slots):
            angle = (freq * depth % self.nz) * (2.0 * math.pi / self.nz)
            real, imag = (np.cos(angle), -np.sin(angle))
            factor = 2.0 * scale
            if freq == 0:
                imag = np.cos(depth * math.pi)
                factor = scale
            for row in range(self.row_block):
                forward[freq, 0, row, :, row, :] = real
                forward[freq, 1, row, :, row, :] = imag
                backward[freq, 0, row, :, row, :] = factor * real
                backward[freq, 1, row, :, row, :] = factor * imag
        shape = (self.slots * 2 * self.row_block, TZ * LANES)
        return (forward.reshape(shape), backward.reshape(shape))

    def y_rows(self):
        parity, cell, step, block, tile, row = np.meshgrid(
            *[np.arange(n) for n in (2, self.cells, self.steps, self.step_blocks, TY // 2, self.row_block)],
            indexing="ij",
        )
        cell_row = ((cell * self.steps + step) * self.step_blocks + block) * self.row_block + row
        return (cell_row * TY + 2 * tile + parity).reshape(2, -1)

    def x_columns(self):
        parity, slab, tile, plane = np.meshgrid(
            *[np.arange(n) for n in (2, self.slabs, TX // 2, self.cell_planes)], indexing="ij"
        )
        return ((slab * self.cell_planes + plane) * TX + 2 * tile + parity).reshape(2, -1)

    def row_of(self, cell, step, place):
        block, tile = (place // TY, place % TY)
        inner = (cell * self.steps + step) * self.step_blocks + block
        return (tile % 2) * (self.ny // 2) + (inner * (TY // 2) + tile // 2) * self.row_block


def split(value):
    high = value.astype(jnp.bfloat16)
    low = (value - high.astype(jnp.float32)).astype(jnp.bfloat16)
    return (high, low)


def product(left, right, dims=((1,), (0,))):
    first = jnp.concatenate([left[0], left[0], left[1]], axis=dims[0][0])
    second = jnp.concatenate([right[0], right[1], right[0]], axis=dims[1][0])
    return lax.dot_general(first, second, (dims, ((), ())), preferred_element_type=jnp.float32)


def swap_groups(parts, width):
    count = len(parts)
    lane = lax.broadcasted_iota(jnp.int32, parts[0].shape, 1)
    parts = list(parts)
    step = count // 2
    while step >= 1:
        shift = step * width
        upper = (lane // shift) % 2 == 1
        for i in range(count):
            if i & step:
                continue
            first, second = (parts[i], parts[i + step])
            parts[i] = jnp.where(upper, pltpu.roll(second, shift, 1), first)
            parts[i + step] = jnp.where(upper, second, pltpu.roll(first, LANES - shift, 1))
        step //= 2
    return parts


def tile_copies(plan, chunk, projection, held, sems):
    return [
        pltpu.make_async_copy(projection.at[:, tx, chunk], held.at[tx], sems.at[tx])
        for tx in range(plan.tx_chunk)
    ]


def project_kernel(plan, chunk, charges_in, counts_in, high_in, low_in, projection, out, scratch, held, sems,
                   charges, counts, high, low):
    planes = plan.cell_planes
    first = plan.tx_chunk
    pairs = ((charges_in, charges), (counts_in, counts), (high_in, high), (low_in, low))
    loads = [pltpu.make_async_copy(*pair, sems.at[first + n]) for n, pair in enumerate(pairs)]
    copies = tile_copies(plan, chunk, projection, held, sems)
    for copy in loads[:2] + copies + loads[2:]:
        copy.start()
    for copy in loads[:2]:
        copy.wait()
    for tx, copy in enumerate(copies):
        copy.wait()

        def body(place, carry, tx=tx):
            lanes = pl.ds(pl.multiple_of(place * LANES, LANES), LANES)
            count = counts[:, lanes]
            own = [jnp.where(count > p, charges[p, :, lanes], 0.0) for p in range(plan.panels)]
            for ty in range(TY):
                row = ((place * TY + ty) * plan.tx_chunk + tx) * planes
                rows = pl.ds(pl.multiple_of(row, planes), planes)
                for tz in range(TZ):
                    t = ty * TZ + tz
                    total = held[tx, 0, t, :, lanes] * own[0]
                    for p in range(1, plan.panels):
                        total = total + held[tx, p, t, :, lanes] * own[p]
                    scratch[rows, tz * LANES : (tz + 1) * LANES] = total
            return carry

        lax.fori_loop(0, plan.steps * plan.step_blocks, body, 0)
    for copy in loads[2:]:
        copy.wait()
    spectra = product(split(scratch[...]), (high[...], low[...])).T
    shape = (plan.slots, 2, plan.row_block, LANES)
    for step in range(plan.steps):
        out[:, :, step] = spectra[:, step * LANES : (step + 1) * LANES].reshape(shape)


def held_shape(plan):
    cols = plan.steps * plan.step_blocks * LANES
    return (plan.tx_chunk, plan.panels, TY * TZ, plan.cell_planes, cols)


def piece_shape(plan):
    return (plan.slots, 2, plan.steps, plan.row_block, LANES)


def whole_spec(shape):
    return pl.BlockSpec(shape, lambda i: (0,) * len(shape))


def projection_call(plan, kernel, name, ready, arrays, projection, out_shape):
    return pl.pallas_call(
        kernel,
        in_specs=[pl.BlockSpec(memory_space=pltpu.VMEM)] * len(ready)
        + [pl.BlockSpec(memory_space=pl.ANY)] * (len(arrays) + 1),
        out_specs=pl.BlockSpec(memory_space=pltpu.VMEM),
        out_shape=jax.ShapeDtypeStruct(out_shape, jnp.float32),
        scratch_shapes=[
            pltpu.VMEM((plan.steps * LANES, TZ * LANES), jnp.float32),
            pltpu.VMEM(held_shape(plan), jnp.float32),
            pltpu.SemaphoreType.DMA((plan.tx_chunk + len(arrays),)),
        ]
        + [pltpu.VMEM(array.shape, array.dtype) for array in arrays],
        compiler_params=pltpu.CompilerParams(vmem_limit_bytes=PLANE_LIMIT),
        cost_estimate=pl.CostEstimate(
            flops=2 * math.prod(held_shape(plan)),
            bytes_accessed=4 * math.prod(held_shape(plan)),
            transcendentals=0,
        ),
        name=name,
    )(*ready, *arrays, projection)


def project(plan, chunk, charges, counts, projection, high, low):
    kernel = functools.partial(project_kernel, plan, chunk)
    arrays = [charges, counts, high, low]
    return projection_call(plan, kernel, "project_depth", [], arrays, projection, piece_shape(plan))


def far_sign(plan, me_ref):
    slab = lax.rem(me_ref[0], plan.slabs)
    return jnp.where(slab >= plan.half, -1.0, 1.0)


def forward_plane(plan, me_ref, pieces, y_table, x_table, rows_ref, freq_ref, waits=()):
    special = me_ref[0] == 0
    sign = far_sign(plan, me_ref)
    rows = 2 * plan.steps * plan.row_block
    width = plan.x_chunk
    middle = plan.ny // 2
    for cell in range(plan.cells):
        for group in range(plan.slabs // plan.y_lanes):
            first = cell * plan.slabs + group * plan.y_lanes
            parts = [pieces[first + i].reshape(rows, LANES) for i in range(plan.y_lanes)]
            parts = swap_groups(parts, plan.width)
            for place, value in enumerate(parts):
                if place % 2 == 1:
                    value = value * sign
                for part in range(2):
                    for step in range(plan.steps):
                        source = (part * plan.steps + step) * plan.row_block
                        row = plan.row_of(cell, step, place)
                        col = part * width + group * LANES
                        rows_ref[row : row + plan.row_block, col : col + LANES] = value[
                            source : source + plan.row_block
                        ]
    for copy in waits:
        copy.wait()
    sums = product((y_table[0][...], y_table[1][...]), split(rows_ref[...]))
    cos_re, cos_im = (sums[:middle, :width], sums[:middle, width:])
    sin_re, sin_im = (sums[middle:, :width], sums[middle:, width:])
    first = lax.broadcasted_iota(jnp.int32, (middle, width), 0) == 0

    @pl.when(jnp.logical_not(special))
    def _():
        freq_ref[:middle] = jnp.where(first, cos_re, cos_re + sin_im)
        freq_ref[middle : 2 * middle] = jnp.where(first, cos_im, cos_im - sin_re)
        freq_ref[2 * middle : 3 * middle] = jnp.where(first, sin_re, cos_re - sin_im)
        freq_ref[3 * middle :] = jnp.where(first, sin_im, cos_im + sin_re)

    @pl.when(special)
    def _():
        freq_ref[:middle] = cos_re
        freq_ref[middle : 2 * middle] = jnp.where(first, sin_re, -sin_re)
        freq_ref[2 * middle : 3 * middle] = cos_im
        freq_ref[3 * middle :] = sin_im

    return product(split(freq_ref[...]), (x_table[0][0], x_table[1][0]))


def backward_plane(plan, me_ref, freqs, x_table, y_table, out, rows_ref):
    special = me_ref[0] == 0
    sign = far_sign(plan, me_ref)
    width = plan.x_chunk
    middle = plan.ny // 2
    sums = product(split(freqs), (x_table[0][0], x_table[1][0]))
    parts = []
    for mirrored, turn in ((0, 1.0), (1, -1.0)):
        re = slice(2 * mirrored * middle, (2 * mirrored + 1) * middle)
        im = slice((2 * mirrored + 1) * middle, (2 * mirrored + 2) * middle)
        parts.append(sums[re, :width] - turn * sums[im, width:])
        parts.append(sums[im, :width] + turn * sums[re, width:])
    re_n, im_n, re_m, im_m = parts
    first = lax.broadcasted_iota(jnp.int32, (middle, width), 0) == 0

    @pl.when(jnp.logical_not(special))
    def _():
        rows_ref[:middle, :width] = jnp.where(first, re_n, re_n + re_m)
        rows_ref[:middle, width:] = jnp.where(first, im_n, im_n + im_m)
        rows_ref[middle:, :width] = jnp.where(first, -re_m, im_n - im_m)
        rows_ref[middle:, width:] = jnp.where(first, -im_m, re_m - re_n)

    @pl.when(special)
    def _():
        rows_ref[:middle, :width] = jnp.where(first, re_n, 2.0 * re_n)
        rows_ref[:middle, width:] = jnp.where(first, re_m, 2.0 * re_m)
        rows_ref[middle:, :width] = jnp.where(first, -im_n, 2.0 * im_n)
        rows_ref[middle:, width:] = jnp.where(first, -im_m, -2.0 * im_m)

    rows_ref[...] = product((y_table[0][...], y_table[1][...]), split(rows_ref[...]))
    for cell in range(plan.cells):
        for group in range(plan.slabs // plan.y_lanes):
            parts = []
            for place in range(plan.y_lanes):
                tiles = []
                for part in range(2):
                    for step in range(plan.steps):
                        row = plan.row_of(cell, step, place)
                        col = part * width + group * LANES
                        tiles.append(rows_ref[row : row + plan.row_block, col : col + LANES])
                value = jnp.concatenate(tiles, axis=0)
                parts.append(value * sign if place % 2 == 1 else value)
            parts = swap_groups(parts, plan.width)
            first = cell * plan.slabs + group * plan.y_lanes
            for i in range(plan.y_lanes):
                out[first + i] = parts[i].reshape(2, plan.steps, plan.row_block, LANES)


def first_plane_kernel(plan, me_ref, pieces, y_high, y_low, x_high, x_low, out, rows_ref, freq_ref):
    out[...] = forward_plane(plan, me_ref, pieces, (y_high, y_low), (x_high, x_low), rows_ref, freq_ref)


def middle_plane_kernel(plan, me_ref, pieces, even, edge, *refs):
    strips, refs = (refs[: plan.inner], refs[plan.inner :])
    blocks, refs = (refs[: plan.outer], refs[plan.outer :])
    late, refs = (refs[:8], refs[8:])
    out, rest, rows_ref, freq_ref, sum_ref, rest_ref, weights = refs[:7]
    held, sems = (refs[7:15], refs[15])
    yf_high, yf_low, xf_high, xf_low, xb_high, xb_low, yb_high, yb_low = held
    slab = lax.rem(me_ref[0], plan.slabs)
    place = lax.rem(slab, plan.half)
    outer_id, inner_id = (place // plan.inner, lax.rem(place, plan.inner))
    copies = [pltpu.make_async_copy(late[n], held[n], sems.at[n]) for n in range(len(held))]
    count = plan.ky_local
    for i in range(plan.inner):
        for j in range(plan.outer):
            owner = lax.rem(outer_id - j + plan.outer, plan.outer) * plan.inner
            owner = owner + lax.rem(inner_id - i + plan.inner, plan.inner)
            rows = pl.ds(pl.multiple_of(owner * count, count), count)
            n = len(copies)
            source = strips[i].at[pl.ds(j * count, count)]
            copies.append(pltpu.make_async_copy(source, weights.at[0, rows], sems.at[n]))
            copies.append(pltpu.make_async_copy(blocks[j].at[i], weights.at[1, rows], sems.at[n + 1]))
    for copy in copies:
        copy.start()
    own_edge = strips[0][plan.outer * count : plan.outer * count + 1]
    for i in range(1, plan.inner):
        row = strips[i][plan.outer * count : plan.outer * count + 1]
        own_edge = jnp.where(inner_id == i, row, own_edge)
    special = me_ref[0] == 0
    width = plan.x_chunk
    middle = plan.ny // 2
    x_table = (xf_high.at[pl.ds(0, 1)], xf_low.at[pl.ds(0, 1)])
    odd = forward_plane(
        plan, me_ref, pieces, (yf_high, yf_low), x_table, rows_ref, freq_ref, copies[:4]
    )
    for copy in copies[len(held) :]:
        copy.wait()
    row = lax.broadcasted_iota(jnp.int32, (middle, width), 0)
    at_first = row == 0
    for mirrored, turn in ((0, 1.0), (1, -1.0)):
        re = slice(2 * mirrored * middle, (2 * mirrored + 1) * middle)
        im = slice((2 * mirrored + 1) * middle, (2 * mirrored + 2) * middle)
        results = []
        for upper in range(2):
            cols = slice(upper * width, (upper + 1) * width)
            plane = weights[mirrored, :, cols]
            if mirrored:
                second = jnp.where(at_first, own_edge[:, cols], plane)
                weight = jnp.where(special, plane, second)
            else:
                weight = plane
                second = jnp.where(at_first & special, edge[0:1, cols], plane)
            re_sums = even[re] - odd[re] if upper else even[re] + odd[re]
            im_sums = even[im] - odd[im] if upper else even[im] + odd[im]
            real = weight * re_sums[:, :width] + (turn * second) * im_sums[:, width:]
            imag = second * im_sums[:, :width] - (turn * weight) * re_sums[:, width:]
            results.append((real, imag))
        for part, rows in enumerate((re, im)):
            below, above = (results[0][part], results[1][part])
            sum_ref[rows] = below + above
            rest_ref[rows] = below - above
    last = pltpu.make_async_copy(rest_ref, rest, sems.at[len(held) + 2 * plan.half])
    last.start()
    for copy in copies[4 : len(held)]:
        copy.wait()
    backward_plane(plan, me_ref, sum_ref[...], (xb_high, xb_low), (yb_high, yb_low), out, rows_ref)
    last.wait()


def last_plane_kernel(plan, me_ref, freqs, x_high, x_low, y_high, y_low, out, rows_ref):
    backward_plane(plan, me_ref, freqs[...], (x_high, x_low), (y_high, y_low), out, rows_ref)


def plane_call(plan, kernel, name, me, ready, arrays, tables, late, out_specs, out_shapes, scratch, work):
    specs = [pl.BlockSpec(memory_space=pltpu.VMEM)] * len(ready)
    specs += [whole_spec(array.shape) for array in arrays]
    flat = []
    for pair, chunk in tables:
        for table in pair:
            if chunk is None:
                specs.append(whole_spec(table.shape))
            else:
                specs.append(pl.BlockSpec((1,) + table.shape[1:], lambda i, chunk=chunk: (chunk, 0, 0)))
            flat.append(table)
    specs += [pl.BlockSpec(memory_space=pl.ANY)] * len(late)
    size = sum(4 * array.size for array in list(ready) + list(arrays) + list(late))
    return pl.pallas_call(
        functools.partial(kernel, plan),
        grid=(1,) if tables else (),
        in_specs=[pl.BlockSpec(memory_space=pltpu.SMEM)] + specs,
        out_specs=out_specs,
        out_shape=[jax.ShapeDtypeStruct(shape, jnp.float32) for shape in out_shapes],
        scratch_shapes=scratch,
        compiler_params=pltpu.CompilerParams(vmem_limit_bytes=PLANE_LIMIT),
        cost_estimate=pl.CostEstimate(
            flops=work * 12 * plan.nx * plan.ny * plan.x_chunk,
            bytes_accessed=size + sum(2 * table.size for table in flat),
            transcendentals=0,
        ),
        name=name,
    )(me, *ready, *arrays, *flat, *late)


def gather_kernel(
    plan, chunk, pieces, high_in, low_in, before_in, counts_in, projection, out, scratch, held, sems,
    high, low, before, counts
):
    planes = plan.cell_planes
    rows = plan.slots * 2 * plan.row_block
    first = plan.tx_chunk
    copies = tile_copies(plan, chunk, projection, held, sems)
    pairs = ((high_in, high), (low_in, low), (before_in, before), (counts_in, counts))
    loads = [pltpu.make_async_copy(*pair, sems.at[first + n]) for n, pair in enumerate(pairs)]
    for copy in loads[:2] + copies + loads[2:]:
        copy.start()
    for copy in loads[:2]:
        copy.wait()
    columns = [pieces[:, :, step].reshape(rows, LANES) for step in range(plan.steps)]
    scratch[...] = product(split(jnp.concatenate(columns, axis=1).T), (high[...], low[...]))
    for copy in loads[2:]:
        copy.wait()
    for tx in range(plan.tx_chunk):
        copies[tx].wait()
        last = chunk == CHUNKS - 1 and tx == plan.tx_chunk - 1

        def body(place, carry, tx=tx, last=last):
            lanes = pl.ds(pl.multiple_of(place * LANES, LANES), LANES)
            far = [(before if tx == 0 else out)[p, :, lanes] for p in range(plan.panels)]
            for ty in range(TY):
                row = ((place * TY + ty) * plan.tx_chunk + tx) * planes
                rows_at = pl.ds(pl.multiple_of(row, planes), planes)
                for tz in range(TZ):
                    t = ty * TZ + tz
                    potential = scratch[rows_at, tz * LANES : (tz + 1) * LANES]
                    for p in range(plan.panels):
                        far[p] = far[p] + held[tx, p, t, :, lanes] * potential
            for p in range(plan.panels):
                out[p, :, lanes] = jnp.where(counts[:, lanes] > p, far[p], 0.0) if last else far[p]
            return carry

        lax.fori_loop(0, plan.steps * plan.step_blocks, body, 0)


def gather(plan, chunk, counts, before, projection, high, low, pieces):
    kernel = functools.partial(gather_kernel, plan, chunk)
    arrays = [high, low, before, counts]
    return projection_call(plan, kernel, "depth_gather", [pieces], arrays, projection, before.shape)


def near_kernel(plan, extended, codes, blocks_ref, out):
    step = pl.program_id(0)
    lane = lax.broadcasted_iota(jnp.int32, (plan.cell_planes, LANES), 1)
    depth = lane % NZC
    digits = []
    for k in range(plan.near):
        code = codes[k]
        digits.append((code // 9, code // 3 % 3, code % 3))
    total = [None] * plan.panels
    for q in range(plan.panels):
        shifted = []
        for dx in range(3):
            before, here, after = (
                extended[q, dx, :, pl.ds(pl.multiple_of((step + i) * LANES, LANES), LANES)] for i in range(3)
            )
            up = jnp.where(lane < NZC, pltpu.roll(before, NZC, 1), pltpu.roll(here, NZC, 1))
            down = jnp.where(
                lane >= LANES - NZC, pltpu.roll(after, LANES - NZC, 1), pltpu.roll(here, LANES - NZC, 1)
            )
            for value in (up, here, down):
                under = jnp.where(
                    depth == 0, pltpu.roll(value, LANES - NZC + 1, 1), pltpu.roll(value, 1, 1)
                )
                over = jnp.where(
                    depth == NZC - 1, pltpu.roll(value, NZC - 1, 1), pltpu.roll(value, LANES - 1, 1)
                )
                shifted.append((under, value, over))
        for k in range(plan.near):
            digit_x, digit_y, digit_z = digits[k]

            def choose(digit, options):
                return jnp.where(digit == 0, options[0], jnp.where(digit == 1, options[1], options[2]))

            by_z = [choose(digit_z, options) for options in shifted]
            by_y = [choose(digit_y, by_z[3 * i : 3 * i + 3]) for i in range(3)]
            picked = choose(digit_x, by_y)
            for p in range(plan.panels):
                term = blocks_ref[k, p, q] * picked
                total[p] = term if total[p] is None else total[p] + term
    for p in range(plan.panels):
        out[p] = total[p]


def near_field(plan, extended, neighbours, near_blocks):
    return pl.pallas_call(
        functools.partial(near_kernel, plan),
        grid=(plan.cell_cols // LANES,),
        in_specs=[
            whole_spec(extended.shape),
            pl.BlockSpec((plan.near, plan.cell_planes, LANES), lambda i: (0, 0, i)),
            pl.BlockSpec(
                (plan.near, plan.panels, plan.panels, plan.cell_planes, LANES), lambda i: (0, 0, 0, 0, i)
            ),
        ],
        out_specs=pl.BlockSpec((plan.panels, plan.cell_planes, LANES), lambda i: (0, 0, i)),
        out_shape=jax.ShapeDtypeStruct((plan.panels, plan.cell_planes, plan.cell_cols), jnp.float32),
        compiler_params=pltpu.CompilerParams(vmem_limit_bytes=VMEM_LIMIT),
        cost_estimate=pl.CostEstimate(
            flops=2 * near_blocks.size, bytes_accessed=4 * near_blocks.size, transcendentals=0
        ),
        name="near_blocks",
    )(extended, neighbours, near_blocks)


def ring_pairs(axis):
    count = lax.axis_size(axis)
    up = [(i, (i + 1) % count) for i in range(count)]
    return (up, [(j, i) for i, j in up])


def extend_rows(plan, masked):
    up, down = ring_pairs("cell")
    left = lax.ppermute(masked[:, :, -NZC:], "cell", up)
    right = lax.ppermute(masked[:, :, :NZC], "cell", down)
    return (left, right)


def extend_planes(plan, masked, left, right):
    rest = jnp.zeros((plan.panels, plan.cell_planes, LANES - NZC), jnp.float32)
    wide = jnp.concatenate([rest, left, masked, right, rest], axis=2)
    up, down = ring_pairs("slab")
    before = lax.ppermute(wide[:, -1:], "slab", up)
    after = lax.ppermute(wide[:, :1], "slab", down)
    whole = jnp.concatenate([before, wide, after], axis=1)
    planes = plan.cell_planes
    return jnp.stack([whole[:, i : i + planes] for i in range(3)], axis=1)


def pick_kernel(plan, ids_ref, by_depth, *refs):
    outs, sems = (refs[:-1], refs[-1])
    cell, slab = (ids_ref[0], ids_ref[1])
    half_id, place = (slab // plan.half, lax.rem(slab, plan.half))
    first = cell * plan.slabs + half_id * plan.half
    copies = []
    for j in range(plan.outer):
        part = lax.rem(place // plan.inner + j, plan.outer) * plan.inner
        for i in range(plan.inner):
            n = len(copies)
            copies.append(
                pltpu.make_async_copy(by_depth.at[first + part + i], outs[j].at[i], sems.at[n])
            )
            freq = first + part + lax.rem(place + i, plan.inner)
            mirror = jnp.where(freq == 0, plan.nz // 2, plan.nz - freq)
            copies.append(
                pltpu.make_async_copy(by_depth.at[mirror], outs[plan.outer + i].at[j], sems.at[n + 1])
            )
    for copy in copies:
        copy.start()
    for copy in copies:
        copy.wait()


def pick_planes(plan, ids, spectrum):
    by_depth = jnp.transpose(spectrum, (1, 2, 0))
    shapes = [(plan.inner,) + by_depth.shape[1:]] * plan.outer
    shapes += [(plan.outer,) + by_depth.shape[1:]] * plan.inner
    picked = pl.pallas_call(
        functools.partial(pick_kernel, plan),
        in_specs=[pl.BlockSpec(memory_space=pltpu.SMEM), pl.BlockSpec(memory_space=pl.ANY)],
        out_specs=[pl.BlockSpec(memory_space=pltpu.VMEM)] * len(shapes),
        out_shape=[jax.ShapeDtypeStruct(shape, jnp.float32) for shape in shapes],
        scratch_shapes=[pltpu.SemaphoreType.DMA((2 * plan.half,))],
        cost_estimate=pl.CostEstimate(
            flops=0, bytes_accessed=8 * sum(math.prod(shape) for shape in shapes), transcendentals=0
        ),
        name="pick_planes",
    )(ids, by_depth)
    return (picked[: plan.outer], picked[plan.outer :])


def outer_shift(plan, value, j):
    if j == 0:
        return value
    pairs = []
    for source in range(plan.slabs):
        base = source // plan.half * plan.half
        pairs.append((source, base + (source - base + j * plan.inner) % plan.half))
    return lax.ppermute(value, "slab", pairs)


def inner_shift(plan, value, i):
    if i == 0:
        return value
    pairs = []
    for source in range(plan.slabs):
        base = source // plan.inner * plan.inner
        pairs.append((source, base + (source + i) % plan.inner))
    return lax.ppermute(value, "slab", pairs)


def edge_weights(plan, rows):
    slab, cell = (lax.axis_index("slab"), lax.axis_index("cell"))
    middle = plan.nz // 2
    turned = jnp.concatenate([rows[middle : middle + 1], jnp.flip(rows, 0)], axis=0)
    other = cell * plan.slabs + (1 - slab // plan.half) * plan.half
    total = 0.0
    for j in range(plan.outer):
        sent = lax.dynamic_slice_in_dim(turned, other + j * plan.inner, plan.inner, 0)
        sent = jnp.concatenate([sent, rows[:1]], axis=0)
        pairs = [(plan.half, j * plan.inner), (0, plan.half + j * plan.inner)]
        total = total + lax.ppermute(sent, "slab", pairs)
    return total


def second_weights(plan, plain, mirror, turned):
    slab = lax.axis_index("slab")
    strips = []
    for i in range(plan.inner):
        place = lax.rem(slab + i, plan.inner)
        rows = [lax.dynamic_slice_in_dim(block, place, 1, 0)[0] for block in plain]
        last = lax.dynamic_slice_in_dim(turned, place, 1, 0)
        rows.append(jnp.broadcast_to(last, (8,) + last.shape[1:]))
        strips.append(inner_shift(plan, jnp.concatenate(rows, axis=0), i))
    blocks = [outer_shift(plan, jnp.stack([m[j] for m in mirror]), j) for j in range(plan.outer)]
    return strips + blocks


def per_device(charges, counts, projection, near_blocks, neighbours, spectrum):
    panels, cell_planes, cell_cols = charges.shape
    cells, slabs = (lax.axis_size("cell"), lax.axis_size("slab"))
    nx, nz, local = spectrum.shape
    plan = Plan(slabs, cells, panels, cell_planes, cell_cols, neighbours.shape[0], nx, nz, local * slabs)
    if not plan.fits():
        return plain_device(charges, counts, projection, near_blocks, neighbours, spectrum)
    me = (lax.axis_index("cell") * slabs + lax.axis_index("slab")).astype(jnp.int32).reshape(1)
    forward_table, backward_table = plan.depth_tables()
    depth_forward, depth_backward = (halves(forward_table.T), halves(backward_table))
    y_rows, x_cols, low_ids = (plan.y_rows().reshape(-1), plan.x_columns(), np.arange(plan.ny // 2))
    cos_y, sin_y = wave(low_ids, y_rows, plan.ny)
    sin_y[0] = 1.0 - 2.0 * (y_rows % 2)
    y_forward = halves(np.concatenate([cos_y, sin_y], axis=0))
    y_backward = halves(np.concatenate([cos_y.T, -sin_y.T], axis=1))
    x_waves = [wave(cols, low_ids, plan.nx) for cols in x_cols]
    x_forward = halves(np.stack([np.concatenate(pair, axis=1) for pair in x_waves]))
    x_backward = halves(np.stack([np.concatenate([t.T for t in pair], axis=1) for pair in x_waves]))
    split_projection = projection.reshape(
        (panels, TX // CHUNKS, CHUNKS, TY * TZ, cell_planes, cell_cols)
    )
    axes = ("cell", "slab")

    def exchange(pieces):
        return lax.all_to_all(pieces, axes, split_axis=0, concat_axis=0, tiled=True)

    def values(*shapes):
        return [pltpu.VMEM(shape, jnp.float32) for shape in shapes]

    rows_shape = (plan.ny, 2 * plan.x_chunk)
    freq_shape = (2 * plan.ny, plan.x_chunk)
    both_shape = (2 * plan.ny, plan.nx)
    ids = jnp.stack([lax.axis_index("cell"), lax.axis_index("slab")]).astype(jnp.int32)
    slot = lax.broadcasted_iota(jnp.int32, charges.shape, 0)
    masked = jnp.where(slot < counts[None], charges, 0.0)
    rows = jnp.transpose(spectrum[:, :, 0], (1, 0))
    pieces = [project(plan, i, charges, counts, split_projection, *depth_forward) for i in range(CHUNKS)]
    pieces[0], ids = lax.optimization_barrier((pieces[0], ids))
    even_pieces = exchange(pieces[0])
    plain, mirror = pick_planes(plan, ids, spectrum)
    plain = [outer_shift(plan, value, j) for j, value in enumerate(plain)]
    mirror = [inner_shift(plan, value, i) for i, value in enumerate(mirror)]
    pieces[1], masked, rows = lax.optimization_barrier((pieces[1], masked, rows))
    turned = edge_weights(plan, rows)
    left, right = extend_rows(plan, masked)
    pieces[1], left, right, turned, *moved = lax.optimization_barrier(
        (pieces[1], left, right, turned, *plain, *mirror)
    )
    plain, mirror = (moved[: plan.outer], moved[plan.outer :])
    odd_pieces = exchange(pieces[1])
    strips = second_weights(plan, plain, mirror, turned)
    in_vmem = pl.BlockSpec(memory_space=pltpu.VMEM)
    in_place = pl.BlockSpec(memory_space=pl.ANY)
    (even,) = plane_call(
        plan, first_plane_kernel, "even_planes", me, [even_pieces], [],
        [(y_forward, None), (x_forward, 0)], [], [in_vmem], [both_shape],
        values(rows_shape, freq_shape), 2,
    )
    even, masked = lax.optimization_barrier((even, masked))
    extended = extend_planes(plan, masked, left, right)
    odd_pieces, extended = lax.optimization_barrier((odd_pieces, extended))
    late = [*y_forward, x_forward[0][1:], x_forward[1][1:]]
    late += [x_backward[0][:1], x_backward[1][:1], *y_backward]
    copies = [pltpu.VMEM(array.shape, array.dtype) for array in late]
    copies.append(pltpu.SemaphoreType.DMA((len(late) + 2 * plan.half + 1,)))
    back, rest = plane_call(
        plan, middle_plane_kernel, "middle_planes", me, [odd_pieces, even, turned[plan.inner :]] + strips,
        [], [], late, [in_vmem, in_place], [piece_shape(plan), freq_shape],
        values(rows_shape, freq_shape, freq_shape, freq_shape, (2, plan.ny // 2, plan.nx)) + copies, 4,
    )
    even_back = exchange(back)
    (back,) = plane_call(
        plan, last_plane_kernel, "odd_planes", me, [], [rest],
        [(x_backward, 1), (y_backward, None)], [], [whole_spec(piece_shape(plan))], [piece_shape(plan)],
        values(rows_shape), 2,
    )
    total = near_field(plan, extended, neighbours, near_blocks)
    back, total = lax.optimization_barrier((back, total))
    odd_back = exchange(back)
    total = gather(plan, 0, counts, total, split_projection, *depth_backward, even_back)
    return gather(plan, 1, counts, total, split_projection, *depth_backward, odd_back)


def padded(value, sides, width):
    for axis, dim in sides:
        count, length = (lax.axis_size(axis), value.shape[dim])
        up = [(i, (i + 1) % count) for i in range(count)]
        down = [(j, i) for i, j in up]
        last = lax.slice_in_dim(value, length - width, length, axis=dim)
        first = lax.slice_in_dim(value, 0, width, axis=dim)
        before = lax.ppermute(last, axis, up)
        after = lax.ppermute(first, axis, down)
        value = jnp.concatenate([before, value, after], axis=dim)
    return value


def wave_tables(row_count, col_count, length):
    products = (
        lax.broadcasted_iota(jnp.int32, (row_count, col_count), 0)
        * lax.broadcasted_iota(jnp.int32, (row_count, col_count), 1)
        % length
    )
    angle_rad = products.astype(jnp.float32) * (2.0 * math.pi / length)
    return (jnp.cos(angle_rad), jnp.sin(angle_rad))


def depth_rows(nz, freq_ids, valid, weights):
    depth_ids = lax.broadcasted_iota(jnp.int32, (freq_ids.shape[0], nz), 1)
    products = freq_ids[:, None] * depth_ids % nz
    angle_rad = products.astype(jnp.float32) * (2.0 * math.pi / nz)
    basis = jnp.stack([jnp.cos(angle_rad), -jnp.sin(angle_rad)])
    return (basis * valid[None, :, None], basis * weights[None, :, None])


def half_depth_tables(nz, cell_count):
    lower = nz // (2 * cell_count)
    row_ids = lax.broadcasted_iota(jnp.int32, (cell_count * (lower + 1),), 0)
    block_ids = row_ids // (lower + 1)
    slot_ids = row_ids % (lower + 1)
    freq_ids = jnp.where(slot_ids < lower, block_ids * lower + slot_ids, nz // 2)
    valid = jnp.where((slot_ids < lower) | (block_ids == 0), 1.0, 0.0).astype(jnp.float32)
    doubled = jnp.where((slot_ids < lower) & (freq_ids > 0), 2.0, 1.0).astype(jnp.float32)
    forward_table, backward_table = depth_rows(nz, freq_ids, valid, valid * doubled)
    return (forward_table, backward_table, freq_ids)


def combine_halves(first_part, second, orient):
    half_width = first_part.shape[-1] // 2
    real_part = first_part[..., :half_width] + orient * second[..., half_width:]
    imag_part = first_part[..., half_width:] - orient * second[..., :half_width]
    return jnp.concatenate([real_part, imag_part], axis=-1)


def transform_axis(pattern, cosine, sine_tab, values, orient):
    first_part = jnp.einsum(pattern, cosine, values, precision=lax.Precision.HIGHEST)
    second = jnp.einsum(pattern, sine_tab, values, precision=lax.Precision.HIGHEST)
    return combine_halves(first_part, second, orient)


def twiddle(values, twist_cos, twist_sin, orient):
    half_width = values.shape[-1] // 2
    real_part = values[..., :half_width]
    imag_part = values[..., half_width:]
    new_real = real_part * twist_cos + orient * imag_part * twist_sin
    new_imag = imag_part * twist_cos - orient * real_part * twist_sin
    return jnp.concatenate([new_real, new_imag], axis=-1)


def transform_rows(planes_block, cosine, sine_tab, orient):
    flat_rows = planes_block.reshape(-1, planes_block.shape[-1])
    first_part = jnp.dot(flat_rows, cosine, precision=lax.Precision.HIGHEST).reshape(
        planes_block.shape
    )
    second = jnp.dot(flat_rows, sine_tab, precision=lax.Precision.HIGHEST).reshape(
        planes_block.shape
    )
    real_part = first_part[:, 0] + orient * second[:, 1]
    imag_part = first_part[:, 1] - orient * second[:, 0]
    return jnp.stack([real_part, imag_part], axis=1)


def plain_device(charges, counts, projection, near_blocks, neighbours, spectrum):
    panels, cell_planes, cell_cols = charges.shape
    nx, nz, ny = (spectrum.shape[0], spectrum.shape[1], spectrum.shape[2] * lax.axis_size("slab"))
    planes = cell_planes * TX
    rows_cell = cell_cols // NZC
    slot_ids = lax.broadcasted_iota(jnp.int32, charges.shape, 0)
    panel_mask = (slot_ids < counts[None]).astype(jnp.float32)
    masked = charges * panel_mask
    tile_values = jnp.einsum("ptxc,pxc->txc", projection, masked, precision=lax.Precision.HIGHEST)
    grid_field = (
        tile_values.reshape(TX, TY, TZ, cell_planes, rows_cell, NZC)
        .transpose(3, 0, 5, 2, 4, 1)
        .reshape(planes, nz, rows_cell * TY)
    )
    cell_count = lax.axis_size("cell")
    forward_table, backward_table, freq_ids = half_depth_tables(nz, cell_count)
    depth_count = forward_table.shape[1] // cell_count
    spectra_z = jnp.einsum(
        "wkz,xzy->xwky", forward_table, grid_field, precision=lax.Precision.HIGHEST
    )
    cosine_y, sine_y = wave_tables(ny, ny, ny)
    pencils = transform_rows(
        lax.all_to_all(spectra_z, "cell", split_axis=2, concat_axis=3, tiled=True),
        cosine_y,
        sine_y,
        1.0,
    )
    columns = lax.all_to_all(pencils, "slab", split_axis=3, concat_axis=0, tiled=True)
    col_width = columns.shape[2] * columns.shape[3]
    flat_rows = columns.reshape(nx, 2 * col_width)
    first_row = lax.axis_index("cell") * depth_count
    kernel_ids = lax.dynamic_slice_in_dim(freq_ids, first_row, depth_count, 0)
    kernel = jnp.take(spectrum, kernel_ids, axis=1).reshape(nx, col_width) * (1.0 / (nx * ny * nz))
    kernel_both = jnp.concatenate([kernel, kernel], axis=1)
    slab_count = lax.axis_size("slab")
    local_rows = nx // slab_count
    cosine_s, sine_s = wave_tables(slab_count, slab_count, slab_count)
    cosine_r, sine_r = wave_tables(local_rows, local_rows, local_rows)
    twist_cos, twist_sin = wave_tables(slab_count, local_rows, nx)
    twist_cos = twist_cos[:, :, None]
    twist_sin = twist_sin[:, :, None]
    section_one = transform_axis(
        "ks,src->krc",
        cosine_s,
        sine_s,
        flat_rows.reshape(slab_count, local_rows, 2 * col_width),
        1.0,
    )
    section_one = twiddle(section_one, twist_cos, twist_sin, 1.0)
    section_two = transform_axis("jr,krc->jkc", cosine_r, sine_r, section_one, 1.0)
    weighted = section_two.reshape(nx, 2 * col_width) * kernel_both
    section_one = transform_axis(
        "rj,jkc->krc",
        cosine_r,
        sine_r,
        weighted.reshape(local_rows, slab_count, 2 * col_width),
        -1.0,
    )
    section_one = twiddle(section_one, twist_cos, twist_sin, -1.0)
    section_two = transform_axis("sk,krc->src", cosine_s, sine_s, section_one, -1.0)
    returned_x = section_two.reshape(nx, 2 * col_width)
    returned = lax.all_to_all(
        returned_x.reshape(columns.shape), "slab", split_axis=0, concat_axis=3, tiled=True
    )
    inverse_rows = transform_rows(returned, cosine_y, sine_y, -1.0)
    grid_potential = jnp.einsum(
        "wkz,xwky->xzy",
        backward_table,
        lax.all_to_all(inverse_rows, "cell", split_axis=3, concat_axis=2, tiled=True),
        precision=lax.Precision.HIGHEST,
    )
    tile_potential = (
        grid_potential.reshape(cell_planes, TX, NZC, TZ, rows_cell, TY)
        .transpose(1, 5, 3, 0, 4, 2)
        .reshape(TX * TY * TZ, cell_planes, cell_cols)
    )
    far_field = jnp.einsum(
        "ptxc,txc->pxc", projection, tile_potential, precision=lax.Precision.HIGHEST
    )
    block = masked.reshape(panels, cell_planes, rows_cell, NZC)
    extended = padded(block, (("slab", 1), ("cell", 2)), 1)
    flat_ext = extended.reshape(panels, -1)
    step_x = neighbours // 9 - 1
    step_y = neighbours // 3 % 3 - 1
    step_z = neighbours % 3 - 1
    plane_ids = lax.broadcasted_iota(jnp.int32, neighbours.shape, 1)
    col_ids = lax.broadcasted_iota(jnp.int32, neighbours.shape, 2)
    row_ids = col_ids // NZC
    depth_ids = col_ids % NZC
    near_ids = ((plane_ids + step_x + 1) * (rows_cell + 2) + row_ids + step_y + 1) * NZC + (
        depth_ids + step_z
    ) % NZC
    near_count = neighbours.shape[0]
    picked = jnp.take(flat_ext, near_ids.reshape(-1), axis=1).reshape(
        panels, near_count, cell_planes, cell_cols
    )
    near_field = jnp.einsum("kpqxc,qkxc->pxc", near_blocks, picked, precision=lax.Precision.HIGHEST)
    return (far_field + near_field) * panel_mask


def solution(mesh):
    in_specs = (
        P(None, "slab", "cell"),
        P("slab", "cell"),
        P(None, None, "slab", "cell"),
        P(None, None, None, "slab", "cell"),
        P(None, "slab", "cell"),
        P(None, None, "slab"),
    )
    out_specs = P(None, "slab", "cell")
    return jax.shard_map(
        per_device, mesh=mesh, in_specs=in_specs, out_specs=out_specs, check_vma=False
    )
```

```python
import functools
import math

import jax
import jax.numpy as jnp
import ml_dtypes
import numpy as np
from jax import lax
from jax.experimental import pallas as pl
from jax.experimental.pallas import tpu as pltpu
from jax.sharding import PartitionSpec as P

TX = 4
TY = 4
TZ = 4
NZC = 16
LANES = 128
CHUNKS = 2
VMEM_LIMIT = 62 * 1024 * 1024


def halves(table):
    high = table.astype(np.float32).astype(ml_dtypes.bfloat16)
    low = (table - high.astype(np.float64)).astype(np.float32).astype(ml_dtypes.bfloat16)
    return (high, low)


def wave(rows, cols, length):
    angle = (rows[:, None] * cols[None, :] % length) * (2.0 * math.pi / length)
    return (np.cos(angle), np.sin(angle))


class Plan:
    def __init__(self, slabs, cells, panels, cell_planes, cell_cols, near, nx, nz, ny):
        self.slabs, self.cells = (slabs, cells)
        self.panels, self.cell_planes, self.cell_cols, self.near = (panels, cell_planes, cell_cols, near)
        self.nx, self.ny, self.nz = (nx, ny, nz)
        self.slots = slabs * cells
        self.tx_chunk = TX // CHUNKS
        self.width = cell_planes * self.tx_chunk
        self.y_lanes = LANES // self.width if self.width else 1
        self.row_block = LANES // NZC
        self.step_blocks = self.y_lanes // TY
        self.steps = cell_cols // (LANES * self.step_blocks) if self.step_blocks else 0
        self.x_chunk = nx // CHUNKS
        self.ky_local = ny // slabs
        self.piece_rows = 2 * self.steps * self.row_block
        self.half = slabs // 2
        self.outer = math.gcd(self.half, 2)
        self.inner = self.half // self.outer

    def fits(self):
        return (
            self.slots * 2 == self.nz
            and self.cell_planes == 8
            and self.step_blocks * TY * self.width == LANES
            and self.slabs % self.y_lanes == 0
            and self.ky_local % 8 == 0
            and self.steps * self.step_blocks * LANES == self.cell_cols
            and self.x_chunk % LANES == 0
            and self.nx == self.ny == 4 * LANES
            and self.ny % 1024 == self.nx % 1024 == 512
        )

    def depth_tables(self):
        depth = np.arange(NZC)[None, :] * TZ + np.arange(TZ)[:, None]
        scale = 1.0 / (self.nx * self.ny * self.nz)
        forward = np.zeros((self.slots, 2, self.row_block, TZ, self.row_block, NZC))
        backward = np.zeros_like(forward)
        for freq in range(self.slots):
            angle = (freq * depth % self.nz) * (2.0 * math.pi / self.nz)
            real, imag = (np.cos(angle), -np.sin(angle))
            factor = 2.0 * scale
            if freq == 0:
                imag = np.cos(depth * math.pi)
                factor = scale
            for row in range(self.row_block):
                forward[freq, 0, row, :, row, :] = real
                forward[freq, 1, row, :, row, :] = imag
                backward[freq, 0, row, :, row, :] = factor * real
                backward[freq, 1, row, :, row, :] = factor * imag
        shape = (self.slots * 2 * self.row_block, TZ * LANES)
        return (forward.reshape(shape), backward.reshape(shape))

    def y_rows(self):
        parity, cell, step, block, tile, row = np.meshgrid(
            *[np.arange(n) for n in (2, self.cells, self.steps, self.step_blocks, TY // 2, self.row_block)],
            indexing="ij",
        )
        cell_row = ((cell * self.steps + step) * self.step_blocks + block) * self.row_block + row
        return (cell_row * TY + 2 * tile + parity).reshape(2, -1)

    def x_columns(self):
        parity, slab, tile, plane = np.meshgrid(
            *[np.arange(n) for n in (2, self.slabs, TX // 2, self.cell_planes)], indexing="ij"
        )
        return ((slab * self.cell_planes + plane) * TX + 2 * tile + parity).reshape(2, -1)

    def row_of(self, cell, step, place):
        block, tile = (place // TY, place % TY)
        inner = (cell * self.steps + step) * self.step_blocks + block
        return (tile % 2) * (self.ny // 2) + (inner * (TY // 2) + tile // 2) * self.row_block


def split(value):
    high = value.astype(jnp.bfloat16)
    low = (value - high.astype(jnp.float32)).astype(jnp.bfloat16)
    return (high, low)


def product(left, right, dims=((1,), (0,))):
    first = jnp.concatenate([left[0], left[0], left[1]], axis=dims[0][0])
    second = jnp.concatenate([right[0], right[1], right[0]], axis=dims[1][0])
    return lax.dot_general(first, second, (dims, ((), ())), preferred_element_type=jnp.float32)


def swap_groups(parts, width):
    count = len(parts)
    lane = lax.broadcasted_iota(jnp.int32, parts[0].shape, 1)
    parts = list(parts)
    step = count // 2
    while step >= 1:
        shift = step * width
        upper = (lane // shift) % 2 == 1
        for i in range(count):
            if i & step:
                continue
            first, second = (parts[i], parts[i + step])
            parts[i] = jnp.where(upper, pltpu.roll(second, shift, 1), first)
            parts[i + step] = jnp.where(upper, second, pltpu.roll(first, LANES - shift, 1))
        step //= 2
    return parts


def tile_copies(plan, chunk, projection, held, sems):
    return [
        pltpu.make_async_copy(projection.at[:, tx, chunk], held.at[tx], sems.at[tx])
        for tx in range(plan.tx_chunk)
    ]


def project_kernel(plan, chunk, *refs):
    edges = chunk == CHUNKS - 1
    count_in = 5 if edges else 4
    arrays_in, projection, out = (refs[:count_in], refs[count_in], refs[count_in + 1])
    scratch, held, sems = refs[count_in + 2 : count_in + 5]
    arrays = refs[count_in + 5 :]
    charges, counts, high, low = arrays[:4]
    planes = plan.cell_planes
    first = plan.tx_chunk
    loads = [
        pltpu.make_async_copy(source, place, sems.at[first + n])
        for n, (source, place) in enumerate(zip(arrays_in, arrays))
    ]
    copies = tile_copies(plan, chunk, projection, held, sems)
    for copy in loads[:2] + copies + loads[2:]:
        copy.start()
    for copy in loads[:2]:
        copy.wait()
    for tx, copy in enumerate(copies):
        copy.wait()

        def body(place, carry, tx=tx):
            lanes = pl.ds(pl.multiple_of(place * LANES, LANES), LANES)
            count = counts[:, lanes]
            own = [jnp.where(count > p, charges[p, :, lanes], 0.0) for p in range(plan.panels)]
            for ty in range(TY):
                row = ((place * TY + ty) * plan.tx_chunk + tx) * planes
                rows = pl.ds(pl.multiple_of(row, planes), planes)
                for tz in range(TZ):
                    t = ty * TZ + tz
                    total = held[tx, 0, t, :, lanes] * own[0]
                    for p in range(1, plan.panels):
                        total = total + held[tx, p, t, :, lanes] * own[p]
                    scratch[rows, tz * LANES : (tz + 1) * LANES] = total
            return carry

        lax.fori_loop(0, plan.steps * plan.step_blocks, body, 0)
    for copy in loads[2:]:
        copy.wait()
    spectra = product(split(scratch[...]), (high[...], low[...])).T
    shape = (plan.slots, 2, plan.row_block, LANES)
    for step in range(plan.steps):
        value = spectra[:, step * LANES : (step + 1) * LANES].reshape(shape)
        for part in range(2):
            row = (part * plan.steps + step) * plan.row_block
            out[:, row : row + plan.row_block] = value[:, part]
    if edges:
        out[:, plan.piece_rows :] = arrays[4][...]


def held_shape(plan):
    cols = plan.steps * plan.step_blocks * LANES
    return (plan.tx_chunk, plan.panels, TY * TZ, plan.cell_planes, cols)


def piece_shape(plan):
    return (plan.slots, 2, plan.steps, plan.row_block, LANES)


def whole_spec(shape):
    return pl.BlockSpec(shape, lambda i: (0,) * len(shape))


def projection_call(plan, kernel, name, arrays, projection, out_shape):
    return pl.pallas_call(
        kernel,
        in_specs=[pl.BlockSpec(memory_space=pl.ANY)] * (len(arrays) + 1),
        out_specs=pl.BlockSpec(memory_space=pltpu.VMEM),
        out_shape=jax.ShapeDtypeStruct(out_shape, jnp.float32),
        scratch_shapes=[
            pltpu.VMEM((plan.steps * LANES, TZ * LANES), jnp.float32),
            pltpu.VMEM(held_shape(plan), jnp.float32),
            pltpu.SemaphoreType.DMA((plan.tx_chunk + len(arrays),)),
        ]
        + [pltpu.VMEM(array.shape, array.dtype) for array in arrays],
        compiler_params=pltpu.CompilerParams(vmem_limit_bytes=VMEM_LIMIT),
        cost_estimate=pl.CostEstimate(
            flops=2 * math.prod(held_shape(plan)),
            bytes_accessed=4 * math.prod(held_shape(plan)),
            transcendentals=0,
        ),
        name=name,
    )(*arrays, projection)


def project(plan, chunk, charges, counts, projection, high, low, edges):
    kernel = functools.partial(project_kernel, plan, chunk)
    arrays = [charges, counts, high, low] + ([] if edges is None else [edges])
    rows = plan.piece_rows + (0 if edges is None else edges.shape[1])
    return projection_call(plan, kernel, "project_depth", arrays, projection, (plan.slots, rows, LANES))


def far_sign(plan, me_ref):
    slab = lax.rem(me_ref[0], plan.slabs)
    return jnp.where(slab >= plan.half, -1.0, 1.0)


def forward_plane(plan, me_ref, pieces, y_table, x_table, rows_ref, freq_ref, waits=()):
    special = me_ref[0] == 0
    sign = far_sign(plan, me_ref)
    rows = 2 * plan.steps * plan.row_block
    width = plan.x_chunk
    middle = plan.ny // 2
    for cell in range(plan.cells):
        for group in range(plan.slabs // plan.y_lanes):
            first = cell * plan.slabs + group * plan.y_lanes
            parts = [pieces[first + i, :rows] for i in range(plan.y_lanes)]
            parts = swap_groups(parts, plan.width)
            for place, value in enumerate(parts):
                if place % 2 == 1:
                    value = value * sign
                for part in range(2):
                    for step in range(plan.steps):
                        source = (part * plan.steps + step) * plan.row_block
                        row = plan.row_of(cell, step, place)
                        col = part * width + group * LANES
                        rows_ref[row : row + plan.row_block, col : col + LANES] = value[
                            source : source + plan.row_block
                        ]
    for copy in waits:
        copy.wait()
    sums = product((y_table[0][...], y_table[1][...]), split(rows_ref[...]))
    cos_re, cos_im = (sums[:middle, :width], sums[:middle, width:])
    sin_re, sin_im = (sums[middle:, :width], sums[middle:, width:])
    first = lax.broadcasted_iota(jnp.int32, (middle, width), 0) == 0

    @pl.when(jnp.logical_not(special))
    def _():
        freq_ref[:middle] = jnp.where(first, cos_re, cos_re + sin_im)
        freq_ref[middle : 2 * middle] = jnp.where(first, cos_im, cos_im - sin_re)
        freq_ref[2 * middle : 3 * middle] = jnp.where(first, sin_re, cos_re - sin_im)
        freq_ref[3 * middle :] = jnp.where(first, sin_im, cos_im + sin_re)

    @pl.when(special)
    def _():
        freq_ref[:middle] = cos_re
        freq_ref[middle : 2 * middle] = jnp.where(first, sin_re, -sin_re)
        freq_ref[2 * middle : 3 * middle] = cos_im
        freq_ref[3 * middle :] = sin_im

    return product(split(freq_ref[...]), (x_table[0][0], x_table[1][0]))


def backward_plane(plan, me_ref, freqs, x_table, y_table, out, rows_ref):
    special = me_ref[0] == 0
    sign = far_sign(plan, me_ref)
    width = plan.x_chunk
    middle = plan.ny // 2
    sums = product(split(freqs), (x_table[0][0], x_table[1][0]))
    parts = []
    for mirrored, turn in ((0, 1.0), (1, -1.0)):
        re = slice(2 * mirrored * middle, (2 * mirrored + 1) * middle)
        im = slice((2 * mirrored + 1) * middle, (2 * mirrored + 2) * middle)
        parts.append(sums[re, :width] - turn * sums[im, width:])
        parts.append(sums[im, :width] + turn * sums[re, width:])
    re_n, im_n, re_m, im_m = parts
    first = lax.broadcasted_iota(jnp.int32, (middle, width), 0) == 0

    @pl.when(jnp.logical_not(special))
    def _():
        rows_ref[:middle, :width] = jnp.where(first, re_n, re_n + re_m)
        rows_ref[:middle, width:] = jnp.where(first, im_n, im_n + im_m)
        rows_ref[middle:, :width] = jnp.where(first, -re_m, im_n - im_m)
        rows_ref[middle:, width:] = jnp.where(first, -im_m, re_m - re_n)

    @pl.when(special)
    def _():
        rows_ref[:middle, :width] = jnp.where(first, re_n, 2.0 * re_n)
        rows_ref[:middle, width:] = jnp.where(first, re_m, 2.0 * re_m)
        rows_ref[middle:, :width] = jnp.where(first, -im_n, 2.0 * im_n)
        rows_ref[middle:, width:] = jnp.where(first, -im_m, -2.0 * im_m)

    rows_ref[...] = product((y_table[0][...], y_table[1][...]), split(rows_ref[...]))
    for cell in range(plan.cells):
        for group in range(plan.slabs // plan.y_lanes):
            parts = []
            for place in range(plan.y_lanes):
                tiles = []
                for part in range(2):
                    for step in range(plan.steps):
                        row = plan.row_of(cell, step, place)
                        col = part * width + group * LANES
                        tiles.append(rows_ref[row : row + plan.row_block, col : col + LANES])
                value = jnp.concatenate(tiles, axis=0)
                parts.append(value * sign if place % 2 == 1 else value)
            parts = swap_groups(parts, plan.width)
            first = cell * plan.slabs + group * plan.y_lanes
            for i in range(plan.y_lanes):
                out[first + i] = parts[i].reshape(2, plan.steps, plan.row_block, LANES)


def first_plane_kernel(plan, me_ref, pieces, y_high, y_low, x_high, x_low, out, rows_ref, freq_ref):
    out[...] = forward_plane(plan, me_ref, pieces, (y_high, y_low), (x_high, x_low), rows_ref, freq_ref)


def middle_plane_kernel(plan, me_ref, *refs):
    late, refs = (refs[:10], refs[10:])
    strips, refs = (refs[: plan.inner], refs[plan.inner :])
    blocks, refs = (refs[: plan.outer], refs[plan.outer :])
    out, rest, rows_ref, freq_ref, sum_ref, rest_ref, weights = refs[:7]
    held, sems = (refs[7:17], refs[17])
    pieces, yf_high, yf_low, xf_high, xf_low, even, xb_high, xb_low, yb_high, yb_low = held
    slab = lax.rem(me_ref[0], plan.slabs)
    place = lax.rem(slab, plan.half)
    outer_id, inner_id = (place // plan.inner, lax.rem(place, plan.inner))
    copies = [pltpu.make_async_copy(late[n], held[n], sems.at[n]) for n in range(len(held))]
    count = plan.ky_local
    placed = []
    for i in range(plan.inner):
        for j in range(plan.outer):
            owner = lax.rem(outer_id - j + plan.outer, plan.outer) * plan.inner
            owner = owner + lax.rem(inner_id - i + plan.inner, plan.inner)
            rows = pl.ds(pl.multiple_of(owner * count, count), count)
            for m, source in enumerate((strips[i].at[j], blocks[j].at[i])):
                sem = sems.at[len(held) + len(placed)]
                placed.append(pltpu.make_async_copy(source, weights.at[m, rows], sem))
    for copy in copies[:6] + placed + copies[6:]:
        copy.start()
    copies[0].wait()
    cell_first = me_ref[0] - slab
    tile = pieces[cell_first + jnp.where(slab < plan.half, plan.half, 0), plan.piece_rows :]
    parts = plan.nx // LANES
    own_edge = jnp.concatenate([tile[n : n + 1] for n in range(parts)], axis=1)
    edge = jnp.concatenate([tile[n : n + 1] for n in range(parts, 2 * parts)], axis=1)
    special = me_ref[0] == 0
    width = plan.x_chunk
    middle = plan.ny // 2
    x_table = (xf_high.at[pl.ds(0, 1)], xf_low.at[pl.ds(0, 1)])
    odd = forward_plane(
        plan, me_ref, pieces, (yf_high, yf_low), x_table, rows_ref, freq_ref, copies[1:5]
    )
    for copy in copies[5:6] + placed:
        copy.wait()
    row = lax.broadcasted_iota(jnp.int32, (middle, width), 0)
    at_first = row == 0
    for mirrored, turn in ((0, 1.0), (1, -1.0)):
        re = slice(2 * mirrored * middle, (2 * mirrored + 1) * middle)
        im = slice((2 * mirrored + 1) * middle, (2 * mirrored + 2) * middle)
        results = []
        for upper in range(2):
            cols = slice(upper * width, (upper + 1) * width)
            plane = weights[mirrored, :, cols]
            if mirrored:
                second = jnp.where(at_first, own_edge[:, cols], plane)
                weight = jnp.where(special, plane, second)
            else:
                weight = plane
                second = jnp.where(at_first & special, edge[0:1, cols], plane)
            re_sums = even[re] - odd[re] if upper else even[re] + odd[re]
            im_sums = even[im] - odd[im] if upper else even[im] + odd[im]
            real = weight * re_sums[:, :width] + (turn * second) * im_sums[:, width:]
            imag = second * im_sums[:, :width] - (turn * weight) * re_sums[:, width:]
            results.append((real, imag))
        for part, rows in enumerate((re, im)):
            below, above = (results[0][part], results[1][part])
            sum_ref[rows] = below + above
            rest_ref[rows] = below - above
    last = pltpu.make_async_copy(rest_ref, rest, sems.at[len(held) + 2 * plan.half])
    last.start()
    for copy in copies[6:]:
        copy.wait()
    backward_plane(plan, me_ref, sum_ref[...], (xb_high, xb_low), (yb_high, yb_low), out, rows_ref)
    last.wait()


def last_plane_kernel(plan, me_ref, freqs, x_high, x_low, y_high, y_low, out, rows_ref):
    backward_plane(plan, me_ref, freqs[...], (x_high, x_low), (y_high, y_low), out, rows_ref)


def plane_call(plan, kernel, name, me, ready, arrays, tables, late, out_specs, out_shapes, scratch, work):
    specs = [pl.BlockSpec(memory_space=pltpu.VMEM)] * len(ready)
    specs += [whole_spec(array.shape) for array in arrays]
    flat = []
    for pair, chunk in tables:
        for table in pair:
            if chunk is None:
                specs.append(whole_spec(table.shape))
            else:
                specs.append(pl.BlockSpec((1,) + table.shape[1:], lambda i, chunk=chunk: (chunk, 0, 0)))
            flat.append(table)
    specs += [pl.BlockSpec(memory_space=pl.ANY)] * len(late)
    size = sum(4 * array.size for array in list(ready) + list(arrays) + list(late))
    return pl.pallas_call(
        functools.partial(kernel, plan),
        grid=(1,) if tables else (),
        in_specs=[pl.BlockSpec(memory_space=pltpu.SMEM)] + specs,
        out_specs=out_specs,
        out_shape=[jax.ShapeDtypeStruct(shape, jnp.float32) for shape in out_shapes],
        scratch_shapes=scratch,
        compiler_params=pltpu.CompilerParams(vmem_limit_bytes=VMEM_LIMIT),
        cost_estimate=pl.CostEstimate(
            flops=work * 12 * plan.nx * plan.ny * plan.x_chunk,
            bytes_accessed=size + sum(2 * table.size for table in flat),
            transcendentals=0,
        ),
        name=name,
    )(me, *ready, *arrays, *flat, *late)


def gather_kernel(
    plan, chunk, sent, high_in, low_in, before_in, counts_in, projection, out, scratch, held, sems,
    pieces, high, low, before, counts
):
    planes = plan.cell_planes
    rows = plan.slots * 2 * plan.row_block
    first = plan.tx_chunk
    copies = tile_copies(plan, chunk, projection, held, sems)
    pairs = ((sent, pieces), (high_in, high), (low_in, low), (before_in, before), (counts_in, counts))
    loads = [pltpu.make_async_copy(*pair, sems.at[first + n]) for n, pair in enumerate(pairs)]
    for copy in loads[:3] + copies + loads[3:]:
        copy.start()
    for copy in loads[:3]:
        copy.wait()
    columns = [pieces[:, :, step].reshape(rows, LANES) for step in range(plan.steps)]
    scratch[...] = product(split(jnp.concatenate(columns, axis=1).T), (high[...], low[...]))
    for copy in loads[3:]:
        copy.wait()
    for tx in range(plan.tx_chunk):
        copies[tx].wait()
        last = chunk == CHUNKS - 1 and tx == plan.tx_chunk - 1

        def body(place, carry, tx=tx, last=last):
            lanes = pl.ds(pl.multiple_of(place * LANES, LANES), LANES)
            far = [(before if tx == 0 else out)[p, :, lanes] for p in range(plan.panels)]
            for ty in range(TY):
                row = ((place * TY + ty) * plan.tx_chunk + tx) * planes
                rows_at = pl.ds(pl.multiple_of(row, planes), planes)
                for tz in range(TZ):
                    t = ty * TZ + tz
                    potential = scratch[rows_at, tz * LANES : (tz + 1) * LANES]
                    for p in range(plan.panels):
                        far[p] = far[p] + held[tx, p, t, :, lanes] * potential
            for p in range(plan.panels):
                out[p, :, lanes] = jnp.where(counts[:, lanes] > p, far[p], 0.0) if last else far[p]
            return carry

        lax.fori_loop(0, plan.steps * plan.step_blocks, body, 0)


def gather(plan, chunk, counts, before, projection, high, low, pieces):
    kernel = functools.partial(gather_kernel, plan, chunk)
    arrays = [pieces, high, low, before, counts]
    return projection_call(plan, kernel, "depth_gather", arrays, projection, before.shape)


def near_kernel(plan, extended, codes, blocks_ref, out):
    step = pl.program_id(0)
    lane = lax.broadcasted_iota(jnp.int32, (plan.cell_planes, LANES), 1)
    depth = lane % NZC
    digits = []
    for k in range(plan.near):
        code = codes[k]
        digits.append((code // 9, code // 3 % 3, code % 3))
    total = [None] * plan.panels
    for q in range(plan.panels):
        shifted = []
        for dx in range(3):
            before, here, after = (
                extended[q, dx, :, pl.ds(pl.multiple_of((step + i) * LANES, LANES), LANES)] for i in range(3)
            )
            up = jnp.where(lane < NZC, pltpu.roll(before, NZC, 1), pltpu.roll(here, NZC, 1))
            down = jnp.where(
                lane >= LANES - NZC, pltpu.roll(after, LANES - NZC, 1), pltpu.roll(here, LANES - NZC, 1)
            )
            for value in (up, here, down):
                under = jnp.where(
                    depth == 0, pltpu.roll(value, LANES - NZC + 1, 1), pltpu.roll(value, 1, 1)
                )
                over = jnp.where(
                    depth == NZC - 1, pltpu.roll(value, NZC - 1, 1), pltpu.roll(value, LANES - 1, 1)
                )
                shifted.append((under, value, over))
        for k in range(plan.near):
            digit_x, digit_y, digit_z = digits[k]

            def choose(digit, options):
                return jnp.where(digit == 0, options[0], jnp.where(digit == 1, options[1], options[2]))

            by_z = [choose(digit_z, options) for options in shifted]
            by_y = [choose(digit_y, by_z[3 * i : 3 * i + 3]) for i in range(3)]
            picked = choose(digit_x, by_y)
            for p in range(plan.panels):
                term = blocks_ref[k, p, q] * picked
                total[p] = term if total[p] is None else total[p] + term
    for p in range(plan.panels):
        out[p] = total[p]


def near_field(plan, extended, neighbours, near_blocks):
    return pl.pallas_call(
        functools.partial(near_kernel, plan),
        grid=(plan.cell_cols // LANES,),
        in_specs=[
            whole_spec(extended.shape),
            pl.BlockSpec((plan.near, plan.cell_planes, LANES), lambda i: (0, 0, i)),
            pl.BlockSpec(
                (plan.near, plan.panels, plan.panels, plan.cell_planes, LANES), lambda i: (0, 0, 0, 0, i)
            ),
        ],
        out_specs=pl.BlockSpec((plan.panels, plan.cell_planes, LANES), lambda i: (0, 0, i)),
        out_shape=jax.ShapeDtypeStruct((plan.panels, plan.cell_planes, plan.cell_cols), jnp.float32),
        compiler_params=pltpu.CompilerParams(vmem_limit_bytes=VMEM_LIMIT),
        cost_estimate=pl.CostEstimate(
            flops=2 * near_blocks.size, bytes_accessed=4 * near_blocks.size, transcendentals=0
        ),
        name="near_blocks",
    )(extended, neighbours, near_blocks)


def ring_pairs(axis):
    count = lax.axis_size(axis)
    up = [(i, (i + 1) % count) for i in range(count)]
    return (up, [(j, i) for i, j in up])


def extend_rows(plan, masked):
    up, down = ring_pairs("cell")
    left = lax.ppermute(masked[:, :, -NZC:], "cell", up)
    right = lax.ppermute(masked[:, :, :NZC], "cell", down)
    return (left, right)


def extend_planes(plan, masked, left, right):
    rest = jnp.zeros((plan.panels, plan.cell_planes, LANES - NZC), jnp.float32)
    wide = jnp.concatenate([rest, left, masked, right, rest], axis=2)
    up, down = ring_pairs("slab")
    before = lax.ppermute(wide[:, -1:], "slab", up)
    after = lax.ppermute(wide[:, :1], "slab", down)
    whole = jnp.concatenate([before, wide, after], axis=1)
    planes = plan.cell_planes
    return jnp.stack([whole[:, i : i + planes] for i in range(3)], axis=1)


def pick_kernel(plan, ids_ref, by_depth, *refs):
    outs, sems = (refs[:-1], refs[-1])
    cell, slab = (ids_ref[0], ids_ref[1])
    half_id, place = (slab // plan.half, lax.rem(slab, plan.half))
    first = cell * plan.slabs + half_id * plan.half
    copies = []
    for j in range(plan.outer):
        part = lax.rem(place // plan.inner + j, plan.outer) * plan.inner
        for i in range(plan.inner):
            n = len(copies)
            copies.append(
                pltpu.make_async_copy(by_depth.at[first + part + i], outs[j].at[i], sems.at[n])
            )
            freq = first + part + lax.rem(place + i, plan.inner)
            mirror = jnp.where(freq == 0, plan.nz // 2, plan.nz - freq)
            copies.append(
                pltpu.make_async_copy(by_depth.at[mirror], outs[plan.outer + i].at[j], sems.at[n + 1])
            )
    for copy in copies:
        copy.start()
    for copy in copies:
        copy.wait()


def pick_planes(plan, ids, spectrum):
    by_depth = jnp.transpose(spectrum, (1, 2, 0))
    shapes = [(plan.inner,) + by_depth.shape[1:]] * plan.outer
    shapes += [(plan.outer,) + by_depth.shape[1:]] * plan.inner
    picked = pl.pallas_call(
        functools.partial(pick_kernel, plan),
        in_specs=[pl.BlockSpec(memory_space=pltpu.SMEM), pl.BlockSpec(memory_space=pl.ANY)],
        out_specs=[pl.BlockSpec(memory_space=pltpu.VMEM)] * len(shapes),
        out_shape=[jax.ShapeDtypeStruct(shape, jnp.float32) for shape in shapes],
        scratch_shapes=[pltpu.SemaphoreType.DMA((2 * plan.half,))],
        cost_estimate=pl.CostEstimate(
            flops=0, bytes_accessed=8 * sum(math.prod(shape) for shape in shapes), transcendentals=0
        ),
        name="pick_planes",
    )(ids, by_depth)
    return (picked[: plan.outer], picked[plan.outer :])


def outer_shift(plan, value, j):
    if j == 0:
        return value
    pairs = []
    for source in range(plan.slabs):
        base = source // plan.half * plan.half
        pairs.append((source, base + (source - base + j * plan.inner) % plan.half))
    return lax.ppermute(value, "slab", pairs)


def inner_shift(plan, value, i):
    if i == 0:
        return value
    pairs = []
    for source in range(plan.slabs):
        base = source // plan.inner * plan.inner
        pairs.append((source, base + (source + i) % plan.inner))
    return lax.ppermute(value, "slab", pairs)


def edge_weights(plan, rows):
    middle = plan.nz // 2
    turned = jnp.concatenate([rows[middle : middle + 1], jnp.flip(rows, 0)], axis=0)[: plan.slots]
    shape = (plan.slots, plan.nx // LANES, LANES)
    plane = jnp.broadcast_to(rows[0].reshape(shape[1:]), shape)
    return jnp.concatenate([turned.reshape(shape), plane], axis=1)


def second_weights(plan, plain, mirror):
    slab = lax.axis_index("slab")
    strips = []
    for i in range(plan.inner):
        place = lax.rem(slab + i, plan.inner)
        rows = [lax.dynamic_slice_in_dim(block, place, 1, 0) for block in plain]
        strips.append(inner_shift(plan, jnp.concatenate(rows, axis=0), i))
    blocks = [outer_shift(plan, jnp.stack([m[j] for m in mirror]), j) for j in range(plan.outer)]
    return strips + blocks


def per_device(charges, counts, projection, near_blocks, neighbours, spectrum):
    panels, cell_planes, cell_cols = charges.shape
    cells, slabs = (lax.axis_size("cell"), lax.axis_size("slab"))
    nx, nz, local = spectrum.shape
    plan = Plan(slabs, cells, panels, cell_planes, cell_cols, neighbours.shape[0], nx, nz, local * slabs)
    if not plan.fits():
        return plain_device(charges, counts, projection, near_blocks, neighbours, spectrum)
    me = (lax.axis_index("cell") * slabs + lax.axis_index("slab")).astype(jnp.int32).reshape(1)
    forward_table, backward_table = plan.depth_tables()
    depth_forward, depth_backward = (halves(forward_table.T), halves(backward_table))
    y_rows, x_cols, low_ids = (plan.y_rows().reshape(-1), plan.x_columns(), np.arange(plan.ny // 2))
    cos_y, sin_y = wave(low_ids, y_rows, plan.ny)
    sin_y[0] = 1.0 - 2.0 * (y_rows % 2)
    y_forward = halves(np.concatenate([cos_y, sin_y], axis=0))
    y_backward = halves(np.concatenate([cos_y.T, -sin_y.T], axis=1))
    x_waves = [wave(cols, low_ids, plan.nx) for cols in x_cols]
    x_forward = halves(np.stack([np.concatenate(pair, axis=1) for pair in x_waves]))
    x_backward = halves(np.stack([np.concatenate([t.T for t in pair], axis=1) for pair in x_waves]))
    split_projection = projection.reshape(
        (panels, TX // CHUNKS, CHUNKS, TY * TZ, cell_planes, cell_cols)
    )
    axes = ("cell", "slab")

    def exchange(pieces):
        return lax.all_to_all(pieces, axes, split_axis=0, concat_axis=0, tiled=True)

    def values(*shapes):
        return [pltpu.VMEM(shape, jnp.float32) for shape in shapes]

    rows_shape = (plan.ny, 2 * plan.x_chunk)
    freq_shape = (2 * plan.ny, plan.x_chunk)
    both_shape = (2 * plan.ny, plan.nx)
    ids = jnp.stack([lax.axis_index("cell"), lax.axis_index("slab")]).astype(jnp.int32)
    slot = lax.broadcasted_iota(jnp.int32, charges.shape, 0)
    masked = jnp.where(slot < counts[None], charges, 0.0)
    rows = jnp.transpose(spectrum[:, :, 0], (1, 0))
    first = project(plan, 0, charges, counts, split_projection, *depth_forward, None)
    first, ids = lax.optimization_barrier((first, ids))
    even_pieces = exchange(first)
    edges = edge_weights(plan, rows)
    second = project(plan, 1, charges, counts, split_projection, *depth_forward, edges)
    plain, mirror = pick_planes(plan, ids, spectrum)
    plain = [outer_shift(plan, value, j) for j, value in enumerate(plain)]
    mirror = [inner_shift(plan, value, i) for i, value in enumerate(mirror)]
    second, masked = lax.optimization_barrier((second, masked))
    left, right = extend_rows(plan, masked)
    second, left, right, *moved = lax.optimization_barrier((second, left, right, *plain, *mirror))
    plain, mirror = (moved[: plan.outer], moved[plan.outer :])
    odd_pieces = exchange(second)
    strips = second_weights(plan, plain, mirror)
    in_vmem = pl.BlockSpec(memory_space=pltpu.VMEM)
    in_place = pl.BlockSpec(memory_space=pl.ANY)
    (even,) = plane_call(
        plan, first_plane_kernel, "even_planes", me, [], [even_pieces],
        [(y_forward, None), (x_forward, 0)], [], [whole_spec(both_shape)], [both_shape],
        values(rows_shape, freq_shape), 2,
    )
    even, masked = lax.optimization_barrier((even, masked))
    extended = extend_planes(plan, masked, left, right)
    odd_pieces, extended = lax.optimization_barrier((odd_pieces, extended))
    late = [odd_pieces, *y_forward, x_forward[0][1:], x_forward[1][1:], even]
    late += [x_backward[0][:1], x_backward[1][:1], *y_backward]
    copies = [pltpu.VMEM(array.shape, array.dtype) for array in late]
    copies.append(pltpu.SemaphoreType.DMA((len(late) + 2 * plan.half + 1,)))
    back, rest = plane_call(
        plan, middle_plane_kernel, "middle_planes", me, [], [], [], late + strips, [in_vmem, in_place], [piece_shape(plan), freq_shape],
        values(rows_shape, freq_shape, freq_shape, freq_shape, (2, plan.ny // 2, plan.nx)) + copies, 4,
    )
    even_back = exchange(back)
    (back,) = plane_call(
        plan, last_plane_kernel, "odd_planes", me, [], [rest],
        [(x_backward, 1), (y_backward, None)], [], [whole_spec(piece_shape(plan))], [piece_shape(plan)],
        values(rows_shape), 2,
    )
    total = near_field(plan, extended, neighbours, near_blocks)
    back, total = lax.optimization_barrier((back, total))
    odd_back = exchange(back)
    total = gather(plan, 0, counts, total, split_projection, *depth_backward, even_back)
    return gather(plan, 1, counts, total, split_projection, *depth_backward, odd_back)


def padded(value, sides, width):
    for axis, dim in sides:
        count, length = (lax.axis_size(axis), value.shape[dim])
        up = [(i, (i + 1) % count) for i in range(count)]
        down = [(j, i) for i, j in up]
        last = lax.slice_in_dim(value, length - width, length, axis=dim)
        first = lax.slice_in_dim(value, 0, width, axis=dim)
        before = lax.ppermute(last, axis, up)
        after = lax.ppermute(first, axis, down)
        value = jnp.concatenate([before, value, after], axis=dim)
    return value


def wave_tables(row_count, col_count, length):
    products = (
        lax.broadcasted_iota(jnp.int32, (row_count, col_count), 0)
        * lax.broadcasted_iota(jnp.int32, (row_count, col_count), 1)
        % length
    )
    angle_rad = products.astype(jnp.float32) * (2.0 * math.pi / length)
    return (jnp.cos(angle_rad), jnp.sin(angle_rad))


def depth_rows(nz, freq_ids, valid, weights):
    depth_ids = lax.broadcasted_iota(jnp.int32, (freq_ids.shape[0], nz), 1)
    products = freq_ids[:, None] * depth_ids % nz
    angle_rad = products.astype(jnp.float32) * (2.0 * math.pi / nz)
    basis = jnp.stack([jnp.cos(angle_rad), -jnp.sin(angle_rad)])
    return (basis * valid[None, :, None], basis * weights[None, :, None])


def half_depth_tables(nz, cell_count):
    lower = nz // (2 * cell_count)
    row_ids = lax.broadcasted_iota(jnp.int32, (cell_count * (lower + 1),), 0)
    block_ids = row_ids // (lower + 1)
    slot_ids = row_ids % (lower + 1)
    freq_ids = jnp.where(slot_ids < lower, block_ids * lower + slot_ids, nz // 2)
    valid = jnp.where((slot_ids < lower) | (block_ids == 0), 1.0, 0.0).astype(jnp.float32)
    doubled = jnp.where((slot_ids < lower) & (freq_ids > 0), 2.0, 1.0).astype(jnp.float32)
    forward_table, backward_table = depth_rows(nz, freq_ids, valid, valid * doubled)
    return (forward_table, backward_table, freq_ids)


def combine_halves(first_part, second, orient):
    half_width = first_part.shape[-1] // 2
    real_part = first_part[..., :half_width] + orient * second[..., half_width:]
    imag_part = first_part[..., half_width:] - orient * second[..., :half_width]
    return jnp.concatenate([real_part, imag_part], axis=-1)


def transform_axis(pattern, cosine, sine_tab, values, orient):
    first_part = jnp.einsum(pattern, cosine, values, precision=lax.Precision.HIGHEST)
    second = jnp.einsum(pattern, sine_tab, values, precision=lax.Precision.HIGHEST)
    return combine_halves(first_part, second, orient)


def twiddle(values, twist_cos, twist_sin, orient):
    half_width = values.shape[-1] // 2
    real_part = values[..., :half_width]
    imag_part = values[..., half_width:]
    new_real = real_part * twist_cos + orient * imag_part * twist_sin
    new_imag = imag_part * twist_cos - orient * real_part * twist_sin
    return jnp.concatenate([new_real, new_imag], axis=-1)


def transform_rows(planes_block, cosine, sine_tab, orient):
    flat_rows = planes_block.reshape(-1, planes_block.shape[-1])
    first_part = jnp.dot(flat_rows, cosine, precision=lax.Precision.HIGHEST).reshape(
        planes_block.shape
    )
    second = jnp.dot(flat_rows, sine_tab, precision=lax.Precision.HIGHEST).reshape(
        planes_block.shape
    )
    real_part = first_part[:, 0] + orient * second[:, 1]
    imag_part = first_part[:, 1] - orient * second[:, 0]
    return jnp.stack([real_part, imag_part], axis=1)


def plain_device(charges, counts, projection, near_blocks, neighbours, spectrum):
    panels, cell_planes, cell_cols = charges.shape
    nx, nz, ny = (spectrum.shape[0], spectrum.shape[1], spectrum.shape[2] * lax.axis_size("slab"))
    planes = cell_planes * TX
    rows_cell = cell_cols // NZC
    slot_ids = lax.broadcasted_iota(jnp.int32, charges.shape, 0)
    panel_mask = (slot_ids < counts[None]).astype(jnp.float32)
    masked = charges * panel_mask
    tile_values = jnp.einsum("ptxc,pxc->txc", projection, masked, precision=lax.Precision.HIGHEST)
    grid_field = (
        tile_values.reshape(TX, TY, TZ, cell_planes, rows_cell, NZC)
        .transpose(3, 0, 5, 2, 4, 1)
        .reshape(planes, nz, rows_cell * TY)
    )
    cell_count = lax.axis_size("cell")
    forward_table, backward_table, freq_ids = half_depth_tables(nz, cell_count)
    depth_count = forward_table.shape[1] // cell_count
    spectra_z = jnp.einsum(
        "wkz,xzy->xwky", forward_table, grid_field, precision=lax.Precision.HIGHEST
    )
    cosine_y, sine_y = wave_tables(ny, ny, ny)
    pencils = transform_rows(
        lax.all_to_all(spectra_z, "cell", split_axis=2, concat_axis=3, tiled=True),
        cosine_y,
        sine_y,
        1.0,
    )
    columns = lax.all_to_all(pencils, "slab", split_axis=3, concat_axis=0, tiled=True)
    col_width = columns.shape[2] * columns.shape[3]
    flat_rows = columns.reshape(nx, 2 * col_width)
    first_row = lax.axis_index("cell") * depth_count
    kernel_ids = lax.dynamic_slice_in_dim(freq_ids, first_row, depth_count, 0)
    kernel = jnp.take(spectrum, kernel_ids, axis=1).reshape(nx, col_width) * (1.0 / (nx * ny * nz))
    kernel_both = jnp.concatenate([kernel, kernel], axis=1)
    slab_count = lax.axis_size("slab")
    local_rows = nx // slab_count
    cosine_s, sine_s = wave_tables(slab_count, slab_count, slab_count)
    cosine_r, sine_r = wave_tables(local_rows, local_rows, local_rows)
    twist_cos, twist_sin = wave_tables(slab_count, local_rows, nx)
    twist_cos = twist_cos[:, :, None]
    twist_sin = twist_sin[:, :, None]
    section_one = transform_axis(
        "ks,src->krc",
        cosine_s,
        sine_s,
        flat_rows.reshape(slab_count, local_rows, 2 * col_width),
        1.0,
    )
    section_one = twiddle(section_one, twist_cos, twist_sin, 1.0)
    section_two = transform_axis("jr,krc->jkc", cosine_r, sine_r, section_one, 1.0)
    weighted = section_two.reshape(nx, 2 * col_width) * kernel_both
    section_one = transform_axis(
        "rj,jkc->krc",
        cosine_r,
        sine_r,
        weighted.reshape(local_rows, slab_count, 2 * col_width),
        -1.0,
    )
    section_one = twiddle(section_one, twist_cos, twist_sin, -1.0)
    section_two = transform_axis("sk,krc->src", cosine_s, sine_s, section_one, -1.0)
    returned_x = section_two.reshape(nx, 2 * col_width)
    returned = lax.all_to_all(
        returned_x.reshape(columns.shape), "slab", split_axis=0, concat_axis=3, tiled=True
    )
    inverse_rows = transform_rows(returned, cosine_y, sine_y, -1.0)
    grid_potential = jnp.einsum(
        "wkz,xwky->xzy",
        backward_table,
        lax.all_to_all(inverse_rows, "cell", split_axis=3, concat_axis=2, tiled=True),
        precision=lax.Precision.HIGHEST,
    )
    tile_potential = (
        grid_potential.reshape(cell_planes, TX, NZC, TZ, rows_cell, TY)
        .transpose(1, 5, 3, 0, 4, 2)
        .reshape(TX * TY * TZ, cell_planes, cell_cols)
    )
    far_field = jnp.einsum(
        "ptxc,txc->pxc", projection, tile_potential, precision=lax.Precision.HIGHEST
    )
    block = masked.reshape(panels, cell_planes, rows_cell, NZC)
    extended = padded(block, (("slab", 1), ("cell", 2)), 1)
    flat_ext = extended.reshape(panels, -1)
    step_x = neighbours // 9 - 1
    step_y = neighbours // 3 % 3 - 1
    step_z = neighbours % 3 - 1
    plane_ids = lax.broadcasted_iota(jnp.int32, neighbours.shape, 1)
    col_ids = lax.broadcasted_iota(jnp.int32, neighbours.shape, 2)
    row_ids = col_ids // NZC
    depth_ids = col_ids % NZC
    near_ids = ((plane_ids + step_x + 1) * (rows_cell + 2) + row_ids + step_y + 1) * NZC + (
        depth_ids + step_z
    ) % NZC
    near_count = neighbours.shape[0]
    picked = jnp.take(flat_ext, near_ids.reshape(-1), axis=1).reshape(
        panels, near_count, cell_planes, cell_cols
    )
    near_field = jnp.einsum("kpqxc,qkxc->pxc", near_blocks, picked, precision=lax.Precision.HIGHEST)
    return (far_field + near_field) * panel_mask


def solution(mesh):
    in_specs = (
        P(None, "slab", "cell"),
        P("slab", "cell"),
        P(None, None, "slab", "cell"),
        P(None, None, None, "slab", "cell"),
        P(None, "slab", "cell"),
        P(None, None, "slab"),
    )
    out_specs = P(None, "slab", "cell")
    return jax.shard_map(
        per_device, mesh=mesh, in_specs=in_specs, out_specs=out_specs, check_vma=False
    )
```

```python
import functools
import math

import jax
import jax.numpy as jnp
import ml_dtypes
import numpy as np
from jax import lax
from jax.experimental import pallas as pl
from jax.experimental.pallas import tpu as pltpu
from jax.sharding import PartitionSpec as P

TX = 4
TY = 4
TZ = 4
NZC = 16
LANES = 128
CHUNKS = 2
VMEM_LIMIT = 127 * 512 * 1024


def halves(table):
    high = table.astype(np.float32).astype(ml_dtypes.bfloat16)
    low = (table - high.astype(np.float64)).astype(np.float32).astype(ml_dtypes.bfloat16)
    return (high, low)


def wave(rows, cols, length):
    angle = (rows[:, None] * cols[None, :] % length) * (2.0 * math.pi / length)
    return (np.cos(angle), np.sin(angle))


class Plan:
    def __init__(self, slabs, cells, panels, cell_planes, cell_cols, near, nx, nz, ny):
        self.slabs, self.cells = (slabs, cells)
        self.panels, self.cell_planes, self.cell_cols, self.near = (panels, cell_planes, cell_cols, near)
        self.nx, self.ny, self.nz = (nx, ny, nz)
        self.slots = slabs * cells
        self.tx_chunk = TX // CHUNKS
        self.width = cell_planes * self.tx_chunk
        self.y_lanes = LANES // self.width if self.width else 1
        self.row_block = LANES // NZC
        self.step_blocks = self.y_lanes // TY
        self.steps = cell_cols // (LANES * self.step_blocks) if self.step_blocks else 0
        self.x_chunk = nx // CHUNKS
        self.ky_local = ny // slabs
        self.piece_rows = 2 * self.steps * self.row_block
        self.half = slabs // 2
        self.outer = math.gcd(self.half, 2)
        self.inner = self.half // self.outer

    def fits(self):
        return (
            self.slots * 2 == self.nz
            and self.cell_planes == 8
            and self.step_blocks * TY * self.width == LANES
            and self.slabs % self.y_lanes == 0
            and self.ky_local % 8 == 0
            and self.steps * self.step_blocks * LANES == self.cell_cols
            and self.x_chunk % LANES == 0
            and self.nx == self.ny == 4 * LANES
            and self.ny % 1024 == self.nx % 1024 == 512
        )

    def depth_tables(self):
        depth = np.arange(NZC)[None, :] * TZ + np.arange(TZ)[:, None]
        scale = 1.0 / (self.nx * self.ny * self.nz)
        forward = np.zeros((self.slots, 2, self.row_block, TZ, self.row_block, NZC))
        backward = np.zeros_like(forward)
        for freq in range(self.slots):
            angle = (freq * depth % self.nz) * (2.0 * math.pi / self.nz)
            real, imag = (np.cos(angle), -np.sin(angle))
            factor = 2.0 * scale
            if freq == 0:
                imag = np.cos(depth * math.pi)
                factor = scale
            for row in range(self.row_block):
                forward[freq, 0, row, :, row, :] = real
                forward[freq, 1, row, :, row, :] = imag
                backward[freq, 0, row, :, row, :] = factor * real
                backward[freq, 1, row, :, row, :] = factor * imag
        shape = (self.slots * 2 * self.row_block, TZ * LANES)
        return (forward.reshape(shape), backward.reshape(shape))

    def y_rows(self):
        parity, cell, step, block, tile, row = np.meshgrid(
            *[np.arange(n) for n in (2, self.cells, self.steps, self.step_blocks, TY // 2, self.row_block)],
            indexing="ij",
        )
        cell_row = ((cell * self.steps + step) * self.step_blocks + block) * self.row_block + row
        return (cell_row * TY + 2 * tile + parity).reshape(2, -1)

    def x_columns(self):
        parity, slab, tile, plane = np.meshgrid(
            *[np.arange(n) for n in (2, self.slabs, TX // 2, self.cell_planes)], indexing="ij"
        )
        return ((slab * self.cell_planes + plane) * TX + 2 * tile + parity).reshape(2, -1)

    def row_of(self, cell, step, place):
        block, tile = (place // TY, place % TY)
        inner = (cell * self.steps + step) * self.step_blocks + block
        return (tile % 2) * (self.ny // 2) + (inner * (TY // 2) + tile // 2) * self.row_block


def split(value):
    high = value.astype(jnp.bfloat16)
    low = (value - high.astype(jnp.float32)).astype(jnp.bfloat16)
    return (high, low)


def product(left, right, dims=((1,), (0,))):
    first = jnp.concatenate([left[0], left[0], left[1]], axis=dims[0][0])
    second = jnp.concatenate([right[0], right[1], right[0]], axis=dims[1][0])
    return lax.dot_general(first, second, (dims, ((), ())), preferred_element_type=jnp.float32)


def swap_groups(parts, width):
    count = len(parts)
    lane = lax.broadcasted_iota(jnp.int32, parts[0].shape, 1)
    parts = list(parts)
    step = count // 2
    while step >= 1:
        shift = step * width
        upper = (lane // shift) % 2 == 1
        for i in range(count):
            if i & step:
                continue
            first, second = (parts[i], parts[i + step])
            parts[i] = jnp.where(upper, pltpu.roll(second, shift, 1), first)
            parts[i + step] = jnp.where(upper, second, pltpu.roll(first, LANES - shift, 1))
        step //= 2
    return parts


def tile_copies(plan, chunk, projection, held, sems, parts):
    count = TY * TZ // parts
    copies = []
    for tx in range(plan.tx_chunk):
        for part in range(parts):
            rows = pl.ds(part * count, count)
            source = projection.at[:, tx, chunk, rows]
            copies.append(pltpu.make_async_copy(source, held.at[tx, :, rows], sems.at[len(copies)]))
    return copies


def project_kernel(plan, chunk, *refs):
    edges = chunk == CHUNKS - 1
    count_in = 5 if edges else 4
    arrays_in, projection, out = (refs[:count_in], refs[count_in], refs[count_in + 1])
    scratch, held, sems = refs[count_in + 2 : count_in + 5]
    arrays = refs[count_in + 5 :]
    charges, counts, high, low = arrays[:4]
    planes = plan.cell_planes
    copies = tile_copies(plan, chunk, projection, held, sems, TY)
    loads = [
        pltpu.make_async_copy(source, place, sems.at[len(copies) + n])
        for n, (source, place) in enumerate(zip(arrays_in, arrays))
    ]
    for copy in loads[:2] + copies + loads[2:]:
        copy.start()
    for copy in loads[:2]:
        copy.wait()
    for n, copy in enumerate(copies):
        copy.wait()

        def body(place, carry, tx=n // TY, ty=n % TY):
            lanes = pl.ds(pl.multiple_of(place * LANES, LANES), LANES)
            count = counts[:, lanes]
            own = [jnp.where(count > p, charges[p, :, lanes], 0.0) for p in range(plan.panels)]
            row = ((place * TY + ty) * plan.tx_chunk + tx) * planes
            rows = pl.ds(pl.multiple_of(row, planes), planes)
            for tz in range(TZ):
                t = ty * TZ + tz
                total = held[tx, 0, t, :, lanes] * own[0]
                for p in range(1, plan.panels):
                    total = total + held[tx, p, t, :, lanes] * own[p]
                scratch[rows, tz * LANES : (tz + 1) * LANES] = total
            return carry

        lax.fori_loop(0, plan.steps * plan.step_blocks, body, 0)
    for copy in loads[2:]:
        copy.wait()
    spectra = product(split(scratch[...]), (high[...], low[...])).T
    shape = (plan.slots, 2, plan.row_block, LANES)
    for step in range(plan.steps):
        value = spectra[:, step * LANES : (step + 1) * LANES].reshape(shape)
        for part in range(2):
            row = (part * plan.steps + step) * plan.row_block
            out[:, row : row + plan.row_block] = value[:, part]
    if edges:
        out[:, plan.piece_rows :] = arrays[4][...]


def held_shape(plan):
    cols = plan.steps * plan.step_blocks * LANES
    return (plan.tx_chunk, plan.panels, TY * TZ, plan.cell_planes, cols)


def piece_shape(plan):
    return (plan.slots, 2, plan.steps, plan.row_block, LANES)


def whole_spec(shape):
    return pl.BlockSpec(shape, lambda i: (0,) * len(shape))


def projection_call(plan, kernel, name, arrays, projection, out_shape):
    return pl.pallas_call(
        kernel,
        in_specs=[pl.BlockSpec(memory_space=pl.ANY)] * (len(arrays) + 1),
        out_specs=pl.BlockSpec(memory_space=pltpu.VMEM),
        out_shape=jax.ShapeDtypeStruct(out_shape, jnp.float32),
        scratch_shapes=[
            pltpu.VMEM((plan.steps * LANES, TZ * LANES), jnp.float32),
            pltpu.VMEM(held_shape(plan), jnp.float32),
            pltpu.SemaphoreType.DMA((plan.tx_chunk * TY + len(arrays),)),
        ]
        + [pltpu.VMEM(array.shape, array.dtype) for array in arrays],
        compiler_params=pltpu.CompilerParams(vmem_limit_bytes=VMEM_LIMIT),
        cost_estimate=pl.CostEstimate(
            flops=2 * math.prod(held_shape(plan)),
            bytes_accessed=4 * math.prod(held_shape(plan)),
            transcendentals=0,
        ),
        name=name,
    )(*arrays, projection)


def project(plan, chunk, charges, counts, projection, high, low, edges):
    kernel = functools.partial(project_kernel, plan, chunk)
    arrays = [charges, counts, high, low] + ([] if edges is None else [edges])
    rows = plan.piece_rows + (0 if edges is None else edges.shape[1])
    return projection_call(plan, kernel, "project_depth", arrays, projection, (plan.slots, rows, LANES))


def far_sign(plan, me_ref):
    slab = lax.rem(me_ref[0], plan.slabs)
    return jnp.where(slab >= plan.half, -1.0, 1.0)


def forward_plane(plan, me_ref, pieces, y_table, x_table, rows_ref, freq_ref, waits=()):
    special = me_ref[0] == 0
    sign = far_sign(plan, me_ref)
    rows = 2 * plan.steps * plan.row_block
    width = plan.x_chunk
    middle = plan.ny // 2
    for cell in range(plan.cells):
        for group in range(plan.slabs // plan.y_lanes):
            first = cell * plan.slabs + group * plan.y_lanes
            parts = [pieces[first + i, :rows] for i in range(plan.y_lanes)]
            parts = swap_groups(parts, plan.width)
            for place, value in enumerate(parts):
                if place % 2 == 1:
                    value = value * sign
                for part in range(2):
                    for step in range(plan.steps):
                        source = (part * plan.steps + step) * plan.row_block
                        row = plan.row_of(cell, step, place)
                        col = part * width + group * LANES
                        rows_ref[row : row + plan.row_block, col : col + LANES] = value[
                            source : source + plan.row_block
                        ]
    for copy in waits:
        copy.wait()
    sums = product((y_table[0][...], y_table[1][...]), split(rows_ref[...]))
    cos_re, cos_im = (sums[:middle, :width], sums[:middle, width:])
    sin_re, sin_im = (sums[middle:, :width], sums[middle:, width:])
    first = lax.broadcasted_iota(jnp.int32, (middle, width), 0) == 0

    @pl.when(jnp.logical_not(special))
    def _():
        freq_ref[:middle] = jnp.where(first, cos_re, cos_re + sin_im)
        freq_ref[middle : 2 * middle] = jnp.where(first, cos_im, cos_im - sin_re)
        freq_ref[2 * middle : 3 * middle] = jnp.where(first, sin_re, cos_re - sin_im)
        freq_ref[3 * middle :] = jnp.where(first, sin_im, cos_im + sin_re)

    @pl.when(special)
    def _():
        freq_ref[:middle] = cos_re
        freq_ref[middle : 2 * middle] = jnp.where(first, sin_re, -sin_re)
        freq_ref[2 * middle : 3 * middle] = cos_im
        freq_ref[3 * middle :] = sin_im

    return product(split(freq_ref[...]), (x_table[0][0], x_table[1][0]))


def backward_plane(plan, me_ref, freqs, x_table, y_table, out, rows_ref):
    special = me_ref[0] == 0
    sign = far_sign(plan, me_ref)
    width = plan.x_chunk
    middle = plan.ny // 2
    sums = product(split(freqs), (x_table[0][0], x_table[1][0]))
    parts = []
    for mirrored, turn in ((0, 1.0), (1, -1.0)):
        re = slice(2 * mirrored * middle, (2 * mirrored + 1) * middle)
        im = slice((2 * mirrored + 1) * middle, (2 * mirrored + 2) * middle)
        parts.append(sums[re, :width] - turn * sums[im, width:])
        parts.append(sums[im, :width] + turn * sums[re, width:])
    re_n, im_n, re_m, im_m = parts
    first = lax.broadcasted_iota(jnp.int32, (middle, width), 0) == 0

    @pl.when(jnp.logical_not(special))
    def _():
        rows_ref[:middle, :width] = jnp.where(first, re_n, re_n + re_m)
        rows_ref[:middle, width:] = jnp.where(first, im_n, im_n + im_m)
        rows_ref[middle:, :width] = jnp.where(first, -re_m, im_n - im_m)
        rows_ref[middle:, width:] = jnp.where(first, -im_m, re_m - re_n)

    @pl.when(special)
    def _():
        rows_ref[:middle, :width] = jnp.where(first, re_n, 2.0 * re_n)
        rows_ref[:middle, width:] = jnp.where(first, re_m, 2.0 * re_m)
        rows_ref[middle:, :width] = jnp.where(first, -im_n, 2.0 * im_n)
        rows_ref[middle:, width:] = jnp.where(first, -im_m, -2.0 * im_m)

    rows_ref[...] = product((y_table[0][...], y_table[1][...]), split(rows_ref[...]))
    for cell in range(plan.cells):
        for group in range(plan.slabs // plan.y_lanes):
            parts = []
            for place in range(plan.y_lanes):
                tiles = []
                for part in range(2):
                    for step in range(plan.steps):
                        row = plan.row_of(cell, step, place)
                        col = part * width + group * LANES
                        tiles.append(rows_ref[row : row + plan.row_block, col : col + LANES])
                value = jnp.concatenate(tiles, axis=0)
                parts.append(value * sign if place % 2 == 1 else value)
            parts = swap_groups(parts, plan.width)
            first = cell * plan.slabs + group * plan.y_lanes
            for i in range(plan.y_lanes):
                out[first + i] = parts[i].reshape(2, plan.steps, plan.row_block, LANES)


def first_plane_kernel(plan, me_ref, pieces, y_high, y_low, x_high, x_low, out, rows_ref, freq_ref):
    out[...] = forward_plane(plan, me_ref, pieces, (y_high, y_low), (x_high, x_low), rows_ref, freq_ref)


def middle_plane_kernel(plan, me_ref, *refs):
    late, refs = (refs[:10], refs[10:])
    strips, refs = (refs[: plan.inner], refs[plan.inner :])
    blocks, refs = (refs[: plan.outer], refs[plan.outer :])
    out, rest, rows_ref, freq_ref, sum_ref, rest_ref, weights = refs[:7]
    held, sems = (refs[7:17], refs[17])
    pieces, yf_high, yf_low, xf_high, xf_low, even, xb_high, xb_low, yb_high, yb_low = held
    slab = lax.rem(me_ref[0], plan.slabs)
    place = lax.rem(slab, plan.half)
    outer_id, inner_id = (place // plan.inner, lax.rem(place, plan.inner))
    copies = [pltpu.make_async_copy(late[n], held[n], sems.at[n]) for n in range(len(held))]
    count = plan.ky_local
    placed = []
    for i in range(plan.inner):
        for j in range(plan.outer):
            owner = lax.rem(outer_id - j + plan.outer, plan.outer) * plan.inner
            owner = owner + lax.rem(inner_id - i + plan.inner, plan.inner)
            rows = pl.ds(pl.multiple_of(owner * count, count), count)
            for m, source in enumerate((strips[i].at[j], blocks[j].at[i])):
                sem = sems.at[len(held) + len(placed)]
                placed.append(pltpu.make_async_copy(source, weights.at[m, rows], sem))
    for copy in copies[:6] + placed + copies[6:]:
        copy.start()
    copies[0].wait()
    cell_first = me_ref[0] - slab
    tile = pieces[cell_first + jnp.where(slab < plan.half, plan.half, 0), plan.piece_rows :]
    parts = plan.nx // LANES
    own_edge = jnp.concatenate([tile[n : n + 1] for n in range(parts)], axis=1)
    edge = jnp.concatenate([tile[n : n + 1] for n in range(parts, 2 * parts)], axis=1)
    special = me_ref[0] == 0
    width = plan.x_chunk
    middle = plan.ny // 2
    x_table = (xf_high.at[pl.ds(0, 1)], xf_low.at[pl.ds(0, 1)])
    odd = forward_plane(
        plan, me_ref, pieces, (yf_high, yf_low), x_table, rows_ref, freq_ref, copies[1:5]
    )
    for copy in copies[5:6] + placed:
        copy.wait()
    row = lax.broadcasted_iota(jnp.int32, (middle, width), 0)
    at_first = row == 0
    for mirrored, turn in ((0, 1.0), (1, -1.0)):
        re = slice(2 * mirrored * middle, (2 * mirrored + 1) * middle)
        im = slice((2 * mirrored + 1) * middle, (2 * mirrored + 2) * middle)
        results = []
        for upper in range(2):
            cols = slice(upper * width, (upper + 1) * width)
            plane = weights[mirrored, :, cols]
            if mirrored:
                second = jnp.where(at_first, own_edge[:, cols], plane)
                weight = jnp.where(special, plane, second)
            else:
                weight = plane
                second = jnp.where(at_first & special, edge[0:1, cols], plane)
            re_sums = even[re] - odd[re] if upper else even[re] + odd[re]
            im_sums = even[im] - odd[im] if upper else even[im] + odd[im]
            real = weight * re_sums[:, :width] + (turn * second) * im_sums[:, width:]
            imag = second * im_sums[:, :width] - (turn * weight) * re_sums[:, width:]
            results.append((real, imag))
        for part, rows in enumerate((re, im)):
            below, above = (results[0][part], results[1][part])
            sum_ref[rows] = below + above
            rest_ref[rows] = below - above
    last = pltpu.make_async_copy(rest_ref, rest, sems.at[len(held) + 2 * plan.half])
    last.start()
    for copy in copies[6:]:
        copy.wait()
    backward_plane(plan, me_ref, sum_ref[...], (xb_high, xb_low), (yb_high, yb_low), out, rows_ref)
    last.wait()


def last_plane_kernel(plan, me_ref, freqs, x_high, x_low, y_high, y_low, out, rows_ref):
    backward_plane(plan, me_ref, freqs[...], (x_high, x_low), (y_high, y_low), out, rows_ref)


def plane_call(plan, kernel, name, me, ready, arrays, tables, late, out_specs, out_shapes, scratch, work):
    specs = [pl.BlockSpec(memory_space=pltpu.VMEM)] * len(ready)
    specs += [whole_spec(array.shape) for array in arrays]
    flat = []
    for pair, chunk in tables:
        for table in pair:
            if chunk is None:
                specs.append(whole_spec(table.shape))
            else:
                specs.append(pl.BlockSpec((1,) + table.shape[1:], lambda i, chunk=chunk: (chunk, 0, 0)))
            flat.append(table)
    specs += [pl.BlockSpec(memory_space=pl.ANY)] * len(late)
    size = sum(4 * array.size for array in list(ready) + list(arrays) + list(late))
    return pl.pallas_call(
        functools.partial(kernel, plan),
        grid=(1,) if tables else (),
        in_specs=[pl.BlockSpec(memory_space=pltpu.SMEM)] + specs,
        out_specs=out_specs,
        out_shape=[jax.ShapeDtypeStruct(shape, jnp.float32) for shape in out_shapes],
        scratch_shapes=scratch,
        compiler_params=pltpu.CompilerParams(vmem_limit_bytes=VMEM_LIMIT),
        cost_estimate=pl.CostEstimate(
            flops=work * 12 * plan.nx * plan.ny * plan.x_chunk,
            bytes_accessed=size + sum(2 * table.size for table in flat),
            transcendentals=0,
        ),
        name=name,
    )(me, *ready, *arrays, *flat, *late)


def gather_kernel(
    plan, chunk, sent, high_in, low_in, before_in, counts_in, projection, out, scratch, held, sems,
    pieces, high, low, before, counts
):
    planes = plan.cell_planes
    rows = plan.slots * 2 * plan.row_block
    first = plan.tx_chunk
    copies = tile_copies(plan, chunk, projection, held, sems, 1)
    pairs = ((sent, pieces), (high_in, high), (low_in, low), (before_in, before), (counts_in, counts))
    loads = [pltpu.make_async_copy(*pair, sems.at[first + n]) for n, pair in enumerate(pairs)]
    for copy in loads[:3] + copies + loads[3:]:
        copy.start()
    for copy in loads[:3]:
        copy.wait()
    columns = [pieces[:, :, step].reshape(rows, LANES) for step in range(plan.steps)]
    scratch[...] = product(split(jnp.concatenate(columns, axis=1).T), (high[...], low[...]))
    for copy in loads[3:]:
        copy.wait()
    for tx in range(plan.tx_chunk):
        copies[tx].wait()
        last = chunk == CHUNKS - 1 and tx == plan.tx_chunk - 1

        def body(place, carry, tx=tx, last=last):
            lanes = pl.ds(pl.multiple_of(place * LANES, LANES), LANES)
            far = [(before if tx == 0 else out)[p, :, lanes] for p in range(plan.panels)]
            for ty in range(TY):
                row = ((place * TY + ty) * plan.tx_chunk + tx) * planes
                rows_at = pl.ds(pl.multiple_of(row, planes), planes)
                for tz in range(TZ):
                    t = ty * TZ + tz
                    potential = scratch[rows_at, tz * LANES : (tz + 1) * LANES]
                    for p in range(plan.panels):
                        far[p] = far[p] + held[tx, p, t, :, lanes] * potential
            for p in range(plan.panels):
                out[p, :, lanes] = jnp.where(counts[:, lanes] > p, far[p], 0.0) if last else far[p]
            return carry

        lax.fori_loop(0, plan.steps * plan.step_blocks, body, 0)


def gather(plan, chunk, counts, before, projection, high, low, pieces):
    kernel = functools.partial(gather_kernel, plan, chunk)
    arrays = [pieces, high, low, before, counts]
    return projection_call(plan, kernel, "depth_gather", arrays, projection, before.shape)


def near_kernel(plan, extended, codes, blocks_ref, out):
    step = pl.program_id(0)
    lane = lax.broadcasted_iota(jnp.int32, (plan.cell_planes, LANES), 1)
    depth = lane % NZC
    digits = []
    for k in range(plan.near):
        code = codes[k]
        digits.append((code // 9, code // 3 % 3, code % 3))
    total = [None] * plan.panels
    for q in range(plan.panels):
        shifted = []
        for dx in range(3):
            before, here, after = (
                extended[q, dx, :, pl.ds(pl.multiple_of((step + i) * LANES, LANES), LANES)] for i in range(3)
            )
            up = jnp.where(lane < NZC, pltpu.roll(before, NZC, 1), pltpu.roll(here, NZC, 1))
            down = jnp.where(
                lane >= LANES - NZC, pltpu.roll(after, LANES - NZC, 1), pltpu.roll(here, LANES - NZC, 1)
            )
            for value in (up, here, down):
                under = jnp.where(
                    depth == 0, pltpu.roll(value, LANES - NZC + 1, 1), pltpu.roll(value, 1, 1)
                )
                over = jnp.where(
                    depth == NZC - 1, pltpu.roll(value, NZC - 1, 1), pltpu.roll(value, LANES - 1, 1)
                )
                shifted.append((under, value, over))
        for k in range(plan.near):
            digit_x, digit_y, digit_z = digits[k]

            def choose(digit, options):
                return jnp.where(digit == 0, options[0], jnp.where(digit == 1, options[1], options[2]))

            by_z = [choose(digit_z, options) for options in shifted]
            by_y = [choose(digit_y, by_z[3 * i : 3 * i + 3]) for i in range(3)]
            picked = choose(digit_x, by_y)
            for p in range(plan.panels):
                term = blocks_ref[k, p, q] * picked
                total[p] = term if total[p] is None else total[p] + term
    for p in range(plan.panels):
        out[p] = total[p]


def near_field(plan, extended, neighbours, near_blocks):
    return pl.pallas_call(
        functools.partial(near_kernel, plan),
        grid=(plan.cell_cols // LANES,),
        in_specs=[
            whole_spec(extended.shape),
            pl.BlockSpec((plan.near, plan.cell_planes, LANES), lambda i: (0, 0, i)),
            pl.BlockSpec(
                (plan.near, plan.panels, plan.panels, plan.cell_planes, LANES), lambda i: (0, 0, 0, 0, i)
            ),
        ],
        out_specs=pl.BlockSpec((plan.panels, plan.cell_planes, LANES), lambda i: (0, 0, i)),
        out_shape=jax.ShapeDtypeStruct((plan.panels, plan.cell_planes, plan.cell_cols), jnp.float32),
        compiler_params=pltpu.CompilerParams(vmem_limit_bytes=VMEM_LIMIT),
        cost_estimate=pl.CostEstimate(
            flops=2 * near_blocks.size, bytes_accessed=4 * near_blocks.size, transcendentals=0
        ),
        name="near_blocks",
    )(extended, neighbours, near_blocks)


def ring_pairs(axis):
    count = lax.axis_size(axis)
    up = [(i, (i + 1) % count) for i in range(count)]
    return (up, [(j, i) for i, j in up])


def extend_rows(plan, masked):
    up, down = ring_pairs("cell")
    left = lax.ppermute(masked[:, :, -NZC:], "cell", up)
    right = lax.ppermute(masked[:, :, :NZC], "cell", down)
    return (left, right)


def extend_planes(plan, masked, left, right):
    rest = jnp.zeros((plan.panels, plan.cell_planes, LANES - NZC), jnp.float32)
    wide = jnp.concatenate([rest, left, masked, right, rest], axis=2)
    up, down = ring_pairs("slab")
    before = lax.ppermute(wide[:, -1:], "slab", up)
    after = lax.ppermute(wide[:, :1], "slab", down)
    whole = jnp.concatenate([before, wide, after], axis=1)
    planes = plan.cell_planes
    return jnp.stack([whole[:, i : i + planes] for i in range(3)], axis=1)


def pick_kernel(plan, ids_ref, by_depth, *refs):
    outs, sems = (refs[:-1], refs[-1])
    place = lax.rem(ids_ref[0], plan.half)
    first = ids_ref[0] - place
    copies = []
    for j in range(plan.outer):
        part = lax.rem(place // plan.inner + j, plan.outer) * plan.inner
        for i in range(plan.inner):
            n = len(copies)
            copies.append(
                pltpu.make_async_copy(by_depth.at[first + part + i], outs[j].at[i], sems.at[n])
            )
            freq = first + part + lax.rem(place + i, plan.inner)
            mirror = jnp.where(freq == 0, plan.nz // 2, plan.nz - freq)
            copies.append(
                pltpu.make_async_copy(by_depth.at[mirror], outs[plan.outer + i].at[j], sems.at[n + 1])
            )
    for copy in copies:
        copy.start()
    for copy in copies:
        copy.wait()


def pick_planes(plan, ids, spectrum):
    by_depth = jnp.transpose(spectrum, (1, 2, 0))
    shapes = [(plan.inner,) + by_depth.shape[1:]] * plan.outer
    shapes += [(plan.outer,) + by_depth.shape[1:]] * plan.inner
    picked = pl.pallas_call(
        functools.partial(pick_kernel, plan),
        in_specs=[pl.BlockSpec(memory_space=pltpu.SMEM), pl.BlockSpec(memory_space=pl.ANY)],
        out_specs=[pl.BlockSpec(memory_space=pltpu.VMEM)] * len(shapes),
        out_shape=[jax.ShapeDtypeStruct(shape, jnp.float32) for shape in shapes],
        scratch_shapes=[pltpu.SemaphoreType.DMA((2 * plan.half,))],
        cost_estimate=pl.CostEstimate(
            flops=0, bytes_accessed=8 * sum(math.prod(shape) for shape in shapes), transcendentals=0
        ),
        name="pick_planes",
    )(ids, by_depth)
    return (picked[: plan.outer], picked[plan.outer :])


def outer_shift(plan, value, j):
    if j == 0:
        return value
    pairs = []
    for source in range(plan.slabs):
        base = source // plan.half * plan.half
        pairs.append((source, base + (source - base + j * plan.inner) % plan.half))
    return lax.ppermute(value, "slab", pairs)


def inner_shift(plan, value, i):
    if i == 0:
        return value
    pairs = []
    for source in range(plan.slabs):
        base = source // plan.inner * plan.inner
        pairs.append((source, base + (source + i) % plan.inner))
    return lax.ppermute(value, "slab", pairs)


def edge_weights(plan, rows):
    middle = plan.nz // 2
    turned = jnp.concatenate([rows[middle : middle + 1], jnp.flip(rows, 0)], axis=0)[: plan.slots]
    shape = (plan.slots, plan.nx // LANES, LANES)
    plane = jnp.broadcast_to(rows[0].reshape(shape[1:]), shape)
    return jnp.concatenate([turned.reshape(shape), plane], axis=1)


def second_weights(plan, plain, mirror):
    slab = lax.axis_index("slab")
    strips = []
    for i in range(plan.inner):
        place = lax.rem(slab + i, plan.inner)
        rows = [lax.dynamic_slice_in_dim(block, place, 1, 0) for block in plain]
        strips.append(inner_shift(plan, jnp.concatenate(rows, axis=0), i))
    blocks = [outer_shift(plan, jnp.stack([m[j] for m in mirror]), j) for j in range(plan.outer)]
    return strips + blocks


def per_device(charges, counts, projection, near_blocks, neighbours, spectrum):
    panels, cell_planes, cell_cols = charges.shape
    cells, slabs = (lax.axis_size("cell"), lax.axis_size("slab"))
    nx, nz, local = spectrum.shape
    plan = Plan(slabs, cells, panels, cell_planes, cell_cols, neighbours.shape[0], nx, nz, local * slabs)
    if not plan.fits():
        return plain_device(charges, counts, projection, near_blocks, neighbours, spectrum)
    me = (lax.axis_index("cell") * slabs + lax.axis_index("slab")).astype(jnp.int32).reshape(1)
    forward_table, backward_table = plan.depth_tables()
    depth_forward, depth_backward = (halves(forward_table.T), halves(backward_table))
    y_rows, x_cols, low_ids = (plan.y_rows().reshape(-1), plan.x_columns(), np.arange(plan.ny // 2))
    cos_y, sin_y = wave(low_ids, y_rows, plan.ny)
    sin_y[0] = 1.0 - 2.0 * (y_rows % 2)
    y_forward = halves(np.concatenate([cos_y, sin_y], axis=0))
    y_backward = halves(np.concatenate([cos_y.T, -sin_y.T], axis=1))
    x_waves = [wave(cols, low_ids, plan.nx) for cols in x_cols]
    x_forward = halves(np.stack([np.concatenate(pair, axis=1) for pair in x_waves]))
    x_backward = halves(np.stack([np.concatenate([t.T for t in pair], axis=1) for pair in x_waves]))
    split_projection = projection.reshape(
        (panels, TX // CHUNKS, CHUNKS, TY * TZ, cell_planes, cell_cols)
    )
    axes = ("cell", "slab")

    def exchange(pieces):
        return lax.all_to_all(pieces, axes, split_axis=0, concat_axis=0, tiled=True)

    def values(*shapes):
        return [pltpu.VMEM(shape, jnp.float32) for shape in shapes]

    rows_shape = (plan.ny, 2 * plan.x_chunk)
    freq_shape = (2 * plan.ny, plan.x_chunk)
    both_shape = (2 * plan.ny, plan.nx)
    slot = lax.broadcasted_iota(jnp.int32, charges.shape, 0)
    masked = jnp.where(slot < counts[None], charges, 0.0)
    rows = jnp.transpose(spectrum[:, :, 0], (1, 0))
    first = project(plan, 0, charges, counts, split_projection, *depth_forward, None)
    first, late_me = lax.optimization_barrier((first, me))
    even_pieces = exchange(first)
    edges = edge_weights(plan, rows)
    second = project(plan, 1, charges, counts, split_projection, *depth_forward, edges)
    plain, mirror = pick_planes(plan, late_me, spectrum)
    plain = [outer_shift(plan, value, j) for j, value in enumerate(plain)]
    mirror = [inner_shift(plan, value, i) for i, value in enumerate(mirror)]
    second, masked = lax.optimization_barrier((second, masked))
    left, right = extend_rows(plan, masked)
    second, left, right, *moved = lax.optimization_barrier((second, left, right, *plain, *mirror))
    plain, mirror = (moved[: plan.outer], moved[plan.outer :])
    odd_pieces = exchange(second)
    strips = second_weights(plan, plain, mirror)
    in_vmem = pl.BlockSpec(memory_space=pltpu.VMEM)
    in_place = pl.BlockSpec(memory_space=pl.ANY)
    (even,) = plane_call(
        plan, first_plane_kernel, "even_planes", me, [], [even_pieces],
        [(y_forward, None), (x_forward, 0)], [], [whole_spec(both_shape)], [both_shape],
        values(rows_shape, freq_shape), 2,
    )
    late = [odd_pieces, *y_forward, x_forward[0][1:], x_forward[1][1:], even]
    late += [x_backward[0][:1], x_backward[1][:1], *y_backward]
    copies = [pltpu.VMEM(array.shape, array.dtype) for array in late]
    copies.append(pltpu.SemaphoreType.DMA((len(late) + 2 * plan.half + 1,)))
    back, rest = plane_call(
        plan, middle_plane_kernel, "middle_planes", me, [], [], [], late + strips, [in_vmem, in_place], [piece_shape(plan), freq_shape],
        values(rows_shape, freq_shape, freq_shape, freq_shape, (2, plan.ny // 2, plan.nx)) + copies, 4,
    )
    even_back = exchange(back)
    (back,) = plane_call(
        plan, last_plane_kernel, "odd_planes", me, [], [rest],
        [(x_backward, 1), (y_backward, None)], [], [whole_spec(piece_shape(plan))], [piece_shape(plan)],
        values(rows_shape), 2,
    )
    back, masked = lax.optimization_barrier((back, masked))
    extended = extend_planes(plan, masked, left, right)
    back, extended = lax.optimization_barrier((back, extended))
    odd_back = exchange(back)
    total = near_field(plan, extended, neighbours, near_blocks)
    total = gather(plan, 0, counts, total, split_projection, *depth_backward, even_back)
    return gather(plan, 1, counts, total, split_projection, *depth_backward, odd_back)


def padded(value, sides, width):
    for axis, dim in sides:
        count, length = (lax.axis_size(axis), value.shape[dim])
        up = [(i, (i + 1) % count) for i in range(count)]
        down = [(j, i) for i, j in up]
        last = lax.slice_in_dim(value, length - width, length, axis=dim)
        first = lax.slice_in_dim(value, 0, width, axis=dim)
        before = lax.ppermute(last, axis, up)
        after = lax.ppermute(first, axis, down)
        value = jnp.concatenate([before, value, after], axis=dim)
    return value


def wave_tables(row_count, col_count, length):
    products = (
        lax.broadcasted_iota(jnp.int32, (row_count, col_count), 0)
        * lax.broadcasted_iota(jnp.int32, (row_count, col_count), 1)
        % length
    )
    angle_rad = products.astype(jnp.float32) * (2.0 * math.pi / length)
    return (jnp.cos(angle_rad), jnp.sin(angle_rad))


def depth_rows(nz, freq_ids, valid, weights):
    depth_ids = lax.broadcasted_iota(jnp.int32, (freq_ids.shape[0], nz), 1)
    products = freq_ids[:, None] * depth_ids % nz
    angle_rad = products.astype(jnp.float32) * (2.0 * math.pi / nz)
    basis = jnp.stack([jnp.cos(angle_rad), -jnp.sin(angle_rad)])
    return (basis * valid[None, :, None], basis * weights[None, :, None])


def half_depth_tables(nz, cell_count):
    lower = nz // (2 * cell_count)
    row_ids = lax.broadcasted_iota(jnp.int32, (cell_count * (lower + 1),), 0)
    block_ids = row_ids // (lower + 1)
    slot_ids = row_ids % (lower + 1)
    freq_ids = jnp.where(slot_ids < lower, block_ids * lower + slot_ids, nz // 2)
    valid = jnp.where((slot_ids < lower) | (block_ids == 0), 1.0, 0.0).astype(jnp.float32)
    doubled = jnp.where((slot_ids < lower) & (freq_ids > 0), 2.0, 1.0).astype(jnp.float32)
    forward_table, backward_table = depth_rows(nz, freq_ids, valid, valid * doubled)
    return (forward_table, backward_table, freq_ids)


def combine_halves(first_part, second, orient):
    half_width = first_part.shape[-1] // 2
    real_part = first_part[..., :half_width] + orient * second[..., half_width:]
    imag_part = first_part[..., half_width:] - orient * second[..., :half_width]
    return jnp.concatenate([real_part, imag_part], axis=-1)


def transform_axis(pattern, cosine, sine_tab, values, orient):
    first_part = jnp.einsum(pattern, cosine, values, precision=lax.Precision.HIGHEST)
    second = jnp.einsum(pattern, sine_tab, values, precision=lax.Precision.HIGHEST)
    return combine_halves(first_part, second, orient)


def twiddle(values, twist_cos, twist_sin, orient):
    half_width = values.shape[-1] // 2
    real_part = values[..., :half_width]
    imag_part = values[..., half_width:]
    new_real = real_part * twist_cos + orient * imag_part * twist_sin
    new_imag = imag_part * twist_cos - orient * real_part * twist_sin
    return jnp.concatenate([new_real, new_imag], axis=-1)


def transform_rows(planes_block, cosine, sine_tab, orient):
    flat_rows = planes_block.reshape(-1, planes_block.shape[-1])
    first_part = jnp.dot(flat_rows, cosine, precision=lax.Precision.HIGHEST).reshape(
        planes_block.shape
    )
    second = jnp.dot(flat_rows, sine_tab, precision=lax.Precision.HIGHEST).reshape(
        planes_block.shape
    )
    real_part = first_part[:, 0] + orient * second[:, 1]
    imag_part = first_part[:, 1] - orient * second[:, 0]
    return jnp.stack([real_part, imag_part], axis=1)


def plain_device(charges, counts, projection, near_blocks, neighbours, spectrum):
    panels, cell_planes, cell_cols = charges.shape
    nx, nz, ny = (spectrum.shape[0], spectrum.shape[1], spectrum.shape[2] * lax.axis_size("slab"))
    planes = cell_planes * TX
    rows_cell = cell_cols // NZC
    slot_ids = lax.broadcasted_iota(jnp.int32, charges.shape, 0)
    panel_mask = (slot_ids < counts[None]).astype(jnp.float32)
    masked = charges * panel_mask
    tile_values = jnp.einsum("ptxc,pxc->txc", projection, masked, precision=lax.Precision.HIGHEST)
    grid_field = (
        tile_values.reshape(TX, TY, TZ, cell_planes, rows_cell, NZC)
        .transpose(3, 0, 5, 2, 4, 1)
        .reshape(planes, nz, rows_cell * TY)
    )
    cell_count = lax.axis_size("cell")
    forward_table, backward_table, freq_ids = half_depth_tables(nz, cell_count)
    depth_count = forward_table.shape[1] // cell_count
    spectra_z = jnp.einsum(
        "wkz,xzy->xwky", forward_table, grid_field, precision=lax.Precision.HIGHEST
    )
    cosine_y, sine_y = wave_tables(ny, ny, ny)
    pencils = transform_rows(
        lax.all_to_all(spectra_z, "cell", split_axis=2, concat_axis=3, tiled=True),
        cosine_y,
        sine_y,
        1.0,
    )
    columns = lax.all_to_all(pencils, "slab", split_axis=3, concat_axis=0, tiled=True)
    col_width = columns.shape[2] * columns.shape[3]
    flat_rows = columns.reshape(nx, 2 * col_width)
    first_row = lax.axis_index("cell") * depth_count
    kernel_ids = lax.dynamic_slice_in_dim(freq_ids, first_row, depth_count, 0)
    kernel = jnp.take(spectrum, kernel_ids, axis=1).reshape(nx, col_width) * (1.0 / (nx * ny * nz))
    kernel_both = jnp.concatenate([kernel, kernel], axis=1)
    slab_count = lax.axis_size("slab")
    local_rows = nx // slab_count
    cosine_s, sine_s = wave_tables(slab_count, slab_count, slab_count)
    cosine_r, sine_r = wave_tables(local_rows, local_rows, local_rows)
    twist_cos, twist_sin = wave_tables(slab_count, local_rows, nx)
    twist_cos = twist_cos[:, :, None]
    twist_sin = twist_sin[:, :, None]
    section_one = transform_axis(
        "ks,src->krc",
        cosine_s,
        sine_s,
        flat_rows.reshape(slab_count, local_rows, 2 * col_width),
        1.0,
    )
    section_one = twiddle(section_one, twist_cos, twist_sin, 1.0)
    section_two = transform_axis("jr,krc->jkc", cosine_r, sine_r, section_one, 1.0)
    weighted = section_two.reshape(nx, 2 * col_width) * kernel_both
    section_one = transform_axis(
        "rj,jkc->krc",
        cosine_r,
        sine_r,
        weighted.reshape(local_rows, slab_count, 2 * col_width),
        -1.0,
    )
    section_one = twiddle(section_one, twist_cos, twist_sin, -1.0)
    section_two = transform_axis("sk,krc->src", cosine_s, sine_s, section_one, -1.0)
    returned_x = section_two.reshape(nx, 2 * col_width)
    returned = lax.all_to_all(
        returned_x.reshape(columns.shape), "slab", split_axis=0, concat_axis=3, tiled=True
    )
    inverse_rows = transform_rows(returned, cosine_y, sine_y, -1.0)
    grid_potential = jnp.einsum(
        "wkz,xwky->xzy",
        backward_table,
        lax.all_to_all(inverse_rows, "cell", split_axis=3, concat_axis=2, tiled=True),
        precision=lax.Precision.HIGHEST,
    )
    tile_potential = (
        grid_potential.reshape(cell_planes, TX, NZC, TZ, rows_cell, TY)
        .transpose(1, 5, 3, 0, 4, 2)
        .reshape(TX * TY * TZ, cell_planes, cell_cols)
    )
    far_field = jnp.einsum(
        "ptxc,txc->pxc", projection, tile_potential, precision=lax.Precision.HIGHEST
    )
    block = masked.reshape(panels, cell_planes, rows_cell, NZC)
    extended = padded(block, (("slab", 1), ("cell", 2)), 1)
    flat_ext = extended.reshape(panels, -1)
    step_x = neighbours // 9 - 1
    step_y = neighbours // 3 % 3 - 1
    step_z = neighbours % 3 - 1
    plane_ids = lax.broadcasted_iota(jnp.int32, neighbours.shape, 1)
    col_ids = lax.broadcasted_iota(jnp.int32, neighbours.shape, 2)
    row_ids = col_ids // NZC
    depth_ids = col_ids % NZC
    near_ids = ((plane_ids + step_x + 1) * (rows_cell + 2) + row_ids + step_y + 1) * NZC + (
        depth_ids + step_z
    ) % NZC
    near_count = neighbours.shape[0]
    picked = jnp.take(flat_ext, near_ids.reshape(-1), axis=1).reshape(
        panels, near_count, cell_planes, cell_cols
    )
    near_field = jnp.einsum("kpqxc,qkxc->pxc", near_blocks, picked, precision=lax.Precision.HIGHEST)
    return (far_field + near_field) * panel_mask


def solution(mesh):
    in_specs = (
        P(None, "slab", "cell"),
        P("slab", "cell"),
        P(None, None, "slab", "cell"),
        P(None, None, None, "slab", "cell"),
        P(None, "slab", "cell"),
        P(None, None, "slab"),
    )
    out_specs = P(None, "slab", "cell")
    return jax.shard_map(
        per_device, mesh=mesh, in_specs=in_specs, out_specs=out_specs, check_vma=False
    )
```

```python
import functools
import math

import jax
import jax.numpy as jnp
import ml_dtypes
import numpy as np
from jax import lax
from jax.experimental import pallas as pl
from jax.experimental.pallas import tpu as pltpu
from jax.sharding import PartitionSpec as P

TX = 4
TY = 4
TZ = 4
NZC = 16
LANES = 128
CHUNKS = 2
VMEM_LIMIT = 127 * 512 * 1024


def halves(table):
    high = table.astype(np.float32).astype(ml_dtypes.bfloat16)
    low = (table - high.astype(np.float64)).astype(np.float32).astype(ml_dtypes.bfloat16)
    return (high, low)


def wave(rows, cols, length):
    angle = (rows[:, None] * cols[None, :] % length) * (2.0 * math.pi / length)
    return (np.cos(angle), np.sin(angle))


class Plan:
    def __init__(self, slabs, cells, panels, cell_planes, cell_cols, near, nx, nz, ny):
        self.slabs, self.cells = (slabs, cells)
        self.panels, self.cell_planes, self.cell_cols, self.near = (panels, cell_planes, cell_cols, near)
        self.nx, self.ny, self.nz = (nx, ny, nz)
        self.slots = slabs * cells
        self.tx_chunk = TX // CHUNKS
        self.width = cell_planes * self.tx_chunk
        self.y_lanes = LANES // self.width if self.width else 1
        self.row_block = LANES // NZC
        self.step_blocks = self.y_lanes // TY
        self.steps = cell_cols // (LANES * self.step_blocks) if self.step_blocks else 0
        self.x_chunk = nx // CHUNKS
        self.ky_local = ny // slabs
        self.piece_rows = 2 * self.steps * self.row_block
        self.half = slabs // 2
        self.outer = math.gcd(self.half, 2)
        self.inner = self.half // self.outer

    def fits(self):
        return (
            self.slots * 2 == self.nz
            and self.cell_planes == 8
            and self.step_blocks * TY * self.width == LANES
            and self.slabs % self.y_lanes == 0
            and self.ky_local % 8 == 0
            and self.steps * self.step_blocks * LANES == self.cell_cols
            and self.x_chunk % LANES == 0
            and self.nx == self.ny == 4 * LANES
            and self.ny % 1024 == self.nx % 1024 == 512
        )

    def depth_tables(self):
        depth = np.arange(NZC)[None, :] * TZ + np.arange(TZ)[:, None]
        scale = 1.0 / (self.nx * self.ny * self.nz)
        forward = np.zeros((self.slots, 2, self.row_block, TZ, self.row_block, NZC))
        backward = np.zeros_like(forward)
        for freq in range(self.slots):
            angle = (freq * depth % self.nz) * (2.0 * math.pi / self.nz)
            real, imag = (np.cos(angle), -np.sin(angle))
            factor = 2.0 * scale
            if freq == 0:
                imag = np.cos(depth * math.pi)
                factor = scale
            for row in range(self.row_block):
                forward[freq, 0, row, :, row, :] = real
                forward[freq, 1, row, :, row, :] = imag
                backward[freq, 0, row, :, row, :] = factor * real
                backward[freq, 1, row, :, row, :] = factor * imag
        shape = (self.slots * 2 * self.row_block, TZ * LANES)
        return (forward.reshape(shape), backward.reshape(shape))

    def y_rows(self):
        parity, cell, step, block, tile, row = np.meshgrid(
            *[np.arange(n) for n in (2, self.cells, self.steps, self.step_blocks, TY // 2, self.row_block)],
            indexing="ij",
        )
        cell_row = ((cell * self.steps + step) * self.step_blocks + block) * self.row_block + row
        return (cell_row * TY + 2 * tile + parity).reshape(2, -1)

    def x_columns(self):
        parity, slab, tile, plane = np.meshgrid(
            *[np.arange(n) for n in (2, self.slabs, TX // 2, self.cell_planes)], indexing="ij"
        )
        return ((slab * self.cell_planes + plane) * TX + 2 * tile + parity).reshape(2, -1)

    def row_of(self, cell, step, place):
        block, tile = (place // TY, place % TY)
        inner = (cell * self.steps + step) * self.step_blocks + block
        return (tile % 2) * (self.ny // 2) + (inner * (TY // 2) + tile // 2) * self.row_block


def split(value):
    high = value.astype(jnp.bfloat16)
    low = (value - high.astype(jnp.float32)).astype(jnp.bfloat16)
    return (high, low)


def product(left, right, dims=((1,), (0,))):
    first = jnp.concatenate([left[0], left[0], left[1]], axis=dims[0][0])
    second = jnp.concatenate([right[0], right[1], right[0]], axis=dims[1][0])
    return lax.dot_general(first, second, (dims, ((), ())), preferred_element_type=jnp.float32)


def swap_groups(parts, width):
    count = len(parts)
    lane = lax.broadcasted_iota(jnp.int32, parts[0].shape, 1)
    parts = list(parts)
    step = count // 2
    while step >= 1:
        shift = step * width
        upper = (lane // shift) % 2 == 1
        for i in range(count):
            if i & step:
                continue
            first, second = (parts[i], parts[i + step])
            parts[i] = jnp.where(upper, pltpu.roll(second, shift, 1), first)
            parts[i + step] = jnp.where(upper, second, pltpu.roll(first, LANES - shift, 1))
        step //= 2
    return parts


def tile_copies(plan, chunk, projection, held, sems, parts):
    count = TY * TZ // parts
    copies = []
    for tx in range(plan.tx_chunk):
        for part in range(parts):
            rows = pl.ds(part * count, count)
            source = projection.at[:, tx, chunk, rows]
            copies.append(pltpu.make_async_copy(source, held.at[tx, :, rows], sems.at[len(copies)]))
    return copies


def project_kernel(plan, chunk, *refs):
    edges = chunk == CHUNKS - 1
    count_in = 5 if edges else 4
    arrays_in, projection, out = (refs[:count_in], refs[count_in], refs[count_in + 1])
    scratch, held, sems = refs[count_in + 2 : count_in + 5]
    arrays = refs[count_in + 5 :]
    charges, counts, high, low = arrays[:4]
    planes = plan.cell_planes
    copies = tile_copies(plan, chunk, projection, held, sems, TY)
    loads = [
        pltpu.make_async_copy(source, place, sems.at[len(copies) + n])
        for n, (source, place) in enumerate(zip(arrays_in, arrays))
    ]
    for copy in loads[:2] + copies + loads[2:]:
        copy.start()
    for copy in loads[:2]:
        copy.wait()
    for n, copy in enumerate(copies):
        copy.wait()

        def body(place, carry, tx=n // TY, ty=n % TY):
            lanes = pl.ds(pl.multiple_of(place * LANES, LANES), LANES)
            count = counts[:, lanes]
            own = [jnp.where(count > p, charges[p, :, lanes], 0.0) for p in range(plan.panels)]
            row = ((place * TY + ty) * plan.tx_chunk + tx) * planes
            rows = pl.ds(pl.multiple_of(row, planes), planes)
            for tz in range(TZ):
                t = ty * TZ + tz
                total = held[tx, 0, t, :, lanes] * own[0]
                for p in range(1, plan.panels):
                    total = total + held[tx, p, t, :, lanes] * own[p]
                scratch[rows, tz * LANES : (tz + 1) * LANES] = total
            return carry

        lax.fori_loop(0, plan.steps * plan.step_blocks, body, 0, unroll=True)
    for copy in loads[2:]:
        copy.wait()
    spectra = product(split(scratch[...]), (high[...], low[...])).T
    shape = (plan.slots, 2, plan.row_block, LANES)
    for step in range(plan.steps):
        value = spectra[:, step * LANES : (step + 1) * LANES].reshape(shape)
        for part in range(2):
            row = (part * plan.steps + step) * plan.row_block
            out[:, row : row + plan.row_block] = value[:, part]
    if edges:
        out[:, plan.piece_rows :] = arrays[4][...]


def held_shape(plan):
    cols = plan.steps * plan.step_blocks * LANES
    return (plan.tx_chunk, plan.panels, TY * TZ, plan.cell_planes, cols)


def piece_shape(plan):
    return (plan.slots, 2, plan.steps, plan.row_block, LANES)


def whole_spec(shape):
    return pl.BlockSpec(shape, lambda i: (0,) * len(shape))


def projection_call(plan, kernel, name, arrays, projection, out_shape):
    return pl.pallas_call(
        kernel,
        in_specs=[pl.BlockSpec(memory_space=pl.ANY)] * (len(arrays) + 1),
        out_specs=pl.BlockSpec(memory_space=pltpu.VMEM),
        out_shape=jax.ShapeDtypeStruct(out_shape, jnp.float32),
        scratch_shapes=[
            pltpu.VMEM((plan.steps * LANES, TZ * LANES), jnp.float32),
            pltpu.VMEM(held_shape(plan), jnp.float32),
            pltpu.SemaphoreType.DMA((plan.tx_chunk * TY + len(arrays),)),
        ]
        + [pltpu.VMEM(array.shape, array.dtype) for array in arrays],
        compiler_params=pltpu.CompilerParams(vmem_limit_bytes=VMEM_LIMIT),
        cost_estimate=pl.CostEstimate(
            flops=2 * math.prod(held_shape(plan)),
            bytes_accessed=4 * math.prod(held_shape(plan)),
            transcendentals=0,
        ),
        name=name,
    )(*arrays, projection)


def project(plan, chunk, charges, counts, projection, high, low, edges):
    kernel = functools.partial(project_kernel, plan, chunk)
    arrays = [charges, counts, high, low] + ([] if edges is None else [edges])
    rows = plan.piece_rows + (0 if edges is None else edges.shape[1])
    return projection_call(plan, kernel, "project_depth", arrays, projection, (plan.slots, rows, LANES))


def far_sign(plan, me_ref):
    slab = lax.rem(me_ref[0], plan.slabs)
    return jnp.where(slab >= plan.half, -1.0, 1.0)


def piece_copies(plan, source, dest, sems, first):
    copies = []
    for n in range(plan.slots // plan.y_lanes):
        rows = pl.ds(n * plan.y_lanes, plan.y_lanes)
        copies.append(pltpu.make_async_copy(source.at[rows], dest.at[rows], sems.at[first + n]))
    return copies


def forward_plane(
    plan, me_ref, pieces, y_table, x_table, rows_ref, freq_ref, waits=(), arrivals=None
):
    special = me_ref[0] == 0
    sign = far_sign(plan, me_ref)
    rows = 2 * plan.steps * plan.row_block
    width = plan.x_chunk
    middle = plan.ny // 2
    for cell in range(plan.cells):
        for group in range(plan.slabs // plan.y_lanes):
            first = cell * plan.slabs + group * plan.y_lanes
            if arrivals:
                arrivals[first // plan.y_lanes].wait()
            parts = [pieces[first + i, :rows] for i in range(plan.y_lanes)]
            parts = swap_groups(parts, plan.width)
            for place, value in enumerate(parts):
                if place % 2 == 1:
                    value = value * sign
                for part in range(2):
                    for step in range(plan.steps):
                        source = (part * plan.steps + step) * plan.row_block
                        row = plan.row_of(cell, step, place)
                        col = part * width + group * LANES
                        rows_ref[row : row + plan.row_block, col : col + LANES] = value[
                            source : source + plan.row_block
                        ]
    for copy in waits:
        copy.wait()
    sums = product((y_table[0][...], y_table[1][...]), split(rows_ref[...]))
    cos_re, cos_im = (sums[:middle, :width], sums[:middle, width:])
    sin_re, sin_im = (sums[middle:, :width], sums[middle:, width:])
    first = lax.broadcasted_iota(jnp.int32, (middle, width), 0) == 0

    @pl.when(jnp.logical_not(special))
    def _():
        freq_ref[:middle] = jnp.where(first, cos_re, cos_re + sin_im)
        freq_ref[middle : 2 * middle] = jnp.where(first, cos_im, cos_im - sin_re)
        freq_ref[2 * middle : 3 * middle] = jnp.where(first, sin_re, cos_re - sin_im)
        freq_ref[3 * middle :] = jnp.where(first, sin_im, cos_im + sin_re)

    @pl.when(special)
    def _():
        freq_ref[:middle] = cos_re
        freq_ref[middle : 2 * middle] = jnp.where(first, sin_re, -sin_re)
        freq_ref[2 * middle : 3 * middle] = cos_im
        freq_ref[3 * middle :] = sin_im

    return product(split(freq_ref[...]), (x_table[0][0], x_table[1][0]))


def backward_plane(plan, me_ref, freqs, x_table, y_table, out, rows_ref, departures=None):
    special = me_ref[0] == 0
    sign = far_sign(plan, me_ref)
    width = plan.x_chunk
    middle = plan.ny // 2
    sums = product(split(freqs), (x_table[0][0], x_table[1][0]))
    parts = []
    for mirrored, turn in ((0, 1.0), (1, -1.0)):
        re = slice(2 * mirrored * middle, (2 * mirrored + 1) * middle)
        im = slice((2 * mirrored + 1) * middle, (2 * mirrored + 2) * middle)
        parts.append(sums[re, :width] - turn * sums[im, width:])
        parts.append(sums[im, :width] + turn * sums[re, width:])
    re_n, im_n, re_m, im_m = parts
    first = lax.broadcasted_iota(jnp.int32, (middle, width), 0) == 0

    @pl.when(jnp.logical_not(special))
    def _():
        rows_ref[:middle, :width] = jnp.where(first, re_n, re_n + re_m)
        rows_ref[:middle, width:] = jnp.where(first, im_n, im_n + im_m)
        rows_ref[middle:, :width] = jnp.where(first, -re_m, im_n - im_m)
        rows_ref[middle:, width:] = jnp.where(first, -im_m, re_m - re_n)

    @pl.when(special)
    def _():
        rows_ref[:middle, :width] = jnp.where(first, re_n, 2.0 * re_n)
        rows_ref[:middle, width:] = jnp.where(first, re_m, 2.0 * re_m)
        rows_ref[middle:, :width] = jnp.where(first, -im_n, 2.0 * im_n)
        rows_ref[middle:, width:] = jnp.where(first, -im_m, -2.0 * im_m)

    rows_ref[...] = product((y_table[0][...], y_table[1][...]), split(rows_ref[...]))
    for cell in range(plan.cells):
        for group in range(plan.slabs // plan.y_lanes):
            parts = []
            for place in range(plan.y_lanes):
                tiles = []
                for part in range(2):
                    for step in range(plan.steps):
                        row = plan.row_of(cell, step, place)
                        col = part * width + group * LANES
                        tiles.append(rows_ref[row : row + plan.row_block, col : col + LANES])
                value = jnp.concatenate(tiles, axis=0)
                parts.append(value * sign if place % 2 == 1 else value)
            parts = swap_groups(parts, plan.width)
            first = cell * plan.slabs + group * plan.y_lanes
            for i in range(plan.y_lanes):
                out[first + i] = parts[i].reshape(2, plan.steps, plan.row_block, LANES)
            if departures:
                departures[first // plan.y_lanes].start()


def first_plane_kernel(plan, me_ref, pieces, y_high, y_low, x_high, x_low, out, rows_ref, freq_ref):
    out[...] = forward_plane(plan, me_ref, pieces, (y_high, y_low), (x_high, x_low), rows_ref, freq_ref)


def middle_plane_kernel(plan, me_ref, *refs):
    late, refs = (refs[:10], refs[10:])
    strips, refs = (refs[: plan.inner], refs[plan.inner :])
    blocks, refs = (refs[: plan.outer], refs[plan.outer :])
    out, rest, rows_ref, freq_ref, sum_ref, rest_ref, weights, result = refs[:8]
    held, sems, piece_sems = (refs[8:18], refs[18], refs[19])
    pieces, yf_high, yf_low, xf_high, xf_low, even, xb_high, xb_low, yb_high, yb_low = held
    slab = lax.rem(me_ref[0], plan.slabs)
    place = lax.rem(slab, plan.half)
    outer_id, inner_id = (place // plan.inner, lax.rem(place, plan.inner))
    copies = [pltpu.make_async_copy(late[n], held[n], sems.at[n]) for n in range(len(held))]
    arrivals = piece_copies(plan, late[0], pieces, piece_sems, 0)
    departures = piece_copies(plan, result, out, piece_sems, len(arrivals))
    count = plan.ky_local
    placed = []
    for i in range(plan.inner):
        for j in range(plan.outer):
            owner = lax.rem(outer_id - j + plan.outer, plan.outer) * plan.inner
            owner = owner + lax.rem(inner_id - i + plan.inner, plan.inner)
            rows = pl.ds(pl.multiple_of(owner * count, count), count)
            for m, source in enumerate((strips[i].at[j], blocks[j].at[i])):
                sem = sems.at[len(held) + len(placed)]
                placed.append(pltpu.make_async_copy(source, weights.at[m, rows], sem))
    for copy in arrivals + copies[1:6] + placed + copies[6:]:
        copy.start()
    special = me_ref[0] == 0
    width = plan.x_chunk
    middle = plan.ny // 2
    x_table = (xf_high.at[pl.ds(0, 1)], xf_low.at[pl.ds(0, 1)])
    odd = forward_plane(
        plan, me_ref, pieces, (yf_high, yf_low), x_table, rows_ref, freq_ref, copies[1:5], arrivals
    )
    cell_first = me_ref[0] - slab
    tile = pieces[cell_first + jnp.where(slab < plan.half, plan.half, 0), plan.piece_rows :]
    parts = plan.nx // LANES
    own_edge = jnp.concatenate([tile[n : n + 1] for n in range(parts)], axis=1)
    edge = jnp.concatenate([tile[n : n + 1] for n in range(parts, 2 * parts)], axis=1)
    for copy in copies[5:6] + placed:
        copy.wait()
    row = lax.broadcasted_iota(jnp.int32, (middle, width), 0)
    at_first = row == 0
    for mirrored, turn in ((0, 1.0), (1, -1.0)):
        re = slice(2 * mirrored * middle, (2 * mirrored + 1) * middle)
        im = slice((2 * mirrored + 1) * middle, (2 * mirrored + 2) * middle)
        results = []
        for upper in range(2):
            cols = slice(upper * width, (upper + 1) * width)
            plane = weights[mirrored, :, cols]
            if mirrored:
                second = jnp.where(at_first, own_edge[:, cols], plane)
                weight = jnp.where(special, plane, second)
            else:
                weight = plane
                second = jnp.where(at_first & special, edge[0:1, cols], plane)
            re_sums = even[re] - odd[re] if upper else even[re] + odd[re]
            im_sums = even[im] - odd[im] if upper else even[im] + odd[im]
            real = weight * re_sums[:, :width] + (turn * second) * im_sums[:, width:]
            imag = second * im_sums[:, :width] - (turn * weight) * re_sums[:, width:]
            results.append((real, imag))
        for part, rows in enumerate((re, im)):
            below, above = (results[0][part], results[1][part])
            sum_ref[rows] = below + above
            rest_ref[rows] = below - above
    last = pltpu.make_async_copy(rest_ref, rest, sems.at[len(held) + 2 * plan.half])
    last.start()
    for copy in copies[6:]:
        copy.wait()
    tables = ((xb_high, xb_low), (yb_high, yb_low))
    backward_plane(plan, me_ref, sum_ref[...], *tables, result, rows_ref, departures)
    for copy in departures + [last]:
        copy.wait()


def last_plane_kernel(plan, me_ref, freqs, x_high, x_low, y_high, y_low, out, rows_ref):
    backward_plane(plan, me_ref, freqs[...], (x_high, x_low), (y_high, y_low), out, rows_ref)


def plane_call(plan, kernel, name, me, ready, arrays, tables, late, out_specs, out_shapes, scratch, work):
    specs = [pl.BlockSpec(memory_space=pltpu.VMEM)] * len(ready)
    specs += [whole_spec(array.shape) for array in arrays]
    flat = []
    for pair, chunk in tables:
        for table in pair:
            if chunk is None:
                specs.append(whole_spec(table.shape))
            else:
                specs.append(pl.BlockSpec((1,) + table.shape[1:], lambda i, chunk=chunk: (chunk, 0, 0)))
            flat.append(table)
    specs += [pl.BlockSpec(memory_space=pl.ANY)] * len(late)
    size = sum(4 * array.size for array in list(ready) + list(arrays) + list(late))
    return pl.pallas_call(
        functools.partial(kernel, plan),
        grid=(1,) if tables else (),
        in_specs=[pl.BlockSpec(memory_space=pltpu.SMEM)] + specs,
        out_specs=out_specs,
        out_shape=[jax.ShapeDtypeStruct(shape, jnp.float32) for shape in out_shapes],
        scratch_shapes=scratch,
        compiler_params=pltpu.CompilerParams(vmem_limit_bytes=VMEM_LIMIT),
        cost_estimate=pl.CostEstimate(
            flops=work * 12 * plan.nx * plan.ny * plan.x_chunk,
            bytes_accessed=size + sum(2 * table.size for table in flat),
            transcendentals=0,
        ),
        name=name,
    )(me, *ready, *arrays, *flat, *late)


def gather_kernel(
    plan, chunk, sent, high_in, low_in, before_in, counts_in, projection, out, scratch, held, sems,
    pieces, high, low, before, counts
):
    planes = plan.cell_planes
    rows = plan.slots * 2 * plan.row_block
    first = plan.tx_chunk
    copies = tile_copies(plan, chunk, projection, held, sems, 1)
    pairs = ((sent, pieces), (high_in, high), (low_in, low), (before_in, before), (counts_in, counts))
    loads = [pltpu.make_async_copy(*pair, sems.at[first + n]) for n, pair in enumerate(pairs)]
    for copy in loads[:3] + copies + loads[3:]:
        copy.start()
    for copy in loads[:3]:
        copy.wait()
    columns = [pieces[:, :, step].reshape(rows, LANES) for step in range(plan.steps)]
    scratch[...] = product(split(jnp.concatenate(columns, axis=1).T), (high[...], low[...]))
    for copy in loads[3:]:
        copy.wait()
    for tx in range(plan.tx_chunk):
        copies[tx].wait()
        last = chunk == CHUNKS - 1 and tx == plan.tx_chunk - 1

        def body(place, carry, tx=tx, last=last):
            lanes = pl.ds(pl.multiple_of(place * LANES, LANES), LANES)
            far = [(before if tx == 0 else out)[p, :, lanes] for p in range(plan.panels)]
            for ty in range(TY):
                row = ((place * TY + ty) * plan.tx_chunk + tx) * planes
                rows_at = pl.ds(pl.multiple_of(row, planes), planes)
                for tz in range(TZ):
                    t = ty * TZ + tz
                    potential = scratch[rows_at, tz * LANES : (tz + 1) * LANES]
                    for p in range(plan.panels):
                        far[p] = far[p] + held[tx, p, t, :, lanes] * potential
            for p in range(plan.panels):
                out[p, :, lanes] = jnp.where(counts[:, lanes] > p, far[p], 0.0) if last else far[p]
            return carry

        lax.fori_loop(0, plan.steps * plan.step_blocks, body, 0, unroll=True)


def gather(plan, chunk, counts, before, projection, high, low, pieces):
    kernel = functools.partial(gather_kernel, plan, chunk)
    arrays = [pieces, high, low, before, counts]
    return projection_call(plan, kernel, "depth_gather", arrays, projection, before.shape)


def near_kernel(plan, extended, codes, blocks_ref, out):
    step = pl.program_id(0)
    lane = lax.broadcasted_iota(jnp.int32, (plan.cell_planes, LANES), 1)
    depth = lane % NZC
    digits = []
    for k in range(plan.near):
        code = codes[k]
        digits.append((code // 9, code // 3 % 3, code % 3))
    total = [None] * plan.panels
    for q in range(plan.panels):
        shifted = []
        for dx in range(3):
            before, here, after = (
                extended[q, dx, :, pl.ds(pl.multiple_of((step + i) * LANES, LANES), LANES)] for i in range(3)
            )
            up = jnp.where(lane < NZC, pltpu.roll(before, NZC, 1), pltpu.roll(here, NZC, 1))
            down = jnp.where(
                lane >= LANES - NZC, pltpu.roll(after, LANES - NZC, 1), pltpu.roll(here, LANES - NZC, 1)
            )
            for value in (up, here, down):
                under = jnp.where(
                    depth == 0, pltpu.roll(value, LANES - NZC + 1, 1), pltpu.roll(value, 1, 1)
                )
                over = jnp.where(
                    depth == NZC - 1, pltpu.roll(value, NZC - 1, 1), pltpu.roll(value, LANES - 1, 1)
                )
                shifted.append((under, value, over))
        for k in range(plan.near):
            digit_x, digit_y, digit_z = digits[k]

            def choose(digit, options):
                return jnp.where(digit == 0, options[0], jnp.where(digit == 1, options[1], options[2]))

            by_z = [choose(digit_z, options) for options in shifted]
            by_y = [choose(digit_y, by_z[3 * i : 3 * i + 3]) for i in range(3)]
            picked = choose(digit_x, by_y)
            for p in range(plan.panels):
                term = blocks_ref[k, p, q] * picked
                total[p] = term if total[p] is None else total[p] + term
    for p in range(plan.panels):
        out[p] = total[p]


def near_field(plan, extended, neighbours, near_blocks):
    return pl.pallas_call(
        functools.partial(near_kernel, plan),
        grid=(plan.cell_cols // LANES,),
        in_specs=[
            whole_spec(extended.shape),
            pl.BlockSpec((plan.near, plan.cell_planes, LANES), lambda i: (0, 0, i)),
            pl.BlockSpec(
                (plan.near, plan.panels, plan.panels, plan.cell_planes, LANES), lambda i: (0, 0, 0, 0, i)
            ),
        ],
        out_specs=pl.BlockSpec((plan.panels, plan.cell_planes, LANES), lambda i: (0, 0, i)),
        out_shape=jax.ShapeDtypeStruct((plan.panels, plan.cell_planes, plan.cell_cols), jnp.float32),
        compiler_params=pltpu.CompilerParams(vmem_limit_bytes=VMEM_LIMIT),
        cost_estimate=pl.CostEstimate(
            flops=2 * near_blocks.size, bytes_accessed=4 * near_blocks.size, transcendentals=0
        ),
        name="near_blocks",
    )(extended, neighbours, near_blocks)


def ring_pairs(axis):
    count = lax.axis_size(axis)
    up = [(i, (i + 1) % count) for i in range(count)]
    return (up, [(j, i) for i, j in up])


def extend_rows(plan, masked):
    up, down = ring_pairs("cell")
    left = lax.ppermute(masked[:, :, -NZC:], "cell", up)
    right = lax.ppermute(masked[:, :, :NZC], "cell", down)
    return (left, right)


def extend_planes(plan, masked, left, right):
    rest = jnp.zeros((plan.panels, plan.cell_planes, LANES - NZC), jnp.float32)
    wide = jnp.concatenate([rest, left, masked, right, rest], axis=2)
    up, down = ring_pairs("slab")
    before = lax.ppermute(wide[:, -1:], "slab", up)
    after = lax.ppermute(wide[:, :1], "slab", down)
    whole = jnp.concatenate([before, wide, after], axis=1)
    planes = plan.cell_planes
    return jnp.stack([whole[:, i : i + planes] for i in range(3)], axis=1)


def pick_kernel(plan, ids_ref, by_depth, *refs):
    outs, sems = (refs[:-1], refs[-1])
    place = lax.rem(ids_ref[0], plan.half)
    first = ids_ref[0] - place
    copies = []
    for j in range(plan.outer):
        part = lax.rem(place // plan.inner + j, plan.outer) * plan.inner
        for i in range(plan.inner):
            n = len(copies)
            copies.append(
                pltpu.make_async_copy(by_depth.at[first + part + i], outs[j].at[i], sems.at[n])
            )
            freq = first + part + lax.rem(place + i, plan.inner)
            mirror = jnp.where(freq == 0, plan.nz // 2, plan.nz - freq)
            copies.append(
                pltpu.make_async_copy(by_depth.at[mirror], outs[plan.outer + i].at[j], sems.at[n + 1])
            )
    for copy in copies:
        copy.start()
    for copy in copies:
        copy.wait()


def pick_planes(plan, ids, spectrum):
    by_depth = jnp.transpose(spectrum, (1, 2, 0))
    shapes = [(plan.inner,) + by_depth.shape[1:]] * plan.outer
    shapes += [(plan.outer,) + by_depth.shape[1:]] * plan.inner
    picked = pl.pallas_call(
        functools.partial(pick_kernel, plan),
        in_specs=[pl.BlockSpec(memory_space=pltpu.SMEM), pl.BlockSpec(memory_space=pl.ANY)],
        out_specs=[pl.BlockSpec(memory_space=pltpu.VMEM)] * len(shapes),
        out_shape=[jax.ShapeDtypeStruct(shape, jnp.float32) for shape in shapes],
        scratch_shapes=[pltpu.SemaphoreType.DMA((2 * plan.half,))],
        cost_estimate=pl.CostEstimate(
            flops=0, bytes_accessed=8 * sum(math.prod(shape) for shape in shapes), transcendentals=0
        ),
        name="pick_planes",
    )(ids, by_depth)
    return (picked[: plan.outer], picked[plan.outer :])


def outer_shift(plan, value, j):
    if j == 0:
        return value
    pairs = []
    for source in range(plan.slabs):
        base = source // plan.half * plan.half
        pairs.append((source, base + (source - base + j * plan.inner) % plan.half))
    return lax.ppermute(value, "slab", pairs)


def inner_shift(plan, value, i):
    if i == 0:
        return value
    pairs = []
    for source in range(plan.slabs):
        base = source // plan.inner * plan.inner
        pairs.append((source, base + (source + i) % plan.inner))
    return lax.ppermute(value, "slab", pairs)


def edge_weights(plan, rows):
    middle = plan.nz // 2
    turned = jnp.concatenate([rows[middle : middle + 1], jnp.flip(rows, 0)], axis=0)[: plan.slots]
    shape = (plan.slots, plan.nx // LANES, LANES)
    plane = jnp.broadcast_to(rows[0].reshape(shape[1:]), shape)
    return jnp.concatenate([turned.reshape(shape), plane], axis=1)


def second_weights(plan, plain, mirror):
    slab = lax.axis_index("slab")
    strips = []
    for i in range(plan.inner):
        place = lax.rem(slab + i, plan.inner)
        rows = [lax.dynamic_slice_in_dim(block, place, 1, 0) for block in plain]
        strips.append(inner_shift(plan, jnp.concatenate(rows, axis=0), i))
    blocks = [outer_shift(plan, jnp.stack([m[j] for m in mirror]), j) for j in range(plan.outer)]
    return strips + blocks


def per_device(charges, counts, projection, near_blocks, neighbours, spectrum):
    panels, cell_planes, cell_cols = charges.shape
    cells, slabs = (lax.axis_size("cell"), lax.axis_size("slab"))
    nx, nz, local = spectrum.shape
    plan = Plan(slabs, cells, panels, cell_planes, cell_cols, neighbours.shape[0], nx, nz, local * slabs)
    if not plan.fits():
        return plain_device(charges, counts, projection, near_blocks, neighbours, spectrum)
    me = (lax.axis_index("cell") * slabs + lax.axis_index("slab")).astype(jnp.int32).reshape(1)
    forward_table, backward_table = plan.depth_tables()
    depth_forward, depth_backward = (halves(forward_table.T), halves(backward_table))
    y_rows, x_cols, low_ids = (plan.y_rows().reshape(-1), plan.x_columns(), np.arange(plan.ny // 2))
    cos_y, sin_y = wave(low_ids, y_rows, plan.ny)
    sin_y[0] = 1.0 - 2.0 * (y_rows % 2)
    y_forward = halves(np.concatenate([cos_y, sin_y], axis=0))
    y_backward = halves(np.concatenate([cos_y.T, -sin_y.T], axis=1))
    x_waves = [wave(cols, low_ids, plan.nx) for cols in x_cols]
    x_forward = halves(np.stack([np.concatenate(pair, axis=1) for pair in x_waves]))
    x_backward = halves(np.stack([np.concatenate([t.T for t in pair], axis=1) for pair in x_waves]))
    split_projection = projection.reshape(
        (panels, TX // CHUNKS, CHUNKS, TY * TZ, cell_planes, cell_cols)
    )
    axes = ("cell", "slab")

    def exchange(pieces):
        return lax.all_to_all(pieces, axes, split_axis=0, concat_axis=0, tiled=True)

    def values(*shapes):
        return [pltpu.VMEM(shape, jnp.float32) for shape in shapes]

    rows_shape = (plan.ny, 2 * plan.x_chunk)
    freq_shape = (2 * plan.ny, plan.x_chunk)
    both_shape = (2 * plan.ny, plan.nx)
    slot = lax.broadcasted_iota(jnp.int32, charges.shape, 0)
    masked = jnp.where(slot < counts[None], charges, 0.0)
    rows = jnp.transpose(spectrum[:, :, 0], (1, 0))
    first = project(plan, 0, charges, counts, split_projection, *depth_forward, None)
    first, late_me = lax.optimization_barrier((first, me))
    even_pieces = exchange(first)
    edges = edge_weights(plan, rows)
    second = project(plan, 1, charges, counts, split_projection, *depth_forward, edges)
    plain, mirror = pick_planes(plan, late_me, spectrum)
    plain = [outer_shift(plan, value, j) for j, value in enumerate(plain)]
    mirror = [inner_shift(plan, value, i) for i, value in enumerate(mirror)]
    second, masked = lax.optimization_barrier((second, masked))
    left, right = extend_rows(plan, masked)
    second, left, right, *moved = lax.optimization_barrier((second, left, right, *plain, *mirror))
    plain, mirror = (moved[: plan.outer], moved[plan.outer :])
    odd_pieces = exchange(second)
    strips = second_weights(plan, plain, mirror)
    in_place = pl.BlockSpec(memory_space=pl.ANY)
    (even,) = plane_call(
        plan, first_plane_kernel, "even_planes", me, [], [even_pieces],
        [(y_forward, None), (x_forward, 0)], [], [whole_spec(both_shape)], [both_shape],
        values(rows_shape, freq_shape), 2,
    )
    late = [odd_pieces, *y_forward, x_forward[0][1:], x_forward[1][1:], even]
    late += [x_backward[0][:1], x_backward[1][:1], *y_backward]
    copies = [pltpu.VMEM(array.shape, array.dtype) for array in late]
    copies.append(pltpu.SemaphoreType.DMA((len(late) + 2 * plan.half + 1,)))
    copies.append(pltpu.SemaphoreType.DMA((2 * plan.slots // plan.y_lanes,)))
    back, rest = plane_call(
        plan, middle_plane_kernel, "middle_planes", me, [], [], [], late + strips,
        [in_place, in_place], [piece_shape(plan), freq_shape],
        values(rows_shape, freq_shape, freq_shape, freq_shape, (2, plan.ny // 2, plan.nx))
        + values(piece_shape(plan)) + copies, 4,
    )
    even_back = exchange(back)
    (back,) = plane_call(
        plan, last_plane_kernel, "odd_planes", me, [], [rest],
        [(x_backward, 1), (y_backward, None)], [], [whole_spec(piece_shape(plan))], [piece_shape(plan)],
        values(rows_shape), 2,
    )
    back, masked = lax.optimization_barrier((back, masked))
    extended = extend_planes(plan, masked, left, right)
    back, extended = lax.optimization_barrier((back, extended))
    odd_back = exchange(back)
    total = near_field(plan, extended, neighbours, near_blocks)
    total = gather(plan, 0, counts, total, split_projection, *depth_backward, even_back)
    return gather(plan, 1, counts, total, split_projection, *depth_backward, odd_back)


def padded(value, sides, width):
    for axis, dim in sides:
        count, length = (lax.axis_size(axis), value.shape[dim])
        up = [(i, (i + 1) % count) for i in range(count)]
        down = [(j, i) for i, j in up]
        last = lax.slice_in_dim(value, length - width, length, axis=dim)
        first = lax.slice_in_dim(value, 0, width, axis=dim)
        before = lax.ppermute(last, axis, up)
        after = lax.ppermute(first, axis, down)
        value = jnp.concatenate([before, value, after], axis=dim)
    return value


def wave_tables(row_count, col_count, length):
    products = (
        lax.broadcasted_iota(jnp.int32, (row_count, col_count), 0)
        * lax.broadcasted_iota(jnp.int32, (row_count, col_count), 1)
        % length
    )
    angle_rad = products.astype(jnp.float32) * (2.0 * math.pi / length)
    return (jnp.cos(angle_rad), jnp.sin(angle_rad))


def depth_rows(nz, freq_ids, valid, weights):
    depth_ids = lax.broadcasted_iota(jnp.int32, (freq_ids.shape[0], nz), 1)
    products = freq_ids[:, None] * depth_ids % nz
    angle_rad = products.astype(jnp.float32) * (2.0 * math.pi / nz)
    basis = jnp.stack([jnp.cos(angle_rad), -jnp.sin(angle_rad)])
    return (basis * valid[None, :, None], basis * weights[None, :, None])


def half_depth_tables(nz, cell_count):
    lower = nz // (2 * cell_count)
    row_ids = lax.broadcasted_iota(jnp.int32, (cell_count * (lower + 1),), 0)
    block_ids = row_ids // (lower + 1)
    slot_ids = row_ids % (lower + 1)
    freq_ids = jnp.where(slot_ids < lower, block_ids * lower + slot_ids, nz // 2)
    valid = jnp.where((slot_ids < lower) | (block_ids == 0), 1.0, 0.0).astype(jnp.float32)
    doubled = jnp.where((slot_ids < lower) & (freq_ids > 0), 2.0, 1.0).astype(jnp.float32)
    forward_table, backward_table = depth_rows(nz, freq_ids, valid, valid * doubled)
    return (forward_table, backward_table, freq_ids)


def combine_halves(first_part, second, orient):
    half_width = first_part.shape[-1] // 2
    real_part = first_part[..., :half_width] + orient * second[..., half_width:]
    imag_part = first_part[..., half_width:] - orient * second[..., :half_width]
    return jnp.concatenate([real_part, imag_part], axis=-1)


def transform_axis(pattern, cosine, sine_tab, values, orient):
    first_part = jnp.einsum(pattern, cosine, values, precision=lax.Precision.HIGHEST)
    second = jnp.einsum(pattern, sine_tab, values, precision=lax.Precision.HIGHEST)
    return combine_halves(first_part, second, orient)


def twiddle(values, twist_cos, twist_sin, orient):
    half_width = values.shape[-1] // 2
    real_part = values[..., :half_width]
    imag_part = values[..., half_width:]
    new_real = real_part * twist_cos + orient * imag_part * twist_sin
    new_imag = imag_part * twist_cos - orient * real_part * twist_sin
    return jnp.concatenate([new_real, new_imag], axis=-1)


def transform_rows(planes_block, cosine, sine_tab, orient):
    flat_rows = planes_block.reshape(-1, planes_block.shape[-1])
    first_part = jnp.dot(flat_rows, cosine, precision=lax.Precision.HIGHEST).reshape(
        planes_block.shape
    )
    second = jnp.dot(flat_rows, sine_tab, precision=lax.Precision.HIGHEST).reshape(
        planes_block.shape
    )
    real_part = first_part[:, 0] + orient * second[:, 1]
    imag_part = first_part[:, 1] - orient * second[:, 0]
    return jnp.stack([real_part, imag_part], axis=1)


def plain_device(charges, counts, projection, near_blocks, neighbours, spectrum):
    panels, cell_planes, cell_cols = charges.shape
    nx, nz, ny = (spectrum.shape[0], spectrum.shape[1], spectrum.shape[2] * lax.axis_size("slab"))
    planes = cell_planes * TX
    rows_cell = cell_cols // NZC
    slot_ids = lax.broadcasted_iota(jnp.int32, charges.shape, 0)
    panel_mask = (slot_ids < counts[None]).astype(jnp.float32)
    masked = charges * panel_mask
    tile_values = jnp.einsum("ptxc,pxc->txc", projection, masked, precision=lax.Precision.HIGHEST)
    grid_field = (
        tile_values.reshape(TX, TY, TZ, cell_planes, rows_cell, NZC)
        .transpose(3, 0, 5, 2, 4, 1)
        .reshape(planes, nz, rows_cell * TY)
    )
    cell_count = lax.axis_size("cell")
    forward_table, backward_table, freq_ids = half_depth_tables(nz, cell_count)
    depth_count = forward_table.shape[1] // cell_count
    spectra_z = jnp.einsum(
        "wkz,xzy->xwky", forward_table, grid_field, precision=lax.Precision.HIGHEST
    )
    cosine_y, sine_y = wave_tables(ny, ny, ny)
    pencils = transform_rows(
        lax.all_to_all(spectra_z, "cell", split_axis=2, concat_axis=3, tiled=True),
        cosine_y,
        sine_y,
        1.0,
    )
    columns = lax.all_to_all(pencils, "slab", split_axis=3, concat_axis=0, tiled=True)
    col_width = columns.shape[2] * columns.shape[3]
    flat_rows = columns.reshape(nx, 2 * col_width)
    first_row = lax.axis_index("cell") * depth_count
    kernel_ids = lax.dynamic_slice_in_dim(freq_ids, first_row, depth_count, 0)
    kernel = jnp.take(spectrum, kernel_ids, axis=1).reshape(nx, col_width) * (1.0 / (nx * ny * nz))
    kernel_both = jnp.concatenate([kernel, kernel], axis=1)
    slab_count = lax.axis_size("slab")
    local_rows = nx // slab_count
    cosine_s, sine_s = wave_tables(slab_count, slab_count, slab_count)
    cosine_r, sine_r = wave_tables(local_rows, local_rows, local_rows)
    twist_cos, twist_sin = wave_tables(slab_count, local_rows, nx)
    twist_cos = twist_cos[:, :, None]
    twist_sin = twist_sin[:, :, None]
    section_one = transform_axis(
        "ks,src->krc",
        cosine_s,
        sine_s,
        flat_rows.reshape(slab_count, local_rows, 2 * col_width),
        1.0,
    )
    section_one = twiddle(section_one, twist_cos, twist_sin, 1.0)
    section_two = transform_axis("jr,krc->jkc", cosine_r, sine_r, section_one, 1.0)
    weighted = section_two.reshape(nx, 2 * col_width) * kernel_both
    section_one = transform_axis(
        "rj,jkc->krc",
        cosine_r,
        sine_r,
        weighted.reshape(local_rows, slab_count, 2 * col_width),
        -1.0,
    )
    section_one = twiddle(section_one, twist_cos, twist_sin, -1.0)
    section_two = transform_axis("sk,krc->src", cosine_s, sine_s, section_one, -1.0)
    returned_x = section_two.reshape(nx, 2 * col_width)
    returned = lax.all_to_all(
        returned_x.reshape(columns.shape), "slab", split_axis=0, concat_axis=3, tiled=True
    )
    inverse_rows = transform_rows(returned, cosine_y, sine_y, -1.0)
    grid_potential = jnp.einsum(
        "wkz,xwky->xzy",
        backward_table,
        lax.all_to_all(inverse_rows, "cell", split_axis=3, concat_axis=2, tiled=True),
        precision=lax.Precision.HIGHEST,
    )
    tile_potential = (
        grid_potential.reshape(cell_planes, TX, NZC, TZ, rows_cell, TY)
        .transpose(1, 5, 3, 0, 4, 2)
        .reshape(TX * TY * TZ, cell_planes, cell_cols)
    )
    far_field = jnp.einsum(
        "ptxc,txc->pxc", projection, tile_potential, precision=lax.Precision.HIGHEST
    )
    block = masked.reshape(panels, cell_planes, rows_cell, NZC)
    extended = padded(block, (("slab", 1), ("cell", 2)), 1)
    flat_ext = extended.reshape(panels, -1)
    step_x = neighbours // 9 - 1
    step_y = neighbours // 3 % 3 - 1
    step_z = neighbours % 3 - 1
    plane_ids = lax.broadcasted_iota(jnp.int32, neighbours.shape, 1)
    col_ids = lax.broadcasted_iota(jnp.int32, neighbours.shape, 2)
    row_ids = col_ids // NZC
    depth_ids = col_ids % NZC
    near_ids = ((plane_ids + step_x + 1) * (rows_cell + 2) + row_ids + step_y + 1) * NZC + (
        depth_ids + step_z
    ) % NZC
    near_count = neighbours.shape[0]
    picked = jnp.take(flat_ext, near_ids.reshape(-1), axis=1).reshape(
        panels, near_count, cell_planes, cell_cols
    )
    near_field = jnp.einsum("kpqxc,qkxc->pxc", near_blocks, picked, precision=lax.Precision.HIGHEST)
    return (far_field + near_field) * panel_mask


def solution(mesh):
    in_specs = (
        P(None, "slab", "cell"),
        P("slab", "cell"),
        P(None, None, "slab", "cell"),
        P(None, None, None, "slab", "cell"),
        P(None, "slab", "cell"),
        P(None, None, "slab"),
    )
    out_specs = P(None, "slab", "cell")
    return jax.shard_map(
        per_device, mesh=mesh, in_specs=in_specs, out_specs=out_specs, check_vma=False
    )
```

```python
import functools
import math

import jax
import jax.numpy as jnp
import ml_dtypes
import numpy as np
from jax import lax
from jax.experimental import pallas as pl
from jax.experimental.pallas import tpu as pltpu
from jax.sharding import PartitionSpec as P

TX = 4
TY = 4
TZ = 4
NZC = 16
LANES = 128
CHUNKS = 2
VMEM_LIMIT = 127 * 512 * 1024


def halves(table):
    high = table.astype(np.float32).astype(ml_dtypes.bfloat16)
    low = (table - high.astype(np.float64)).astype(np.float32).astype(ml_dtypes.bfloat16)
    return (high, low)


def wave(rows, cols, length):
    angle = (rows[:, None] * cols[None, :] % length) * (2.0 * math.pi / length)
    return (np.cos(angle), np.sin(angle))


class Plan:
    def __init__(self, slabs, cells, panels, cell_planes, cell_cols, near, nx, nz, ny):
        self.slabs, self.cells = (slabs, cells)
        self.panels, self.cell_planes, self.cell_cols, self.near = (panels, cell_planes, cell_cols, near)
        self.nx, self.ny, self.nz = (nx, ny, nz)
        self.slots = slabs * cells
        self.tx_chunk = TX // CHUNKS
        self.width = cell_planes * self.tx_chunk
        self.y_lanes = LANES // self.width if self.width else 1
        self.row_block = LANES // NZC
        self.step_blocks = self.y_lanes // TY
        self.steps = cell_cols // (LANES * self.step_blocks) if self.step_blocks else 0
        self.x_chunk = nx // CHUNKS
        self.ky_local = ny // slabs
        self.piece_rows = 2 * self.steps * self.row_block
        self.half = slabs // 2
        self.outer = math.gcd(self.half, 2)
        self.inner = self.half // self.outer

    def fits(self):
        return (
            self.slots * 2 == self.nz
            and self.cell_planes == 8
            and self.step_blocks * TY * self.width == LANES
            and self.slabs % self.y_lanes == 0
            and self.ky_local % 8 == 0
            and self.steps * self.step_blocks * LANES == self.cell_cols
            and self.x_chunk % LANES == 0
            and self.nx == self.ny == 4 * LANES
            and self.ny % 1024 == self.nx % 1024 == 512
        )

    def depth_tables(self):
        depth = np.arange(NZC)[None, :] * TZ + np.arange(TZ)[:, None]
        scale = 1.0 / (self.nx * self.ny * self.nz)
        forward = np.zeros((self.slots, 2, self.row_block, TZ, self.row_block, NZC))
        backward = np.zeros_like(forward)
        for freq in range(self.slots):
            angle = (freq * depth % self.nz) * (2.0 * math.pi / self.nz)
            real, imag = (np.cos(angle), -np.sin(angle))
            factor = 2.0 * scale
            if freq == 0:
                imag = np.cos(depth * math.pi)
                factor = scale
            for row in range(self.row_block):
                forward[freq, 0, row, :, row, :] = real
                forward[freq, 1, row, :, row, :] = imag
                backward[freq, 0, row, :, row, :] = factor * real
                backward[freq, 1, row, :, row, :] = factor * imag
        shape = (self.slots * 2 * self.row_block, TZ * LANES)
        return (forward.reshape(shape), backward.reshape(shape))

    def y_rows(self):
        parity, cell, step, block, tile, row = np.meshgrid(
            *[np.arange(n) for n in (2, self.cells, self.steps, self.step_blocks, TY // 2, self.row_block)],
            indexing="ij",
        )
        cell_row = ((cell * self.steps + step) * self.step_blocks + block) * self.row_block + row
        return (cell_row * TY + 2 * tile + parity).reshape(2, -1)

    def x_columns(self):
        parity, slab, tile, plane = np.meshgrid(
            *[np.arange(n) for n in (2, self.slabs, TX // 2, self.cell_planes)], indexing="ij"
        )
        return ((slab * self.cell_planes + plane) * TX + 2 * tile + parity).reshape(2, -1)

    def row_of(self, cell, step, place):
        block, tile = (place // TY, place % TY)
        inner = (cell * self.steps + step) * self.step_blocks + block
        return (tile % 2) * (self.ny // 2) + (inner * (TY // 2) + tile // 2) * self.row_block


def split(value):
    high = value.astype(jnp.bfloat16)
    low = (value - high.astype(jnp.float32)).astype(jnp.bfloat16)
    return (high, low)


def product(left, right, dims=((1,), (0,))):
    first = jnp.concatenate([left[0], left[0], left[1]], axis=dims[0][0])
    second = jnp.concatenate([right[0], right[1], right[0]], axis=dims[1][0])
    return lax.dot_general(first, second, (dims, ((), ())), preferred_element_type=jnp.float32)


def swap_groups(parts, width):
    count = len(parts)
    lane = lax.broadcasted_iota(jnp.int32, parts[0].shape, 1)
    parts = list(parts)
    step = count // 2
    while step >= 1:
        shift = step * width
        upper = (lane // shift) % 2 == 1
        for i in range(count):
            if i & step:
                continue
            first, second = (parts[i], parts[i + step])
            parts[i] = jnp.where(upper, pltpu.roll(second, shift, 1), first)
            parts[i + step] = jnp.where(upper, second, pltpu.roll(first, LANES - shift, 1))
        step //= 2
    return parts


def tile_copies(plan, chunk, projection, held, sems, parts):
    count = TY * TZ // parts
    copies = []
    for tx in range(plan.tx_chunk):
        for part in range(parts):
            rows = pl.ds(part * count, count)
            source = projection.at[:, tx, chunk, rows]
            copies.append(pltpu.make_async_copy(source, held.at[tx, :, rows], sems.at[len(copies)]))
    return copies


def project_kernel(plan, chunk, *refs):
    edges = chunk == CHUNKS - 1
    count_in = 5 if edges else 4
    arrays_in, projection, out = (refs[:count_in], refs[count_in], refs[count_in + 1])
    scratch, held, sems = refs[count_in + 2 : count_in + 5]
    arrays = refs[count_in + 5 :]
    charges, counts, high, low = arrays[:4]
    planes = plan.cell_planes
    copies = tile_copies(plan, chunk, projection, held, sems, TY)
    loads = [
        pltpu.make_async_copy(source, place, sems.at[len(copies) + n])
        for n, (source, place) in enumerate(zip(arrays_in, arrays))
    ]
    for copy in loads[:2] + copies + loads[2:]:
        copy.start()
    for copy in loads[:2]:
        copy.wait()
    for n, copy in enumerate(copies):
        copy.wait()

        def body(place, carry, tx=n // TY, ty=n % TY):
            lanes = pl.ds(pl.multiple_of(place * LANES, LANES), LANES)
            count = counts[:, lanes]
            own = [jnp.where(count > p, charges[p, :, lanes], 0.0) for p in range(plan.panels)]
            row = ((place * TY + ty) * plan.tx_chunk + tx) * planes
            rows = pl.ds(pl.multiple_of(row, planes), planes)
            for tz in range(TZ):
                t = ty * TZ + tz
                total = held[tx, 0, t, :, lanes] * own[0]
                for p in range(1, plan.panels):
                    total = total + held[tx, p, t, :, lanes] * own[p]
                scratch[rows, tz * LANES : (tz + 1) * LANES] = total
            return carry

        lax.fori_loop(0, plan.steps * plan.step_blocks, body, 0, unroll=True)
    for copy in loads[2:]:
        copy.wait()
    spectra = product(split(scratch[...]), (high[...], low[...])).T
    shape = (plan.slots, 2, plan.row_block, LANES)
    for step in range(plan.steps):
        value = spectra[:, step * LANES : (step + 1) * LANES].reshape(shape)
        for part in range(2):
            row = (part * plan.steps + step) * plan.row_block
            out[:, row : row + plan.row_block] = value[:, part]
    if edges:
        out[:, plan.piece_rows :] = arrays[4][...]


def held_shape(plan):
    cols = plan.steps * plan.step_blocks * LANES
    return (plan.tx_chunk, plan.panels, TY * TZ, plan.cell_planes, cols)


def piece_shape(plan):
    return (plan.slots, 2, plan.steps, plan.row_block, LANES)


def whole_spec(shape):
    return pl.BlockSpec(shape, lambda i: (0,) * len(shape))


def projection_call(plan, kernel, name, arrays, projection, out_shape):
    return pl.pallas_call(
        kernel,
        in_specs=[pl.BlockSpec(memory_space=pl.ANY)] * (len(arrays) + 1),
        out_specs=pl.BlockSpec(memory_space=pltpu.VMEM),
        out_shape=jax.ShapeDtypeStruct(out_shape, jnp.float32),
        scratch_shapes=[
            pltpu.VMEM((plan.steps * LANES, TZ * LANES), jnp.float32),
            pltpu.VMEM(held_shape(plan), jnp.float32),
            pltpu.SemaphoreType.DMA((plan.tx_chunk * TY + len(arrays),)),
        ]
        + [pltpu.VMEM(array.shape, array.dtype) for array in arrays],
        compiler_params=pltpu.CompilerParams(vmem_limit_bytes=VMEM_LIMIT),
        cost_estimate=pl.CostEstimate(
            flops=2 * math.prod(held_shape(plan)),
            bytes_accessed=4 * math.prod(held_shape(plan)),
            transcendentals=0,
        ),
        name=name,
    )(*arrays, projection)


def project(plan, chunk, charges, counts, projection, high, low, edges):
    kernel = functools.partial(project_kernel, plan, chunk)
    arrays = [charges, counts, high, low] + ([] if edges is None else [edges])
    rows = plan.piece_rows + (0 if edges is None else edges.shape[1])
    return projection_call(plan, kernel, "project_depth", arrays, projection, (plan.slots, rows, LANES))


def far_sign(plan, me_ref):
    slab = lax.rem(me_ref[0], plan.slabs)
    return jnp.where(slab >= plan.half, -1.0, 1.0)


def forward_plane(plan, me_ref, pieces, y_table, x_table, rows_ref, freq_ref, waits=()):
    special = me_ref[0] == 0
    sign = far_sign(plan, me_ref)
    rows = 2 * plan.steps * plan.row_block
    width = plan.x_chunk
    middle = plan.ny // 2
    for cell in range(plan.cells):
        for group in range(plan.slabs // plan.y_lanes):
            first = cell * plan.slabs + group * plan.y_lanes
            parts = [pieces[first + i, :rows] for i in range(plan.y_lanes)]
            parts = swap_groups(parts, plan.width)
            for place, value in enumerate(parts):
                if place % 2 == 1:
                    value = value * sign
                for part in range(2):
                    for step in range(plan.steps):
                        source = (part * plan.steps + step) * plan.row_block
                        row = plan.row_of(cell, step, place)
                        col = part * width + group * LANES
                        rows_ref[row : row + plan.row_block, col : col + LANES] = value[
                            source : source + plan.row_block
                        ]
    for copy in waits:
        copy.wait()
    sums = product((y_table[0][...], y_table[1][...]), split(rows_ref[...]))
    cos_re, cos_im = (sums[:middle, :width], sums[:middle, width:])
    sin_re, sin_im = (sums[middle:, :width], sums[middle:, width:])
    first = lax.broadcasted_iota(jnp.int32, (middle, width), 0) == 0

    @pl.when(jnp.logical_not(special))
    def _():
        freq_ref[:middle] = jnp.where(first, cos_re, cos_re + sin_im)
        freq_ref[middle : 2 * middle] = jnp.where(first, cos_im, cos_im - sin_re)
        freq_ref[2 * middle : 3 * middle] = jnp.where(first, sin_re, cos_re - sin_im)
        freq_ref[3 * middle :] = jnp.where(first, sin_im, cos_im + sin_re)

    @pl.when(special)
    def _():
        freq_ref[:middle] = cos_re
        freq_ref[middle : 2 * middle] = jnp.where(first, sin_re, -sin_re)
        freq_ref[2 * middle : 3 * middle] = cos_im
        freq_ref[3 * middle :] = sin_im

    return product(split(freq_ref[...]), (x_table[0][0], x_table[1][0]))


def backward_plane(plan, me_ref, freqs, x_table, y_table, out, rows_ref):
    special = me_ref[0] == 0
    sign = far_sign(plan, me_ref)
    width = plan.x_chunk
    middle = plan.ny // 2
    sums = product(split(freqs), (x_table[0][0], x_table[1][0]))
    parts = []
    for mirrored, turn in ((0, 1.0), (1, -1.0)):
        re = slice(2 * mirrored * middle, (2 * mirrored + 1) * middle)
        im = slice((2 * mirrored + 1) * middle, (2 * mirrored + 2) * middle)
        parts.append(sums[re, :width] - turn * sums[im, width:])
        parts.append(sums[im, :width] + turn * sums[re, width:])
    re_n, im_n, re_m, im_m = parts
    first = lax.broadcasted_iota(jnp.int32, (middle, width), 0) == 0

    @pl.when(jnp.logical_not(special))
    def _():
        rows_ref[:middle, :width] = jnp.where(first, re_n, re_n + re_m)
        rows_ref[:middle, width:] = jnp.where(first, im_n, im_n + im_m)
        rows_ref[middle:, :width] = jnp.where(first, -re_m, im_n - im_m)
        rows_ref[middle:, width:] = jnp.where(first, -im_m, re_m - re_n)

    @pl.when(special)
    def _():
        rows_ref[:middle, :width] = jnp.where(first, re_n, 2.0 * re_n)
        rows_ref[:middle, width:] = jnp.where(first, re_m, 2.0 * re_m)
        rows_ref[middle:, :width] = jnp.where(first, -im_n, 2.0 * im_n)
        rows_ref[middle:, width:] = jnp.where(first, -im_m, -2.0 * im_m)

    rows_ref[...] = product((y_table[0][...], y_table[1][...]), split(rows_ref[...]))
    for cell in range(plan.cells):
        for group in range(plan.slabs // plan.y_lanes):
            parts = []
            for place in range(plan.y_lanes):
                tiles = []
                for part in range(2):
                    for step in range(plan.steps):
                        row = plan.row_of(cell, step, place)
                        col = part * width + group * LANES
                        tiles.append(rows_ref[row : row + plan.row_block, col : col + LANES])
                value = jnp.concatenate(tiles, axis=0)
                parts.append(value * sign if place % 2 == 1 else value)
            parts = swap_groups(parts, plan.width)
            first = cell * plan.slabs + group * plan.y_lanes
            for i in range(plan.y_lanes):
                out[first + i] = parts[i].reshape(2, plan.steps, plan.row_block, LANES)


def first_plane_kernel(plan, me_ref, pieces, y_high, y_low, x_high, x_low, out, rows_ref, freq_ref):
    out[...] = forward_plane(plan, me_ref, pieces, (y_high, y_low), (x_high, x_low), rows_ref, freq_ref)


def middle_plane_kernel(plan, me_ref, *refs):
    late, refs = (refs[:10], refs[10:])
    strips, refs = (refs[: plan.inner], refs[plan.inner :])
    blocks, refs = (refs[: plan.outer], refs[plan.outer :])
    out, rest, rows_ref, freq_ref, sum_ref, rest_ref, weights = refs[:7]
    held, sems = (refs[7:17], refs[17])
    pieces, yf_high, yf_low, xf_high, xf_low, even, xb_high, xb_low, yb_high, yb_low = held
    slab = lax.rem(me_ref[0], plan.slabs)
    place = lax.rem(slab, plan.half)
    outer_id, inner_id = (place // plan.inner, lax.rem(place, plan.inner))
    copies = [pltpu.make_async_copy(late[n], held[n], sems.at[n]) for n in range(len(held))]
    count = plan.ky_local
    placed = []
    for i in range(plan.inner):
        for j in range(plan.outer):
            owner = lax.rem(outer_id - j + plan.outer, plan.outer) * plan.inner
            owner = owner + lax.rem(inner_id - i + plan.inner, plan.inner)
            rows = pl.ds(pl.multiple_of(owner * count, count), count)
            for m, source in enumerate((strips[i].at[j], blocks[j].at[i])):
                sem = sems.at[len(held) + len(placed)]
                placed.append(pltpu.make_async_copy(source, weights.at[m, rows], sem))
    for copy in copies[:3]:
        copy.start()
    copies[0].wait()
    for copy in copies[3:6] + placed + copies[6:]:
        copy.start()
    cell_first = me_ref[0] - slab
    tile = pieces[cell_first + jnp.where(slab < plan.half, plan.half, 0), plan.piece_rows :]
    parts = plan.nx // LANES
    own_edge = jnp.concatenate([tile[n : n + 1] for n in range(parts)], axis=1)
    edge = jnp.concatenate([tile[n : n + 1] for n in range(parts, 2 * parts)], axis=1)
    special = me_ref[0] == 0
    width = plan.x_chunk
    middle = plan.ny // 2
    x_table = (xf_high.at[pl.ds(0, 1)], xf_low.at[pl.ds(0, 1)])
    odd = forward_plane(
        plan, me_ref, pieces, (yf_high, yf_low), x_table, rows_ref, freq_ref, copies[1:5]
    )
    for copy in copies[5:6] + placed:
        copy.wait()
    row = lax.broadcasted_iota(jnp.int32, (middle, width), 0)
    at_first = row == 0
    for mirrored, turn in ((0, 1.0), (1, -1.0)):
        re = slice(2 * mirrored * middle, (2 * mirrored + 1) * middle)
        im = slice((2 * mirrored + 1) * middle, (2 * mirrored + 2) * middle)
        results = []
        for upper in range(2):
            cols = slice(upper * width, (upper + 1) * width)
            plane = weights[mirrored, :, cols]
            if mirrored:
                second = jnp.where(at_first, own_edge[:, cols], plane)
                weight = jnp.where(special, plane, second)
            else:
                weight = plane
                second = jnp.where(at_first & special, edge[0:1, cols], plane)
            re_sums = even[re] - odd[re] if upper else even[re] + odd[re]
            im_sums = even[im] - odd[im] if upper else even[im] + odd[im]
            real = weight * re_sums[:, :width] + (turn * second) * im_sums[:, width:]
            imag = second * im_sums[:, :width] - (turn * weight) * re_sums[:, width:]
            results.append((real, imag))
        for part, rows in enumerate((re, im)):
            below, above = (results[0][part], results[1][part])
            sum_ref[rows] = below + above
            rest_ref[rows] = below - above
    last = pltpu.make_async_copy(rest_ref, rest, sems.at[len(held) + 2 * plan.half])
    last.start()
    for copy in copies[6:]:
        copy.wait()
    backward_plane(plan, me_ref, sum_ref[...], (xb_high, xb_low), (yb_high, yb_low), out, rows_ref)
    last.wait()


def last_plane_kernel(plan, me_ref, freqs, x_high, x_low, y_high, y_low, out, rows_ref):
    backward_plane(plan, me_ref, freqs[...], (x_high, x_low), (y_high, y_low), out, rows_ref)


def plane_call(plan, kernel, name, me, ready, arrays, tables, late, out_specs, out_shapes, scratch, work):
    specs = [pl.BlockSpec(memory_space=pltpu.VMEM)] * len(ready)
    specs += [whole_spec(array.shape) for array in arrays]
    flat = []
    for pair, chunk in tables:
        for table in pair:
            if chunk is None:
                specs.append(whole_spec(table.shape))
            else:
                specs.append(pl.BlockSpec((1,) + table.shape[1:], lambda i, chunk=chunk: (chunk, 0, 0)))
            flat.append(table)
    specs += [pl.BlockSpec(memory_space=pl.ANY)] * len(late)
    size = sum(4 * array.size for array in list(ready) + list(arrays) + list(late))
    return pl.pallas_call(
        functools.partial(kernel, plan),
        grid=(1,) if tables else (),
        in_specs=[pl.BlockSpec(memory_space=pltpu.SMEM)] + specs,
        out_specs=out_specs,
        out_shape=[jax.ShapeDtypeStruct(shape, jnp.float32) for shape in out_shapes],
        scratch_shapes=scratch,
        compiler_params=pltpu.CompilerParams(vmem_limit_bytes=VMEM_LIMIT),
        cost_estimate=pl.CostEstimate(
            flops=work * 12 * plan.nx * plan.ny * plan.x_chunk,
            bytes_accessed=size + sum(2 * table.size for table in flat),
            transcendentals=0,
        ),
        name=name,
    )(me, *ready, *arrays, *flat, *late)


def gather_kernel(
    plan, chunk, sent, high_in, low_in, before_in, counts_in, projection, out, scratch, held, sems,
    pieces, high, low, before, counts
):
    planes = plan.cell_planes
    rows = plan.slots * 2 * plan.row_block
    first = plan.tx_chunk
    copies = tile_copies(plan, chunk, projection, held, sems, 1)
    pairs = ((sent, pieces), (high_in, high), (low_in, low), (before_in, before), (counts_in, counts))
    loads = [pltpu.make_async_copy(*pair, sems.at[first + n]) for n, pair in enumerate(pairs)]
    for copy in loads[:3] + copies + loads[3:]:
        copy.start()
    for copy in loads[:3]:
        copy.wait()
    columns = [pieces[:, :, step].reshape(rows, LANES) for step in range(plan.steps)]
    scratch[...] = product(split(jnp.concatenate(columns, axis=1).T), (high[...], low[...]))
    for copy in loads[3:]:
        copy.wait()
    for tx in range(plan.tx_chunk):
        copies[tx].wait()
        last = chunk == CHUNKS - 1 and tx == plan.tx_chunk - 1

        def body(place, carry, tx=tx, last=last):
            lanes = pl.ds(pl.multiple_of(place * LANES, LANES), LANES)
            far = [(before if tx == 0 else out)[p, :, lanes] for p in range(plan.panels)]
            for ty in range(TY):
                row = ((place * TY + ty) * plan.tx_chunk + tx) * planes
                rows_at = pl.ds(pl.multiple_of(row, planes), planes)
                for tz in range(TZ):
                    t = ty * TZ + tz
                    potential = scratch[rows_at, tz * LANES : (tz + 1) * LANES]
                    for p in range(plan.panels):
                        far[p] = far[p] + held[tx, p, t, :, lanes] * potential
            for p in range(plan.panels):
                out[p, :, lanes] = jnp.where(counts[:, lanes] > p, far[p], 0.0) if last else far[p]
            return carry

        lax.fori_loop(0, plan.steps * plan.step_blocks, body, 0, unroll=True)


def gather(plan, chunk, counts, before, projection, high, low, pieces):
    kernel = functools.partial(gather_kernel, plan, chunk)
    arrays = [pieces, high, low, before, counts]
    return projection_call(plan, kernel, "depth_gather", arrays, projection, before.shape)


def near_kernel(plan, extended, codes, blocks_ref, out):
    step = pl.program_id(0)
    lane = lax.broadcasted_iota(jnp.int32, (plan.cell_planes, LANES), 1)
    depth = lane % NZC
    digits = []
    for k in range(plan.near):
        code = codes[k]
        digits.append((code // 9, code // 3 % 3, code % 3))
    total = [None] * plan.panels
    for q in range(plan.panels):
        shifted = []
        for dx in range(3):
            before, here, after = (
                extended[q, dx, :, pl.ds(pl.multiple_of((step + i) * LANES, LANES), LANES)] for i in range(3)
            )
            up = jnp.where(lane < NZC, pltpu.roll(before, NZC, 1), pltpu.roll(here, NZC, 1))
            down = jnp.where(
                lane >= LANES - NZC, pltpu.roll(after, LANES - NZC, 1), pltpu.roll(here, LANES - NZC, 1)
            )
            for value in (up, here, down):
                under = jnp.where(
                    depth == 0, pltpu.roll(value, LANES - NZC + 1, 1), pltpu.roll(value, 1, 1)
                )
                over = jnp.where(
                    depth == NZC - 1, pltpu.roll(value, NZC - 1, 1), pltpu.roll(value, LANES - 1, 1)
                )
                shifted.append((under, value, over))
        for k in range(plan.near):
            digit_x, digit_y, digit_z = digits[k]

            def choose(digit, options):
                return jnp.where(digit == 0, options[0], jnp.where(digit == 1, options[1], options[2]))

            by_z = [choose(digit_z, options) for options in shifted]
            by_y = [choose(digit_y, by_z[3 * i : 3 * i + 3]) for i in range(3)]
            picked = choose(digit_x, by_y)
            for p in range(plan.panels):
                term = blocks_ref[k, p, q] * picked
                total[p] = term if total[p] is None else total[p] + term
    for p in range(plan.panels):
        out[p] = total[p]


def near_field(plan, extended, neighbours, near_blocks):
    return pl.pallas_call(
        functools.partial(near_kernel, plan),
        grid=(plan.cell_cols // LANES,),
        in_specs=[
            whole_spec(extended.shape),
            pl.BlockSpec((plan.near, plan.cell_planes, LANES), lambda i: (0, 0, i)),
            pl.BlockSpec(
                (plan.near, plan.panels, plan.panels, plan.cell_planes, LANES), lambda i: (0, 0, 0, 0, i)
            ),
        ],
        out_specs=pl.BlockSpec((plan.panels, plan.cell_planes, LANES), lambda i: (0, 0, i)),
        out_shape=jax.ShapeDtypeStruct((plan.panels, plan.cell_planes, plan.cell_cols), jnp.float32),
        compiler_params=pltpu.CompilerParams(vmem_limit_bytes=VMEM_LIMIT),
        cost_estimate=pl.CostEstimate(
            flops=2 * near_blocks.size, bytes_accessed=4 * near_blocks.size, transcendentals=0
        ),
        name="near_blocks",
    )(extended, neighbours, near_blocks)


def ring_pairs(axis):
    count = lax.axis_size(axis)
    up = [(i, (i + 1) % count) for i in range(count)]
    return (up, [(j, i) for i, j in up])


def extend_rows(plan, masked):
    up, down = ring_pairs("cell")
    left = lax.ppermute(masked[:, :, -NZC:], "cell", up)
    right = lax.ppermute(masked[:, :, :NZC], "cell", down)
    return (left, right)


def extend_planes(plan, masked, left, right):
    rest = jnp.zeros((plan.panels, plan.cell_planes, LANES - NZC), jnp.float32)
    wide = jnp.concatenate([rest, left, masked, right, rest], axis=2)
    up, down = ring_pairs("slab")
    before = lax.ppermute(wide[:, -1:], "slab", up)
    after = lax.ppermute(wide[:, :1], "slab", down)
    whole = jnp.concatenate([before, wide, after], axis=1)
    planes = plan.cell_planes
    return jnp.stack([whole[:, i : i + planes] for i in range(3)], axis=1)


def pick_kernel(plan, ids_ref, by_depth, *refs):
    outs, sems = (refs[:-1], refs[-1])
    place = lax.rem(ids_ref[0], plan.half)
    first = ids_ref[0] - place
    copies = []
    for j in range(plan.outer):
        part = lax.rem(place // plan.inner + j, plan.outer) * plan.inner
        for i in range(plan.inner):
            n = len(copies)
            copies.append(
                pltpu.make_async_copy(by_depth.at[first + part + i], outs[j].at[i], sems.at[n])
            )
            freq = first + part + lax.rem(place + i, plan.inner)
            mirror = jnp.where(freq == 0, plan.nz // 2, plan.nz - freq)
            copies.append(
                pltpu.make_async_copy(by_depth.at[mirror], outs[plan.outer + i].at[j], sems.at[n + 1])
            )
    for copy in copies:
        copy.start()
    for copy in copies:
        copy.wait()


def pick_planes(plan, ids, spectrum):
    by_depth = jnp.transpose(spectrum, (1, 2, 0))
    shapes = [(plan.inner,) + by_depth.shape[1:]] * plan.outer
    shapes += [(plan.outer,) + by_depth.shape[1:]] * plan.inner
    picked = pl.pallas_call(
        functools.partial(pick_kernel, plan),
        in_specs=[pl.BlockSpec(memory_space=pltpu.SMEM), pl.BlockSpec(memory_space=pl.ANY)],
        out_specs=[pl.BlockSpec(memory_space=pltpu.VMEM)] * len(shapes),
        out_shape=[jax.ShapeDtypeStruct(shape, jnp.float32) for shape in shapes],
        scratch_shapes=[pltpu.SemaphoreType.DMA((2 * plan.half,))],
        cost_estimate=pl.CostEstimate(
            flops=0, bytes_accessed=8 * sum(math.prod(shape) for shape in shapes), transcendentals=0
        ),
        name="pick_planes",
    )(ids, by_depth)
    return (picked[: plan.outer], picked[plan.outer :])


def outer_shift(plan, value, j):
    if j == 0:
        return value
    pairs = []
    for source in range(plan.slabs):
        base = source // plan.half * plan.half
        pairs.append((source, base + (source - base + j * plan.inner) % plan.half))
    return lax.ppermute(value, "slab", pairs)


def inner_shift(plan, value, i):
    if i == 0:
        return value
    pairs = []
    for source in range(plan.slabs):
        base = source // plan.inner * plan.inner
        pairs.append((source, base + (source + i) % plan.inner))
    return lax.ppermute(value, "slab", pairs)


def edge_weights(plan, rows):
    middle = plan.nz // 2
    turned = jnp.concatenate([rows[middle : middle + 1], jnp.flip(rows, 0)], axis=0)[: plan.slots]
    shape = (plan.slots, plan.nx // LANES, LANES)
    plane = jnp.broadcast_to(rows[0].reshape(shape[1:]), shape)
    return jnp.concatenate([turned.reshape(shape), plane], axis=1)


def second_weights(plan, plain, mirror):
    slab = lax.axis_index("slab")
    strips = []
    for i in range(plan.inner):
        place = lax.rem(slab + i, plan.inner)
        rows = [lax.dynamic_slice_in_dim(block, place, 1, 0) for block in plain]
        strips.append(inner_shift(plan, jnp.concatenate(rows, axis=0), i))
    blocks = [outer_shift(plan, jnp.stack([m[j] for m in mirror]), j) for j in range(plan.outer)]
    return strips + blocks


def per_device(charges, counts, projection, near_blocks, neighbours, spectrum):
    panels, cell_planes, cell_cols = charges.shape
    cells, slabs = (lax.axis_size("cell"), lax.axis_size("slab"))
    nx, nz, local = spectrum.shape
    plan = Plan(slabs, cells, panels, cell_planes, cell_cols, neighbours.shape[0], nx, nz, local * slabs)
    if not plan.fits():
        return plain_device(charges, counts, projection, near_blocks, neighbours, spectrum)
    me = (lax.axis_index("cell") * slabs + lax.axis_index("slab")).astype(jnp.int32).reshape(1)
    forward_table, backward_table = plan.depth_tables()
    depth_forward, depth_backward = (halves(forward_table.T), halves(backward_table))
    y_rows, x_cols, low_ids = (plan.y_rows().reshape(-1), plan.x_columns(), np.arange(plan.ny // 2))
    cos_y, sin_y = wave(low_ids, y_rows, plan.ny)
    sin_y[0] = 1.0 - 2.0 * (y_rows % 2)
    y_forward = halves(np.concatenate([cos_y, sin_y], axis=0))
    y_backward = halves(np.concatenate([cos_y.T, -sin_y.T], axis=1))
    x_waves = [wave(cols, low_ids, plan.nx) for cols in x_cols]
    x_forward = halves(np.stack([np.concatenate(pair, axis=1) for pair in x_waves]))
    x_backward = halves(np.stack([np.concatenate([t.T for t in pair], axis=1) for pair in x_waves]))
    split_projection = projection.reshape(
        (panels, TX // CHUNKS, CHUNKS, TY * TZ, cell_planes, cell_cols)
    )
    axes = ("cell", "slab")

    def exchange(pieces):
        return lax.all_to_all(pieces, axes, split_axis=0, concat_axis=0, tiled=True)

    def values(*shapes):
        return [pltpu.VMEM(shape, jnp.float32) for shape in shapes]

    rows_shape = (plan.ny, 2 * plan.x_chunk)
    freq_shape = (2 * plan.ny, plan.x_chunk)
    both_shape = (2 * plan.ny, plan.nx)
    slot = lax.broadcasted_iota(jnp.int32, charges.shape, 0)
    masked = jnp.where(slot < counts[None], charges, 0.0)
    rows = jnp.transpose(spectrum[:, :, 0], (1, 0))
    first = project(plan, 0, charges, counts, split_projection, *depth_forward, None)
    first, late_me = lax.optimization_barrier((first, me))
    even_pieces = exchange(first)
    edges = edge_weights(plan, rows)
    second = project(plan, 1, charges, counts, split_projection, *depth_forward, edges)
    plain, mirror = pick_planes(plan, late_me, spectrum)
    plain = [outer_shift(plan, value, j) for j, value in enumerate(plain)]
    mirror = [inner_shift(plan, value, i) for i, value in enumerate(mirror)]
    second, masked = lax.optimization_barrier((second, masked))
    left, right = extend_rows(plan, masked)
    second, left, right, *moved = lax.optimization_barrier((second, left, right, *plain, *mirror))
    plain, mirror = (moved[: plan.outer], moved[plan.outer :])
    odd_pieces = exchange(second)
    strips = second_weights(plan, plain, mirror)
    in_vmem = pl.BlockSpec(memory_space=pltpu.VMEM)
    in_place = pl.BlockSpec(memory_space=pl.ANY)
    (even,) = plane_call(
        plan, first_plane_kernel, "even_planes", me, [], [even_pieces],
        [(y_forward, None), (x_forward, 0)], [], [whole_spec(both_shape)], [both_shape],
        values(rows_shape, freq_shape), 2,
    )
    late = [odd_pieces, *y_forward, x_forward[0][1:], x_forward[1][1:], even]
    late += [x_backward[0][:1], x_backward[1][:1], *y_backward]
    copies = [pltpu.VMEM(array.shape, array.dtype) for array in late]
    copies.append(pltpu.SemaphoreType.DMA((len(late) + 2 * plan.half + 1,)))
    back, rest = plane_call(
        plan, middle_plane_kernel, "middle_planes", me, [], [], [], late + strips, [in_vmem, in_place], [piece_shape(plan), freq_shape],
        values(rows_shape, freq_shape, freq_shape, freq_shape, (2, plan.ny // 2, plan.nx)) + copies, 4,
    )
    even_back = exchange(back)
    (back,) = plane_call(
        plan, last_plane_kernel, "odd_planes", me, [], [rest],
        [(x_backward, 1), (y_backward, None)], [], [whole_spec(piece_shape(plan))], [piece_shape(plan)],
        values(rows_shape), 2,
    )
    back, masked = lax.optimization_barrier((back, masked))
    extended = extend_planes(plan, masked, left, right)
    back, extended = lax.optimization_barrier((back, extended))
    odd_back = exchange(back)
    total = near_field(plan, extended, neighbours, near_blocks)
    total = gather(plan, 0, counts, total, split_projection, *depth_backward, even_back)
    return gather(plan, 1, counts, total, split_projection, *depth_backward, odd_back)


def padded(value, sides, width):
    for axis, dim in sides:
        count, length = (lax.axis_size(axis), value.shape[dim])
        up = [(i, (i + 1) % count) for i in range(count)]
        down = [(j, i) for i, j in up]
        last = lax.slice_in_dim(value, length - width, length, axis=dim)
        first = lax.slice_in_dim(value, 0, width, axis=dim)
        before = lax.ppermute(last, axis, up)
        after = lax.ppermute(first, axis, down)
        value = jnp.concatenate([before, value, after], axis=dim)
    return value


def wave_tables(row_count, col_count, length):
    products = (
        lax.broadcasted_iota(jnp.int32, (row_count, col_count), 0)
        * lax.broadcasted_iota(jnp.int32, (row_count, col_count), 1)
        % length
    )
    angle_rad = products.astype(jnp.float32) * (2.0 * math.pi / length)
    return (jnp.cos(angle_rad), jnp.sin(angle_rad))


def depth_rows(nz, freq_ids, valid, weights):
    depth_ids = lax.broadcasted_iota(jnp.int32, (freq_ids.shape[0], nz), 1)
    products = freq_ids[:, None] * depth_ids % nz
    angle_rad = products.astype(jnp.float32) * (2.0 * math.pi / nz)
    basis = jnp.stack([jnp.cos(angle_rad), -jnp.sin(angle_rad)])
    return (basis * valid[None, :, None], basis * weights[None, :, None])


def half_depth_tables(nz, cell_count):
    lower = nz // (2 * cell_count)
    row_ids = lax.broadcasted_iota(jnp.int32, (cell_count * (lower + 1),), 0)
    block_ids = row_ids // (lower + 1)
    slot_ids = row_ids % (lower + 1)
    freq_ids = jnp.where(slot_ids < lower, block_ids * lower + slot_ids, nz // 2)
    valid = jnp.where((slot_ids < lower) | (block_ids == 0), 1.0, 0.0).astype(jnp.float32)
    doubled = jnp.where((slot_ids < lower) & (freq_ids > 0), 2.0, 1.0).astype(jnp.float32)
    forward_table, backward_table = depth_rows(nz, freq_ids, valid, valid * doubled)
    return (forward_table, backward_table, freq_ids)


def combine_halves(first_part, second, orient):
    half_width = first_part.shape[-1] // 2
    real_part = first_part[..., :half_width] + orient * second[..., half_width:]
    imag_part = first_part[..., half_width:] - orient * second[..., :half_width]
    return jnp.concatenate([real_part, imag_part], axis=-1)


def transform_axis(pattern, cosine, sine_tab, values, orient):
    first_part = jnp.einsum(pattern, cosine, values, precision=lax.Precision.HIGHEST)
    second = jnp.einsum(pattern, sine_tab, values, precision=lax.Precision.HIGHEST)
    return combine_halves(first_part, second, orient)


def twiddle(values, twist_cos, twist_sin, orient):
    half_width = values.shape[-1] // 2
    real_part = values[..., :half_width]
    imag_part = values[..., half_width:]
    new_real = real_part * twist_cos + orient * imag_part * twist_sin
    new_imag = imag_part * twist_cos - orient * real_part * twist_sin
    return jnp.concatenate([new_real, new_imag], axis=-1)


def transform_rows(planes_block, cosine, sine_tab, orient):
    flat_rows = planes_block.reshape(-1, planes_block.shape[-1])
    first_part = jnp.dot(flat_rows, cosine, precision=lax.Precision.HIGHEST).reshape(
        planes_block.shape
    )
    second = jnp.dot(flat_rows, sine_tab, precision=lax.Precision.HIGHEST).reshape(
        planes_block.shape
    )
    real_part = first_part[:, 0] + orient * second[:, 1]
    imag_part = first_part[:, 1] - orient * second[:, 0]
    return jnp.stack([real_part, imag_part], axis=1)


def plain_device(charges, counts, projection, near_blocks, neighbours, spectrum):
    panels, cell_planes, cell_cols = charges.shape
    nx, nz, ny = (spectrum.shape[0], spectrum.shape[1], spectrum.shape[2] * lax.axis_size("slab"))
    planes = cell_planes * TX
    rows_cell = cell_cols // NZC
    slot_ids = lax.broadcasted_iota(jnp.int32, charges.shape, 0)
    panel_mask = (slot_ids < counts[None]).astype(jnp.float32)
    masked = charges * panel_mask
    tile_values = jnp.einsum("ptxc,pxc->txc", projection, masked, precision=lax.Precision.HIGHEST)
    grid_field = (
        tile_values.reshape(TX, TY, TZ, cell_planes, rows_cell, NZC)
        .transpose(3, 0, 5, 2, 4, 1)
        .reshape(planes, nz, rows_cell * TY)
    )
    cell_count = lax.axis_size("cell")
    forward_table, backward_table, freq_ids = half_depth_tables(nz, cell_count)
    depth_count = forward_table.shape[1] // cell_count
    spectra_z = jnp.einsum(
        "wkz,xzy->xwky", forward_table, grid_field, precision=lax.Precision.HIGHEST
    )
    cosine_y, sine_y = wave_tables(ny, ny, ny)
    pencils = transform_rows(
        lax.all_to_all(spectra_z, "cell", split_axis=2, concat_axis=3, tiled=True),
        cosine_y,
        sine_y,
        1.0,
    )
    columns = lax.all_to_all(pencils, "slab", split_axis=3, concat_axis=0, tiled=True)
    col_width = columns.shape[2] * columns.shape[3]
    flat_rows = columns.reshape(nx, 2 * col_width)
    first_row = lax.axis_index("cell") * depth_count
    kernel_ids = lax.dynamic_slice_in_dim(freq_ids, first_row, depth_count, 0)
    kernel = jnp.take(spectrum, kernel_ids, axis=1).reshape(nx, col_width) * (1.0 / (nx * ny * nz))
    kernel_both = jnp.concatenate([kernel, kernel], axis=1)
    slab_count = lax.axis_size("slab")
    local_rows = nx // slab_count
    cosine_s, sine_s = wave_tables(slab_count, slab_count, slab_count)
    cosine_r, sine_r = wave_tables(local_rows, local_rows, local_rows)
    twist_cos, twist_sin = wave_tables(slab_count, local_rows, nx)
    twist_cos = twist_cos[:, :, None]
    twist_sin = twist_sin[:, :, None]
    section_one = transform_axis(
        "ks,src->krc",
        cosine_s,
        sine_s,
        flat_rows.reshape(slab_count, local_rows, 2 * col_width),
        1.0,
    )
    section_one = twiddle(section_one, twist_cos, twist_sin, 1.0)
    section_two = transform_axis("jr,krc->jkc", cosine_r, sine_r, section_one, 1.0)
    weighted = section_two.reshape(nx, 2 * col_width) * kernel_both
    section_one = transform_axis(
        "rj,jkc->krc",
        cosine_r,
        sine_r,
        weighted.reshape(local_rows, slab_count, 2 * col_width),
        -1.0,
    )
    section_one = twiddle(section_one, twist_cos, twist_sin, -1.0)
    section_two = transform_axis("sk,krc->src", cosine_s, sine_s, section_one, -1.0)
    returned_x = section_two.reshape(nx, 2 * col_width)
    returned = lax.all_to_all(
        returned_x.reshape(columns.shape), "slab", split_axis=0, concat_axis=3, tiled=True
    )
    inverse_rows = transform_rows(returned, cosine_y, sine_y, -1.0)
    grid_potential = jnp.einsum(
        "wkz,xwky->xzy",
        backward_table,
        lax.all_to_all(inverse_rows, "cell", split_axis=3, concat_axis=2, tiled=True),
        precision=lax.Precision.HIGHEST,
    )
    tile_potential = (
        grid_potential.reshape(cell_planes, TX, NZC, TZ, rows_cell, TY)
        .transpose(1, 5, 3, 0, 4, 2)
        .reshape(TX * TY * TZ, cell_planes, cell_cols)
    )
    far_field = jnp.einsum(
        "ptxc,txc->pxc", projection, tile_potential, precision=lax.Precision.HIGHEST
    )
    block = masked.reshape(panels, cell_planes, rows_cell, NZC)
    extended = padded(block, (("slab", 1), ("cell", 2)), 1)
    flat_ext = extended.reshape(panels, -1)
    step_x = neighbours // 9 - 1
    step_y = neighbours // 3 % 3 - 1
    step_z = neighbours % 3 - 1
    plane_ids = lax.broadcasted_iota(jnp.int32, neighbours.shape, 1)
    col_ids = lax.broadcasted_iota(jnp.int32, neighbours.shape, 2)
    row_ids = col_ids // NZC
    depth_ids = col_ids % NZC
    near_ids = ((plane_ids + step_x + 1) * (rows_cell + 2) + row_ids + step_y + 1) * NZC + (
        depth_ids + step_z
    ) % NZC
    near_count = neighbours.shape[0]
    picked = jnp.take(flat_ext, near_ids.reshape(-1), axis=1).reshape(
        panels, near_count, cell_planes, cell_cols
    )
    near_field = jnp.einsum("kpqxc,qkxc->pxc", near_blocks, picked, precision=lax.Precision.HIGHEST)
    return (far_field + near_field) * panel_mask


def solution(mesh):
    in_specs = (
        P(None, "slab", "cell"),
        P("slab", "cell"),
        P(None, None, "slab", "cell"),
        P(None, None, None, "slab", "cell"),
        P(None, "slab", "cell"),
        P(None, None, "slab"),
    )
    out_specs = P(None, "slab", "cell")
    return jax.shard_map(
        per_device, mesh=mesh, in_specs=in_specs, out_specs=out_specs, check_vma=False
    )
```

```python
import functools
import math

import jax
import jax.numpy as jnp
import ml_dtypes
import numpy as np
from jax import lax
from jax.experimental import pallas as pl
from jax.experimental.pallas import tpu as pltpu
from jax.sharding import PartitionSpec as P

TX = 4
TY = 4
TZ = 4
NZC = 16
LANES = 128
CHUNKS = 2
VMEM_LIMIT = 127 * 512 * 1024


def halves(table):
    high = table.astype(np.float32).astype(ml_dtypes.bfloat16)
    low = (table - high.astype(np.float64)).astype(np.float32).astype(ml_dtypes.bfloat16)
    return (high, low)


def wave(rows, cols, length):
    angle = (rows[:, None] * cols[None, :] % length) * (2.0 * math.pi / length)
    return (np.cos(angle), np.sin(angle))


class Plan:
    def __init__(self, slabs, cells, panels, cell_planes, cell_cols, near, nx, nz, ny):
        self.slabs, self.cells = (slabs, cells)
        self.panels, self.cell_planes, self.cell_cols, self.near = (panels, cell_planes, cell_cols, near)
        self.nx, self.ny, self.nz = (nx, ny, nz)
        self.slots = slabs * cells
        self.tx_chunk = TX // CHUNKS
        self.width = cell_planes * self.tx_chunk
        self.y_lanes = LANES // self.width if self.width else 1
        self.row_block = LANES // NZC
        self.step_blocks = self.y_lanes // TY
        self.steps = cell_cols // (LANES * self.step_blocks) if self.step_blocks else 0
        self.x_chunk = nx // CHUNKS
        self.ky_local = ny // slabs
        self.piece_rows = 2 * self.steps * self.row_block
        self.half = slabs // 2
        self.outer = math.gcd(self.half, 2)
        self.inner = self.half // self.outer

    def fits(self):
        return (
            self.slots * 2 == self.nz
            and self.cell_planes == 8
            and self.step_blocks * TY * self.width == LANES
            and self.slabs % self.y_lanes == 0
            and self.ky_local % 8 == 0
            and self.steps * self.step_blocks * LANES == self.cell_cols
            and self.x_chunk % LANES == 0
            and self.nx == self.ny == 4 * LANES
            and self.ny % 1024 == self.nx % 1024 == 512
        )

    def depth_tables(self):
        depth = np.arange(NZC)[None, :] * TZ + np.arange(TZ)[:, None]
        scale = 1.0 / (self.nx * self.ny * self.nz)
        forward = np.zeros((self.slots, 2, self.row_block, TZ, self.row_block, NZC))
        backward = np.zeros_like(forward)
        for freq in range(self.slots):
            angle = (freq * depth % self.nz) * (2.0 * math.pi / self.nz)
            real, imag = (np.cos(angle), -np.sin(angle))
            factor = 2.0 * scale
            if freq == 0:
                imag = np.cos(depth * math.pi)
                factor = scale
            for row in range(self.row_block):
                forward[freq, 0, row, :, row, :] = real
                forward[freq, 1, row, :, row, :] = imag
                backward[freq, 0, row, :, row, :] = factor * real
                backward[freq, 1, row, :, row, :] = factor * imag
        shape = (self.slots * 2 * self.row_block, TZ * LANES)
        return (forward.reshape(shape), backward.reshape(shape))

    def y_rows(self):
        parity, cell, step, block, tile, row = np.meshgrid(
            *[np.arange(n) for n in (2, self.cells, self.steps, self.step_blocks, TY // 2, self.row_block)],
            indexing="ij",
        )
        cell_row = ((cell * self.steps + step) * self.step_blocks + block) * self.row_block + row
        return (cell_row * TY + 2 * tile + parity).reshape(2, -1)

    def x_columns(self):
        parity, slab, tile, plane = np.meshgrid(
            *[np.arange(n) for n in (2, self.slabs, TX // 2, self.cell_planes)], indexing="ij"
        )
        return ((slab * self.cell_planes + plane) * TX + 2 * tile + parity).reshape(2, -1)

    def row_of(self, cell, step, place):
        block, tile = (place // TY, place % TY)
        inner = (cell * self.steps + step) * self.step_blocks + block
        return (tile % 2) * (self.ny // 2) + (inner * (TY // 2) + tile // 2) * self.row_block


def split(value):
    high = value.astype(jnp.bfloat16)
    low = (value - high.astype(jnp.float32)).astype(jnp.bfloat16)
    return (high, low)


def product(left, right, dims=((1,), (0,))):
    first = jnp.concatenate([left[0], left[0], left[1]], axis=dims[0][0])
    second = jnp.concatenate([right[0], right[1], right[0]], axis=dims[1][0])
    return lax.dot_general(first, second, (dims, ((), ())), preferred_element_type=jnp.float32)


def swap_groups(parts, width):
    count = len(parts)
    lane = lax.broadcasted_iota(jnp.int32, parts[0].shape, 1)
    parts = list(parts)
    step = count // 2
    while step >= 1:
        shift = step * width
        upper = (lane // shift) % 2 == 1
        for i in range(count):
            if i & step:
                continue
            first, second = (parts[i], parts[i + step])
            parts[i] = jnp.where(upper, pltpu.roll(second, shift, 1), first)
            parts[i + step] = jnp.where(upper, second, pltpu.roll(first, LANES - shift, 1))
        step //= 2
    return parts


def tile_copies(plan, chunk, projection, held, sems, parts):
    count = TY * TZ // parts
    copies = []
    for tx in range(plan.tx_chunk):
        for part in range(parts):
            rows = pl.ds(part * count, count)
            source = projection.at[:, tx, chunk, rows]
            copies.append(pltpu.make_async_copy(source, held.at[tx, :, rows], sems.at[len(copies)]))
    return copies


def project_kernel(plan, chunk, *refs):
    edges = chunk == CHUNKS - 1
    count_in = 5 if edges else 4
    arrays_in, projection, out = (refs[:count_in], refs[count_in], refs[count_in + 1])
    scratch, held, sems = refs[count_in + 2 : count_in + 5]
    arrays = refs[count_in + 5 :]
    charges, counts, high, low = arrays[:4]
    planes = plan.cell_planes
    copies = tile_copies(plan, chunk, projection, held, sems, TY)
    loads = [
        pltpu.make_async_copy(source, place, sems.at[len(copies) + n])
        for n, (source, place) in enumerate(zip(arrays_in, arrays))
    ]
    for copy in loads[:2] + copies + loads[2:]:
        copy.start()
    for copy in loads[:2]:
        copy.wait()
    for n, copy in enumerate(copies):
        copy.wait()

        def body(place, carry, tx=n // TY, ty=n % TY):
            lanes = pl.ds(pl.multiple_of(place * LANES, LANES), LANES)
            count = counts[:, lanes]
            own = [jnp.where(count > p, charges[p, :, lanes], 0.0) for p in range(plan.panels)]
            row = ((place * TY + ty) * plan.tx_chunk + tx) * planes
            rows = pl.ds(pl.multiple_of(row, planes), planes)
            for tz in range(TZ):
                t = ty * TZ + tz
                total = held[tx, 0, t, :, lanes] * own[0]
                for p in range(1, plan.panels):
                    total = total + held[tx, p, t, :, lanes] * own[p]
                scratch[rows, tz * LANES : (tz + 1) * LANES] = total
            return carry

        lax.fori_loop(0, plan.steps * plan.step_blocks, body, 0, unroll=True)
    for copy in loads[2:]:
        copy.wait()
    spectra = product(split(scratch[...]), (high[...], low[...])).T
    shape = (plan.slots, 2, plan.row_block, LANES)
    for step in range(plan.steps):
        value = spectra[:, step * LANES : (step + 1) * LANES].reshape(shape)
        for part in range(2):
            row = (part * plan.steps + step) * plan.row_block
            out[:, row : row + plan.row_block] = value[:, part]
    if edges:
        out[:, plan.piece_rows :] = arrays[4][...]


def held_shape(plan):
    cols = plan.steps * plan.step_blocks * LANES
    return (plan.tx_chunk, plan.panels, TY * TZ, plan.cell_planes, cols)


def piece_shape(plan):
    return (plan.slots, 2, plan.steps, plan.row_block, LANES)


def whole_spec(shape):
    return pl.BlockSpec(shape, lambda i: (0,) * len(shape))


def projection_call(plan, kernel, name, arrays, projection, out_shape):
    return pl.pallas_call(
        kernel,
        in_specs=[pl.BlockSpec(memory_space=pl.ANY)] * (len(arrays) + 1),
        out_specs=pl.BlockSpec(memory_space=pltpu.VMEM),
        out_shape=jax.ShapeDtypeStruct(out_shape, jnp.float32),
        scratch_shapes=[
            pltpu.VMEM((plan.steps * LANES, TZ * LANES), jnp.float32),
            pltpu.VMEM(held_shape(plan), jnp.float32),
            pltpu.SemaphoreType.DMA((plan.tx_chunk * TY + len(arrays),)),
        ]
        + [pltpu.VMEM(array.shape, array.dtype) for array in arrays],
        compiler_params=pltpu.CompilerParams(vmem_limit_bytes=VMEM_LIMIT),
        cost_estimate=pl.CostEstimate(
            flops=2 * math.prod(held_shape(plan)),
            bytes_accessed=4 * math.prod(held_shape(plan)),
            transcendentals=0,
        ),
        name=name,
    )(*arrays, projection)


def project(plan, chunk, charges, counts, projection, high, low, edges):
    kernel = functools.partial(project_kernel, plan, chunk)
    arrays = [charges, counts, high, low] + ([] if edges is None else [edges])
    rows = plan.piece_rows + (0 if edges is None else edges.shape[1])
    return projection_call(plan, kernel, "project_depth", arrays, projection, (plan.slots, rows, LANES))


def far_sign(plan, me_ref):
    slab = lax.rem(me_ref[0], plan.slabs)
    return jnp.where(slab >= plan.half, -1.0, 1.0)


def forward_plane(plan, me_ref, pieces, y_table, x_table, rows_ref, freq_ref, waits=()):
    special = me_ref[0] == 0
    sign = far_sign(plan, me_ref)
    rows = 2 * plan.steps * plan.row_block
    width = plan.x_chunk
    middle = plan.ny // 2
    for cell in range(plan.cells):
        for group in range(plan.slabs // plan.y_lanes):
            first = cell * plan.slabs + group * plan.y_lanes
            parts = [pieces[first + i, :rows] for i in range(plan.y_lanes)]
            parts = swap_groups(parts, plan.width)
            for place, value in enumerate(parts):
                if place % 2 == 1:
                    value = value * sign
                for part in range(2):
                    for step in range(plan.steps):
                        source = (part * plan.steps + step) * plan.row_block
                        row = plan.row_of(cell, step, place)
                        col = part * width + group * LANES
                        rows_ref[row : row + plan.row_block, col : col + LANES] = value[
                            source : source + plan.row_block
                        ]
    for copy in waits:
        copy.wait()
    sums = product((y_table[0][...], y_table[1][...]), split(rows_ref[...]))
    cos_re, cos_im = (sums[:middle, :width], sums[:middle, width:])
    sin_re, sin_im = (sums[middle:, :width], sums[middle:, width:])
    first = lax.broadcasted_iota(jnp.int32, (middle, width), 0) == 0

    @pl.when(jnp.logical_not(special))
    def _():
        freq_ref[:middle] = jnp.where(first, cos_re, cos_re + sin_im)
        freq_ref[middle : 2 * middle] = jnp.where(first, cos_im, cos_im - sin_re)
        freq_ref[2 * middle : 3 * middle] = jnp.where(first, sin_re, cos_re - sin_im)
        freq_ref[3 * middle :] = jnp.where(first, sin_im, cos_im + sin_re)

    @pl.when(special)
    def _():
        freq_ref[:middle] = cos_re
        freq_ref[middle : 2 * middle] = jnp.where(first, sin_re, -sin_re)
        freq_ref[2 * middle : 3 * middle] = cos_im
        freq_ref[3 * middle :] = sin_im

    return product(split(freq_ref[...]), (x_table[0][0], x_table[1][0]))


def backward_plane(plan, me_ref, freqs, x_table, y_table, out, rows_ref):
    special = me_ref[0] == 0
    sign = far_sign(plan, me_ref)
    width = plan.x_chunk
    middle = plan.ny // 2
    sums = product(split(freqs), (x_table[0][0], x_table[1][0]))
    parts = []
    for mirrored, turn in ((0, 1.0), (1, -1.0)):
        re = slice(2 * mirrored * middle, (2 * mirrored + 1) * middle)
        im = slice((2 * mirrored + 1) * middle, (2 * mirrored + 2) * middle)
        parts.append(sums[re, :width] - turn * sums[im, width:])
        parts.append(sums[im, :width] + turn * sums[re, width:])
    re_n, im_n, re_m, im_m = parts
    first = lax.broadcasted_iota(jnp.int32, (middle, width), 0) == 0

    @pl.when(jnp.logical_not(special))
    def _():
        rows_ref[:middle, :width] = jnp.where(first, re_n, re_n + re_m)
        rows_ref[:middle, width:] = jnp.where(first, im_n, im_n + im_m)
        rows_ref[middle:, :width] = jnp.where(first, -re_m, im_n - im_m)
        rows_ref[middle:, width:] = jnp.where(first, -im_m, re_m - re_n)

    @pl.when(special)
    def _():
        rows_ref[:middle, :width] = jnp.where(first, re_n, 2.0 * re_n)
        rows_ref[:middle, width:] = jnp.where(first, re_m, 2.0 * re_m)
        rows_ref[middle:, :width] = jnp.where(first, -im_n, 2.0 * im_n)
        rows_ref[middle:, width:] = jnp.where(first, -im_m, -2.0 * im_m)

    rows_ref[...] = product((y_table[0][...], y_table[1][...]), split(rows_ref[...]))
    for cell in range(plan.cells):
        for group in range(plan.slabs // plan.y_lanes):
            parts = []
            for place in range(plan.y_lanes):
                tiles = []
                for part in range(2):
                    for step in range(plan.steps):
                        row = plan.row_of(cell, step, place)
                        col = part * width + group * LANES
                        tiles.append(rows_ref[row : row + plan.row_block, col : col + LANES])
                value = jnp.concatenate(tiles, axis=0)
                parts.append(value * sign if place % 2 == 1 else value)
            parts = swap_groups(parts, plan.width)
            first = cell * plan.slabs + group * plan.y_lanes
            for i in range(plan.y_lanes):
                out[first + i] = parts[i].reshape(2, plan.steps, plan.row_block, LANES)


def first_plane_kernel(plan, me_ref, pieces, y_high, y_low, x_high, x_low, out, rows_ref, freq_ref):
    out[...] = forward_plane(plan, me_ref, pieces, (y_high, y_low), (x_high, x_low), rows_ref, freq_ref)


def middle_plane_kernel(plan, me_ref, *refs):
    late, refs = (refs[:10], refs[10:])
    strips, refs = (refs[: plan.inner], refs[plan.inner :])
    blocks, refs = (refs[: plan.outer], refs[plan.outer :])
    out, rest, rows_ref, freq_ref, sum_ref, rest_ref, weights = refs[:7]
    held, sems = (refs[7:17], refs[17])
    pieces, yf_high, yf_low, xf_high, xf_low, even, xb_high, xb_low, yb_high, yb_low = held
    slab = lax.rem(me_ref[0], plan.slabs)
    place = lax.rem(slab, plan.half)
    outer_id, inner_id = (place // plan.inner, lax.rem(place, plan.inner))
    copies = [pltpu.make_async_copy(late[n], held[n], sems.at[n]) for n in range(len(held))]
    count = plan.ky_local
    placed = []
    for i in range(plan.inner):
        for j in range(plan.outer):
            owner = lax.rem(outer_id - j + plan.outer, plan.outer) * plan.inner
            owner = owner + lax.rem(inner_id - i + plan.inner, plan.inner)
            rows = pl.ds(pl.multiple_of(owner * count, count), count)
            for m, source in enumerate((strips[i].at[j], blocks[j].at[i])):
                sem = sems.at[len(held) + len(placed)]
                placed.append(pltpu.make_async_copy(source, weights.at[m, rows], sem))
    for copy in copies[:6] + placed + copies[6:]:
        copy.start()
    copies[0].wait()
    cell_first = me_ref[0] - slab
    tile = pieces[cell_first + jnp.where(slab < plan.half, plan.half, 0), plan.piece_rows :]
    parts = plan.nx // LANES
    own_edge = jnp.concatenate([tile[n : n + 1] for n in range(parts)], axis=1)
    edge = jnp.concatenate([tile[n : n + 1] for n in range(parts, 2 * parts)], axis=1)
    special = me_ref[0] == 0
    width = plan.x_chunk
    middle = plan.ny // 2
    x_table = (xf_high.at[pl.ds(0, 1)], xf_low.at[pl.ds(0, 1)])
    odd = forward_plane(
        plan, me_ref, pieces, (yf_high, yf_low), x_table, rows_ref, freq_ref, copies[1:5]
    )
    for copy in copies[5:6] + placed:
        copy.wait()
    row = lax.broadcasted_iota(jnp.int32, (middle, width), 0)
    at_first = row == 0
    for mirrored, turn in ((0, 1.0), (1, -1.0)):
        re = slice(2 * mirrored * middle, (2 * mirrored + 1) * middle)
        im = slice((2 * mirrored + 1) * middle, (2 * mirrored + 2) * middle)
        results = []
        for upper in range(2):
            cols = slice(upper * width, (upper + 1) * width)
            plane = weights[mirrored, :, cols]
            if mirrored:
                second = jnp.where(at_first, own_edge[:, cols], plane)
                weight = jnp.where(special, plane, second)
            else:
                weight = plane
                second = jnp.where(at_first & special, edge[0:1, cols], plane)
            re_sums = even[re] - odd[re] if upper else even[re] + odd[re]
            im_sums = even[im] - odd[im] if upper else even[im] + odd[im]
            real = weight * re_sums[:, :width] + (turn * second) * im_sums[:, width:]
            imag = second * im_sums[:, :width] - (turn * weight) * re_sums[:, width:]
            results.append((real, imag))
        for part, rows in enumerate((re, im)):
            below, above = (results[0][part], results[1][part])
            sum_ref[rows] = below + above
            rest_ref[rows] = below - above
    last = pltpu.make_async_copy(rest_ref, rest, sems.at[len(held) + 2 * plan.half])
    last.start()
    for copy in copies[6:]:
        copy.wait()
    backward_plane(plan, me_ref, sum_ref[...], (xb_high, xb_low), (yb_high, yb_low), out, rows_ref)
    last.wait()


def last_plane_kernel(plan, me_ref, freqs, x_high, x_low, y_high, y_low, out, rows_ref):
    backward_plane(plan, me_ref, freqs[...], (x_high, x_low), (y_high, y_low), out, rows_ref)


def plane_call(plan, kernel, name, me, ready, arrays, tables, late, out_specs, out_shapes, scratch, work):
    specs = [pl.BlockSpec(memory_space=pltpu.VMEM)] * len(ready)
    specs += [whole_spec(array.shape) for array in arrays]
    flat = []
    for pair, chunk in tables:
        for table in pair:
            if chunk is None:
                specs.append(whole_spec(table.shape))
            else:
                specs.append(pl.BlockSpec((1,) + table.shape[1:], lambda i, chunk=chunk: (chunk, 0, 0)))
            flat.append(table)
    specs += [pl.BlockSpec(memory_space=pl.ANY)] * len(late)
    size = sum(4 * array.size for array in list(ready) + list(arrays) + list(late))
    return pl.pallas_call(
        functools.partial(kernel, plan),
        grid=(1,) if tables else (),
        in_specs=[pl.BlockSpec(memory_space=pltpu.SMEM)] + specs,
        out_specs=out_specs,
        out_shape=[jax.ShapeDtypeStruct(shape, jnp.float32) for shape in out_shapes],
        scratch_shapes=scratch,
        compiler_params=pltpu.CompilerParams(vmem_limit_bytes=VMEM_LIMIT),
        cost_estimate=pl.CostEstimate(
            flops=work * 12 * plan.nx * plan.ny * plan.x_chunk,
            bytes_accessed=size + sum(2 * table.size for table in flat),
            transcendentals=0,
        ),
        name=name,
    )(me, *ready, *arrays, *flat, *late)


def gather_kernel(
    plan, chunk, sent, high_in, low_in, before_in, counts_in, projection, out, scratch, held, sems,
    pieces, high, low, before, counts
):
    planes = plan.cell_planes
    rows = plan.slots * 2 * plan.row_block
    first = plan.tx_chunk
    copies = tile_copies(plan, chunk, projection, held, sems, 1)
    pairs = ((sent, pieces), (high_in, high), (low_in, low), (before_in, before), (counts_in, counts))
    loads = [pltpu.make_async_copy(*pair, sems.at[first + n]) for n, pair in enumerate(pairs)]
    for copy in loads[:3] + copies + loads[3:]:
        copy.start()
    for copy in loads[:3]:
        copy.wait()
    columns = [pieces[:, :, step].reshape(rows, LANES) for step in range(plan.steps)]
    scratch[...] = product(split(jnp.concatenate(columns, axis=1).T), (high[...], low[...]))
    for copy in loads[3:]:
        copy.wait()
    for tx in range(plan.tx_chunk):
        copies[tx].wait()
        last = chunk == CHUNKS - 1 and tx == plan.tx_chunk - 1

        def body(place, carry, tx=tx, last=last):
            lanes = pl.ds(pl.multiple_of(place * LANES, LANES), LANES)
            far = [(before if tx == 0 else out)[p, :, lanes] for p in range(plan.panels)]
            for ty in range(TY):
                row = ((place * TY + ty) * plan.tx_chunk + tx) * planes
                rows_at = pl.ds(pl.multiple_of(row, planes), planes)
                for tz in range(TZ):
                    t = ty * TZ + tz
                    potential = scratch[rows_at, tz * LANES : (tz + 1) * LANES]
                    for p in range(plan.panels):
                        far[p] = far[p] + held[tx, p, t, :, lanes] * potential
            for p in range(plan.panels):
                out[p, :, lanes] = jnp.where(counts[:, lanes] > p, far[p], 0.0) if last else far[p]
            return carry

        lax.fori_loop(0, plan.steps * plan.step_blocks, body, 0, unroll=True)


def gather(plan, chunk, counts, before, projection, high, low, pieces):
    kernel = functools.partial(gather_kernel, plan, chunk)
    arrays = [pieces, high, low, before, counts]
    return projection_call(plan, kernel, "depth_gather", arrays, projection, before.shape)


def near_kernel(plan, extended, codes, blocks_ref, out):
    step = pl.program_id(0)
    lane = lax.broadcasted_iota(jnp.int32, (plan.cell_planes, LANES), 1)
    depth = lane % NZC
    digits = []
    for k in range(plan.near):
        code = codes[k]
        digits.append((code // 9, code // 3 % 3, code % 3))
    total = [None] * plan.panels
    for q in range(plan.panels):
        shifted = []
        for dx in range(3):
            before, here, after = (
                extended[q, dx, :, pl.ds(pl.multiple_of((step + i) * LANES, LANES), LANES)] for i in range(3)
            )
            up = jnp.where(lane < NZC, pltpu.roll(before, NZC, 1), pltpu.roll(here, NZC, 1))
            down = jnp.where(
                lane >= LANES - NZC, pltpu.roll(after, LANES - NZC, 1), pltpu.roll(here, LANES - NZC, 1)
            )
            for value in (up, here, down):
                under = jnp.where(
                    depth == 0, pltpu.roll(value, LANES - NZC + 1, 1), pltpu.roll(value, 1, 1)
                )
                over = jnp.where(
                    depth == NZC - 1, pltpu.roll(value, NZC - 1, 1), pltpu.roll(value, LANES - 1, 1)
                )
                shifted.append((under, value, over))
        for k in range(plan.near):
            digit_x, digit_y, digit_z = digits[k]

            def choose(digit, options):
                return jnp.where(digit == 0, options[0], jnp.where(digit == 1, options[1], options[2]))

            by_z = [choose(digit_z, options) for options in shifted]
            by_y = [choose(digit_y, by_z[3 * i : 3 * i + 3]) for i in range(3)]
            picked = choose(digit_x, by_y)
            for p in range(plan.panels):
                term = blocks_ref[k, p, q] * picked
                total[p] = term if total[p] is None else total[p] + term
    for p in range(plan.panels):
        out[p] = total[p]


def near_field(plan, extended, neighbours, near_blocks):
    return pl.pallas_call(
        functools.partial(near_kernel, plan),
        grid=(plan.cell_cols // LANES,),
        in_specs=[
            whole_spec(extended.shape),
            pl.BlockSpec((plan.near, plan.cell_planes, LANES), lambda i: (0, 0, i)),
            pl.BlockSpec(
                (plan.near, plan.panels, plan.panels, plan.cell_planes, LANES), lambda i: (0, 0, 0, 0, i)
            ),
        ],
        out_specs=pl.BlockSpec((plan.panels, plan.cell_planes, LANES), lambda i: (0, 0, i)),
        out_shape=jax.ShapeDtypeStruct((plan.panels, plan.cell_planes, plan.cell_cols), jnp.float32),
        compiler_params=pltpu.CompilerParams(vmem_limit_bytes=VMEM_LIMIT),
        cost_estimate=pl.CostEstimate(
            flops=2 * near_blocks.size, bytes_accessed=4 * near_blocks.size, transcendentals=0
        ),
        name="near_blocks",
    )(extended, neighbours, near_blocks)


def ring_pairs(axis):
    count = lax.axis_size(axis)
    up = [(i, (i + 1) % count) for i in range(count)]
    return (up, [(j, i) for i, j in up])


def extend_rows(plan, masked):
    up, down = ring_pairs("cell")
    first, last = (masked[:, :, :NZC], masked[:, :, -NZC:])
    if plan.cells == 2:
        both = lax.ppermute(jnp.concatenate([last, first], axis=2), "cell", up)
        return (both[:, :, :NZC], both[:, :, NZC:])
    return (lax.ppermute(last, "cell", up), lax.ppermute(first, "cell", down))


def extend_planes(plan, masked, left, right):
    rest = jnp.zeros((plan.panels, plan.cell_planes, LANES - NZC), jnp.float32)
    wide = jnp.concatenate([rest, left, masked, right, rest], axis=2)
    up, down = ring_pairs("slab")
    before = lax.ppermute(wide[:, -1:], "slab", up)
    after = lax.ppermute(wide[:, :1], "slab", down)
    whole = jnp.concatenate([before, wide, after], axis=1)
    planes = plan.cell_planes
    return jnp.stack([whole[:, i : i + planes] for i in range(3)], axis=1)


def pick_kernel(plan, ids_ref, by_depth, *refs):
    outs, sems = (refs[:-1], refs[-1])
    place = lax.rem(ids_ref[0], plan.half)
    first = ids_ref[0] - place
    copies = []
    for j in range(plan.outer):
        part = lax.rem(place // plan.inner + j, plan.outer) * plan.inner
        for i in range(plan.inner):
            n = len(copies)
            copies.append(
                pltpu.make_async_copy(by_depth.at[first + part + i], outs[j].at[i], sems.at[n])
            )
            freq = first + part + lax.rem(place + i, plan.inner)
            mirror = jnp.where(freq == 0, plan.nz // 2, plan.nz - freq)
            copies.append(
                pltpu.make_async_copy(by_depth.at[mirror], outs[plan.outer + i].at[j], sems.at[n + 1])
            )
    for copy in copies:
        copy.start()
    for copy in copies:
        copy.wait()


def pick_planes(plan, ids, spectrum):
    by_depth = jnp.transpose(spectrum, (1, 2, 0))
    shapes = [(plan.inner,) + by_depth.shape[1:]] * plan.outer
    shapes += [(plan.outer,) + by_depth.shape[1:]] * plan.inner
    picked = pl.pallas_call(
        functools.partial(pick_kernel, plan),
        in_specs=[pl.BlockSpec(memory_space=pltpu.SMEM), pl.BlockSpec(memory_space=pl.ANY)],
        out_specs=[pl.BlockSpec(memory_space=pltpu.VMEM)] * len(shapes),
        out_shape=[jax.ShapeDtypeStruct(shape, jnp.float32) for shape in shapes],
        scratch_shapes=[pltpu.SemaphoreType.DMA((2 * plan.half,))],
        cost_estimate=pl.CostEstimate(
            flops=0, bytes_accessed=8 * sum(math.prod(shape) for shape in shapes), transcendentals=0
        ),
        name="pick_planes",
    )(ids, by_depth)
    return (picked[: plan.outer], picked[plan.outer :])


def outer_shift(plan, value, j):
    if j == 0:
        return value
    pairs = []
    for source in range(plan.slabs):
        base = source // plan.half * plan.half
        pairs.append((source, base + (source - base + j * plan.inner) % plan.half))
    return lax.ppermute(value, "slab", pairs)


def inner_shift(plan, value, i):
    if i == 0:
        return value
    pairs = []
    for source in range(plan.slabs):
        base = source // plan.inner * plan.inner
        pairs.append((source, base + (source + i) % plan.inner))
    return lax.ppermute(value, "slab", pairs)


def edge_weights(plan, rows):
    middle = plan.nz // 2
    turned = jnp.concatenate([rows[middle : middle + 1], jnp.flip(rows, 0)], axis=0)[: plan.slots]
    shape = (plan.slots, plan.nx // LANES, LANES)
    plane = jnp.broadcast_to(rows[0].reshape(shape[1:]), shape)
    return jnp.concatenate([turned.reshape(shape), plane], axis=1)


def second_weights(plan, plain, mirror):
    slab = lax.axis_index("slab")
    strips = []
    for i in range(plan.inner):
        place = lax.rem(slab + i, plan.inner)
        rows = [lax.dynamic_slice_in_dim(block, place, 1, 0) for block in plain]
        strips.append(inner_shift(plan, jnp.concatenate(rows, axis=0), i))
    blocks = [outer_shift(plan, jnp.stack([m[j] for m in mirror]), j) for j in range(plan.outer)]
    return strips + blocks


def per_device(charges, counts, projection, near_blocks, neighbours, spectrum):
    panels, cell_planes, cell_cols = charges.shape
    cells, slabs = (lax.axis_size("cell"), lax.axis_size("slab"))
    nx, nz, local = spectrum.shape
    plan = Plan(slabs, cells, panels, cell_planes, cell_cols, neighbours.shape[0], nx, nz, local * slabs)
    if not plan.fits():
        return plain_device(charges, counts, projection, near_blocks, neighbours, spectrum)
    me = (lax.axis_index("cell") * slabs + lax.axis_index("slab")).astype(jnp.int32).reshape(1)
    forward_table, backward_table = plan.depth_tables()
    depth_forward, depth_backward = (halves(forward_table.T), halves(backward_table))
    y_rows, x_cols, low_ids = (plan.y_rows().reshape(-1), plan.x_columns(), np.arange(plan.ny // 2))
    cos_y, sin_y = wave(low_ids, y_rows, plan.ny)
    sin_y[0] = 1.0 - 2.0 * (y_rows % 2)
    y_forward = halves(np.concatenate([cos_y, sin_y], axis=0))
    y_backward = halves(np.concatenate([cos_y.T, -sin_y.T], axis=1))
    x_waves = [wave(cols, low_ids, plan.nx) for cols in x_cols]
    x_forward = halves(np.stack([np.concatenate(pair, axis=1) for pair in x_waves]))
    x_backward = halves(np.stack([np.concatenate([t.T for t in pair], axis=1) for pair in x_waves]))
    split_projection = projection.reshape(
        (panels, TX // CHUNKS, CHUNKS, TY * TZ, cell_planes, cell_cols)
    )
    axes = ("cell", "slab")

    def exchange(pieces):
        return lax.all_to_all(pieces, axes, split_axis=0, concat_axis=0, tiled=True)

    def values(*shapes):
        return [pltpu.VMEM(shape, jnp.float32) for shape in shapes]

    rows_shape = (plan.ny, 2 * plan.x_chunk)
    freq_shape = (2 * plan.ny, plan.x_chunk)
    both_shape = (2 * plan.ny, plan.nx)
    slot = lax.broadcasted_iota(jnp.int32, charges.shape, 0)
    masked = jnp.where(slot < counts[None], charges, 0.0)
    rows = jnp.transpose(spectrum[:, :, 0], (1, 0))
    first = project(plan, 0, charges, counts, split_projection, *depth_forward, None)
    first, late_me = lax.optimization_barrier((first, me))
    even_pieces = exchange(first)
    edges = edge_weights(plan, rows)
    second = project(plan, 1, charges, counts, split_projection, *depth_forward, edges)
    plain, mirror = pick_planes(plan, late_me, spectrum)
    plain = [outer_shift(plan, value, j) for j, value in enumerate(plain)]
    mirror = [inner_shift(plan, value, i) for i, value in enumerate(mirror)]
    second, masked = lax.optimization_barrier((second, masked))
    left, right = extend_rows(plan, masked)
    second, left, right, *moved = lax.optimization_barrier((second, left, right, *plain, *mirror))
    plain, mirror = (moved[: plan.outer], moved[plan.outer :])
    odd_pieces = exchange(second)
    strips = second_weights(plan, plain, mirror)
    in_vmem = pl.BlockSpec(memory_space=pltpu.VMEM)
    in_place = pl.BlockSpec(memory_space=pl.ANY)
    (even,) = plane_call(
        plan, first_plane_kernel, "even_planes", me, [], [even_pieces],
        [(y_forward, None), (x_forward, 0)], [], [whole_spec(both_shape)], [both_shape],
        values(rows_shape, freq_shape), 2,
    )
    late = [odd_pieces, *y_forward, x_forward[0][1:], x_forward[1][1:], even]
    late += [x_backward[0][:1], x_backward[1][:1], *y_backward]
    copies = [pltpu.VMEM(array.shape, array.dtype) for array in late]
    copies.append(pltpu.SemaphoreType.DMA((len(late) + 2 * plan.half + 1,)))
    back, rest = plane_call(
        plan, middle_plane_kernel, "middle_planes", me, [], [], [], late + strips, [in_vmem, in_place], [piece_shape(plan), freq_shape],
        values(rows_shape, freq_shape, freq_shape, freq_shape, (2, plan.ny // 2, plan.nx)) + copies, 4,
    )
    even_back = exchange(back)
    (back,) = plane_call(
        plan, last_plane_kernel, "odd_planes", me, [], [rest],
        [(x_backward, 1), (y_backward, None)], [], [whole_spec(piece_shape(plan))], [piece_shape(plan)],
        values(rows_shape), 2,
    )
    back, masked = lax.optimization_barrier((back, masked))
    extended = extend_planes(plan, masked, left, right)
    back, extended = lax.optimization_barrier((back, extended))
    odd_back = exchange(back)
    total = near_field(plan, extended, neighbours, near_blocks)
    total = gather(plan, 0, counts, total, split_projection, *depth_backward, even_back)
    return gather(plan, 1, counts, total, split_projection, *depth_backward, odd_back)


def padded(value, sides, width):
    for axis, dim in sides:
        count, length = (lax.axis_size(axis), value.shape[dim])
        up = [(i, (i + 1) % count) for i in range(count)]
        down = [(j, i) for i, j in up]
        last = lax.slice_in_dim(value, length - width, length, axis=dim)
        first = lax.slice_in_dim(value, 0, width, axis=dim)
        before = lax.ppermute(last, axis, up)
        after = lax.ppermute(first, axis, down)
        value = jnp.concatenate([before, value, after], axis=dim)
    return value


def wave_tables(row_count, col_count, length):
    products = (
        lax.broadcasted_iota(jnp.int32, (row_count, col_count), 0)
        * lax.broadcasted_iota(jnp.int32, (row_count, col_count), 1)
        % length
    )
    angle_rad = products.astype(jnp.float32) * (2.0 * math.pi / length)
    return (jnp.cos(angle_rad), jnp.sin(angle_rad))


def depth_rows(nz, freq_ids, valid, weights):
    depth_ids = lax.broadcasted_iota(jnp.int32, (freq_ids.shape[0], nz), 1)
    products = freq_ids[:, None] * depth_ids % nz
    angle_rad = products.astype(jnp.float32) * (2.0 * math.pi / nz)
    basis = jnp.stack([jnp.cos(angle_rad), -jnp.sin(angle_rad)])
    return (basis * valid[None, :, None], basis * weights[None, :, None])


def half_depth_tables(nz, cell_count):
    lower = nz // (2 * cell_count)
    row_ids = lax.broadcasted_iota(jnp.int32, (cell_count * (lower + 1),), 0)
    block_ids = row_ids // (lower + 1)
    slot_ids = row_ids % (lower + 1)
    freq_ids = jnp.where(slot_ids < lower, block_ids * lower + slot_ids, nz // 2)
    valid = jnp.where((slot_ids < lower) | (block_ids == 0), 1.0, 0.0).astype(jnp.float32)
    doubled = jnp.where((slot_ids < lower) & (freq_ids > 0), 2.0, 1.0).astype(jnp.float32)
    forward_table, backward_table = depth_rows(nz, freq_ids, valid, valid * doubled)
    return (forward_table, backward_table, freq_ids)


def combine_halves(first_part, second, orient):
    half_width = first_part.shape[-1] // 2
    real_part = first_part[..., :half_width] + orient * second[..., half_width:]
    imag_part = first_part[..., half_width:] - orient * second[..., :half_width]
    return jnp.concatenate([real_part, imag_part], axis=-1)


def transform_axis(pattern, cosine, sine_tab, values, orient):
    first_part = jnp.einsum(pattern, cosine, values, precision=lax.Precision.HIGHEST)
    second = jnp.einsum(pattern, sine_tab, values, precision=lax.Precision.HIGHEST)
    return combine_halves(first_part, second, orient)


def twiddle(values, twist_cos, twist_sin, orient):
    half_width = values.shape[-1] // 2
    real_part = values[..., :half_width]
    imag_part = values[..., half_width:]
    new_real = real_part * twist_cos + orient * imag_part * twist_sin
    new_imag = imag_part * twist_cos - orient * real_part * twist_sin
    return jnp.concatenate([new_real, new_imag], axis=-1)


def transform_rows(planes_block, cosine, sine_tab, orient):
    flat_rows = planes_block.reshape(-1, planes_block.shape[-1])
    first_part = jnp.dot(flat_rows, cosine, precision=lax.Precision.HIGHEST).reshape(
        planes_block.shape
    )
    second = jnp.dot(flat_rows, sine_tab, precision=lax.Precision.HIGHEST).reshape(
        planes_block.shape
    )
    real_part = first_part[:, 0] + orient * second[:, 1]
    imag_part = first_part[:, 1] - orient * second[:, 0]
    return jnp.stack([real_part, imag_part], axis=1)


def plain_device(charges, counts, projection, near_blocks, neighbours, spectrum):
    panels, cell_planes, cell_cols = charges.shape
    nx, nz, ny = (spectrum.shape[0], spectrum.shape[1], spectrum.shape[2] * lax.axis_size("slab"))
    planes = cell_planes * TX
    rows_cell = cell_cols // NZC
    slot_ids = lax.broadcasted_iota(jnp.int32, charges.shape, 0)
    panel_mask = (slot_ids < counts[None]).astype(jnp.float32)
    masked = charges * panel_mask
    tile_values = jnp.einsum("ptxc,pxc->txc", projection, masked, precision=lax.Precision.HIGHEST)
    grid_field = (
        tile_values.reshape(TX, TY, TZ, cell_planes, rows_cell, NZC)
        .transpose(3, 0, 5, 2, 4, 1)
        .reshape(planes, nz, rows_cell * TY)
    )
    cell_count = lax.axis_size("cell")
    forward_table, backward_table, freq_ids = half_depth_tables(nz, cell_count)
    depth_count = forward_table.shape[1] // cell_count
    spectra_z = jnp.einsum(
        "wkz,xzy->xwky", forward_table, grid_field, precision=lax.Precision.HIGHEST
    )
    cosine_y, sine_y = wave_tables(ny, ny, ny)
    pencils = transform_rows(
        lax.all_to_all(spectra_z, "cell", split_axis=2, concat_axis=3, tiled=True),
        cosine_y,
        sine_y,
        1.0,
    )
    columns = lax.all_to_all(pencils, "slab", split_axis=3, concat_axis=0, tiled=True)
    col_width = columns.shape[2] * columns.shape[3]
    flat_rows = columns.reshape(nx, 2 * col_width)
    first_row = lax.axis_index("cell") * depth_count
    kernel_ids = lax.dynamic_slice_in_dim(freq_ids, first_row, depth_count, 0)
    kernel = jnp.take(spectrum, kernel_ids, axis=1).reshape(nx, col_width) * (1.0 / (nx * ny * nz))
    kernel_both = jnp.concatenate([kernel, kernel], axis=1)
    slab_count = lax.axis_size("slab")
    local_rows = nx // slab_count
    cosine_s, sine_s = wave_tables(slab_count, slab_count, slab_count)
    cosine_r, sine_r = wave_tables(local_rows, local_rows, local_rows)
    twist_cos, twist_sin = wave_tables(slab_count, local_rows, nx)
    twist_cos = twist_cos[:, :, None]
    twist_sin = twist_sin[:, :, None]
    section_one = transform_axis(
        "ks,src->krc",
        cosine_s,
        sine_s,
        flat_rows.reshape(slab_count, local_rows, 2 * col_width),
        1.0,
    )
    section_one = twiddle(section_one, twist_cos, twist_sin, 1.0)
    section_two = transform_axis("jr,krc->jkc", cosine_r, sine_r, section_one, 1.0)
    weighted = section_two.reshape(nx, 2 * col_width) * kernel_both
    section_one = transform_axis(
        "rj,jkc->krc",
        cosine_r,
        sine_r,
        weighted.reshape(local_rows, slab_count, 2 * col_width),
        -1.0,
    )
    section_one = twiddle(section_one, twist_cos, twist_sin, -1.0)
    section_two = transform_axis("sk,krc->src", cosine_s, sine_s, section_one, -1.0)
    returned_x = section_two.reshape(nx, 2 * col_width)
    returned = lax.all_to_all(
        returned_x.reshape(columns.shape), "slab", split_axis=0, concat_axis=3, tiled=True
    )
    inverse_rows = transform_rows(returned, cosine_y, sine_y, -1.0)
    grid_potential = jnp.einsum(
        "wkz,xwky->xzy",
        backward_table,
        lax.all_to_all(inverse_rows, "cell", split_axis=3, concat_axis=2, tiled=True),
        precision=lax.Precision.HIGHEST,
    )
    tile_potential = (
        grid_potential.reshape(cell_planes, TX, NZC, TZ, rows_cell, TY)
        .transpose(1, 5, 3, 0, 4, 2)
        .reshape(TX * TY * TZ, cell_planes, cell_cols)
    )
    far_field = jnp.einsum(
        "ptxc,txc->pxc", projection, tile_potential, precision=lax.Precision.HIGHEST
    )
    block = masked.reshape(panels, cell_planes, rows_cell, NZC)
    extended = padded(block, (("slab", 1), ("cell", 2)), 1)
    flat_ext = extended.reshape(panels, -1)
    step_x = neighbours // 9 - 1
    step_y = neighbours // 3 % 3 - 1
    step_z = neighbours % 3 - 1
    plane_ids = lax.broadcasted_iota(jnp.int32, neighbours.shape, 1)
    col_ids = lax.broadcasted_iota(jnp.int32, neighbours.shape, 2)
    row_ids = col_ids // NZC
    depth_ids = col_ids % NZC
    near_ids = ((plane_ids + step_x + 1) * (rows_cell + 2) + row_ids + step_y + 1) * NZC + (
        depth_ids + step_z
    ) % NZC
    near_count = neighbours.shape[0]
    picked = jnp.take(flat_ext, near_ids.reshape(-1), axis=1).reshape(
        panels, near_count, cell_planes, cell_cols
    )
    near_field = jnp.einsum("kpqxc,qkxc->pxc", near_blocks, picked, precision=lax.Precision.HIGHEST)
    return (far_field + near_field) * panel_mask


def solution(mesh):
    in_specs = (
        P(None, "slab", "cell"),
        P("slab", "cell"),
        P(None, None, "slab", "cell"),
        P(None, None, None, "slab", "cell"),
        P(None, "slab", "cell"),
        P(None, None, "slab"),
    )
    out_specs = P(None, "slab", "cell")
    return jax.shard_map(
        per_device, mesh=mesh, in_specs=in_specs, out_specs=out_specs, check_vma=False
    )
```
